32 devices in a mesh: dp: 16 (over z, x, core), mp: 2 (over y).
Axes of the slice: x: 2, y: 2, z: 4, core: 2. Of those that a mesh axis runs over, the one named last changes fastest.
Arguments:
- source_rows: bfloat16 [2048, 16, 512], P('mp', 'dp'), may hold values from -6 to 6
- target_rows: bfloat16 [2048, 16, 512], P('mp', 'dp'), may hold values from -6 to 6
- source_segment: int32 [16, 2048], P('dp'), may hold values from 0 to 7, as said below
- target_segment: int32 [16, 2048], P('dp'), may hold values from 0 to 7, as said below
- running: int32 [2, 16, 2048], P(None, 'dp', 'mp'), may hold values 0 or 1
- enc_qkv: bfloat16 [3, 512, 512], P(None, None, 'mp'), may hold values from -0.25 to 0.25
- enc_proj: bfloat16 [512, 512], P('mp'), may hold values from -1 to 1
- enc_up: bfloat16 [512, 2048], P(None, 'mp'), may hold values from -0.25 to 0.25
- enc_down: bfloat16 [2048, 512], P('mp'), may hold values from -0.1875 to 0.1875
- enc_gains: float32 [2, 512], replicated, may hold values from 0.25 to 1.75
- enc_shifts: float32 [2, 512], replicated, may hold values from -1.8 to 1.8
- dec_qkv: bfloat16 [3, 512, 512], P(None, None, 'mp'), may hold values from -0.25 to 0.25
- dec_proj: bfloat16 [512, 512], P('mp'), may hold values from -1 to 1
- cross_query: bfloat16 [512, 512], P(None, 'mp'), may hold values from -0.25 to 0.25
- cross_kv: bfloat16 [2, 512, 512], P(None, None, 'mp'), may hold values from -0.25 to 0.25
- cross_proj: bfloat16 [512, 512], P('mp'), may hold values from -1 to 1
- dec_up: bfloat16 [512, 2048], P(None, 'mp'), may hold values from -0.25 to 0.25
- dec_down: bfloat16 [2048, 512], P('mp'), may hold values from -0.1875 to 0.1875
- dec_gains: float32 [3, 512], replicated, may hold values from 0.25 to 1.75
- dec_shifts: float32 [3, 512], replicated, may hold values from -1.8 to 1.8
- halt_weight: float32 [2, 512], replicated, may hold values from -0.25 to 0.25
- enc_cotangent: float32 [2048, 16, 512], P('mp', 'dp'), may hold values from -6 to 6
- dec_cotangent: float32 [2048, 16, 512], P('mp', 'dp'), may hold values from -6 to 6
Outputs:
- enc_states: bfloat16 [2048, 16, 512], P('mp', 'dp')
- dec_states: bfloat16 [2048, 16, 512], P('mp', 'dp')
- source_grad: float32 [2048, 16, 512], P('mp', 'dp')
- target_grad: float32 [2048, 16, 512], P('mp', 'dp')
- enc_qkv_grad: float32 [3, 512, 512], P(None, None, 'mp')
- enc_proj_grad: float32 [512, 512], P('mp')
- enc_up_grad: float32 [512, 2048], P(None, 'mp')
- enc_down_grad: float32 [2048, 512], P('mp')
- enc_gains_grad: float32 [2, 512], replicated
- enc_shifts_grad: float32 [2, 512], replicated
- dec_qkv_grad: float32 [3, 512, 512], P(None, None, 'mp')
- dec_proj_grad: float32 [512, 512], P('mp')
- cross_query_grad: float32 [512, 512], P(None, 'mp')
- cross_kv_grad: float32 [2, 512, 512], P(None, None, 'mp')
- cross_proj_grad: float32 [512, 512], P('mp')
- dec_up_grad: float32 [512, 2048], P(None, 'mp')
- dec_down_grad: float32 [2048, 512], P('mp')
- dec_gains_grad: float32 [3, 512], replicated
- dec_shifts_grad: float32 [3, 512], replicated
- halt_weight_grad: float32 [2, 512], replicated
The draws below stay inside these ranges and needn't reach their ends.
Inputs may be any that keep to these rules, and one draw needn't show every extreme that they name: Each row holds 8 sentences numbered 0 to 7 in order, each one position or more, in both source_segment and target_segment; a target sentence is paired with the source sentence of the same number. In every row one sentence begins within the first 256 positions and ends within the last 256. `target_segment`: as for source_segment, drawn independently.
All inputs are finite; a program needn't handle non-finite values. No bound on the sum of `running` on one device may be relied on, other than what follows from the above.
Results may differ from the reference program's by a relative error of at most 0.04.
Values may be sent and summed in bfloat16 or wider, within the bound.
No kernel may reach another device: no remote copies, remote signals or barrier semaphores. Data moves between devices by JAX's collectives and lax.ppermute only.
A program may use at most 256 MiB of HBM per device.

```python
import jax
import jax.numpy as jnp
from jax import lax

D = 512
FF = 2048
H = 8
DH = 64
L = 2048
SEGS = 8
ROWS = 16


def segment_rows(key):
    margin = L // 8
    split_keys = jax.random.split(key, 3)
    before = jax.random.randint(split_keys[0], (ROWS, 1), 0, SEGS)
    left_keys = jax.random.split(split_keys[1], ROWS)
    right_keys = jax.random.split(split_keys[2], ROWS)
    left_cuts = jax.vmap(lambda row_key: jax.random.permutation(row_key, margin - 1))(left_keys)[:, :SEGS - 1] + 1
    right_cuts = jax.vmap(lambda row_key: jax.random.permutation(row_key, margin - 1))(right_keys)[:, :SEGS - 1] + (L - margin + 1)
    left_cuts = jnp.sort(left_cuts, axis=1).astype(jnp.int32)
    right_cuts = jnp.sort(right_cuts, axis=1).astype(jnp.int32)
    cut_number = jnp.arange(1, SEGS, dtype=jnp.int32)[None, :]
    all_cuts = jnp.where(cut_number <= before, left_cuts, right_cuts)
    position = jnp.arange(L, dtype=jnp.int32)
    return jnp.sum((all_cuts[:, None, :] <= position[None, :, None]).astype(jnp.int32), axis=2)


def draw_source_segment(key, part):
    key = jax.random.fold_in(key, 11)
    return segment_rows(key)


def draw_target_segment(key, part):
    key = jax.random.fold_in(key, 23)
    return segment_rows(key)


def place_ends(values, key, smallest, high):
    place = [jax.random.randint(jax.random.fold_in(key, axis), (), 0, length) for axis, length in enumerate(values.shape)]
    widest = values.shape.index(max(values.shape))
    next_to = place[:widest] + [(place[widest] + 1) % values.shape[widest]] + place[widest + 1:]
    return values.at[tuple(place)].set(smallest).at[tuple(next_to)].set(high)


def shard_levels(key, dims, cuts, least, high):
    def one(dim, blocks):
        heights = jax.random.uniform(jax.random.fold_in(jax.random.fold_in(key, 6), dim), (blocks,), jnp.float32, least / len(cuts), high / len(cuts))
        return jnp.repeat(jnp.exp(heights), dims[dim] // blocks).reshape((-1,) + (1,) * (len(dims) - dim - 1))

    factor_of = one(*cuts[0])
    for cut in cuts[1:]:
        factor_of = factor_of * one(*cut)
    return factor_of


def scatter_about(key, dims, width, most, cuts=(), kind=jnp.bfloat16):
    array = width * jax.random.normal(key, dims, jnp.float32)
    if cuts:
        array = array * shard_levels(key, dims, cuts, -0.22, 0.18)
    return jnp.clip(array, -most, most).astype(kind)


def setup_inputs(seed: int = 0) -> dict:
    keys = jax.random.split(jax.random.key(seed), 24)
    return {
        "source_rows": scatter_about(keys[0], (L, ROWS, D), 1.0, 6.0, ((0, 2), (1, 16))),
        "target_rows": scatter_about(keys[1], (L, ROWS, D), 1.0, 6.0, ((0, 2), (1, 16))),
        "source_segment": draw_source_segment(jax.random.fold_in(keys[23], 71), 0),
        "target_segment": draw_target_segment(jax.random.fold_in(keys[23], 71), 0),
        "running": place_ends((jax.random.randint(keys[4], (2, ROWS, L), 0, 4) < 3).astype(jnp.int32), jax.random.fold_in(keys[4], 1), 0, 1),
        "enc_qkv": scatter_about(keys[5], (3, D, D), D ** -0.5, 0.25, ((2, 2),)),
        "enc_proj": scatter_about(keys[6], (D, D), (D // 16) ** -0.5, 1.0, ((0, 2),)),
        "enc_up": scatter_about(keys[7], (D, FF), D ** -0.5, 0.25, ((1, 2),)),
        "enc_down": scatter_about(keys[8], (FF, D), (FF // 2) ** -0.5, 0.1875, ((0, 2),)),
        "enc_gains": jnp.clip(1.0 + 0.15 * jax.random.normal(keys[9], (2, D), jnp.float32), 0.25, 1.75),
        "enc_shifts": scatter_about(keys[10], (2, D), 0.3, 1.8, (), jnp.float32),
        "dec_qkv": scatter_about(keys[11], (3, D, D), D ** -0.5, 0.25, ((2, 2),)),
        "dec_proj": scatter_about(keys[12], (D, D), (D // 16) ** -0.5, 1.0, ((0, 2),)),
        "cross_query": scatter_about(keys[13], (D, D), D ** -0.5, 0.25, ((1, 2),)),
        "cross_kv": scatter_about(keys[14], (2, D, D), D ** -0.5, 0.25, ((2, 2),)),
        "cross_proj": scatter_about(keys[15], (D, D), (D // 16) ** -0.5, 1.0, ((0, 2),)),
        "dec_up": scatter_about(keys[16], (D, FF), D ** -0.5, 0.25, ((1, 2),)),
        "dec_down": scatter_about(keys[17], (FF, D), (FF // 2) ** -0.5, 0.1875, ((0, 2),)),
        "dec_gains": jnp.clip(1.0 + 0.15 * jax.random.normal(keys[18], (3, D), jnp.float32), 0.25, 1.75),
        "dec_shifts": scatter_about(keys[19], (3, D), 0.3, 1.8, (), jnp.float32),
        "halt_weight": scatter_about(keys[20], (2, D), D ** -0.5, 0.25, (), jnp.float32),
        "enc_cotangent": scatter_about(keys[21], (L, ROWS, D), 1.0, 6.0, ((0, 2), (1, 16)), jnp.float32),
        "dec_cotangent": scatter_about(keys[22], (L, ROWS, D), 1.0, 6.0, ((0, 2), (1, 16)), jnp.float32),
    }


EPS = 1e-05
NEGATIVE = -1000000000.0

@jax.custom_vjp
def low(v):
    return lax.optimization_barrier(v.astype(jnp.bfloat16)).astype(jnp.float32)

@jax.custom_vjp
def low_back(v):
    return v

def low_keep(v):
    return (low(v), None)

def low_pass(kept, grad):
    return (grad,)

def back_keep(v):
    return (v, None)

def back_low(kept, grad):
    return (low(grad),)
low.defvjp(low_keep, low_pass)
low_back.defvjp(back_keep, back_low)

def mult(left, right):
    return jnp.dot(left, right, precision=lax.Precision.HIGHEST, preferred_element_type=jnp.float32)

def signal(position):
    half_width = D // 2
    inverse_rates = jnp.exp(jnp.arange(half_width, dtype=jnp.float32) * (-jnp.log(10000.0) / (half_width - 1)))
    angles = position[:, None] * inverse_rates[None, :]
    return jnp.concatenate([jnp.sin(angles), jnp.cos(angles)], axis=1)

def normalize(values, norm_gain, norm_shift):
    centred = values - lax.optimization_barrier(jnp.mean(values, axis=-1, keepdims=True))
    spread = lax.optimization_barrier(jnp.mean(centred * centred, axis=-1, keepdims=True))
    return centred * lax.rsqrt(spread + EPS) * norm_gain + norm_shift

def halting(running_now, initial, updated, weight):
    halt_prob = jax.nn.sigmoid(lax.optimization_barrier(jnp.sum(updated * weight, axis=-1, keepdims=True)))
    return initial + running_now * halt_prob * (updated - initial)

def attention(query_low, key_low, weight_query, weight_key, weight_value, weight_out, allowed):
    length = query_low.shape[0]
    queries = low(low_back(mult(query_low, weight_query))).reshape(length, H, DH)
    keys_low = low(low_back(mult(key_low, weight_key))).reshape(-1, H, DH)
    values_low = low(low_back(mult(key_low, weight_value))).reshape(-1, H, DH)
    scores = jnp.einsum('qhd,khd->hqk', queries, keys_low, precision=lax.Precision.HIGHEST, preferred_element_type=jnp.float32)
    scores = low_back(scores * DH ** (-0.5))
    scores = jnp.where(allowed[None], scores, NEGATIVE)
    highest = lax.optimization_barrier(jnp.max(scores, axis=2, keepdims=True))
    exponent = jnp.exp(scores - highest)
    probs = exponent / lax.optimization_barrier(jnp.sum(exponent, axis=2, keepdims=True))
    mixed = jnp.einsum('hqk,khd->qhd', low(probs), values_low, precision=lax.Precision.HIGHEST, preferred_element_type=jnp.float32)
    mixed = low(low_back(mixed.reshape(length, D)))
    return low_back(mult(mixed, weight_out))

def feed(source_low, weight_up, weight_down):
    hidden = low_back(mult(source_low, weight_up))
    return low_back(mult(low(jax.nn.gelu(hidden)), weight_down))

def row_forward(params, source, target, source_seg, target_seg, runs):
    enc_qkv, enc_proj, enc_up, enc_down, enc_gains, enc_shifts, dec_qkv, dec_proj, cross_query, cross_kv, cross_proj, dec_up, dec_down, dec_gains, dec_shifts, halt_weight = params
    position = jnp.arange(L, dtype=jnp.int32)
    embedding = signal(position.astype(jnp.float32)) + signal(jnp.ones((1,), jnp.float32))
    enc_start = source + embedding
    start_low = low(enc_start)
    enc_allowed = source_seg[:, None] == source_seg[None, :]
    branch = attention(start_low, start_low, enc_qkv[0], enc_qkv[1], enc_qkv[2], enc_proj, enc_allowed)
    enc_middle = normalize(enc_start + branch, enc_gains[0], enc_shifts[0])
    enc_last = normalize(enc_middle + feed(low(enc_middle), enc_up, enc_down), enc_gains[1], enc_shifts[1])
    enc_final = halting(runs[0][:, None], enc_start, enc_last, halt_weight[0])
    dec_start = target + embedding
    dec_low = low(dec_start)
    self_allowed = (target_seg[:, None] == target_seg[None, :]) & (position[None, :] <= position[:, None])
    branch = attention(dec_low, dec_low, dec_qkv[0], dec_qkv[1], dec_qkv[2], dec_proj, self_allowed)
    dec_middle = normalize(dec_start + branch, dec_gains[0], dec_shifts[0])
    cross_allowed = target_seg[:, None] == source_seg[None, :]
    branch = attention(low(dec_middle), low(enc_final), cross_query, cross_kv[0], cross_kv[1], cross_proj, cross_allowed)
    dec_mixed = normalize(dec_middle + branch, dec_gains[1], dec_shifts[1])
    dec_last = normalize(dec_mixed + feed(low(dec_mixed), dec_up, dec_down), dec_gains[2], dec_shifts[2])
    dec_final = halting(runs[1][:, None], dec_start, dec_last, halt_weight[1])
    return (enc_final, dec_final)

def reference(source_rows, target_rows, source_segment, target_segment, running, enc_qkv, enc_proj, enc_up, enc_down, enc_gains, enc_shifts, dec_qkv, dec_proj, cross_query, cross_kv, cross_proj, dec_up, dec_down, dec_gains, dec_shifts, halt_weight, enc_cotangent, dec_cotangent):
    params = (enc_qkv.astype(jnp.float32), enc_proj.astype(jnp.float32), enc_up.astype(jnp.float32), enc_down.astype(jnp.float32), enc_gains.astype(jnp.float32), enc_shifts.astype(jnp.float32), dec_qkv.astype(jnp.float32), dec_proj.astype(jnp.float32), cross_query.astype(jnp.float32), cross_kv.astype(jnp.float32), cross_proj.astype(jnp.float32), dec_up.astype(jnp.float32), dec_down.astype(jnp.float32), dec_gains.astype(jnp.float32), dec_shifts.astype(jnp.float32), halt_weight.astype(jnp.float32))
    sources = jnp.transpose(source_rows.astype(jnp.float32), (1, 0, 2))
    targets = jnp.transpose(target_rows.astype(jnp.float32), (1, 0, 2))
    runs_all = jnp.transpose(running, (1, 0, 2)).astype(jnp.float32)
    checked = jax.checkpoint(row_forward)

    def whole(weights, source_all, target_all):

        def one_row(carry, pieces):
            return (carry, checked(weights, *pieces))
        _, outputs = lax.scan(one_row, jnp.zeros((), jnp.float32), (source_all, target_all, source_segment, target_segment, runs_all))
        return outputs
    outputs, pullback = jax.vjp(whole, params, sources, targets)
    cotangents = (jnp.transpose(enc_cotangent.astype(jnp.float32), (1, 0, 2)), jnp.transpose(dec_cotangent.astype(jnp.float32), (1, 0, 2)))
    weight_grads, source_grad, target_grad = pullback(cotangents)
    return (jnp.transpose(outputs[0], (1, 0, 2)).astype(jnp.bfloat16), jnp.transpose(outputs[1], (1, 0, 2)).astype(jnp.bfloat16), jnp.transpose(source_grad, (1, 0, 2)), jnp.transpose(target_grad, (1, 0, 2)), weight_grads[0], weight_grads[1], weight_grads[2], weight_grads[3], weight_grads[4], weight_grads[5], weight_grads[6], weight_grads[7], weight_grads[8], weight_grads[9], weight_grads[10], weight_grads[11], weight_grads[12], weight_grads[13], weight_grads[14], weight_grads[15])
```

```python
import math
from functools import partial

import jax
import jax.numpy as jnp
from jax import lax
from jax.experimental import pallas as pl
from jax.experimental.pallas import tpu as pltpu
from jax.sharding import PartitionSpec as P

D = 512
DH = 64


EPS = 1e-05
NEGATIVE = -1000000000.0


def signal(position):
    half_width = D // 2
    inverse_rates = jnp.exp(
        jnp.arange(half_width, dtype=jnp.float32) * (-jnp.log(10000.0) / (half_width - 1))
    )
    angles = position[:, None] * inverse_rates[None, :]
    return jnp.concatenate([jnp.sin(angles), jnp.cos(angles)], axis=1)


def normalize(values, norm_gain, norm_shift):
    centred = values - jnp.mean(values, axis=-1, keepdims=True)
    spread = jnp.mean(centred * centred, axis=-1, keepdims=True)
    return centred * lax.rsqrt(spread + EPS) * norm_gain + norm_shift


def halting(running_now, initial, updated, weight):
    halt_prob = jax.nn.sigmoid(jnp.sum(updated * weight, axis=-1, keepdims=True))
    return initial + running_now * halt_prob * (updated - initial)


def dot_last(left, right):
    return lax.dot_general(
        left, right, (((left.ndim - 1,), (1,)), ((), ())), preferred_element_type=jnp.float32
    )


def collect(piece_rows):
    return lax.all_gather(piece_rows, "mp", axis=0, tiled=True)


def collect_grad(piece_rows):
    return lax.all_gather(piece_rows.astype(jnp.bfloat16), "mp", axis=0, tiled=True)


def project_out(hidden, weight, rows):

    def partial_term(begin_row, row_count):
        return jnp.dot(hidden, weight, preferred_element_type=jnp.float32)

    return lax.psum_scatter(
        partial_term(jnp.int32(0), lax.axis_size("mp") * rows).astype(jnp.bfloat16),
        "mp",
        scatter_dimension=0,
        tiled=True,
    ).astype(jnp.float32)


def project_back(gradients, matrices, rows):

    def partial_term(begin_row, row_count):
        summed = jnp.zeros(
            (row_count,) + gradients[0].shape[1:-1] + (matrices[0].shape[0],), jnp.float32
        )
        for gradient, matrix in zip(gradients, matrices):
            summed = summed + dot_last(gradient, matrix)
        return summed

    return lax.psum_scatter(
        partial_term(jnp.int32(0), lax.axis_size("mp") * rows).astype(jnp.bfloat16),
        "mp",
        scatter_dimension=0,
        tiled=True,
    ).astype(jnp.float32)


def to_pairs(values):
    length, row_count, width = values.shape
    return (
        values.reshape(length, row_count, width // DH, DH)
        .transpose(1, 2, 0, 3)
        .reshape(-1, length, DH)
    )


def from_pairs(values, row_count):
    pairs, length, unused = values.shape
    heads_here = pairs // row_count
    return (
        values.reshape(row_count, heads_here, length, DH)
        .transpose(2, 0, 1, 3)
        .reshape(length, row_count, heads_here * DH)
    )


def per_pair(segments, width):
    return jnp.repeat(segments, width // DH, axis=0)


def pair_scores(query_block, key_rows, segment_block, segment_keys, first_row, causal):
    scores = lax.dot_general(
        query_block, key_rows, (((1,), (1,)), ((), ())), preferred_element_type=jnp.float32
    )
    scores = scores * DH ** (-0.5)
    allowed = segment_block[:, None] == segment_keys[None, :]
    if causal:
        query_place = first_row + jnp.arange(query_block.shape[0], dtype=jnp.int32)
        key_place = jnp.arange(key_rows.shape[0], dtype=jnp.int32)
        allowed = allowed & (key_place[None, :] <= query_place[:, None])
    return jnp.where(allowed, scores, NEGATIVE)


def attend_pair(inputs, causal):
    query_rows, key_rows, value_rows, segment_query, segment_keys = inputs
    length = query_rows.shape[0]
    block_rows = min(512, length)
    blocks = length // block_rows
    firsts = jnp.arange(blocks, dtype=jnp.int32) * block_rows

    def one_block(pieces):
        query_block, segment_block, first_row = pieces
        scores = pair_scores(query_block, key_rows, segment_block, segment_keys, first_row, causal)
        highest = jnp.max(scores, axis=1, keepdims=True)
        exponent = jnp.exp(scores - highest)
        totals = jnp.sum(exponent, axis=1, keepdims=True)
        weights = (exponent / totals).astype(jnp.bfloat16)
        mixed = jnp.dot(weights, value_rows, preferred_element_type=jnp.float32)
        return (mixed.astype(jnp.bfloat16), (highest + jnp.log(totals))[:, 0])

    mixed, log_total = lax.map(
        one_block,
        (
            query_rows.reshape(blocks, block_rows, -1),
            segment_query.reshape(blocks, block_rows),
            firsts,
        ),
    )
    return (mixed.reshape(length, -1), log_total.reshape(length))


def attend_pair_back(inputs, causal):
    query_rows, key_rows, value_rows, mixed_grad, log_total, segment_query, segment_keys = inputs
    length = query_rows.shape[0]
    block_rows = min(512, length)
    blocks = length // block_rows
    firsts = jnp.arange(blocks, dtype=jnp.int32) * block_rows

    def one_block(carry, pieces):
        key_total, value_total = carry
        query_block, grad_block, log_block, segment_block, first_row = pieces
        scores = pair_scores(query_block, key_rows, segment_block, segment_keys, first_row, causal)
        probs = jnp.exp(scores - log_block[:, None])
        weights = probs.astype(jnp.bfloat16)
        prob_grad = lax.dot_general(
            grad_block, value_rows, (((1,), (1,)), ((), ())), preferred_element_type=jnp.float32
        )
        inner = jnp.sum(probs * prob_grad, axis=1, keepdims=True)
        score_grad = (probs * (prob_grad - inner)).astype(jnp.bfloat16)
        query_grad = jnp.dot(score_grad, key_rows, preferred_element_type=jnp.float32) * DH ** (
            -0.5
        )
        key_total = key_total + lax.dot_general(
            score_grad, query_block, (((0,), (0,)), ((), ())), preferred_element_type=jnp.float32
        ) * DH ** (-0.5)
        value_total = value_total + lax.dot_general(
            weights, grad_block, (((0,), (0,)), ((), ())), preferred_element_type=jnp.float32
        )
        return ((key_total, value_total), query_grad.astype(jnp.bfloat16))

    zeros_start = jnp.zeros(key_rows.shape, jnp.float32)
    (key_total, value_total), query_grad = lax.scan(
        one_block,
        (zeros_start, zeros_start),
        (
            query_rows.reshape(blocks, block_rows, -1),
            mixed_grad.reshape(blocks, block_rows, -1),
            log_total.reshape(blocks, block_rows),
            segment_query.reshape(blocks, block_rows),
            firsts,
        ),
    )
    return (
        query_grad.reshape(length, -1),
        key_total.astype(jnp.bfloat16),
        value_total.astype(jnp.bfloat16),
    )


def attention_forward(
    query_full,
    key_full,
    weight_query,
    weight_key,
    weight_value,
    weight_out,
    segment_query,
    segment_keys,
    causal,
    rows,
):
    queries = jnp.dot(query_full, weight_query, preferred_element_type=jnp.float32).astype(
        jnp.bfloat16
    )
    keys_low = jnp.dot(key_full, weight_key, preferred_element_type=jnp.float32).astype(
        jnp.bfloat16
    )
    values_low = jnp.dot(key_full, weight_value, preferred_element_type=jnp.float32).astype(
        jnp.bfloat16
    )
    width = queries.shape[2]
    row_count = queries.shape[1]
    mixed, log_total = lax.map(
        partial(attend_pair, causal=causal),
        (
            to_pairs(queries),
            to_pairs(keys_low),
            to_pairs(values_low),
            per_pair(segment_query, width),
            per_pair(segment_keys, width),
        ),
    )
    mixed = from_pairs(mixed, row_count)
    branch = project_out(mixed, weight_out, rows)
    return (branch, (queries, keys_low, values_low, mixed, log_total))


def attention_backward(
    branch_grad, kept, query_full, key_full, weight_out, segment_query, segment_keys, causal
):
    queries, keys_low, values_low, kept_mixed, log_total = kept
    grad_full = collect_grad(branch_grad)
    out_weight_grad = jnp.einsum(
        "lrc,lrd->cd", kept_mixed, grad_full, preferred_element_type=jnp.float32
    )
    mixed_grad = dot_last(grad_full, weight_out).astype(jnp.bfloat16)
    width = queries.shape[2]
    row_count = queries.shape[1]
    query_grad, key_grad, value_grad = lax.map(
        partial(attend_pair_back, causal=causal),
        (
            to_pairs(queries),
            to_pairs(keys_low),
            to_pairs(values_low),
            to_pairs(mixed_grad),
            log_total,
            per_pair(segment_query, width),
            per_pair(segment_keys, width),
        ),
    )
    query_grad = from_pairs(query_grad, row_count)
    key_grad = from_pairs(key_grad, row_count)
    value_grad = from_pairs(value_grad, row_count)
    weight_grads = (
        jnp.einsum("lrd,lrc->dc", query_full, query_grad, preferred_element_type=jnp.float32),
        jnp.einsum("lrd,lrc->dc", key_full, key_grad, preferred_element_type=jnp.float32),
        jnp.einsum("lrd,lrc->dc", key_full, value_grad, preferred_element_type=jnp.float32),
    )
    return (query_grad, key_grad, value_grad, weight_grads, out_weight_grad)


def feed_forward(source_full, weight_up, weight_down, rows):
    hidden = jnp.dot(source_full, weight_up, preferred_element_type=jnp.float32)
    active = jax.nn.gelu(hidden).astype(jnp.bfloat16)
    return (project_out(active, weight_down, rows), hidden)


def feed_backward(branch_grad, source_full, hidden, weight_up, weight_down, rows):
    grad_full = collect_grad(branch_grad)
    active, gelu_back = jax.vjp(jax.nn.gelu, hidden)
    active = active.astype(jnp.bfloat16)
    down_grad = jnp.einsum("lrf,lrd->fd", active, grad_full, preferred_element_type=jnp.float32)
    hidden_grad = gelu_back(dot_last(grad_full, weight_down))[0].astype(jnp.bfloat16)
    up_grad = jnp.einsum(
        "lrd,lrf->df", source_full, hidden_grad, preferred_element_type=jnp.float32
    )
    input_grad = project_back((hidden_grad,), (weight_up,), rows)
    return (input_grad, up_grad, down_grad)


def local(
    source_rows,
    target_rows,
    source_segment,
    target_segment,
    running,
    enc_qkv,
    enc_proj,
    enc_up,
    enc_down,
    enc_gains,
    enc_shifts,
    dec_qkv,
    dec_proj,
    cross_query,
    cross_kv,
    cross_proj,
    dec_up,
    dec_down,
    dec_gains,
    dec_shifts,
    halt_weight,
    enc_cotangent,
    dec_cotangent,
):
    rows = source_rows.shape[0]
    position = (lax.axis_index("mp") * rows + jnp.arange(rows, dtype=jnp.int32)).astype(jnp.float32)
    embedding = (signal(position) + signal(jnp.ones((1,), jnp.float32)))[:, None, :]
    runs_now = jnp.transpose(running, (0, 2, 1)).astype(jnp.float32)[..., None]
    enc_start = source_rows.astype(jnp.float32) + embedding
    enc_start_low = enc_start.astype(jnp.bfloat16)
    enc_start_full = collect(enc_start_low)
    enc_attn, enc_attn_kept = attention_forward(
        enc_start_full,
        enc_start_full,
        enc_qkv[0],
        enc_qkv[1],
        enc_qkv[2],
        enc_proj,
        source_segment,
        source_segment,
        False,
        rows,
    )
    enc_sum_one = enc_start + enc_attn
    enc_middle = normalize(enc_sum_one, enc_gains[0], enc_shifts[0])
    enc_middle_low = enc_middle.astype(jnp.bfloat16)
    enc_middle_full = collect(enc_middle_low)
    enc_ffn, enc_hidden = feed_forward(enc_middle_full, enc_up, enc_down, rows)
    enc_sum_two = enc_middle + enc_ffn
    enc_last = normalize(enc_sum_two, enc_gains[1], enc_shifts[1])
    enc_final = halting(runs_now[0], enc_start, enc_last, halt_weight[0])
    enc_states = enc_final.astype(jnp.bfloat16)
    enc_states_full = collect(enc_states)
    dec_start = target_rows.astype(jnp.float32) + embedding
    dec_start_low = dec_start.astype(jnp.bfloat16)
    dec_start_full = collect(dec_start_low)
    dec_self, dec_self_kept = attention_forward(
        dec_start_full,
        dec_start_full,
        dec_qkv[0],
        dec_qkv[1],
        dec_qkv[2],
        dec_proj,
        target_segment,
        target_segment,
        True,
        rows,
    )
    dec_sum_one = dec_start + dec_self
    dec_middle = normalize(dec_sum_one, dec_gains[0], dec_shifts[0])
    dec_middle_low = dec_middle.astype(jnp.bfloat16)
    dec_middle_full = collect(dec_middle_low)
    dec_cross, dec_cross_kept = attention_forward(
        dec_middle_full,
        enc_states_full,
        cross_query,
        cross_kv[0],
        cross_kv[1],
        cross_proj,
        target_segment,
        source_segment,
        False,
        rows,
    )
    dec_sum_two = dec_middle + dec_cross
    dec_mixed = normalize(dec_sum_two, dec_gains[1], dec_shifts[1])
    dec_mixed_low = dec_mixed.astype(jnp.bfloat16)
    dec_mixed_full = collect(dec_mixed_low)
    dec_ffn, dec_hidden = feed_forward(dec_mixed_full, dec_up, dec_down, rows)
    dec_sum_three = dec_mixed + dec_ffn
    dec_last = normalize(dec_sum_three, dec_gains[2], dec_shifts[2])
    dec_final = halting(runs_now[1], dec_start, dec_last, halt_weight[1])
    dec_states = dec_final.astype(jnp.bfloat16)
    unused, halt_back = jax.vjp(partial(halting, runs_now[1]), dec_start, dec_last, halt_weight[1])
    dec_start_grad, last_grad, dec_halt_grad = halt_back(dec_cotangent)
    unused, norm_back = jax.vjp(normalize, dec_sum_three, dec_gains[2], dec_shifts[2])
    sum_grad, dec_gain_three, dec_shift_three = norm_back(last_grad)
    ffn_input_grad, dec_up_grad, dec_down_grad = feed_backward(
        sum_grad, dec_mixed_full, dec_hidden, dec_up, dec_down, rows
    )
    mixed_grad = sum_grad + ffn_input_grad
    unused, norm_back = jax.vjp(normalize, dec_sum_two, dec_gains[1], dec_shifts[1])
    sum_grad, dec_gain_two, dec_shift_two = norm_back(mixed_grad)
    query_grad, key_grad, value_grad, cross_grads, cross_proj_grad = attention_backward(
        sum_grad,
        dec_cross_kept,
        dec_middle_full,
        enc_states_full,
        cross_proj,
        target_segment,
        source_segment,
        False,
    )
    middle_grad = sum_grad + project_back((query_grad,), (cross_query,), rows)
    enc_extra = project_back((key_grad, value_grad), (cross_kv[0], cross_kv[1]), rows)
    unused, norm_back = jax.vjp(normalize, dec_sum_one, dec_gains[0], dec_shifts[0])
    sum_grad, dec_gain_one, dec_shift_one = norm_back(middle_grad)
    query_grad, key_grad, value_grad, self_grads, dec_proj_grad = attention_backward(
        sum_grad,
        dec_self_kept,
        dec_start_full,
        dec_start_full,
        dec_proj,
        target_segment,
        target_segment,
        True,
    )
    target_grad = (
        sum_grad
        + dec_start_grad
        + project_back(
            (query_grad, key_grad, value_grad), (dec_qkv[0], dec_qkv[1], dec_qkv[2]), rows
        )
    )
    dec_qkv_grad = jnp.stack(self_grads)
    cross_query_grad = cross_grads[0]
    cross_kv_grad = jnp.stack([cross_grads[1], cross_grads[2]])
    enc_final_grad = enc_cotangent + enc_extra
    unused, halt_back = jax.vjp(partial(halting, runs_now[0]), enc_start, enc_last, halt_weight[0])
    enc_start_grad, last_grad, enc_halt_grad = halt_back(enc_final_grad)
    unused, norm_back = jax.vjp(normalize, enc_sum_two, enc_gains[1], enc_shifts[1])
    sum_grad, enc_gain_two, enc_shift_two = norm_back(last_grad)
    ffn_input_grad, enc_up_grad, enc_down_grad = feed_backward(
        sum_grad, enc_middle_full, enc_hidden, enc_up, enc_down, rows
    )
    middle_grad = sum_grad + ffn_input_grad
    unused, norm_back = jax.vjp(normalize, enc_sum_one, enc_gains[0], enc_shifts[0])
    sum_grad, enc_gain_one, enc_shift_one = norm_back(middle_grad)
    query_grad, key_grad, value_grad, self_grads, enc_proj_grad = attention_backward(
        sum_grad,
        enc_attn_kept,
        enc_start_full,
        enc_start_full,
        enc_proj,
        source_segment,
        source_segment,
        False,
    )
    source_grad = (
        sum_grad
        + enc_start_grad
        + project_back(
            (query_grad, key_grad, value_grad), (enc_qkv[0], enc_qkv[1], enc_qkv[2]), rows
        )
    )
    enc_qkv_grad = jnp.stack(self_grads)
    (
        enc_qkv_grad,
        enc_proj_grad,
        enc_up_grad,
        enc_down_grad,
        dec_qkv_grad,
        dec_proj_grad,
        cross_query_grad,
        cross_kv_grad,
        cross_proj_grad,
        dec_up_grad,
        dec_down_grad,
    ) = (
        lax.psum(enc_qkv_grad.astype(jnp.bfloat16), "dp").astype(jnp.float32),
        lax.psum(enc_proj_grad.astype(jnp.bfloat16), "dp").astype(jnp.float32),
        lax.psum(enc_up_grad.astype(jnp.bfloat16), "dp").astype(jnp.float32),
        lax.psum(enc_down_grad.astype(jnp.bfloat16), "dp").astype(jnp.float32),
        lax.psum(dec_qkv_grad.astype(jnp.bfloat16), "dp").astype(jnp.float32),
        lax.psum(dec_proj_grad.astype(jnp.bfloat16), "dp").astype(jnp.float32),
        lax.psum(cross_query_grad.astype(jnp.bfloat16), "dp").astype(jnp.float32),
        lax.psum(cross_kv_grad.astype(jnp.bfloat16), "dp").astype(jnp.float32),
        lax.psum(cross_proj_grad.astype(jnp.bfloat16), "dp").astype(jnp.float32),
        lax.psum(dec_up_grad.astype(jnp.bfloat16), "dp").astype(jnp.float32),
        lax.psum(dec_down_grad.astype(jnp.bfloat16), "dp").astype(jnp.float32),
    )
    enc_gains_grad, enc_shifts_grad, dec_gains_grad, dec_shifts_grad, halt_weight_grad = lax.psum(
        (
            jnp.stack([enc_gain_one, enc_gain_two]),
            jnp.stack([enc_shift_one, enc_shift_two]),
            jnp.stack([dec_gain_one, dec_gain_two, dec_gain_three]),
            jnp.stack([dec_shift_one, dec_shift_two, dec_shift_three]),
            jnp.stack([enc_halt_grad, dec_halt_grad]),
        ),
        ("dp", "mp"),
    )
    return (
        enc_states,
        dec_states,
        source_grad,
        target_grad,
        enc_qkv_grad,
        enc_proj_grad,
        enc_up_grad,
        enc_down_grad,
        enc_gains_grad,
        enc_shifts_grad,
        dec_qkv_grad,
        dec_proj_grad,
        cross_query_grad,
        cross_kv_grad,
        cross_proj_grad,
        dec_up_grad,
        dec_down_grad,
        dec_gains_grad,
        dec_shifts_grad,
        halt_weight_grad,
    )


BIG=-1e30
BF=jnp.bfloat16; F32=jnp.float32
NT=(((1,),(1,)),((),()))
NN=(((1,),(0,)),((),()))
TN=(((0,),(0,)),((),()))
def dg(a,b,d): return lax.dot_general(a,b,d,preferred_element_type=F32)

def fwd_kernel(c_ref,q_ref,ko_ref,kx_ref,vo_ref,vx_ref,qe_ref,ke_ref,o_ref,lse_ref,K,V,*,causal,bq,n,sub):
    qb=pl.program_id(1)
    half=n//2
    L=2*n
    c=c_ref[0]
    lane=lax.broadcasted_iota(jnp.int32,(1,128),1)
    left=lane<64
    @pl.when(qb==0)
    def _():
        for src_k,src_v,base in ((ko_ref,vo_ref,c),(kx_ref,vx_ref,1-c)):
            for j in range(2):
                pos=jnp.where(base==0,0 if j==0 else 3,1 if j==0 else 2)*half
                pos=pl.multiple_of(pos,half)
                kk=src_k[pl.ds(j*half,half),:]; vv=src_v[pl.ds(j*half,half),:]
                ke=ke_ref[pl.ds(pos,half),:]
                one=jnp.ones_like(vv)
                K[0,pl.ds(pos,half),:]=jnp.where(left,kk,ke)
                K[1,pl.ds(pos,half),:]=jnp.where(left,ke,kk)
                V[0,pl.ds(pos,half),:]=jnp.where(left,vv,one)
                V[1,pl.ds(pos,half),:]=jnp.where(left,one,vv)
    qp=q_ref[...]; qe=qe_ref[...]
    def finish(R,m,r0,rows):
        Re,Ro=R; me,mo=m
        lb=jnp.where(left,Ro,Re)
        O=jnp.where(left,Re,Ro)/pltpu.roll(lb,64,1)
        o_ref[pl.ds(r0,rows),:]=O.astype(BF)
        lse_ref[pl.ds(r0,rows),:]=jnp.where(left,mo,me)+jnp.log2(lb)
    def block(nk,diag_row):
        for r0 in range(0,bq,sub):
            R=[];M=[]
            for e in range(2):
                qq=(jnp.where(left,qp,qe) if e==0 else jnp.where(left,qe,qp))[r0:r0+sub]
                if diag_row is None:
                    S=dg(qq,K[e,:nk,:],NT)
                    m=jnp.max(S,axis=1,keepdims=True)
                    p=jnp.exp2(S-m).astype(BF)
                    R.append(dg(p,V[e,:nk,:],NN)); M.append(m)
                else:
                    S2=dg(qq,K[e,nk-half:nk,:],NT)
                    ri=lax.broadcasted_iota(jnp.int32,(sub,half),0)+(diag_row+r0)
                    ci=lax.broadcasted_iota(jnp.int32,(sub,half),1)
                    S2=jnp.where(ci<=ri,S2,BIG)
                    m=jnp.max(S2,axis=1,keepdims=True)
                    if nk>half:
                        S1=dg(qq,K[e,:nk-half,:],NT)
                        m=jnp.maximum(m,jnp.max(S1,axis=1,keepdims=True))
                        r=dg(jnp.exp2(S2-m).astype(BF),V[e,nk-half:nk,:],NN)+dg(jnp.exp2(S1-m).astype(BF),V[e,:nk-half,:],NN)
                    else:
                        r=dg(jnp.exp2(S2-m).astype(BF),V[e,nk-half:nk,:],NN)
                    R.append(r); M.append(m)
            finish(R,M,r0,sub)
    if not causal:
        block(L,None)
    else:
        per=half//bq
        chunk=qb//per
        pos=jnp.where(c==0,chunk*3,chunk+1)
        drow=(qb-chunk*per)*bq
        for t in range(4):
            @pl.when(pos==t)
            def _(t=t): block((t+1)*half,drow)

def attn_fwd(c,q,ko,kx,vo,vx,qe,ke,*,causal,bq=256,sub=None,vmem=100):
    n,D=q.shape; L=2*n
    sub=sub or bq
    np_=D//128
    kern=partial(fwd_kernel,causal=causal,bq=bq,n=n,sub=sub)
    full=pl.BlockSpec((n,128),lambda p,b:(0,p))
    qs=pl.BlockSpec((bq,128),lambda p,b:(b,p))
    return pl.pallas_call(kern,grid=(np_,n//bq),
        in_specs=[pl.BlockSpec(memory_space=pltpu.SMEM),qs,full,full,full,full,
            pl.BlockSpec((bq,128),lambda p,b:(b,0)),pl.BlockSpec((L,128),lambda p,b:(0,0))],
        out_specs=[qs,qs],
        out_shape=[jax.ShapeDtypeStruct((n,D),BF),jax.ShapeDtypeStruct((n,D),F32)],
        scratch_shapes=[pltpu.VMEM((2,L,128),BF),pltpu.VMEM((2,L,128),BF)],
        compiler_params=pltpu.CompilerParams(vmem_limit_bytes=56*1024*1024),
        cost_estimate=pl.CostEstimate(flops=4*n*L*D,bytes_accessed=n*D*2*8,transcendentals=n*L*8),
        name="attn_fwd_causal" if causal else "attn_fwd")(c,q,ko,kx,vo,vx,qe,ke)

def bwd_kernel(c_ref,q_ref,ko_ref,kx_ref,vo_ref,vx_ref,qe_ref,keo_ref,kex_ref,do_ref,o_ref,lse_ref,
     dq_ref,dko_ref,dkx_ref,dvo_ref,dvx_ref,Q,DO,DQT,*,causal,bk,n,sub,dqt):
    kb=pl.program_id(1); nb=n//bk
    half=n//2; L=2*n
    c=c_ref[0]
    lane=lax.broadcasted_iota(jnp.int32,(1,128),1)
    left=lane<64
    l64=lane%64
    @pl.when(kb==0)
    def _():
        lse=lse_ref[...]
        h=lse.astype(BF).astype(F32); r=lse-h; h2=r.astype(BF).astype(F32); h3=r-h2
        ext=jnp.where(l64==8,-h,jnp.where(l64==9,-h2,jnp.where(l64==10,-h3,qe_ref[...].astype(F32)))).astype(BF)
        qp=q_ref[...]
        Q[0]=jnp.where(left,qp,ext); Q[1]=jnp.where(left,ext,qp)
        dop=do_ref[...]
        pr=dop.astype(F32)*o_ref[...].astype(F32)
        hi=pr.astype(BF); lo=(pr-hi.astype(F32)).astype(BF)
        ii=lax.broadcasted_iota(jnp.int32,(128,128),0); jj=lax.broadcasted_iota(jnp.int32,(128,128),1)
        J=((ii<64)!=(jj<64)).astype(BF)
        dl=dg(hi,J,NN)+dg(lo,J,NN)
        h=dl.astype(BF).astype(F32); r=dl-h
        ext=jnp.where(l64==8,-h,jnp.where(l64==9,-r,0.0)).astype(BF)
        DO[0]=jnp.where(left,dop,ext); DO[1]=jnp.where(left,ext,dop)
        DQT[...]=jnp.zeros_like(DQT)
    own=kb<nb
    kp=jnp.where(own,ko_ref[...],kx_ref[...]); vp=jnp.where(own,vo_ref[...],vx_ref[...]); ke=jnp.where(own,keo_ref[...],kex_ref[...])
    one=jnp.ones_like(vp)
    Kx=(jnp.where(left,kp,ke),jnp.where(left,ke,kp))
    Vx=(jnp.where(left,vp,one),jnp.where(left,one,vp))
    if dqt: KT=kp.T
    def body(q0,rows,diag_off):
        acck=[];accv=[]
        for e in range(2):
            qq=Q[e,pl.ds(q0,rows),:]; dd=DO[e,pl.ds(q0,rows),:]
            S=dg(Kx[e],qq,NT)
            if diag_off is not None:
                ki=lax.broadcasted_iota(jnp.int32,S.shape,0)+diag_off
                qi=lax.broadcasted_iota(jnp.int32,S.shape,1)
                S=jnp.where(ki<=qi,S,BIG)
            p=jnp.exp2(S)
            dp=dg(Vx[e],dd,NT)
            ds=(p*dp).astype(BF)
            accv.append(dg(p.astype(BF),dd,NN))
            acck.append(dg(ds,qq,NN))
            if dqt:
                DQT[64*e:64*e+64,pl.ds(q0,rows)]+=dg(KT[64*e:64*e+64],ds,NN)
            else:
                DQT[e,pl.ds(q0,rows),:]+=dg(ds,Kx[e],TN)
        return jnp.where(left,acck[0],acck[1]),jnp.where(left,accv[0],accv[1])
    def put(dk,dv):
        dk=(dk*math.log(2.0)).astype(BF); dv=dv.astype(BF)
        @pl.when(own)
        def _(): dko_ref[...]=dk; dvo_ref[...]=dv
        @pl.when(jnp.logical_not(own))
        def _(): dkx_ref[...]=dk; dvx_ref[...]=dv
    if not causal:
        dk=dv=0
        for q0 in range(0,n,sub):
            a,b=body(q0,sub,None); dk=dk+a; dv=dv+b
        put(dk,dv)
    else:
        per=half//bk
        kbl=jnp.where(own,kb,kb-nb)
        j=kbl//per
        base=jnp.where(own,c,1-c)
        kpos=jnp.where(base==0,j*3,j+1)
        koff=(kbl-j*per)*bk
        pa=jnp.where(c==0,0,1); pb=jnp.where(c==0,3,2)
        def case(am,bm):
            dk=dv=0
            for q0,mode in ((0,am),(half,bm)):
                if mode==0: continue
                a,b=body(q0,half,koff if mode==1 else None); dk=dk+a; dv=dv+b
            if am==0 and bm==0: dk=dv=jnp.zeros((bk,128),F32)
            put(dk,dv)
        for am in range(3):
            for bm in range(3):
                if am>bm or (am==bm==1): continue
                if am>0 and bm!=2: continue
                ca=(kpos>pa,kpos==pa,kpos<pa)[am]; cb=(kpos>pb,kpos==pb,kpos<pb)[bm]
                @pl.when(jnp.logical_and(ca,cb))
                def _(am=am,bm=bm): case(am,bm)
    @pl.when(kb==2*nb-1)
    def _():
        if dqt:
            dq_ref[...]=(DQT[...]*0.125).T.astype(BF)
        else:
            dq_ref[...]=(jnp.where(left,DQT[0],DQT[1])*0.125).astype(BF)

def attn_bwd(c,q,ko,kx,vo,vx,qe,keo,kex,do,o,lse,*,causal,bk=256,sub=None,dqt=True):
    n,D=q.shape; L=2*n; np_=D//128; nb=n//bk
    sub=sub or n
    kern=partial(bwd_kernel,causal=causal,bk=bk,n=n,sub=sub,dqt=dqt)
    full=pl.BlockSpec((n,128),lambda p,b:(0,p))
    ow=pl.BlockSpec((bk,128),lambda p,b:(jnp.minimum(b,nb-1),p)); ot=pl.BlockSpec((bk,128),lambda p,b:(jnp.maximum(b-nb,0),p))
    keo_s=pl.BlockSpec((bk,128),lambda p,b:(jnp.minimum(b,nb-1),0)); kex_s=pl.BlockSpec((bk,128),lambda p,b:(jnp.maximum(b-nb,0),0))
    sh=jax.ShapeDtypeStruct((n,D),BF)
    return pl.pallas_call(kern,grid=(np_,2*nb),
        in_specs=[pl.BlockSpec(memory_space=pltpu.SMEM),full,ow,ot,ow,ot,
            pl.BlockSpec((n,128),lambda p,b:(0,0)),keo_s,kex_s,full,full,full],
        out_specs=[full,ow,ot,ow,ot],
        out_shape=[sh]*5,
        scratch_shapes=[pltpu.VMEM((2,n,128),BF),pltpu.VMEM((2,n,128),BF),pltpu.VMEM((128,n) if dqt else (2,n,128),F32)],
        compiler_params=pltpu.CompilerParams(vmem_limit_bytes=56*1024*1024),
        cost_estimate=pl.CostEstimate(flops=10*n*L*D,bytes_accessed=n*D*2*12,transcendentals=n*L*8),
        name="attn_bwd_causal" if causal else "attn_bwd")(c,q,ko,kx,vo,vx,qe,keo,kex,do,o,lse)


def split_rows(values, bit):
    half = values.shape[0] // 2
    keep = lax.dynamic_slice_in_dim(values, bit * half, half, 0)
    send = lax.dynamic_slice_in_dim(values, (1 - bit) * half, half, 0)
    return keep, send


def join_rows(mine, other, bit):
    return jnp.where(bit == 0, jnp.concatenate([mine, other]), jnp.concatenate([other, mine]))


class Place:
    def __init__(self, dp_size):
        self.dp_size = dp_size
        self.dp = lax.axis_index("dp")
        self.y = lax.axis_index("mp")
        self.c = self.dp % 2
        self.bits = [1 << b for b in range(1, dp_size.bit_length() - 1)]

    def flip(self, values, mask):
        return lax.ppermute(values, "dp", [(d, d ^ mask) for d in range(self.dp_size)])

    def core_swap(self, values):
        return self.flip(values, 1)

    def y_swap(self, values):
        return lax.ppermute(values, "mp", [(0, 1), (1, 0)])

    def move(self, values, pairs):
        perm = []
        for d in range(0, self.dp_size, 2):
            for (y0, c0), (y1, c1) in pairs:
                perm.append(((d + c0) * 2 + y0, (d + c1) * 2 + y1))
        return lax.ppermute(values, ("dp", "mp"), perm)

    def pick(self, v00, v01, v10, v11):
        return jnp.where(
            self.y == 0, jnp.where(self.c == 0, v00, v01), jnp.where(self.c == 0, v10, v11)
        )

    def to_row(self, low, high):
        a = self.move(high, [((0, 0), (0, 1)), ((1, 1), (1, 0))])
        b = self.move(low, [((1, 0), (0, 1)), ((0, 1), (1, 0))])
        e = self.move(high, [((1, 0), (0, 0)), ((0, 1), (1, 1))])
        return self.pick(low, a, b, e), self.pick(e, b, a, low)

    def from_row(self, first, second):
        a = self.move(
            jnp.where(self.y == 0, first, second), [((0, 1), (0, 0)), ((1, 0), (1, 1))]
        )
        by_core = jnp.where(self.c == 0, first, second)
        b = self.move(by_core, [((0, 1), (1, 0)), ((1, 0), (0, 1))])
        e = self.move(
            jnp.where(self.c == 0, second, first), [((0, 0), (1, 0)), ((1, 1), (0, 1))]
        )
        return a, b, e

    def native(self, first, second, a, b, e):
        return jnp.concatenate([self.pick(first, b, b, second), self.pick(a, e, e, a)])

    def other_half(self, weight, axis):
        size = weight.shape[axis] // 2
        piece = lax.dynamic_slice_in_dim(weight, self.c * size, size, axis)
        near = self.y_swap(piece)
        far = self.core_swap(near)
        return jnp.where(
            self.c == 0,
            jnp.concatenate([near, far], axis=axis),
            jnp.concatenate([far, near], axis=axis),
        )

    def reduce_bucket(self, own, other):
        rows = own.shape[0]
        own_keep, own_send = split_rows(own, self.c)
        other_keep, other_send = split_rows(other, self.c)
        got = self.core_swap(jnp.concatenate([own_send, other_send]).astype(BF))
        own_keep = own_keep + got[: rows // 2].astype(F32)
        other_keep = other_keep + got[rows // 2 :].astype(F32)
        total = own_keep + self.y_swap(other_keep.astype(BF)).astype(F32)
        for mask in self.bits:
            keep, send = split_rows(total, (self.dp // mask) % 2)
            total = keep + self.flip(send.astype(BF), mask).astype(F32)
        total = total.astype(BF)
        for mask in self.bits[::-1] + [1]:
            total = join_rows(total, self.flip(total, mask), (self.dp // mask) % 2)
        return total.astype(F32)

    def reduce_all(self, values):
        for mask in [1] + self.bits:
            values = values + self.flip(values, mask)
        return values + self.y_swap(values)


def rows_of(grad):
    if grad.ndim == 3:
        kinds, depth, width = grad.shape
        folded = jnp.concatenate([grad[:, : depth // 2], grad[:, depth // 2 :]], axis=2)
        return folded.reshape(kinds * depth // 2, 2 * width)
    depth, width = grad.shape
    if width == D:
        return grad
    if width < D:
        return jnp.concatenate([grad[: depth // 2], grad[depth // 2 :]], axis=1)
    return jnp.concatenate([grad[:, :D], grad[:, D:]], axis=0)


def rows_back(rows, shape):
    if len(shape) == 3:
        kinds, depth, width = shape
        folded = rows.reshape(kinds, depth // 2, 2 * width)
        return jnp.concatenate([folded[..., :width], folded[..., width:]], axis=1)
    depth, width = shape
    if width == D:
        return rows
    if width < D:
        return jnp.concatenate([rows[:, :width], rows[:, width:]], axis=0)
    return jnp.concatenate([rows[:depth], rows[depth:]], axis=1)


def extensions(segments):
    lane = jnp.arange(128, dtype=jnp.int32)[None, :] % DH
    same = segments[:, None] == lane
    for_query = jnp.where((lane < 8) & ~same, BIG, 0.0).astype(BF)
    for_key = jnp.where(lane < 8, same.astype(F32), jnp.where(lane < 11, 1.0, 0.0)).astype(BF)
    return for_query, for_key


def dots(left, right):
    return jnp.dot(left, right, preferred_element_type=F32)


def dots_t(left, right):
    return lax.dot_general(left, right, (((1,), (1,)), ((), ())), preferred_element_type=F32)


def weight_dots(left, right):
    return lax.dot_general(left, right, (((0,), (0,)), ((), ())), preferred_element_type=F32)


Q_SCALE = DH**-0.5 * math.log2(math.e)


def chip_rows(
    source_rows,
    target_rows,
    source_segment,
    target_segment,
    running,
    enc_qkv,
    enc_proj,
    enc_up,
    enc_down,
    enc_gains,
    enc_shifts,
    dec_qkv,
    dec_proj,
    cross_query,
    cross_kv,
    cross_proj,
    dec_up,
    dec_down,
    dec_gains,
    dec_shifts,
    halt_weight,
    enc_cotangent,
    dec_cotangent,
    *,
    dp_size,
):
    at = Place(dp_size)
    rows = source_rows.shape[0]
    quarter = rows // 2
    length = 2 * rows
    core = at.c.astype(jnp.int32).reshape(1)

    def to_row(values):
        first, second = at.to_row(values[:quarter], values[quarter:])
        return jnp.concatenate([first, second])

    source = to_row(source_rows[:, 0]).astype(F32)
    enc_qkv_other = at.other_half(enc_qkv, 1)
    segments = jnp.concatenate([source_segment, target_segment])
    segments = jnp.where(at.c == at.y, segments, at.core_swap(segments))
    runs = jnp.transpose(running[:, 0]).astype(F32)
    runs = to_row(jnp.concatenate([runs, jnp.zeros((rows, 126), F32)], axis=1))
    runs_enc, runs_dec = runs[:, :1], runs[:, 1:2]
    target = to_row(target_rows[:, 0]).astype(F32)

    place = jnp.arange(rows, dtype=jnp.int32)
    first_place = at.c * quarter + place
    second_place = jnp.where(at.c == 0, 3 * quarter, 2 * quarter) + place - quarter
    place = jnp.where(place < quarter, first_place, second_place)
    embedding = signal(place.astype(F32)) + signal(jnp.ones((1,), F32))

    def own_part(rows_all, core_of):
        first = lax.dynamic_slice_in_dim(rows_all, core_of * quarter, quarter, 0)
        second = lax.dynamic_slice_in_dim(
            rows_all, jnp.where(core_of == 0, 3, 2) * quarter, quarter, 0
        )
        return jnp.concatenate([first, second])

    source_q_all, source_k_all = extensions(segments[0])
    target_q_all, target_k_all = extensions(segments[1])
    source_q = own_part(source_q_all, at.c)
    target_q = own_part(target_q_all, at.c)
    source_k = (source_k_all, own_part(source_k_all, at.c), own_part(source_k_all, 1 - at.c))
    target_k = (target_k_all, own_part(target_k_all, at.c), own_part(target_k_all, 1 - at.c))

    def full(own, axis, other=None):
        other = at.other_half(own, axis) if other is None else other
        return other

    enc_proj_other = at.other_half(enc_proj, 0)
    enc_up_other = at.other_half(enc_up, 0)
    enc_down_other = at.other_half(enc_down, 0)
    dec_qkv_other = at.other_half(dec_qkv, 1)
    dec_proj_other = at.other_half(dec_proj, 0)
    cross_query_other = at.other_half(cross_query, 0)
    cross_kv_other = at.other_half(cross_kv, 1)
    cross_proj_other = at.other_half(cross_proj, 0)
    dec_up_other = at.other_half(dec_up, 0)
    dec_down_other = at.other_half(dec_down, 0)
    enc_qkv = jnp.concatenate([enc_qkv, enc_qkv_other], axis=2)
    enc_proj = jnp.concatenate([enc_proj, enc_proj_other], axis=0)
    enc_up = jnp.concatenate([enc_up, enc_up_other], axis=1)
    enc_down = jnp.concatenate([enc_down, enc_down_other], axis=0)
    dec_qkv = jnp.concatenate([dec_qkv, dec_qkv_other], axis=2)
    dec_proj = jnp.concatenate([dec_proj, dec_proj_other], axis=0)
    cross_query = jnp.concatenate([cross_query, cross_query_other], axis=1)
    cross_kv = jnp.concatenate([cross_kv, cross_kv_other], axis=2)
    cross_proj = jnp.concatenate([cross_proj, cross_proj_other], axis=0)
    dec_up = jnp.concatenate([dec_up, dec_up_other], axis=1)
    dec_down = jnp.concatenate([dec_down, dec_down_other], axis=0)
    cotangents = jnp.concatenate([enc_cotangent[:, 0], dec_cotangent[:, 0]], axis=1)
    cotangents = to_row(cotangents.astype(BF)).astype(F32)
    enc_cot, dec_cot = cotangents[:, :D], cotangents[:, D:]

    def attend(query_in, key_in, w_query, w_key, w_value, query_ext, key_ext, causal):
        queries = (dots(query_in, w_query) * Q_SCALE).astype(BF)
        keys_own = dots(key_in, w_key).astype(BF)
        values_own = dots(key_in, w_value).astype(BF)
        keys_other = at.core_swap(keys_own)
        values_other = at.core_swap(values_own)
        mixed, log_total = attn_fwd(
            core, queries, keys_own, keys_other, values_own, values_other, query_ext, key_ext[0],
            causal=causal, bq=512, sub=256,
        )
        return mixed, (queries, keys_own, keys_other, values_own, values_other, query_ext, key_ext, mixed, log_total)

    def attend_back(kept, out_grad, w_out, causal):
        queries, keys_own, keys_other, values_own, values_other, query_ext, key_ext, mixed, log_total = kept
        mixed_grad = dots_t(out_grad, w_out).astype(BF)
        out_weight_grad = weight_dots(mixed, out_grad)
        query_grad, key_own, key_other, value_own, value_other = attn_bwd(
            core, queries, keys_own, keys_other, values_own, values_other, query_ext,
            key_ext[1], key_ext[2], mixed_grad, mixed, log_total, causal=causal, bk=512,
        )
        key_grad = (key_own.astype(F32) + at.core_swap(key_other).astype(F32)).astype(BF)
        value_grad = (value_own.astype(F32) + at.core_swap(value_other).astype(F32)).astype(BF)
        return query_grad, key_grad, value_grad, out_weight_grad

    def feed(low, up, down):
        hidden = dots(low, up)
        return dots(jax.nn.gelu(hidden).astype(BF), down), hidden

    def feed_back(low, hidden, up, down, out_grad):
        active, gelu_back = jax.vjp(jax.nn.gelu, hidden)
        down_grad = weight_dots(active.astype(BF), out_grad)
        hidden_grad = gelu_back(dots_t(out_grad, down))[0].astype(BF)
        up_grad = weight_dots(low, hidden_grad)
        return dots_t(hidden_grad, up), up_grad, down_grad

    enc_start = source + embedding
    enc_start_low = enc_start.astype(BF)
    enc_mixed, enc_kept = attend(
        enc_start_low, enc_start_low, enc_qkv[0], enc_qkv[1], enc_qkv[2], source_q, source_k, False
    )
    enc_sum_one = enc_start + dots(enc_mixed, enc_proj)
    enc_middle = normalize(enc_sum_one, enc_gains[0], enc_shifts[0])
    enc_middle_low = enc_middle.astype(BF)
    enc_ffn, enc_hidden = feed(enc_middle_low, enc_up, enc_down)
    enc_sum_two = enc_middle + enc_ffn
    enc_last = normalize(enc_sum_two, enc_gains[1], enc_shifts[1])
    enc_states = halting(runs_enc, enc_start, enc_last, halt_weight[0]).astype(BF)
    enc_states_moved = at.from_row(enc_states[:quarter], enc_states[quarter:])

    dec_start = target + embedding
    dec_start_low = dec_start.astype(BF)
    dec_mixed_heads, self_kept = attend(
        dec_start_low, dec_start_low, dec_qkv[0], dec_qkv[1], dec_qkv[2], target_q, target_k, True
    )
    dec_sum_one = dec_start + dots(dec_mixed_heads, dec_proj)
    dec_middle = normalize(dec_sum_one, dec_gains[0], dec_shifts[0])
    dec_middle_low = dec_middle.astype(BF)
    cross_mixed, cross_kept = attend(
        dec_middle_low, enc_states, cross_query, cross_kv[0], cross_kv[1], target_q, source_k, False
    )
    dec_sum_two = dec_middle + dots(cross_mixed, cross_proj)
    dec_mixed = normalize(dec_sum_two, dec_gains[1], dec_shifts[1])
    dec_mixed_low = dec_mixed.astype(BF)
    dec_ffn, dec_hidden = feed(dec_mixed_low, dec_up, dec_down)
    dec_sum_three = dec_mixed + dec_ffn
    dec_last = normalize(dec_sum_three, dec_gains[2], dec_shifts[2])
    dec_states = halting(runs_dec, dec_start, dec_last, halt_weight[1]).astype(BF)
    dec_states_moved = at.from_row(dec_states[:quarter], dec_states[quarter:])

    _, halt_back = jax.vjp(partial(halting, runs_dec), dec_start, dec_last, halt_weight[1])
    dec_start_grad, last_grad, dec_halt_grad = halt_back(dec_cot)
    _, norm_back = jax.vjp(normalize, dec_sum_three, dec_gains[2], dec_shifts[2])
    sum_grad, dec_gain_three, dec_shift_three = norm_back(last_grad)
    ffn_input_grad, dec_up_grad, dec_down_grad = feed_back(
        dec_mixed_low, dec_hidden, dec_up, dec_down, sum_grad.astype(BF)
    )

    def halves(grad, axis):
        size = grad.shape[axis] // 2
        return (
            rows_of(lax.slice_in_dim(grad, 0, size, axis=axis)),
            rows_of(lax.slice_in_dim(grad, size, 2 * size, axis=axis)),
        )

    def reduced(grads, axes, shapes):
        parts = [halves(grad, axis) for grad, axis in zip(grads, axes)]
        total = at.reduce_bucket(
            jnp.concatenate([p[0] for p in parts]), jnp.concatenate([p[1] for p in parts])
        )
        outs, begin = [], 0
        for part, shape in zip(parts, shapes):
            count = part[0].shape[0]
            outs.append(rows_back(total[begin : begin + count], shape))
            begin += count
        return outs

    half_of = lambda shape, axis: tuple(s // 2 if i == axis else s for i, s in enumerate(shape))

    def bucket(grads, axes):
        return reduced(grads, axes, [half_of(g.shape, a) for g, a in zip(grads, axes)])

    dec_up_grad, dec_down_grad = bucket((dec_up_grad, dec_down_grad), (1, 0))
    mixed_grad = sum_grad + ffn_input_grad
    _, norm_back = jax.vjp(normalize, dec_sum_two, dec_gains[1], dec_shifts[1])
    sum_grad, dec_gain_two, dec_shift_two = norm_back(mixed_grad)
    query_grad, key_grad, value_grad, cross_proj_grad = attend_back(
        cross_kept, sum_grad.astype(BF), cross_proj, False
    )
    cross_query_grad = weight_dots(dec_middle_low, query_grad)
    cross_kv_grad = jnp.stack(
        [weight_dots(enc_states, key_grad), weight_dots(enc_states, value_grad)]
    )
    cross_query_grad, cross_kv_grad, cross_proj_grad = bucket(
        (cross_query_grad, cross_kv_grad, cross_proj_grad), (1, 2, 0)
    )
    middle_grad = sum_grad + dots_t(query_grad, cross_query)
    enc_extra = dots_t(key_grad, cross_kv[0]) + dots_t(value_grad, cross_kv[1])
    _, norm_back = jax.vjp(normalize, dec_sum_one, dec_gains[0], dec_shifts[0])
    self_sum_grad, dec_gain_one, dec_shift_one = norm_back(middle_grad)

    enc_final_grad = enc_cot + enc_extra
    _, halt_back = jax.vjp(partial(halting, runs_enc), enc_start, enc_last, halt_weight[0])
    enc_start_grad, last_grad, enc_halt_grad = halt_back(enc_final_grad)
    _, norm_back = jax.vjp(normalize, enc_sum_two, enc_gains[1], enc_shifts[1])
    sum_grad, enc_gain_two, enc_shift_two = norm_back(last_grad)
    ffn_input_grad, enc_up_grad, enc_down_grad = feed_back(
        enc_middle_low, enc_hidden, enc_up, enc_down, sum_grad.astype(BF)
    )
    enc_up_grad, enc_down_grad = bucket((enc_up_grad, enc_down_grad), (1, 0))
    middle_grad = sum_grad + ffn_input_grad
    _, norm_back = jax.vjp(normalize, enc_sum_one, enc_gains[0], enc_shifts[0])
    enc_sum_grad, enc_gain_one, enc_shift_one = norm_back(middle_grad)
    small = at.reduce_all(
        jnp.stack(
            [
                enc_gain_one, enc_gain_two, enc_shift_one, enc_shift_two,
                dec_gain_one, dec_gain_two, dec_gain_three,
                dec_shift_one, dec_shift_two, dec_shift_three,
                enc_halt_grad, dec_halt_grad,
            ]
        )
    )

    query_grad, key_grad, value_grad, enc_proj_grad = attend_back(
        enc_kept, enc_sum_grad.astype(BF), enc_proj, False
    )
    enc_qkv_grad = jnp.stack(
        [weight_dots(enc_start_low, g) for g in (query_grad, key_grad, value_grad)]
    )
    enc_qkv_grad, enc_proj_grad = bucket((enc_qkv_grad, enc_proj_grad), (2, 0))
    source_grad = (
        enc_sum_grad
        + enc_start_grad
        + dots_t(query_grad, enc_qkv[0])
        + dots_t(key_grad, enc_qkv[1])
        + dots_t(value_grad, enc_qkv[2])
    )
    source_low = source_grad.astype(BF)
    source_moved = at.from_row(source_low[:quarter], source_low[quarter:])

    query_grad, key_grad, value_grad, dec_proj_grad = attend_back(
        self_kept, self_sum_grad.astype(BF), dec_proj, True
    )
    dec_qkv_grad = jnp.stack(
        [weight_dots(dec_start_low, g) for g in (query_grad, key_grad, value_grad)]
    )
    dec_qkv_grad, dec_proj_grad = bucket((dec_qkv_grad, dec_proj_grad), (2, 0))
    target_grad = (
        self_sum_grad
        + dec_start_grad
        + dots_t(query_grad, dec_qkv[0])
        + dots_t(key_grad, dec_qkv[1])
        + dots_t(value_grad, dec_qkv[2])
    )
    target_low = target_grad.astype(BF)
    target_moved = at.from_row(target_low[:quarter], target_low[quarter:])

    def back_home(values, moved):
        moved = [m.astype(values.dtype) for m in moved]
        return at.native(values[:quarter], values[quarter:], *moved)[:, None]

    return (
        back_home(enc_states, enc_states_moved),
        back_home(dec_states, dec_states_moved),
        back_home(source_grad, source_moved),
        back_home(target_grad, target_moved),
        enc_qkv_grad,
        enc_proj_grad,
        enc_up_grad,
        enc_down_grad,
        small[0:2],
        small[2:4],
        dec_qkv_grad,
        dec_proj_grad,
        cross_query_grad,
        cross_kv_grad,
        cross_proj_grad,
        dec_up_grad,
        dec_down_grad,
        small[4:7],
        small[7:10],
        small[10:12],
    )


def solution(mesh):
    dp_size, mp_size = mesh.shape["dp"], mesh.shape["mp"]
    by_chip = mp_size == 2 and dp_size >= 4 and dp_size & (dp_size - 1) == 0
    body = partial(chip_rows, dp_size=dp_size) if by_chip else local
    return jax.shard_map(
        body,
        mesh=mesh,
        in_specs=(
            P("mp", "dp", None),
            P("mp", "dp", None),
            P("dp", None),
            P("dp", None),
            P(None, "dp", "mp"),
            P(None, None, "mp"),
            P("mp", None),
            P(None, "mp"),
            P("mp", None),
            P(),
            P(),
            P(None, None, "mp"),
            P("mp", None),
            P(None, "mp"),
            P(None, None, "mp"),
            P("mp", None),
            P(None, "mp"),
            P("mp", None),
            P(),
            P(),
            P(),
            P("mp", "dp", None),
            P("mp", "dp", None),
        ),
        out_specs=(
            P("mp", "dp", None),
            P("mp", "dp", None),
            P("mp", "dp", None),
            P("mp", "dp", None),
            P(None, None, "mp"),
            P("mp", None),
            P(None, "mp"),
            P("mp", None),
            P(),
            P(),
            P(None, None, "mp"),
            P("mp", None),
            P(None, "mp"),
            P(None, None, "mp"),
            P("mp", None),
            P(None, "mp"),
            P("mp", None),
            P(),
            P(),
            P(),
        ),
        check_vma=False,
    )
```

```python
import math
from functools import partial

import jax
import jax.numpy as jnp
from jax import lax
from jax.experimental import pallas as pl
from jax.experimental.pallas import tpu as pltpu
from jax.sharding import PartitionSpec as P

D = 512
DH = 64


EPS = 1e-05
NEGATIVE = -1000000000.0


def signal(position):
    half_width = D // 2
    inverse_rates = jnp.exp(
        jnp.arange(half_width, dtype=jnp.float32) * (-jnp.log(10000.0) / (half_width - 1))
    )
    angles = position[:, None] * inverse_rates[None, :]
    return jnp.concatenate([jnp.sin(angles), jnp.cos(angles)], axis=1)


def normalize(values, norm_gain, norm_shift):
    centred = values - jnp.mean(values, axis=-1, keepdims=True)
    spread = jnp.mean(centred * centred, axis=-1, keepdims=True)
    return centred * lax.rsqrt(spread + EPS) * norm_gain + norm_shift


def halting(running_now, initial, updated, weight):
    halt_prob = jax.nn.sigmoid(jnp.sum(updated * weight, axis=-1, keepdims=True))
    return initial + running_now * halt_prob * (updated - initial)


def dot_last(left, right):
    return lax.dot_general(
        left, right, (((left.ndim - 1,), (1,)), ((), ())), preferred_element_type=jnp.float32
    )


def collect(piece_rows):
    return lax.all_gather(piece_rows, "mp", axis=0, tiled=True)


def collect_grad(piece_rows):
    return lax.all_gather(piece_rows.astype(jnp.bfloat16), "mp", axis=0, tiled=True)


def project_out(hidden, weight, rows):

    def partial_term(begin_row, row_count):
        return jnp.dot(hidden, weight, preferred_element_type=jnp.float32)

    return lax.psum_scatter(
        partial_term(jnp.int32(0), lax.axis_size("mp") * rows).astype(jnp.bfloat16),
        "mp",
        scatter_dimension=0,
        tiled=True,
    ).astype(jnp.float32)


def project_back(gradients, matrices, rows):

    def partial_term(begin_row, row_count):
        summed = jnp.zeros(
            (row_count,) + gradients[0].shape[1:-1] + (matrices[0].shape[0],), jnp.float32
        )
        for gradient, matrix in zip(gradients, matrices):
            summed = summed + dot_last(gradient, matrix)
        return summed

    return lax.psum_scatter(
        partial_term(jnp.int32(0), lax.axis_size("mp") * rows).astype(jnp.bfloat16),
        "mp",
        scatter_dimension=0,
        tiled=True,
    ).astype(jnp.float32)


def to_pairs(values):
    length, row_count, width = values.shape
    return (
        values.reshape(length, row_count, width // DH, DH)
        .transpose(1, 2, 0, 3)
        .reshape(-1, length, DH)
    )


def from_pairs(values, row_count):
    pairs, length, unused = values.shape
    heads_here = pairs // row_count
    return (
        values.reshape(row_count, heads_here, length, DH)
        .transpose(2, 0, 1, 3)
        .reshape(length, row_count, heads_here * DH)
    )


def per_pair(segments, width):
    return jnp.repeat(segments, width // DH, axis=0)


def pair_scores(query_block, key_rows, segment_block, segment_keys, first_row, causal):
    scores = lax.dot_general(
        query_block, key_rows, (((1,), (1,)), ((), ())), preferred_element_type=jnp.float32
    )
    scores = scores * DH ** (-0.5)
    allowed = segment_block[:, None] == segment_keys[None, :]
    if causal:
        query_place = first_row + jnp.arange(query_block.shape[0], dtype=jnp.int32)
        key_place = jnp.arange(key_rows.shape[0], dtype=jnp.int32)
        allowed = allowed & (key_place[None, :] <= query_place[:, None])
    return jnp.where(allowed, scores, NEGATIVE)


def attend_pair(inputs, causal):
    query_rows, key_rows, value_rows, segment_query, segment_keys = inputs
    length = query_rows.shape[0]
    block_rows = min(512, length)
    blocks = length // block_rows
    firsts = jnp.arange(blocks, dtype=jnp.int32) * block_rows

    def one_block(pieces):
        query_block, segment_block, first_row = pieces
        scores = pair_scores(query_block, key_rows, segment_block, segment_keys, first_row, causal)
        highest = jnp.max(scores, axis=1, keepdims=True)
        exponent = jnp.exp(scores - highest)
        totals = jnp.sum(exponent, axis=1, keepdims=True)
        weights = (exponent / totals).astype(jnp.bfloat16)
        mixed = jnp.dot(weights, value_rows, preferred_element_type=jnp.float32)
        return (mixed.astype(jnp.bfloat16), (highest + jnp.log(totals))[:, 0])

    mixed, log_total = lax.map(
        one_block,
        (
            query_rows.reshape(blocks, block_rows, -1),
            segment_query.reshape(blocks, block_rows),
            firsts,
        ),
    )
    return (mixed.reshape(length, -1), log_total.reshape(length))


def attend_pair_back(inputs, causal):
    query_rows, key_rows, value_rows, mixed_grad, log_total, segment_query, segment_keys = inputs
    length = query_rows.shape[0]
    block_rows = min(512, length)
    blocks = length // block_rows
    firsts = jnp.arange(blocks, dtype=jnp.int32) * block_rows

    def one_block(carry, pieces):
        key_total, value_total = carry
        query_block, grad_block, log_block, segment_block, first_row = pieces
        scores = pair_scores(query_block, key_rows, segment_block, segment_keys, first_row, causal)
        probs = jnp.exp(scores - log_block[:, None])
        weights = probs.astype(jnp.bfloat16)
        prob_grad = lax.dot_general(
            grad_block, value_rows, (((1,), (1,)), ((), ())), preferred_element_type=jnp.float32
        )
        inner = jnp.sum(probs * prob_grad, axis=1, keepdims=True)
        score_grad = (probs * (prob_grad - inner)).astype(jnp.bfloat16)
        query_grad = jnp.dot(score_grad, key_rows, preferred_element_type=jnp.float32) * DH ** (
            -0.5
        )
        key_total = key_total + lax.dot_general(
            score_grad, query_block, (((0,), (0,)), ((), ())), preferred_element_type=jnp.float32
        ) * DH ** (-0.5)
        value_total = value_total + lax.dot_general(
            weights, grad_block, (((0,), (0,)), ((), ())), preferred_element_type=jnp.float32
        )
        return ((key_total, value_total), query_grad.astype(jnp.bfloat16))

    zeros_start = jnp.zeros(key_rows.shape, jnp.float32)
    (key_total, value_total), query_grad = lax.scan(
        one_block,
        (zeros_start, zeros_start),
        (
            query_rows.reshape(blocks, block_rows, -1),
            mixed_grad.reshape(blocks, block_rows, -1),
            log_total.reshape(blocks, block_rows),
            segment_query.reshape(blocks, block_rows),
            firsts,
        ),
    )
    return (
        query_grad.reshape(length, -1),
        key_total.astype(jnp.bfloat16),
        value_total.astype(jnp.bfloat16),
    )


def attention_forward(
    query_full,
    key_full,
    weight_query,
    weight_key,
    weight_value,
    weight_out,
    segment_query,
    segment_keys,
    causal,
    rows,
):
    queries = jnp.dot(query_full, weight_query, preferred_element_type=jnp.float32).astype(
        jnp.bfloat16
    )
    keys_low = jnp.dot(key_full, weight_key, preferred_element_type=jnp.float32).astype(
        jnp.bfloat16
    )
    values_low = jnp.dot(key_full, weight_value, preferred_element_type=jnp.float32).astype(
        jnp.bfloat16
    )
    width = queries.shape[2]
    row_count = queries.shape[1]
    mixed, log_total = lax.map(
        partial(attend_pair, causal=causal),
        (
            to_pairs(queries),
            to_pairs(keys_low),
            to_pairs(values_low),
            per_pair(segment_query, width),
            per_pair(segment_keys, width),
        ),
    )
    mixed = from_pairs(mixed, row_count)
    branch = project_out(mixed, weight_out, rows)
    return (branch, (queries, keys_low, values_low, mixed, log_total))


def attention_backward(
    branch_grad, kept, query_full, key_full, weight_out, segment_query, segment_keys, causal
):
    queries, keys_low, values_low, kept_mixed, log_total = kept
    grad_full = collect_grad(branch_grad)
    out_weight_grad = jnp.einsum(
        "lrc,lrd->cd", kept_mixed, grad_full, preferred_element_type=jnp.float32
    )
    mixed_grad = dot_last(grad_full, weight_out).astype(jnp.bfloat16)
    width = queries.shape[2]
    row_count = queries.shape[1]
    query_grad, key_grad, value_grad = lax.map(
        partial(attend_pair_back, causal=causal),
        (
            to_pairs(queries),
            to_pairs(keys_low),
            to_pairs(values_low),
            to_pairs(mixed_grad),
            log_total,
            per_pair(segment_query, width),
            per_pair(segment_keys, width),
        ),
    )
    query_grad = from_pairs(query_grad, row_count)
    key_grad = from_pairs(key_grad, row_count)
    value_grad = from_pairs(value_grad, row_count)
    weight_grads = (
        jnp.einsum("lrd,lrc->dc", query_full, query_grad, preferred_element_type=jnp.float32),
        jnp.einsum("lrd,lrc->dc", key_full, key_grad, preferred_element_type=jnp.float32),
        jnp.einsum("lrd,lrc->dc", key_full, value_grad, preferred_element_type=jnp.float32),
    )
    return (query_grad, key_grad, value_grad, weight_grads, out_weight_grad)


def feed_forward(source_full, weight_up, weight_down, rows):
    hidden = jnp.dot(source_full, weight_up, preferred_element_type=jnp.float32)
    active = jax.nn.gelu(hidden).astype(jnp.bfloat16)
    return (project_out(active, weight_down, rows), hidden)


def feed_backward(branch_grad, source_full, hidden, weight_up, weight_down, rows):
    grad_full = collect_grad(branch_grad)
    active, gelu_back = jax.vjp(jax.nn.gelu, hidden)
    active = active.astype(jnp.bfloat16)
    down_grad = jnp.einsum("lrf,lrd->fd", active, grad_full, preferred_element_type=jnp.float32)
    hidden_grad = gelu_back(dot_last(grad_full, weight_down))[0].astype(jnp.bfloat16)
    up_grad = jnp.einsum(
        "lrd,lrf->df", source_full, hidden_grad, preferred_element_type=jnp.float32
    )
    input_grad = project_back((hidden_grad,), (weight_up,), rows)
    return (input_grad, up_grad, down_grad)


def local(
    source_rows,
    target_rows,
    source_segment,
    target_segment,
    running,
    enc_qkv,
    enc_proj,
    enc_up,
    enc_down,
    enc_gains,
    enc_shifts,
    dec_qkv,
    dec_proj,
    cross_query,
    cross_kv,
    cross_proj,
    dec_up,
    dec_down,
    dec_gains,
    dec_shifts,
    halt_weight,
    enc_cotangent,
    dec_cotangent,
):
    rows = source_rows.shape[0]
    position = (lax.axis_index("mp") * rows + jnp.arange(rows, dtype=jnp.int32)).astype(jnp.float32)
    embedding = (signal(position) + signal(jnp.ones((1,), jnp.float32)))[:, None, :]
    runs_now = jnp.transpose(running, (0, 2, 1)).astype(jnp.float32)[..., None]
    enc_start = source_rows.astype(jnp.float32) + embedding
    enc_start_low = enc_start.astype(jnp.bfloat16)
    enc_start_full = collect(enc_start_low)
    enc_attn, enc_attn_kept = attention_forward(
        enc_start_full,
        enc_start_full,
        enc_qkv[0],
        enc_qkv[1],
        enc_qkv[2],
        enc_proj,
        source_segment,
        source_segment,
        False,
        rows,
    )
    enc_sum_one = enc_start + enc_attn
    enc_middle = normalize(enc_sum_one, enc_gains[0], enc_shifts[0])
    enc_middle_low = enc_middle.astype(jnp.bfloat16)
    enc_middle_full = collect(enc_middle_low)
    enc_ffn, enc_hidden = feed_forward(enc_middle_full, enc_up, enc_down, rows)
    enc_sum_two = enc_middle + enc_ffn
    enc_last = normalize(enc_sum_two, enc_gains[1], enc_shifts[1])
    enc_final = halting(runs_now[0], enc_start, enc_last, halt_weight[0])
    enc_states = enc_final.astype(jnp.bfloat16)
    enc_states_full = collect(enc_states)
    dec_start = target_rows.astype(jnp.float32) + embedding
    dec_start_low = dec_start.astype(jnp.bfloat16)
    dec_start_full = collect(dec_start_low)
    dec_self, dec_self_kept = attention_forward(
        dec_start_full,
        dec_start_full,
        dec_qkv[0],
        dec_qkv[1],
        dec_qkv[2],
        dec_proj,
        target_segment,
        target_segment,
        True,
        rows,
    )
    dec_sum_one = dec_start + dec_self
    dec_middle = normalize(dec_sum_one, dec_gains[0], dec_shifts[0])
    dec_middle_low = dec_middle.astype(jnp.bfloat16)
    dec_middle_full = collect(dec_middle_low)
    dec_cross, dec_cross_kept = attention_forward(
        dec_middle_full,
        enc_states_full,
        cross_query,
        cross_kv[0],
        cross_kv[1],
        cross_proj,
        target_segment,
        source_segment,
        False,
        rows,
    )
    dec_sum_two = dec_middle + dec_cross
    dec_mixed = normalize(dec_sum_two, dec_gains[1], dec_shifts[1])
    dec_mixed_low = dec_mixed.astype(jnp.bfloat16)
    dec_mixed_full = collect(dec_mixed_low)
    dec_ffn, dec_hidden = feed_forward(dec_mixed_full, dec_up, dec_down, rows)
    dec_sum_three = dec_mixed + dec_ffn
    dec_last = normalize(dec_sum_three, dec_gains[2], dec_shifts[2])
    dec_final = halting(runs_now[1], dec_start, dec_last, halt_weight[1])
    dec_states = dec_final.astype(jnp.bfloat16)
    unused, halt_back = jax.vjp(partial(halting, runs_now[1]), dec_start, dec_last, halt_weight[1])
    dec_start_grad, last_grad, dec_halt_grad = halt_back(dec_cotangent)
    unused, norm_back = jax.vjp(normalize, dec_sum_three, dec_gains[2], dec_shifts[2])
    sum_grad, dec_gain_three, dec_shift_three = norm_back(last_grad)
    ffn_input_grad, dec_up_grad, dec_down_grad = feed_backward(
        sum_grad, dec_mixed_full, dec_hidden, dec_up, dec_down, rows
    )
    mixed_grad = sum_grad + ffn_input_grad
    unused, norm_back = jax.vjp(normalize, dec_sum_two, dec_gains[1], dec_shifts[1])
    sum_grad, dec_gain_two, dec_shift_two = norm_back(mixed_grad)
    query_grad, key_grad, value_grad, cross_grads, cross_proj_grad = attention_backward(
        sum_grad,
        dec_cross_kept,
        dec_middle_full,
        enc_states_full,
        cross_proj,
        target_segment,
        source_segment,
        False,
    )
    middle_grad = sum_grad + project_back((query_grad,), (cross_query,), rows)
    enc_extra = project_back((key_grad, value_grad), (cross_kv[0], cross_kv[1]), rows)
    unused, norm_back = jax.vjp(normalize, dec_sum_one, dec_gains[0], dec_shifts[0])
    sum_grad, dec_gain_one, dec_shift_one = norm_back(middle_grad)
    query_grad, key_grad, value_grad, self_grads, dec_proj_grad = attention_backward(
        sum_grad,
        dec_self_kept,
        dec_start_full,
        dec_start_full,
        dec_proj,
        target_segment,
        target_segment,
        True,
    )
    target_grad = (
        sum_grad
        + dec_start_grad
        + project_back(
            (query_grad, key_grad, value_grad), (dec_qkv[0], dec_qkv[1], dec_qkv[2]), rows
        )
    )
    dec_qkv_grad = jnp.stack(self_grads)
    cross_query_grad = cross_grads[0]
    cross_kv_grad = jnp.stack([cross_grads[1], cross_grads[2]])
    enc_final_grad = enc_cotangent + enc_extra
    unused, halt_back = jax.vjp(partial(halting, runs_now[0]), enc_start, enc_last, halt_weight[0])
    enc_start_grad, last_grad, enc_halt_grad = halt_back(enc_final_grad)
    unused, norm_back = jax.vjp(normalize, enc_sum_two, enc_gains[1], enc_shifts[1])
    sum_grad, enc_gain_two, enc_shift_two = norm_back(last_grad)
    ffn_input_grad, enc_up_grad, enc_down_grad = feed_backward(
        sum_grad, enc_middle_full, enc_hidden, enc_up, enc_down, rows
    )
    middle_grad = sum_grad + ffn_input_grad
    unused, norm_back = jax.vjp(normalize, enc_sum_one, enc_gains[0], enc_shifts[0])
    sum_grad, enc_gain_one, enc_shift_one = norm_back(middle_grad)
    query_grad, key_grad, value_grad, self_grads, enc_proj_grad = attention_backward(
        sum_grad,
        enc_attn_kept,
        enc_start_full,
        enc_start_full,
        enc_proj,
        source_segment,
        source_segment,
        False,
    )
    source_grad = (
        sum_grad
        + enc_start_grad
        + project_back(
            (query_grad, key_grad, value_grad), (enc_qkv[0], enc_qkv[1], enc_qkv[2]), rows
        )
    )
    enc_qkv_grad = jnp.stack(self_grads)
    (
        enc_qkv_grad,
        enc_proj_grad,
        enc_up_grad,
        enc_down_grad,
        dec_qkv_grad,
        dec_proj_grad,
        cross_query_grad,
        cross_kv_grad,
        cross_proj_grad,
        dec_up_grad,
        dec_down_grad,
    ) = (
        lax.psum(enc_qkv_grad.astype(jnp.bfloat16), "dp").astype(jnp.float32),
        lax.psum(enc_proj_grad.astype(jnp.bfloat16), "dp").astype(jnp.float32),
        lax.psum(enc_up_grad.astype(jnp.bfloat16), "dp").astype(jnp.float32),
        lax.psum(enc_down_grad.astype(jnp.bfloat16), "dp").astype(jnp.float32),
        lax.psum(dec_qkv_grad.astype(jnp.bfloat16), "dp").astype(jnp.float32),
        lax.psum(dec_proj_grad.astype(jnp.bfloat16), "dp").astype(jnp.float32),
        lax.psum(cross_query_grad.astype(jnp.bfloat16), "dp").astype(jnp.float32),
        lax.psum(cross_kv_grad.astype(jnp.bfloat16), "dp").astype(jnp.float32),
        lax.psum(cross_proj_grad.astype(jnp.bfloat16), "dp").astype(jnp.float32),
        lax.psum(dec_up_grad.astype(jnp.bfloat16), "dp").astype(jnp.float32),
        lax.psum(dec_down_grad.astype(jnp.bfloat16), "dp").astype(jnp.float32),
    )
    enc_gains_grad, enc_shifts_grad, dec_gains_grad, dec_shifts_grad, halt_weight_grad = lax.psum(
        (
            jnp.stack([enc_gain_one, enc_gain_two]),
            jnp.stack([enc_shift_one, enc_shift_two]),
            jnp.stack([dec_gain_one, dec_gain_two, dec_gain_three]),
            jnp.stack([dec_shift_one, dec_shift_two, dec_shift_three]),
            jnp.stack([enc_halt_grad, dec_halt_grad]),
        ),
        ("dp", "mp"),
    )
    return (
        enc_states,
        dec_states,
        source_grad,
        target_grad,
        enc_qkv_grad,
        enc_proj_grad,
        enc_up_grad,
        enc_down_grad,
        enc_gains_grad,
        enc_shifts_grad,
        dec_qkv_grad,
        dec_proj_grad,
        cross_query_grad,
        cross_kv_grad,
        cross_proj_grad,
        dec_up_grad,
        dec_down_grad,
        dec_gains_grad,
        dec_shifts_grad,
        halt_weight_grad,
    )


BIG = -1e30
BF = jnp.bfloat16
F32 = jnp.float32
NN = (((1,), (0,)), ((), ()))
NT = (((1,), (1,)), ((), ()))
TN = (((0,), (0,)), ((), ()))
HALF = D // 2
VMEM_BYTES = 56 * 1024 * 1024
NO_COST = pl.CostEstimate(flops=1, bytes_accessed=1, transcendentals=0)


def dot_nn(a, b):
    return lax.dot_general(a, b, NN, preferred_element_type=F32)


def dot_nt(a, b):
    return lax.dot_general(a, b, NT, preferred_element_type=F32)


def dot_tn(a, b):
    return lax.dot_general(a, b, TN, preferred_element_type=F32)


def lanes():
    lane = lax.broadcasted_iota(jnp.int32, (1, 128), 1)
    return lane < DH, lane % DH


def forward_kernel(
    core_ref, q_ref, own_ref, got_ref, query_ext_ref, key_ext_ref, o_ref, log_ref, keys, values,
    *, causal, rows,
):
    step = pl.program_id(1)
    block = q_ref.shape[0]
    quarter = own_ref.shape[1] // 2
    core = core_ref[0]
    left, _ = lanes()

    @pl.when(step == 0)
    def _():
        n = own_ref.shape[1]
        for ref, of in ((own_ref, core), (got_ref, 1 - core)):
            here = pl.ds(pl.multiple_of(of * n, n), n)
            k, v, ext = ref[0], ref[1], key_ext_ref[here, :]
            ones = jnp.ones_like(v)
            keys[0, here, :] = jnp.where(left, k, ext)
            keys[1, here, :] = jnp.where(left, ext, k)
            values[0, here, :] = jnp.where(left, v, ones)
            values[1, here, :] = jnp.where(left, ones, v)

    def attend(count, first_row):
        for begin in range(0, block, rows):
            here = slice(begin, begin + rows)
            pair, ext = q_ref[here, :], query_ext_ref[here, :]
            mixed, highest = [], []
            for head in range(2):
                q = jnp.where(left, pair, ext) if head == 0 else jnp.where(left, ext, pair)
                clear = count - quarter if causal else count
                parts = []
                if clear:
                    parts.append((dot_nt(q, keys[head, :clear, :]), values[head, :clear, :]))
                if causal:
                    scores = dot_nt(q, keys[head, clear:count, :])
                    row = lax.broadcasted_iota(jnp.int32, scores.shape, 0) + (first_row + begin)
                    column = lax.broadcasted_iota(jnp.int32, scores.shape, 1)
                    scores = jnp.where(column <= row, scores, BIG)
                    parts.append((scores, values[head, clear:count, :]))
                top = jnp.max(parts[0][0], axis=1, keepdims=True)
                for scores, _ in parts[1:]:
                    top = jnp.maximum(top, jnp.max(scores, axis=1, keepdims=True))
                total = 0.0
                for scores, v in parts:
                    total = total + dot_nn(jnp.exp2(scores - top).astype(BF), v)
                mixed.append(total)
                highest.append(top)
            sums = jnp.where(left, mixed[1], mixed[0])
            out = jnp.where(left, mixed[0], mixed[1]) / pltpu.roll(sums, DH, 1)
            o_ref[here, :] = out.astype(BF)
            log_ref[here, :] = jnp.where(left, highest[1], highest[0]) + jnp.log2(sums)

    if not causal:
        attend(2 * own_ref.shape[1], None)
    else:
        each = quarter // block
        piece = step // each
        place = 2 * core + piece
        for case in range(4):

            @pl.when(place == case)
            def _(case=case):
                attend((case + 1) * quarter, (step - piece * each) * block)


def attention_forward_half(core, q, own, got, query_ext, key_ext, causal):
    n, width = q.shape
    length = 2 * n
    block, rows = 512, 256
    keys = pl.BlockSpec((2, n, 128), lambda p, b: (0, 0, p))
    queries = pl.BlockSpec((block, 128), lambda p, b: (b, p))
    return pl.pallas_call(
        partial(forward_kernel, causal=causal, rows=rows),
        grid=(width // 128, n // block),
        in_specs=[
            pl.BlockSpec(memory_space=pltpu.SMEM),
            queries,
            keys,
            keys,
            pl.BlockSpec((block, 128), lambda p, b: (b, 0)),
            pl.BlockSpec((length, 128), lambda p, b: (0, 0)),
        ],
        out_specs=[queries, queries],
        out_shape=[jax.ShapeDtypeStruct((n, width), BF), jax.ShapeDtypeStruct((n, width), F32)],
        scratch_shapes=[pltpu.VMEM((2, length, 128), BF), pltpu.VMEM((2, length, 128), BF)],
        compiler_params=pltpu.CompilerParams(vmem_limit_bytes=VMEM_BYTES),
        cost_estimate=NO_COST,
        name="attention_causal" if causal else "attention",
    )(core, q, own, got, query_ext, key_ext)


def backward_kernel(
    core_ref, q_ref, own_ref, got_ref, query_ext_ref, own_ext_ref, got_ext_ref, grad_ref, o_ref, log_ref,
    q_grad_ref, own_grad_ref, got_grad_ref, queries, grads, q_total, *, causal,
):
    step = pl.program_id(1)
    n, block = q_ref.shape[0], own_ref.shape[1]
    quarter = n // 2
    blocks = n // block
    core = core_ref[0]
    left, lane = lanes()

    @pl.when(step == 0)
    def _():
        log = log_ref[...]
        high = log.astype(BF).astype(F32)
        middle = (log - high).astype(BF).astype(F32)
        low = log - high - middle
        ext = query_ext_ref[...].astype(F32)
        ext = jnp.where(lane == 10, -low, ext)
        ext = jnp.where(lane == 9, -middle, jnp.where(lane == 8, -high, ext)).astype(BF)
        pair = q_ref[...]
        queries[0] = jnp.where(left, pair, ext)
        queries[1] = jnp.where(left, ext, pair)
        pair = grad_ref[...]
        product = pair.astype(F32) * o_ref[...].astype(F32)
        high = product.astype(BF)
        low = (product - high.astype(F32)).astype(BF)
        row = lax.broadcasted_iota(jnp.int32, (128, 128), 0)
        column = lax.broadcasted_iota(jnp.int32, (128, 128), 1)
        across = ((row < DH) != (column < DH)).astype(BF)
        inner = dot_nn(high, across) + dot_nn(low, across)
        high = inner.astype(BF).astype(F32)
        ext = jnp.where(lane == 8, -high, jnp.where(lane == 9, high - inner, 0.0)).astype(BF)
        grads[0] = jnp.where(left, pair, ext)
        grads[1] = jnp.where(left, ext, pair)
        q_total[...] = jnp.zeros_like(q_total)

    own = step < blocks
    k = jnp.where(own, own_ref[0], got_ref[0])
    v = jnp.where(own, own_ref[1], got_ref[1])
    ext = jnp.where(own, own_ext_ref[...], got_ext_ref[...])
    ones = jnp.ones_like(v)
    keys = (jnp.where(left, k, ext), jnp.where(left, ext, k))
    values = (jnp.where(left, v, ones), jnp.where(left, ones, v))
    k_turned = k.T

    def part(begin, rows, diagonal):
        k_grads, v_grads = [], []
        here = slice(begin, begin + rows)
        for head in range(2):
            q, grad = queries[head, here, :], grads[head, here, :]
            scores = dot_nt(keys[head], q)
            if diagonal is not None:
                key = lax.broadcasted_iota(jnp.int32, scores.shape, 0) + diagonal
                query = lax.broadcasted_iota(jnp.int32, scores.shape, 1)
                scores = jnp.where(key <= query, scores, BIG)
            probs = jnp.exp2(scores)
            score_grad = (probs * dot_nt(values[head], grad)).astype(BF)
            v_grads.append(dot_nn(probs.astype(BF), grad))
            k_grads.append(dot_nn(score_grad, q))
            mine = slice(DH * head, DH * (head + 1))
            q_total[mine, here] += dot_nn(k_turned[mine], score_grad)
        return jnp.where(left, k_grads[0], k_grads[1]), jnp.where(left, v_grads[0], v_grads[1])

    def put(k_grad, v_grad):
        k_grad = (k_grad * math.log(2.0)).astype(BF)
        v_grad = v_grad.astype(BF)

        @pl.when(own)
        def _():
            own_grad_ref[0] = k_grad
            own_grad_ref[1] = v_grad

        @pl.when(jnp.logical_not(own))
        def _():
            got_grad_ref[0] = k_grad
            got_grad_ref[1] = v_grad

    if not causal:
        put(*part(0, n, None))
    else:
        each = quarter // block
        local_step = jnp.where(own, step, step - blocks)
        piece = local_step // each
        key_place = 2 * jnp.where(own, core, 1 - core) + piece
        diagonal = (local_step - piece * each) * block
        first, second = 2 * core, 2 * core + 1
        skip, cut, whole = 0, 1, 2

        def kind(query_place):
            return jnp.where(key_place > query_place, skip, jnp.where(key_place == query_place, cut, whole))

        for kinds in ((skip, skip), (skip, cut), (cut, whole), (whole, whole)):

            @pl.when(jnp.logical_and(kind(first) == kinds[0], kind(second) == kinds[1]))
            def _(kinds=kinds):
                k_grad = v_grad = jnp.zeros((block, 128), F32)
                for begin, how in zip((0, quarter), kinds):
                    if how != skip:
                        more = part(begin, quarter, diagonal if how == cut else None)
                        k_grad, v_grad = k_grad + more[0], v_grad + more[1]
                put(k_grad, v_grad)

    @pl.when(step == 2 * blocks - 1)
    def _():
        q_grad_ref[...] = (q_total[...] * DH**-0.5).T.astype(BF)


def attention_backward_half(core, kept, grad, causal):
    q, own, got, query_ext, own_ext, got_ext, o, log = kept
    n, width = q.shape
    block = 512
    blocks = n // block
    first = lambda b: jnp.minimum(b, blocks - 1)
    second = lambda b: jnp.maximum(b - blocks, 0)
    whole = pl.BlockSpec((n, 128), lambda p, b: (0, p))
    own_keys = pl.BlockSpec((2, block, 128), lambda p, b: (0, first(b), p))
    got_keys = pl.BlockSpec((2, block, 128), lambda p, b: (0, second(b), p))
    return pl.pallas_call(
        partial(backward_kernel, causal=causal),
        grid=(width // 128, 2 * blocks),
        in_specs=[
            pl.BlockSpec(memory_space=pltpu.SMEM),
            whole,
            own_keys,
            got_keys,
            pl.BlockSpec((n, 128), lambda p, b: (0, 0)),
            pl.BlockSpec((block, 128), lambda p, b: (first(b), 0)),
            pl.BlockSpec((block, 128), lambda p, b: (second(b), 0)),
            whole,
            whole,
            whole,
        ],
        out_specs=[whole, own_keys, got_keys],
        out_shape=[jax.ShapeDtypeStruct(s, BF) for s in ((n, width), own.shape, own.shape)],
        scratch_shapes=[
            pltpu.VMEM((2, n, 128), BF),
            pltpu.VMEM((2, n, 128), BF),
            pltpu.VMEM((128, n), F32),
        ],
        compiler_params=pltpu.CompilerParams(vmem_limit_bytes=VMEM_BYTES),
        cost_estimate=NO_COST,
        name="attention_causal_back" if causal else "attention_back",
    )(core, q, own, got, query_ext, own_ext, got_ext, grad, o, log)


def fold_dot(x, w):
    return dot_nn(x[:, :HALF], w[:, :HALF]) + dot_nn(x[:, HALF:], w[:, HALF:])


def fold_dot_t(g, w):
    return jnp.concatenate([dot_nt(g, w[:, :HALF]), dot_nt(g, w[:, HALF:])], axis=1)


def fold_grad(x, g):
    return jnp.concatenate([dot_tn(x[:, :HALF], g), dot_tn(x[:, HALF:], g)], axis=1)


def norm(v, gain, shift):
    centred = v - jnp.mean(v, axis=-1, keepdims=True)
    scale = lax.rsqrt(jnp.mean(centred * centred, axis=-1, keepdims=True) + EPS)
    unit = centred * scale
    return unit * gain + shift, unit, scale


def norm_back(grad, unit, scale, gain):
    inner = grad * gain
    mean_inner = jnp.mean(inner, axis=-1, keepdims=True)
    mean_unit = jnp.mean(inner * unit, axis=-1, keepdims=True)
    return scale * (inner - mean_inner - unit * mean_unit)


def over_rows(v):
    return jnp.sum(v, axis=0, keepdims=True)


GELU_C = math.sqrt(2.0 / math.pi)


def gelu(u):
    return 0.5 * u * (1.0 + jnp.tanh(GELU_C * u * (1.0 + 0.044715 * u * u)))


def gelu_both(u):
    square = u * u
    t = jnp.tanh(GELU_C * u * (1.0 + 0.044715 * square))
    half = 0.5 * (1.0 + t)
    slope = half + 0.5 * u * (1.0 - t * t) * (GELU_C * (1.0 + 3 * 0.044715 * square))
    return u * half, slope


def halt_gate(last, weight):
    logit = jnp.sum(last * weight, axis=-1, keepdims=True)
    return 1.0 / (1.0 + jnp.exp(-logit))


def halt_back(grad, start, last, runs, weight):
    gate = halt_gate(last, weight)
    used = runs * gate
    logit_grad = used * (1.0 - gate) * jnp.sum(grad * (last - start), axis=-1, keepdims=True)
    return grad * (1.0 - used), used * grad + logit_grad * weight, over_rows(logit_grad * last)


def ffn_blocks(own_ref, other_ref, begin):
    for which, ref in ((0, own_ref), (1, other_ref)):
        for j in range(2):
            up = begin + j * D
            down = up + 2 * D
            yield which, ref[up : up + D, :], ref[down : down + D, :], up, down


def ffn(low, own_ref, other_ref, begin):
    total = 0.0
    for _, up, down, _, _ in ffn_blocks(own_ref, other_ref, begin):
        total = total + dot_nn(gelu(dot_nn(low, up)).astype(BF), down)
    return total


def ffn_back(low, out_low, own_ref, other_ref, begin, acc, shift):
    total = 0.0
    for which, up, down, up_at, down_at in ffn_blocks(own_ref, other_ref, begin):
        active, slope = gelu_both(dot_nn(low, up))
        hidden = (dot_nt(out_low, down) * slope).astype(BF)
        up_at, down_at = up_at + shift, down_at + shift
        acc[which, down_at : down_at + D, :] += dot_tn(active.astype(BF), out_low)
        acc[which, up_at : up_at + D, :] += dot_tn(low, hidden)
        total = total + dot_nt(hidden, up)
    return total


def proj_back(o_refs, out_low, projs, acc, begin, o_grad_refs):
    for which in range(2):
        o_grad_refs[which][...] = dot_nt(out_low, projs[which]).astype(BF)
        acc[which, begin : begin + HALF, :] += dot_tn(o_refs[which][...], out_low)


def first_step(*refs):
    @pl.when(pl.program_id(0) == 0)
    def _():
        for ref in refs:
            ref[...] = jnp.zeros_like(ref)


def last_step(core_ref, acc, keep_ref, send_ref, small_acc=None, small_ref=None):
    @pl.when(pl.program_id(0) == pl.num_programs(0) - 1)
    def _():
        rows = acc.shape[1] // 2
        for part, ref in ((core_ref[0], keep_ref), (1 - core_ref[0], send_ref)):
            here = pl.ds(pl.multiple_of(part * rows, 16), rows)
            for which in range(acc.shape[0]):
                ref[which] = acc[which, here, :].astype(BF)
        if small_ref is not None:
            small_ref[...] = small_acc[...]


def pre_kernel(
    rows_ref, place_ref, own_ref, other_ref,
    start_ref, q0_ref, q1_ref, kv0_ref, kv1_ref,
):
    start = rows_ref[...].astype(F32) + place_ref[...]
    start_ref[...] = start
    low = start.astype(BF)
    for ref, q_ref, kv_ref in ((own_ref, q0_ref, kv0_ref), (other_ref, q1_ref, kv1_ref)):
        q_ref[...] = (fold_dot(low, ref[0:HALF, :]) * Q_SCALE).astype(BF)
        for kind in range(2):
            w = ref[(kind + 1) * HALF : (kind + 2) * HALF, :]
            kv_ref[kind] = fold_dot(low, w).astype(BF)


def enc_post_kernel(
    o0_ref, o1_ref, start_ref, runs_ref, own_ref, other_ref, small_ref,
    sum_one_ref, sum_two_ref, states_ref,
):
    start = start_ref[...]
    sum_one = start + dot_nn(o0_ref[...], own_ref[:HALF, :]) + dot_nn(o1_ref[...], other_ref[:HALF, :])
    sum_one_ref[...] = sum_one
    middle, _, _ = norm(sum_one, small_ref[0:1, :], small_ref[1:2, :])
    sum_two = middle + ffn(middle.astype(BF), own_ref, other_ref, HALF)
    sum_two_ref[...] = sum_two
    last, _, _ = norm(sum_two, small_ref[2:3, :], small_ref[3:4, :])
    gate = halt_gate(last, small_ref[4:5, :])
    states_ref[...] = (start + runs_ref[:, 0:1] * gate * (last - start)).astype(BF)


def dec_mid_kernel(
    o0_ref, o1_ref, start_ref, states_ref, proj_own_ref, proj_other_ref, own_ref, other_ref, small_ref,
    sum_ref, q0_ref, q1_ref, kv0_ref, kv1_ref,
):
    total = start_ref[...] + dot_nn(o0_ref[...], proj_own_ref[...])
    total = total + dot_nn(o1_ref[...], proj_other_ref[...])
    sum_ref[...] = total
    middle, _, _ = norm(total, small_ref[0:1, :], small_ref[1:2, :])
    low = middle.astype(BF)
    states = states_ref[...]
    for ref, q_ref, kv_ref in ((own_ref, q0_ref, kv0_ref), (other_ref, q1_ref, kv1_ref)):
        q_ref[...] = (fold_dot(low, ref[0:HALF, :]) * Q_SCALE).astype(BF)
        for kind in range(2):
            w = ref[(kind + 1) * HALF : (kind + 2) * HALF, :]
            kv_ref[kind] = fold_dot(states, w).astype(BF)


def dec_post_kernel(
    core_ref, o0_ref, o1_ref, sum_one_ref, start_ref, runs_ref, cot_ref, own_ref, other_ref, small_ref,
    states_ref, start_grad_ref, sum_grad_ref, o0_grad_ref, o1_grad_ref,
    keep_ref, send_ref, small_grad_ref,
    acc, small_acc,
):
    first_step(acc, small_acc)
    start = start_ref[...]
    projs = own_ref[:HALF, :], other_ref[:HALF, :]
    middle, _, _ = norm(sum_one_ref[...], small_ref[0:1, :], small_ref[1:2, :])
    sum_two = middle + dot_nn(o0_ref[...], projs[0]) + dot_nn(o1_ref[...], projs[1])
    gain_two = small_ref[2:3, :]
    mixed, unit_two, scale_two = norm(sum_two, gain_two, small_ref[3:4, :])
    low = mixed.astype(BF)
    sum_three = mixed + ffn(low, own_ref, other_ref, HALF)
    gain_three = small_ref[4:5, :]
    last, unit_three, scale_three = norm(sum_three, gain_three, small_ref[5:6, :])
    weight = small_ref[6:7, :]
    runs = runs_ref[:, 1:2]
    states_ref[...] = (start + runs * halt_gate(last, weight) * (last - start)).astype(BF)
    start_grad, last_grad, weight_grad = halt_back(
        cot_ref[...].astype(F32), start, last, runs, weight
    )
    start_grad_ref[...] = start_grad
    small_acc[4:5, :] += weight_grad
    small_acc[2:3, :] += over_rows(last_grad * unit_three)
    small_acc[3:4, :] += over_rows(last_grad)
    grad = norm_back(last_grad, unit_three, scale_three, gain_three)
    grad = grad + ffn_back(low, grad.astype(BF), own_ref, other_ref, HALF, acc, 0)
    small_acc[0:1, :] += over_rows(grad * unit_two)
    small_acc[1:2, :] += over_rows(grad)
    grad = norm_back(grad, unit_two, scale_two, gain_two)
    sum_grad_ref[...] = grad
    proj_back((o0_ref, o1_ref), grad.astype(BF), projs, acc, 0, (o0_grad_ref, o1_grad_ref))
    last_step(core_ref, acc, keep_ref, send_ref, small_acc, small_grad_ref)


def dec_mid_back_kernel(
    core_ref, q0_grad_ref, q1_grad_ref, sum_grad_ref, sum_one_ref, start_grad_ref, o0_ref, o1_ref,
    cq_own_ref, cq_other_ref, proj_own_ref, proj_other_ref, small_ref,
    out_ref, o0_grad_ref, o1_grad_ref, keep_ref, send_ref, small_grad_ref,
    acc, small_acc,
):
    first_step(acc, small_acc)
    gain = small_ref[0:1, :]
    middle, unit, scale = norm(sum_one_ref[...], gain, small_ref[1:2, :])
    low = middle.astype(BF)
    grad = sum_grad_ref[...]
    for which, (ref, part_ref) in enumerate(((cq_own_ref, q0_grad_ref), (cq_other_ref, q1_grad_ref))):
        grad = grad + fold_dot_t(part_ref[...], ref[...])
        acc[which, :HALF, :] += fold_grad(low, part_ref[...])
    small_acc[0:1, :] += over_rows(grad * unit)
    small_acc[1:2, :] += over_rows(grad)
    grad = norm_back(grad, unit, scale, gain)
    out_ref[...] = start_grad_ref[...] + grad
    projs = proj_own_ref[...], proj_other_ref[...]
    proj_back((o0_ref, o1_ref), grad.astype(BF), projs, acc, HALF, (o0_grad_ref, o1_grad_ref))
    last_step(core_ref, acc, keep_ref, send_ref, small_acc, small_grad_ref)


def kv_total(own_ref, got_ref, kind):
    return (own_ref[kind].astype(F32) + got_ref[kind].astype(F32)).astype(BF)


def enc_back_kernel(
    core_ref, kv0_ref, kv1_ref, got0_ref, got1_ref, states_ref, cot_ref, start_ref, sum_one_ref, sum_two_ref,
    o0_ref, o1_ref, runs_ref, cross_own_ref, cross_other_ref, own_ref, other_ref, small_ref,
    out_ref, o0_grad_ref, o1_grad_ref, keep_ref, send_ref, small_grad_ref,
    acc, small_acc,
):
    first_step(acc, small_acc)
    states = states_ref[...]
    grad = cot_ref[...].astype(F32)
    crosses = (cross_own_ref, kv0_ref, got0_ref), (cross_other_ref, kv1_ref, got1_ref)
    for which, (ref, kv_ref, got_ref) in enumerate(crosses):
        for kind in range(2):
            part = kv_total(kv_ref, got_ref, kind)
            at = kind * HALF
            grad = grad + fold_dot_t(part, ref[at + HALF : at + 2 * HALF, :])
            acc[which, at : at + HALF, :] += fold_grad(states, part)
    gain_one, gain_two, weight = small_ref[0:1, :], small_ref[2:3, :], small_ref[4:5, :]
    last, unit_two, scale_two = norm(sum_two_ref[...], gain_two, small_ref[3:4, :])
    start_grad, last_grad, weight_grad = halt_back(
        grad, start_ref[...], last, runs_ref[:, 0:1], weight
    )
    small_acc[4:5, :] += weight_grad
    small_acc[2:3, :] += over_rows(last_grad * unit_two)
    small_acc[3:4, :] += over_rows(last_grad)
    grad = norm_back(last_grad, unit_two, scale_two, gain_two)
    middle, unit_one, scale_one = norm(sum_one_ref[...], gain_one, small_ref[1:2, :])
    grad = grad + ffn_back(middle.astype(BF), grad.astype(BF), own_ref, other_ref, HALF, acc, 2 * HALF)
    small_acc[0:1, :] += over_rows(grad * unit_one)
    small_acc[1:2, :] += over_rows(grad)
    grad = norm_back(grad, unit_one, scale_one, gain_one)
    out_ref[...] = start_grad + grad
    projs = own_ref[:HALF, :], other_ref[:HALF, :]
    proj_back((o0_ref, o1_ref), grad.astype(BF), projs, acc, 2 * HALF, (o0_grad_ref, o1_grad_ref))
    last_step(core_ref, acc, keep_ref, send_ref, small_acc, small_grad_ref)


def qkv_back_kernel(
    core_ref, q_grad_ref, kv_ref, got_ref, start_ref, base_ref, w_ref,
    out_ref, keep_ref, send_ref,
    acc,
):
    first_step(acc)
    low = start_ref[...].astype(BF)
    grad = base_ref[...]
    parts = q_grad_ref[...], kv_total(kv_ref, got_ref, 0), kv_total(kv_ref, got_ref, 1)
    for kind, part in enumerate(parts):
        rows = slice(kind * HALF, (kind + 1) * HALF)
        grad = grad + fold_dot_t(part, w_ref[rows, :])
        acc[0, rows, :] += fold_grad(low, part)
    out_ref[...] = grad
    last_step(core_ref, acc, keep_ref, send_ref)


def rows_call(kernel, name, by_rows, whole, row_outs, whole_outs=(), scratch=(), core=None, block=512):
    n = by_rows[0].shape[-2]

    def row_spec(shape):
        if len(shape) == 3:
            return pl.BlockSpec((shape[0], block, shape[2]), lambda i: (0, i, 0))
        return pl.BlockSpec((block, shape[1]), lambda i: (i, 0))

    def whole_spec(entry):
        array, rows, index = entry if isinstance(entry, tuple) else (entry, entry.shape[0], 0)
        return pl.BlockSpec((rows, array.shape[1]), lambda i: (index, 0), pipeline_mode=pl.Buffered(1))

    arrays = [e[0] if isinstance(e, tuple) else e for e in whole]
    return pl.pallas_call(
        kernel,
        grid=(n // block,),
        in_specs=([] if core is None else [pl.BlockSpec(memory_space=pltpu.SMEM)])
        + [row_spec(a.shape) for a in by_rows]
        + [whole_spec(e) for e in whole],
        out_specs=[row_spec(s) for s, _ in row_outs]
        + [pl.BlockSpec(s, lambda i, s=s: (0,) * len(s)) for s, _ in whole_outs],
        out_shape=[jax.ShapeDtypeStruct(s, t) for s, t in [*row_outs, *whole_outs]],
        scratch_shapes=[pltpu.VMEM(s, F32) for s in scratch],
        compiler_params=pltpu.CompilerParams(vmem_limit_bytes=VMEM_BYTES),
        cost_estimate=NO_COST,
        name=name,
    )(*([] if core is None else [core]), *by_rows, *arrays)


def in_order_kernel(place_ref, mine_ref, got_ref, out_ref):
    piece, core = place_ref[0], place_ref[1]
    pieces, rows, _ = mine_ref.shape
    for ref, of in ((mine_ref, core), (got_ref, 1 - core)):
        for k in range(pieces):
            begin = (of * pieces + (piece ^ k)) * rows
            out_ref[pl.ds(pl.multiple_of(begin, 16), rows), :] = ref[k]


def in_order(place, mine, got):
    pieces, rows, width = mine.shape
    return pl.pallas_call(
        in_order_kernel,
        in_specs=[pl.BlockSpec(memory_space=pltpu.SMEM)] + [pl.BlockSpec(memory_space=pltpu.VMEM)] * 2,
        out_specs=pl.BlockSpec(memory_space=pltpu.VMEM),
        out_shape=jax.ShapeDtypeStruct((2 * pieces * rows, width), mine.dtype),
        compiler_params=pltpu.CompilerParams(vmem_limit_bytes=VMEM_BYTES),
        cost_estimate=NO_COST,
        name="in_order",
    )(place, mine, got)


class Place:
    def __init__(self, dp_size):
        self.dp_size = dp_size
        dp = lax.axis_index("dp")
        self.c = dp % 2
        self.stays = self.c == lax.axis_index("mp")
        self.masks = [1 << b for b in range(1, dp_size.bit_length() - 1)]
        self.bits = [(dp // mask) % 2 for mask in self.masks]
        self.core = self.c.astype(jnp.int32).reshape(1)
        piece = jnp.int32(0)
        for bit in self.bits:
            piece = 2 * piece + bit.astype(jnp.int32)
        self.order = jnp.concatenate([piece.reshape(1), self.core])
        self.pair = jnp.concatenate([jnp.zeros((1,), jnp.int32), self.core])

    def flip(self, values, mask):
        return lax.ppermute(values, "dp", [(d, d ^ mask) for d in range(self.dp_size)])

    def core_swap(self, values):
        return self.flip(values, 1)

    def y_swap(self, values):
        return lax.ppermute(values, "mp", [(0, 1), (1, 0)])

    def cross(self, values):
        perm = []
        for d in range(0, self.dp_size, 2):
            perm += [(2 * d + 1, 2 * d + 2), (2 * d + 2, 2 * d + 1)]
        return lax.ppermute(values, ("dp", "mp"), perm)


class Flow:
    def __init__(self):
        self.fresh = []
        self.chains = []
        self.results = {}

    def add(self, name, chain):
        self.fresh.append((name, chain, next(chain)))

    def go_on(self, name, chain, arrived):
        try:
            self.fresh.append((name, chain, chain.send(arrived)))
        except StopIteration as stop:
            self.results[name] = stop.value

    def step(self, values):
        due = [chain for chain in self.chains if chain[3] == 1]
        self.chains = [(*chain[:3], chain[3] - 1) for chain in self.chains if chain[3] > 1]
        values, arrived = lax.optimization_barrier((values, [chain[2] for chain in due]))
        for (name, chain, _, _), got in zip(due, arrived):
            self.go_on(name, chain, got)
        fresh, self.fresh = self.fresh, []
        values, operands = lax.optimization_barrier((values, [op[1] for _, _, op in fresh]))
        for (name, chain, (send, _, steps)), operand in zip(fresh, operands):
            self.chains.append((name, chain, send(operand), steps))
        return values

    def finish(self):
        while self.chains:
            name, chain, pending, _ = self.chains.pop(0)
            self.go_on(name, chain, pending)
        while self.fresh:
            name, chain, (send, operand, _) = self.fresh.pop(0)
            self.go_on(name, chain, send(operand))


def gathered(at, own, first=1, second=1):
    rows = own.shape[0] // 2
    near = yield at.y_swap, lax.dynamic_slice_in_dim(own, at.c * rows, rows, 0), first
    far = yield at.core_swap, near, second
    return in_order(at.pair, near[None], far[None])


def moved(at, values, steps):
    got = yield at.cross, values, steps
    return jnp.where(at.stays, values, got)


def plus(*values):
    return sum(v.astype(F32) for v in values).astype(BF)


def over_chips(at, total, steps, last_steps):
    for mask, bit in zip(at.masks, at.bits):
        rows = total.shape[0] // 2
        half = lax.dynamic_slice_in_dim(total, (1 - bit) * rows, rows, 0)
        got = yield partial(at.flip, mask=mask), half, steps
        total = plus(lax.dynamic_slice_in_dim(total, bit * rows, rows, 0), got)
    total = total[None]
    for mask in at.masks[::-1]:
        got = yield partial(at.flip, mask=mask), total, steps
        total = jnp.concatenate([total, got])
    far = yield at.core_swap, total, last_steps
    return in_order(at.order, total, far)


def summed(at, keep, send, core_steps=1, y_steps=1, steps=1, last_steps=1):
    got = yield at.core_swap, send, core_steps
    near = yield at.y_swap, plus(keep[1], got[1]), y_steps
    return (yield from over_chips(at, plus(keep[0], got[0], near), steps, last_steps))


def summed_other(at, keep, got, y_steps):
    near = yield at.y_swap, plus(keep[0], got[0]), y_steps
    return near


def summed_own(at, keep, send, near):
    got = yield at.core_swap, send, 1
    return (yield from over_chips(at, plus(keep[0], got[0], near), 1, 1))


def summed_small(at, values):
    for mask in [1, *at.masks]:
        values = values + (yield partial(at.flip, mask=mask), values, 1)
    return values + (yield at.y_swap, values, 1)


def rows_of(weight):
    if weight.ndim == 3:
        kinds, depth, width = weight.shape
        folded = jnp.concatenate([weight[:, : depth // 2], weight[:, depth // 2 :]], axis=2)
        return folded.reshape(kinds * depth // 2, 2 * width)
    depth, width = weight.shape
    if width == D:
        return weight
    if width < D:
        return jnp.concatenate([weight[: depth // 2], weight[depth // 2 :]], axis=1)
    return jnp.concatenate([weight[:, :D], weight[:, D:]], axis=0)


def rows_back(rows, shape):
    if len(shape) == 3:
        kinds, depth, width = shape
        folded = rows.reshape(kinds, depth // 2, 2 * width)
        return jnp.concatenate([folded[..., :width], folded[..., width:]], axis=1)
    depth, width = shape
    if width == D:
        return rows
    if width < D:
        return jnp.concatenate([rows[:, :width], rows[:, width:]], axis=0)
    return jnp.concatenate([rows[:depth], rows[depth:]], axis=1)


def unpack(rows, *weights):
    outs, begin = [], 0
    for weight in weights:
        count = weight.size // D
        outs.append(rows_back(rows[begin : begin + count].astype(F32), weight.shape))
        begin += count
    return outs


def extensions(segments):
    lane = jnp.arange(128, dtype=jnp.int32)[None, :] % DH
    same = segments[:, None] == lane
    for_query = jnp.where((lane < 8) & ~same, BIG, 0.0).astype(BF)
    for_key = jnp.where(lane < 8, same.astype(F32), jnp.where(lane < 11, 1.0, 0.0)).astype(BF)
    return for_query, for_key


Q_SCALE = DH**-0.5 * math.log2(math.e)


def chip_rows(
    source_rows,
    target_rows,
    source_segment,
    target_segment,
    running,
    enc_qkv,
    enc_proj,
    enc_up,
    enc_down,
    enc_gains,
    enc_shifts,
    dec_qkv,
    dec_proj,
    cross_query,
    cross_kv,
    cross_proj,
    dec_up,
    dec_down,
    dec_gains,
    dec_shifts,
    halt_weight,
    enc_cotangent,
    dec_cotangent,
    *,
    dp_size,
):
    at = Place(dp_size)
    flow = Flow()
    n = source_rows.shape[0]
    row = ((n, D), F32)
    row_low = ((n, D), BF)
    half_low = ((n, HALF), BF)
    kv_low = ((2, n, HALF), BF)

    ints = jnp.concatenate([source_segment[0], target_segment[0], running[0, 0], running[1, 0]])
    w_enc_qkv = rows_of(enc_qkv)
    flow.add("source", moved(at, source_rows[:, 0], 1))
    flow.add("w_enc_qkv", gathered(at, w_enc_qkv))
    flow.add("ints", moved(at, ints.reshape(6, n), 1))
    (target_rows,) = flow.step((target_rows,))

    w_dec_self = jnp.concatenate([rows_of(dec_qkv), rows_of(dec_proj)])
    w_enc = jnp.concatenate([rows_of(enc_proj), rows_of(enc_up), rows_of(enc_down)])
    w_cross = jnp.concatenate([rows_of(cross_query), rows_of(cross_kv)])
    w_dec = jnp.concatenate([rows_of(cross_proj), rows_of(dec_up), rows_of(dec_down)])
    cots = jnp.concatenate([enc_cotangent[:, 0].astype(BF), dec_cotangent[:, 0].astype(BF)], axis=1)
    pad = jnp.zeros((3, D), F32)
    small_enc = jnp.stack(
        [enc_gains[0], enc_shifts[0], enc_gains[1], enc_shifts[1], halt_weight[0]]
    )
    small_enc = jnp.concatenate([small_enc, pad])
    small_dec = jnp.stack(
        [dec_gains[0], dec_shifts[0], dec_gains[1], dec_shifts[1], dec_gains[2], dec_shifts[2], halt_weight[1]]
    )
    small_dec = jnp.concatenate([small_dec, pad[:1]])
    place = at.core[0] * n + jnp.arange(n, dtype=jnp.int32)
    embedding = signal(place.astype(F32)) + signal(jnp.ones((1,), F32))

    flow.add("target", moved(at, target_rows[:, 0], 2))
    flow.add("w_dec_self", gathered(at, w_dec_self, 2, 1))
    w_enc, w_cross, w_dec, embedding, cots = flow.step((w_enc, w_cross, w_dec, embedding, cots))
    source, ints = flow.results["source"], flow.results["ints"]
    source_segments, target_segments = ints[:2].reshape(-1), ints[2:4].reshape(-1)
    runs = jnp.transpose(jnp.pad(ints[4:].astype(F32), ((0, 126), (0, 0))))

    def tables(segments):
        for_query, for_key = extensions(segments)
        own = lax.dynamic_slice_in_dim(for_query, at.c * n, n, 0)
        own_keys = lax.dynamic_slice_in_dim(for_key, at.c * n, n, 0)
        got_keys = lax.dynamic_slice_in_dim(for_key, (1 - at.c) * n, n, 0)
        return own, (for_key, own_keys, got_keys)

    source_q, source_keys = tables(source_segments)
    target_q, target_keys = tables(target_segments)
    source_q, source_keys, target_q, target_keys = flow.step((source_q, source_keys, target_q, target_keys))

    def pre(rows, own, other):
        whole = [(own, 3 * HALF, 0), (other, 3 * HALF, 0)]
        return rows_call(
            pre_kernel, "project", [rows, embedding], whole,
            [row, half_low, half_low, kv_low, kv_low],
        )

    def attend(q, kv, got, query_ext, key_ext, causal=False):
        o, log = attention_forward_half(at.core, q, kv, got, query_ext, key_ext[0], causal)
        return o, (q, kv, got, query_ext, key_ext[1], key_ext[2], o, log)

    def attend_back(kept, grad, causal=False):
        return attention_backward_half(at.core, kept, grad, causal)

    w_enc_qkv_got = flow.results["w_enc_qkv"]
    enc_start, q0, q1, kv0, kv1 = pre(source, w_enc_qkv, w_enc_qkv_got)
    got0, got1 = at.core_swap(kv0), at.core_swap(kv1)
    enc_o0, enc_kept0 = attend(q0, kv0, got0, source_q, source_keys)
    flow.add("w_enc", gathered(at, w_enc, 2, 1))
    enc_o0, q1, kv1, got1 = flow.step((enc_o0, q1, kv1, got1))
    target = flow.results["target"]
    enc_o1, enc_kept1 = attend(q1, kv1, got1, source_q, source_keys)
    enc_o1, target = flow.step((enc_o1, target))

    w_dec_self_got = flow.results["w_dec_self"]
    dec_start, q0, q1, kv0, kv1 = pre(target, w_dec_self, w_dec_self_got)
    got0, got1 = at.core_swap(kv0), at.core_swap(kv1)
    self_o0, self_kept0 = attend(q0, kv0, got0, target_q, target_keys, True)
    flow.add("w_cross", gathered(at, w_cross))
    self_o0, q1, kv1, got1 = flow.step((self_o0, q1, kv1, got1))
    self_o1, self_kept1 = attend(q1, kv1, got1, target_q, target_keys, True)
    flow.add("w_dec", gathered(at, w_dec, 3, 1))
    self_o1, enc_o1 = flow.step((self_o1, enc_o1))
    w_enc_got = flow.results["w_enc"]
    enc_sum_one, enc_sum_two, enc_states = rows_call(
        enc_post_kernel, "encoder_feed", [enc_o0, enc_o1, enc_start, runs], [w_enc, w_enc_got, small_enc],
        [row, row, row_low],
    )
    flow.add("cots", moved(at, cots, 3))
    (enc_states,) = flow.step((enc_states,))
    w_cross_got = flow.results["w_cross"]
    dec_sum_one, q0, q1, kv0, kv1 = rows_call(
        dec_mid_kernel, "cross_project", [self_o0, self_o1, dec_start, enc_states],
        [(w_dec_self, HALF, 3), (w_dec_self_got, HALF, 3), w_cross, w_cross_got, small_dec],
        [row, half_low, half_low, kv_low, kv_low],
    )
    got0, got1 = at.core_swap(kv0), at.core_swap(kv1)
    q0, q1, kv0, kv1 = flow.step((q0, q1, kv0, kv1))
    cross_o0, cross_kept0 = attend(q0, kv0, got0, target_q, source_keys)
    cross_o0, q1, kv1, got1 = flow.step((cross_o0, q1, kv1, got1))
    cross_o1, cross_kept1 = attend(q1, kv1, got1, target_q, source_keys)
    flow.add("enc_states", moved(at, enc_states, 1))
    (cross_o1,) = flow.step((cross_o1,))
    cots = flow.results["cots"]
    enc_cot, dec_cot = cots[:, :D], cots[:, D:]

    def grad_outs(rows):
        return [((2, rows // 2, D), BF)] * 2 + [((8, D), F32)]

    w_dec_got = flow.results["w_dec"]
    (
        dec_states, start_grad, sum_grad, o0_grad, o1_grad, *dec_parts, small_two,
    ) = rows_call(
        dec_post_kernel, "decoder_feed",
        [cross_o0, cross_o1, dec_sum_one, dec_start, runs, dec_cot], [w_dec, w_dec_got, small_dec],
        [row_low, row, row, half_low, half_low], grad_outs(9 * HALF),
        [(2, 9 * HALF, D), (8, D)], at.core,
    )
    flow.add("dec", summed(at, *dec_parts))
    flow.add("dec_states", moved(at, dec_states, 1))
    o0_grad, o1_grad = flow.step((o0_grad, o1_grad))

    q0_grad, kv0_grad, kv0_send = attend_back(cross_kept0, o0_grad)
    q0_grad, kv0_grad, kv0_send, o1_grad = flow.step((q0_grad, kv0_grad, kv0_send, o1_grad))
    kv0_got = at.core_swap(kv0_send)
    q1_grad, kv1_grad, kv1_send = attend_back(cross_kept1, o1_grad)
    q1_grad, kv1_grad, kv1_send, kv0_got = flow.step((q1_grad, kv1_grad, kv1_send, kv0_got))
    kv1_got = at.core_swap(kv1_send)

    (
        enc_base, enc_o0_grad, enc_o1_grad, *enc_parts, small_enc_grad,
    ) = rows_call(
        enc_back_kernel, "encoder_feed_back",
        [kv0_grad, kv1_grad, kv0_got, kv1_got, enc_states, enc_cot, enc_start, enc_sum_one, enc_sum_two,
         enc_o0, enc_o1, runs],
        [w_cross, w_cross_got, w_enc, w_enc_got, small_enc],
        [row, half_low, half_low], grad_outs(11 * HALF), [(2, 11 * HALF, D), (8, D)], at.core,
    )
    flow.add("enc", summed(at, *enc_parts))
    enc_o0_grad, enc_o1_grad, q0_grad = flow.step((enc_o0_grad, enc_o1_grad, q0_grad))
    (
        dec_base, self_o0_grad, self_o1_grad, *mid_parts, small_one,
    ) = rows_call(
        dec_mid_back_kernel, "cross_project_back",
        [q0_grad, q1_grad, sum_grad, dec_sum_one, start_grad, self_o0, self_o1],
        [(w_cross, HALF, 0), (w_cross_got, HALF, 0), (w_dec_self, HALF, 3), (w_dec_self_got, HALF, 3), small_dec],
        [row, half_low, half_low], grad_outs(2 * HALF), [(2, 2 * HALF, D), (8, D)], at.core,
    )
    flow.add("small", summed_small(at, jnp.concatenate([small_enc_grad, small_one, small_two])))
    enc_o1_grad, mid_parts = flow.step((enc_o1_grad, mid_parts))

    def project_back(q_grad, kv_grad, got, start, base, weight):
        return rows_call(
            qkv_back_kernel, "project_back", [q_grad, kv_grad, got, start, base], [(weight, 3 * HALF, 0)],
            [row], [((1, 3 * HALF // 2, D), BF)] * 2, [(1, 3 * HALF, D)], at.core,
        )

    q1_grad, kv1_grad, kv1_send = attend_back(enc_kept1, enc_o1_grad)
    kv1_got = at.core_swap(kv1_send)
    q1_grad, kv1_grad, enc_o0_grad = flow.step((q1_grad, kv1_grad, enc_o0_grad))
    q0_grad, kv0_grad, kv0_send = attend_back(enc_kept0, enc_o0_grad)
    kv0_got = at.core_swap(kv0_send)
    q0_grad, kv0_grad, kv1_got, q1_grad = flow.step((q0_grad, kv0_grad, kv1_got, q1_grad))
    source_grad, keep1, send1 = project_back(q1_grad, kv1_grad, kv1_got, enc_start, enc_base, w_enc_qkv_got)
    source_grad, keep0, send0 = project_back(q0_grad, kv0_grad, kv0_got, enc_start, source_grad, w_enc_qkv)
    keep = jnp.concatenate([jnp.concatenate([keep0, keep1]), mid_parts[0]], axis=1)
    send = jnp.concatenate([jnp.concatenate([send0, send1]), mid_parts[1]], axis=1)
    source_low = source_grad.astype(BF)
    flow.add("enc_qkv", summed(at, keep, send, 1, 2))
    flow.add("source_grad", moved(at, source_low, 1))
    (self_o1_grad,) = flow.step((self_o1_grad,))

    q1_grad, kv1_grad, kv1_send = attend_back(self_kept1, self_o1_grad, True)
    q1_grad, kv1_grad, kv1_send, self_o0_grad = flow.step((q1_grad, kv1_grad, kv1_send, self_o0_grad))
    kv1_got = at.core_swap(kv1_send)
    target_grad, keep1, send1 = project_back(q1_grad, kv1_grad, kv1_got, dec_start, dec_base, w_dec_self_got)
    flow.add("dec_qkv_other", summed_other(at, keep1, at.core_swap(send1), 1))
    target_grad, self_o0_grad = flow.step((target_grad, self_o0_grad))
    q0_grad, kv0_grad, kv0_send = attend_back(self_kept0, self_o0_grad, True)
    q0_grad, kv0_grad, kv0_send, target_grad = flow.step((q0_grad, kv0_grad, kv0_send, target_grad))
    kv0_got = at.core_swap(kv0_send)
    target_grad, keep0, send0 = project_back(q0_grad, kv0_grad, kv0_got, dec_start, target_grad, w_dec_self)
    target_grad, keep0, send0 = flow.step((target_grad, keep0, send0))
    flow.add("dec_qkv", summed_own(at, keep0, send0, flow.results["dec_qkv_other"]))
    flow.add("target_grad", moved(at, target_grad.astype(BF), 1))
    flow.finish()

    done = flow.results
    cross_proj_grad, dec_up_grad, dec_down_grad = unpack(done["dec"], cross_proj, dec_up, dec_down)
    cross_kv_grad, enc_proj_grad, enc_up_grad, enc_down_grad = unpack(
        done["enc"], cross_kv, enc_proj, enc_up, enc_down
    )
    both = done["enc_qkv"].reshape(2, -1, D)
    (enc_qkv_grad,) = unpack(both[:, : 3 * HALF // 2].reshape(-1, D), enc_qkv)
    cross_query_grad, dec_proj_grad = unpack(
        both[:, 3 * HALF // 2 :].reshape(-1, D), cross_query, dec_proj
    )
    (dec_qkv_grad,) = unpack(done["dec_qkv"], dec_qkv)
    small = done["small"]
    enc_small, one, two = small[:8], small[8:16], small[16:]
    return (
        done["enc_states"][:, None],
        done["dec_states"][:, None],
        done["source_grad"].astype(F32)[:, None],
        done["target_grad"].astype(F32)[:, None],
        enc_qkv_grad,
        enc_proj_grad,
        enc_up_grad,
        enc_down_grad,
        enc_small[0:3:2],
        enc_small[1:4:2],
        dec_qkv_grad,
        dec_proj_grad,
        cross_query_grad,
        cross_kv_grad,
        cross_proj_grad,
        dec_up_grad,
        dec_down_grad,
        jnp.concatenate([one[0:1], two[0:3:2]]),
        jnp.concatenate([one[1:2], two[1:4:2]]),
        jnp.stack([enc_small[4], two[4]]),
    )


def solution(mesh):
    dp_size, mp_size = mesh.shape["dp"], mesh.shape["mp"]
    by_chip = mp_size == 2 and dp_size in (4, 8, 16)
    body = partial(chip_rows, dp_size=dp_size) if by_chip else local
    return jax.shard_map(
        body,
        mesh=mesh,
        in_specs=(
            P("mp", "dp", None),
            P("mp", "dp", None),
            P("dp", None),
            P("dp", None),
            P(None, "dp", "mp"),
            P(None, None, "mp"),
            P("mp", None),
            P(None, "mp"),
            P("mp", None),
            P(),
            P(),
            P(None, None, "mp"),
            P("mp", None),
            P(None, "mp"),
            P(None, None, "mp"),
            P("mp", None),
            P(None, "mp"),
            P("mp", None),
            P(),
            P(),
            P(),
            P("mp", "dp", None),
            P("mp", "dp", None),
        ),
        out_specs=(
            P("mp", "dp", None),
            P("mp", "dp", None),
            P("mp", "dp", None),
            P("mp", "dp", None),
            P(None, None, "mp"),
            P("mp", None),
            P(None, "mp"),
            P("mp", None),
            P(),
            P(),
            P(None, None, "mp"),
            P("mp", None),
            P(None, "mp"),
            P(None, None, "mp"),
            P("mp", None),
            P(None, "mp"),
            P("mp", None),
            P(),
            P(),
            P(),
        ),
        check_vma=False,
    )
```

```python
import math
from functools import partial

import jax
import jax.numpy as jnp
from jax import lax
from jax.experimental import pallas as pl
from jax.experimental.pallas import tpu as pltpu
from jax.sharding import PartitionSpec as P

D = 512
DH = 64


EPS = 1e-05
NEGATIVE = -1000000000.0


def signal(position):
    half_width = D // 2
    inverse_rates = jnp.exp(
        jnp.arange(half_width, dtype=jnp.float32) * (-jnp.log(10000.0) / (half_width - 1))
    )
    angles = position[:, None] * inverse_rates[None, :]
    return jnp.concatenate([jnp.sin(angles), jnp.cos(angles)], axis=1)


def normalize(values, norm_gain, norm_shift):
    centred = values - jnp.mean(values, axis=-1, keepdims=True)
    spread = jnp.mean(centred * centred, axis=-1, keepdims=True)
    return centred * lax.rsqrt(spread + EPS) * norm_gain + norm_shift


def halting(running_now, initial, updated, weight):
    halt_prob = jax.nn.sigmoid(jnp.sum(updated * weight, axis=-1, keepdims=True))
    return initial + running_now * halt_prob * (updated - initial)


def dot_last(left, right):
    return lax.dot_general(
        left, right, (((left.ndim - 1,), (1,)), ((), ())), preferred_element_type=jnp.float32
    )


def collect(piece_rows):
    return lax.all_gather(piece_rows, "mp", axis=0, tiled=True)


def collect_grad(piece_rows):
    return lax.all_gather(piece_rows.astype(jnp.bfloat16), "mp", axis=0, tiled=True)


def project_out(hidden, weight, rows):

    def partial_term(begin_row, row_count):
        return jnp.dot(hidden, weight, preferred_element_type=jnp.float32)

    return lax.psum_scatter(
        partial_term(jnp.int32(0), lax.axis_size("mp") * rows).astype(jnp.bfloat16),
        "mp",
        scatter_dimension=0,
        tiled=True,
    ).astype(jnp.float32)


def project_back(gradients, matrices, rows):

    def partial_term(begin_row, row_count):
        summed = jnp.zeros(
            (row_count,) + gradients[0].shape[1:-1] + (matrices[0].shape[0],), jnp.float32
        )
        for gradient, matrix in zip(gradients, matrices):
            summed = summed + dot_last(gradient, matrix)
        return summed

    return lax.psum_scatter(
        partial_term(jnp.int32(0), lax.axis_size("mp") * rows).astype(jnp.bfloat16),
        "mp",
        scatter_dimension=0,
        tiled=True,
    ).astype(jnp.float32)


def to_pairs(values):
    length, row_count, width = values.shape
    return (
        values.reshape(length, row_count, width // DH, DH)
        .transpose(1, 2, 0, 3)
        .reshape(-1, length, DH)
    )


def from_pairs(values, row_count):
    pairs, length, unused = values.shape
    heads_here = pairs // row_count
    return (
        values.reshape(row_count, heads_here, length, DH)
        .transpose(2, 0, 1, 3)
        .reshape(length, row_count, heads_here * DH)
    )


def per_pair(segments, width):
    return jnp.repeat(segments, width // DH, axis=0)


def pair_scores(query_block, key_rows, segment_block, segment_keys, first_row, causal):
    scores = lax.dot_general(
        query_block, key_rows, (((1,), (1,)), ((), ())), preferred_element_type=jnp.float32
    )
    scores = scores * DH ** (-0.5)
    allowed = segment_block[:, None] == segment_keys[None, :]
    if causal:
        query_place = first_row + jnp.arange(query_block.shape[0], dtype=jnp.int32)
        key_place = jnp.arange(key_rows.shape[0], dtype=jnp.int32)
        allowed = allowed & (key_place[None, :] <= query_place[:, None])
    return jnp.where(allowed, scores, NEGATIVE)


def attend_pair(inputs, causal):
    query_rows, key_rows, value_rows, segment_query, segment_keys = inputs
    length = query_rows.shape[0]
    block_rows = min(512, length)
    blocks = length // block_rows
    firsts = jnp.arange(blocks, dtype=jnp.int32) * block_rows

    def one_block(pieces):
        query_block, segment_block, first_row = pieces
        scores = pair_scores(query_block, key_rows, segment_block, segment_keys, first_row, causal)
        highest = jnp.max(scores, axis=1, keepdims=True)
        exponent = jnp.exp(scores - highest)
        totals = jnp.sum(exponent, axis=1, keepdims=True)
        weights = (exponent / totals).astype(jnp.bfloat16)
        mixed = jnp.dot(weights, value_rows, preferred_element_type=jnp.float32)
        return (mixed.astype(jnp.bfloat16), (highest + jnp.log(totals))[:, 0])

    mixed, log_total = lax.map(
        one_block,
        (
            query_rows.reshape(blocks, block_rows, -1),
            segment_query.reshape(blocks, block_rows),
            firsts,
        ),
    )
    return (mixed.reshape(length, -1), log_total.reshape(length))


def attend_pair_back(inputs, causal):
    query_rows, key_rows, value_rows, mixed_grad, log_total, segment_query, segment_keys = inputs
    length = query_rows.shape[0]
    block_rows = min(512, length)
    blocks = length // block_rows
    firsts = jnp.arange(blocks, dtype=jnp.int32) * block_rows

    def one_block(carry, pieces):
        key_total, value_total = carry
        query_block, grad_block, log_block, segment_block, first_row = pieces
        scores = pair_scores(query_block, key_rows, segment_block, segment_keys, first_row, causal)
        probs = jnp.exp(scores - log_block[:, None])
        weights = probs.astype(jnp.bfloat16)
        prob_grad = lax.dot_general(
            grad_block, value_rows, (((1,), (1,)), ((), ())), preferred_element_type=jnp.float32
        )
        inner = jnp.sum(probs * prob_grad, axis=1, keepdims=True)
        score_grad = (probs * (prob_grad - inner)).astype(jnp.bfloat16)
        query_grad = jnp.dot(score_grad, key_rows, preferred_element_type=jnp.float32) * DH ** (
            -0.5
        )
        key_total = key_total + lax.dot_general(
            score_grad, query_block, (((0,), (0,)), ((), ())), preferred_element_type=jnp.float32
        ) * DH ** (-0.5)
        value_total = value_total + lax.dot_general(
            weights, grad_block, (((0,), (0,)), ((), ())), preferred_element_type=jnp.float32
        )
        return ((key_total, value_total), query_grad.astype(jnp.bfloat16))

    zeros_start = jnp.zeros(key_rows.shape, jnp.float32)
    (key_total, value_total), query_grad = lax.scan(
        one_block,
        (zeros_start, zeros_start),
        (
            query_rows.reshape(blocks, block_rows, -1),
            mixed_grad.reshape(blocks, block_rows, -1),
            log_total.reshape(blocks, block_rows),
            segment_query.reshape(blocks, block_rows),
            firsts,
        ),
    )
    return (
        query_grad.reshape(length, -1),
        key_total.astype(jnp.bfloat16),
        value_total.astype(jnp.bfloat16),
    )


def attention_forward(
    query_full,
    key_full,
    weight_query,
    weight_key,
    weight_value,
    weight_out,
    segment_query,
    segment_keys,
    causal,
    rows,
):
    queries = jnp.dot(query_full, weight_query, preferred_element_type=jnp.float32).astype(
        jnp.bfloat16
    )
    keys_low = jnp.dot(key_full, weight_key, preferred_element_type=jnp.float32).astype(
        jnp.bfloat16
    )
    values_low = jnp.dot(key_full, weight_value, preferred_element_type=jnp.float32).astype(
        jnp.bfloat16
    )
    width = queries.shape[2]
    row_count = queries.shape[1]
    mixed, log_total = lax.map(
        partial(attend_pair, causal=causal),
        (
            to_pairs(queries),
            to_pairs(keys_low),
            to_pairs(values_low),
            per_pair(segment_query, width),
            per_pair(segment_keys, width),
        ),
    )
    mixed = from_pairs(mixed, row_count)
    branch = project_out(mixed, weight_out, rows)
    return (branch, (queries, keys_low, values_low, mixed, log_total))


def attention_backward(
    branch_grad, kept, query_full, key_full, weight_out, segment_query, segment_keys, causal
):
    queries, keys_low, values_low, kept_mixed, log_total = kept
    grad_full = collect_grad(branch_grad)
    out_weight_grad = jnp.einsum(
        "lrc,lrd->cd", kept_mixed, grad_full, preferred_element_type=jnp.float32
    )
    mixed_grad = dot_last(grad_full, weight_out).astype(jnp.bfloat16)
    width = queries.shape[2]
    row_count = queries.shape[1]
    query_grad, key_grad, value_grad = lax.map(
        partial(attend_pair_back, causal=causal),
        (
            to_pairs(queries),
            to_pairs(keys_low),
            to_pairs(values_low),
            to_pairs(mixed_grad),
            log_total,
            per_pair(segment_query, width),
            per_pair(segment_keys, width),
        ),
    )
    query_grad = from_pairs(query_grad, row_count)
    key_grad = from_pairs(key_grad, row_count)
    value_grad = from_pairs(value_grad, row_count)
    weight_grads = (
        jnp.einsum("lrd,lrc->dc", query_full, query_grad, preferred_element_type=jnp.float32),
        jnp.einsum("lrd,lrc->dc", key_full, key_grad, preferred_element_type=jnp.float32),
        jnp.einsum("lrd,lrc->dc", key_full, value_grad, preferred_element_type=jnp.float32),
    )
    return (query_grad, key_grad, value_grad, weight_grads, out_weight_grad)


def feed_forward(source_full, weight_up, weight_down, rows):
    hidden = jnp.dot(source_full, weight_up, preferred_element_type=jnp.float32)
    active = jax.nn.gelu(hidden).astype(jnp.bfloat16)
    return (project_out(active, weight_down, rows), hidden)


def feed_backward(branch_grad, source_full, hidden, weight_up, weight_down, rows):
    grad_full = collect_grad(branch_grad)
    active, gelu_back = jax.vjp(jax.nn.gelu, hidden)
    active = active.astype(jnp.bfloat16)
    down_grad = jnp.einsum("lrf,lrd->fd", active, grad_full, preferred_element_type=jnp.float32)
    hidden_grad = gelu_back(dot_last(grad_full, weight_down))[0].astype(jnp.bfloat16)
    up_grad = jnp.einsum(
        "lrd,lrf->df", source_full, hidden_grad, preferred_element_type=jnp.float32
    )
    input_grad = project_back((hidden_grad,), (weight_up,), rows)
    return (input_grad, up_grad, down_grad)


def local(
    source_rows,
    target_rows,
    source_segment,
    target_segment,
    running,
    enc_qkv,
    enc_proj,
    enc_up,
    enc_down,
    enc_gains,
    enc_shifts,
    dec_qkv,
    dec_proj,
    cross_query,
    cross_kv,
    cross_proj,
    dec_up,
    dec_down,
    dec_gains,
    dec_shifts,
    halt_weight,
    enc_cotangent,
    dec_cotangent,
):
    rows = source_rows.shape[0]
    position = (lax.axis_index("mp") * rows + jnp.arange(rows, dtype=jnp.int32)).astype(jnp.float32)
    embedding = (signal(position) + signal(jnp.ones((1,), jnp.float32)))[:, None, :]
    runs_now = jnp.transpose(running, (0, 2, 1)).astype(jnp.float32)[..., None]
    enc_start = source_rows.astype(jnp.float32) + embedding
    enc_start_low = enc_start.astype(jnp.bfloat16)
    enc_start_full = collect(enc_start_low)
    enc_attn, enc_attn_kept = attention_forward(
        enc_start_full,
        enc_start_full,
        enc_qkv[0],
        enc_qkv[1],
        enc_qkv[2],
        enc_proj,
        source_segment,
        source_segment,
        False,
        rows,
    )
    enc_sum_one = enc_start + enc_attn
    enc_middle = normalize(enc_sum_one, enc_gains[0], enc_shifts[0])
    enc_middle_low = enc_middle.astype(jnp.bfloat16)
    enc_middle_full = collect(enc_middle_low)
    enc_ffn, enc_hidden = feed_forward(enc_middle_full, enc_up, enc_down, rows)
    enc_sum_two = enc_middle + enc_ffn
    enc_last = normalize(enc_sum_two, enc_gains[1], enc_shifts[1])
    enc_final = halting(runs_now[0], enc_start, enc_last, halt_weight[0])
    enc_states = enc_final.astype(jnp.bfloat16)
    enc_states_full = collect(enc_states)
    dec_start = target_rows.astype(jnp.float32) + embedding
    dec_start_low = dec_start.astype(jnp.bfloat16)
    dec_start_full = collect(dec_start_low)
    dec_self, dec_self_kept = attention_forward(
        dec_start_full,
        dec_start_full,
        dec_qkv[0],
        dec_qkv[1],
        dec_qkv[2],
        dec_proj,
        target_segment,
        target_segment,
        True,
        rows,
    )
    dec_sum_one = dec_start + dec_self
    dec_middle = normalize(dec_sum_one, dec_gains[0], dec_shifts[0])
    dec_middle_low = dec_middle.astype(jnp.bfloat16)
    dec_middle_full = collect(dec_middle_low)
    dec_cross, dec_cross_kept = attention_forward(
        dec_middle_full,
        enc_states_full,
        cross_query,
        cross_kv[0],
        cross_kv[1],
        cross_proj,
        target_segment,
        source_segment,
        False,
        rows,
    )
    dec_sum_two = dec_middle + dec_cross
    dec_mixed = normalize(dec_sum_two, dec_gains[1], dec_shifts[1])
    dec_mixed_low = dec_mixed.astype(jnp.bfloat16)
    dec_mixed_full = collect(dec_mixed_low)
    dec_ffn, dec_hidden = feed_forward(dec_mixed_full, dec_up, dec_down, rows)
    dec_sum_three = dec_mixed + dec_ffn
    dec_last = normalize(dec_sum_three, dec_gains[2], dec_shifts[2])
    dec_final = halting(runs_now[1], dec_start, dec_last, halt_weight[1])
    dec_states = dec_final.astype(jnp.bfloat16)
    unused, halt_back = jax.vjp(partial(halting, runs_now[1]), dec_start, dec_last, halt_weight[1])
    dec_start_grad, last_grad, dec_halt_grad = halt_back(dec_cotangent)
    unused, norm_back = jax.vjp(normalize, dec_sum_three, dec_gains[2], dec_shifts[2])
    sum_grad, dec_gain_three, dec_shift_three = norm_back(last_grad)
    ffn_input_grad, dec_up_grad, dec_down_grad = feed_backward(
        sum_grad, dec_mixed_full, dec_hidden, dec_up, dec_down, rows
    )
    mixed_grad = sum_grad + ffn_input_grad
    unused, norm_back = jax.vjp(normalize, dec_sum_two, dec_gains[1], dec_shifts[1])
    sum_grad, dec_gain_two, dec_shift_two = norm_back(mixed_grad)
    query_grad, key_grad, value_grad, cross_grads, cross_proj_grad = attention_backward(
        sum_grad,
        dec_cross_kept,
        dec_middle_full,
        enc_states_full,
        cross_proj,
        target_segment,
        source_segment,
        False,
    )
    middle_grad = sum_grad + project_back((query_grad,), (cross_query,), rows)
    enc_extra = project_back((key_grad, value_grad), (cross_kv[0], cross_kv[1]), rows)
    unused, norm_back = jax.vjp(normalize, dec_sum_one, dec_gains[0], dec_shifts[0])
    sum_grad, dec_gain_one, dec_shift_one = norm_back(middle_grad)
    query_grad, key_grad, value_grad, self_grads, dec_proj_grad = attention_backward(
        sum_grad,
        dec_self_kept,
        dec_start_full,
        dec_start_full,
        dec_proj,
        target_segment,
        target_segment,
        True,
    )
    target_grad = (
        sum_grad
        + dec_start_grad
        + project_back(
            (query_grad, key_grad, value_grad), (dec_qkv[0], dec_qkv[1], dec_qkv[2]), rows
        )
    )
    dec_qkv_grad = jnp.stack(self_grads)
    cross_query_grad = cross_grads[0]
    cross_kv_grad = jnp.stack([cross_grads[1], cross_grads[2]])
    enc_final_grad = enc_cotangent + enc_extra
    unused, halt_back = jax.vjp(partial(halting, runs_now[0]), enc_start, enc_last, halt_weight[0])
    enc_start_grad, last_grad, enc_halt_grad = halt_back(enc_final_grad)
    unused, norm_back = jax.vjp(normalize, enc_sum_two, enc_gains[1], enc_shifts[1])
    sum_grad, enc_gain_two, enc_shift_two = norm_back(last_grad)
    ffn_input_grad, enc_up_grad, enc_down_grad = feed_backward(
        sum_grad, enc_middle_full, enc_hidden, enc_up, enc_down, rows
    )
    middle_grad = sum_grad + ffn_input_grad
    unused, norm_back = jax.vjp(normalize, enc_sum_one, enc_gains[0], enc_shifts[0])
    sum_grad, enc_gain_one, enc_shift_one = norm_back(middle_grad)
    query_grad, key_grad, value_grad, self_grads, enc_proj_grad = attention_backward(
        sum_grad,
        enc_attn_kept,
        enc_start_full,
        enc_start_full,
        enc_proj,
        source_segment,
        source_segment,
        False,
    )
    source_grad = (
        sum_grad
        + enc_start_grad
        + project_back(
            (query_grad, key_grad, value_grad), (enc_qkv[0], enc_qkv[1], enc_qkv[2]), rows
        )
    )
    enc_qkv_grad = jnp.stack(self_grads)
    (
        enc_qkv_grad,
        enc_proj_grad,
        enc_up_grad,
        enc_down_grad,
        dec_qkv_grad,
        dec_proj_grad,
        cross_query_grad,
        cross_kv_grad,
        cross_proj_grad,
        dec_up_grad,
        dec_down_grad,
    ) = (
        lax.psum(enc_qkv_grad.astype(jnp.bfloat16), "dp").astype(jnp.float32),
        lax.psum(enc_proj_grad.astype(jnp.bfloat16), "dp").astype(jnp.float32),
        lax.psum(enc_up_grad.astype(jnp.bfloat16), "dp").astype(jnp.float32),
        lax.psum(enc_down_grad.astype(jnp.bfloat16), "dp").astype(jnp.float32),
        lax.psum(dec_qkv_grad.astype(jnp.bfloat16), "dp").astype(jnp.float32),
        lax.psum(dec_proj_grad.astype(jnp.bfloat16), "dp").astype(jnp.float32),
        lax.psum(cross_query_grad.astype(jnp.bfloat16), "dp").astype(jnp.float32),
        lax.psum(cross_kv_grad.astype(jnp.bfloat16), "dp").astype(jnp.float32),
        lax.psum(cross_proj_grad.astype(jnp.bfloat16), "dp").astype(jnp.float32),
        lax.psum(dec_up_grad.astype(jnp.bfloat16), "dp").astype(jnp.float32),
        lax.psum(dec_down_grad.astype(jnp.bfloat16), "dp").astype(jnp.float32),
    )
    enc_gains_grad, enc_shifts_grad, dec_gains_grad, dec_shifts_grad, halt_weight_grad = lax.psum(
        (
            jnp.stack([enc_gain_one, enc_gain_two]),
            jnp.stack([enc_shift_one, enc_shift_two]),
            jnp.stack([dec_gain_one, dec_gain_two, dec_gain_three]),
            jnp.stack([dec_shift_one, dec_shift_two, dec_shift_three]),
            jnp.stack([enc_halt_grad, dec_halt_grad]),
        ),
        ("dp", "mp"),
    )
    return (
        enc_states,
        dec_states,
        source_grad,
        target_grad,
        enc_qkv_grad,
        enc_proj_grad,
        enc_up_grad,
        enc_down_grad,
        enc_gains_grad,
        enc_shifts_grad,
        dec_qkv_grad,
        dec_proj_grad,
        cross_query_grad,
        cross_kv_grad,
        cross_proj_grad,
        dec_up_grad,
        dec_down_grad,
        dec_gains_grad,
        dec_shifts_grad,
        halt_weight_grad,
    )


BIG = -1e30
BF = jnp.bfloat16
F32 = jnp.float32
NN = (((1,), (0,)), ((), ()))
NT = (((1,), (1,)), ((), ()))
TN = (((0,), (0,)), ((), ()))
HALF = D // 2
VMEM_BYTES = 56 * 1024 * 1024
COST = pl.CostEstimate(flops=1, bytes_accessed=1, transcendentals=0)


def dot_nn(a, b):
    return lax.dot_general(a, b, NN, preferred_element_type=F32)


def dot_nt(a, b):
    return lax.dot_general(a, b, NT, preferred_element_type=F32)


def dot_tn(a, b):
    return lax.dot_general(a, b, TN, preferred_element_type=F32)


def lanes():
    lane = lax.broadcasted_iota(jnp.int32, (1, 128), 1)
    return lane < DH, lane % DH


def softmax_tasks(tasks, scores_of, after):
    ahead = scores_of(*tasks[0])
    for i, task in enumerate(tasks):
        now = ahead
        if i + 1 < len(tasks):
            ahead = scores_of(*tasks[i + 1])
        after(now, *task)


def forward_kernel(
    core_ref, q_ref, own_ref, got_ref, hot_ref, key_hot_ref, o_ref, log_ref, keys, values, *, causal
):
    n = q_ref.shape[0]
    chunk = n // 2
    core = core_ref[0]
    left, lane = lanes()
    for ref, of in ((own_ref, core), (got_ref, 1 - core)):
        here = pl.ds(pl.multiple_of(of * n, n), n)
        k, hot = ref[0], key_hot_ref[here, :]
        ext = jnp.where((lane >= 8) & (lane < 11), jnp.ones_like(hot), hot)
        keys[0, here, :] = jnp.where(left, k, ext)
        keys[1, here, :] = jnp.where(left, ext, k)
        turned = ref[1].T
        ones = jnp.ones((DH, n), BF)
        values[0, :, here] = jnp.concatenate([turned[:DH], ones])
        values[1, :, here] = jnp.concatenate([ones, turned[DH:]])
    pair = q_ref[...]
    mine = hot_ref[pl.ds(pl.multiple_of(core * n, n), n), :].astype(F32)
    ext = jnp.where(lane < 8, (1.0 - mine) * BIG, 0.0).astype(BF)
    queries = jnp.where(left, pair, ext), jnp.where(left, ext, pair)

    def run(tasks, rows):
        state = {}

        def scores_of(head, query, key, cut):
            q = queries[head][query * rows : (query + 1) * rows]
            scores = dot_nt(keys[head, key * chunk : (key + 1) * chunk, :], q)
            if cut:
                at = lax.broadcasted_iota(jnp.int32, scores.shape, 0)
                to = lax.broadcasted_iota(jnp.int32, scores.shape, 1)
                scores = jnp.where(at <= to, scores, BIG)
            return scores

        def after(scores, head, query, key, cut):
            top = jnp.max(scores, axis=0, keepdims=True)
            total = 0.0
            if (head, query) in state:
                old_top, total = state[head, query]
                top = jnp.maximum(top, old_top)
                total = total * jnp.exp2(old_top - top)
            probs = jnp.exp2(scores - top).astype(BF)
            total = total + dot_nn(values[head, :, key * chunk : (key + 1) * chunk], probs)
            state[head, query] = top, total

        softmax_tasks(tasks, scores_of, after)
        for query in range(n // rows):
            (top0, total0), (top1, total1) = state[0, query], state[1, query]
            out = jnp.concatenate([total0[:DH] / total0[DH:], total1[DH:] / total1[:DH]])
            logs = jnp.concatenate([top1 + jnp.log2(total1[:DH]), top0 + jnp.log2(total0[DH:])])
            here = slice(query * rows, (query + 1) * rows)
            o_ref[here, :] = out.T.astype(BF)
            log_ref[here, :] = logs.T

    if not causal:
        run([(head, 0, key, False) for head in range(2) for key in range(4)], n)
    else:
        for case in range(2):

            @pl.when(core == case)
            def _(case=case):
                run(
                    [
                        (head, query, key, key == 2 * case + query)
                        for head in range(2)
                        for query in range(2)
                        for key in range(2 * case + query + 1)
                    ],
                    chunk,
                )


def heads_forward(core, q, own, got, hot, key_hot, causal):
    n, width = q.shape
    length = 2 * n
    keys = pl.BlockSpec((2, n, 128), lambda p: (0, 0, p))
    queries = pl.BlockSpec((n, 128), lambda p: (0, p))
    table = pl.BlockSpec((length, 128), lambda p: (0, 0))
    return pl.pallas_call(
        partial(forward_kernel, causal=causal),
        grid=(width // 128,),
        in_specs=[
            pl.BlockSpec(memory_space=pltpu.SMEM),
            queries,
            keys,
            keys,
            table,
            table,
        ],
        out_specs=[queries, queries],
        out_shape=[jax.ShapeDtypeStruct((n, width), BF), jax.ShapeDtypeStruct((n, width), F32)],
        scratch_shapes=[pltpu.VMEM((2, length, 128), BF), pltpu.VMEM((2, 128, length), BF)],
        compiler_params=pltpu.CompilerParams(vmem_limit_bytes=VMEM_BYTES),
        cost_estimate=COST,
        name="attention_causal" if causal else "attention",
    )(core, q, own, got, hot, key_hot)


def backward_kernel(
    core_ref, q_ref, own_ref, got_ref, hot_ref, key_hot_ref, grad_ref, o_ref, log_ref,
    q_grad_ref, own_grad_ref, got_grad_ref, queries, grads, q_turned, grad_turned, q_total, *, causal,
):
    step = pl.program_id(1)
    n, block = q_ref.shape[0], own_ref.shape[1]
    chunk = n // 2
    blocks = n // block
    core = core_ref[0]
    left, lane = lanes()

    @pl.when(step == 0)
    def _():
        log = log_ref[...]
        high = log.astype(BF).astype(F32)
        middle = (log - high).astype(BF).astype(F32)
        low = log - high - middle
        mine = hot_ref[pl.ds(pl.multiple_of(core * n, n), n), :].astype(F32)
        ext = jnp.where(lane < 8, (1.0 - mine) * BIG, 0.0)
        ext = jnp.where(lane == 10, -low, ext)
        ext = jnp.where(lane == 9, -middle, jnp.where(lane == 8, -high, ext)).astype(BF)
        pair = q_ref[...]
        queries[0] = jnp.where(left, pair, ext)
        queries[1] = jnp.where(left, ext, pair)
        q_turned[...] = pair.T
        pair = grad_ref[...]
        product = pair.astype(F32) * o_ref[...].astype(F32)
        high = product.astype(BF)
        low = (product - high.astype(F32)).astype(BF)
        row = lax.broadcasted_iota(jnp.int32, (128, 128), 0)
        column = lax.broadcasted_iota(jnp.int32, (128, 128), 1)
        across = ((row < DH) != (column < DH)).astype(BF)
        inner = dot_nn(high, across) + dot_nn(low, across)
        high = inner.astype(BF).astype(F32)
        ext = jnp.where(lane == 8, -high, jnp.where(lane == 9, high - inner, 0.0)).astype(BF)
        grads[0] = jnp.where(left, pair, ext)
        grads[1] = jnp.where(left, ext, pair)
        grad_turned[...] = pair.T
        q_total[...] = jnp.zeros_like(q_total)

    own = step < blocks
    k = jnp.where(own, own_ref[0], got_ref[0])
    v = jnp.where(own, own_ref[1], got_ref[1])
    place = jnp.where(own, core * n + step * block, (1 - core) * n + (step - blocks) * block)
    hot = key_hot_ref[pl.ds(pl.multiple_of(place, block), block), :]
    ones = jnp.ones_like(v)
    ext = jnp.where((lane >= 8) & (lane < 11), ones, hot)
    keys = (jnp.where(left, k, ext), jnp.where(left, ext, k))
    values = (jnp.where(left, v, ones), jnp.where(left, ones, v))

    def run(tasks):
        k_grads, v_grads = [0.0, 0.0], [0.0, 0.0]

        def scores_of(head, query, cut):
            here = slice(query * chunk, (query + 1) * chunk)
            scores = dot_nt(queries[head, here, :], keys[head])
            if cut:
                to = lax.broadcasted_iota(jnp.int32, scores.shape, 0)
                at = lax.broadcasted_iota(jnp.int32, scores.shape, 1)
                scores = jnp.where(at <= to, scores, BIG)
            return scores, dot_nt(grads[head, here, :], values[head])

        def after(products, head, query, cut):
            here = slice(query * chunk, (query + 1) * chunk)
            probs = jnp.exp2(products[0])
            score_grad = (probs * products[1]).astype(BF)
            v_grads[head] = v_grads[head] + dot_nn(grad_turned[:, here], probs.astype(BF))
            k_grads[head] = k_grads[head] + dot_nn(q_turned[:, here], score_grad)
            q_total[head, here, :] += dot_nn(score_grad, keys[head])

        softmax_tasks(tasks, scores_of, after)
        k_grad = jnp.concatenate([k_grads[0][:DH], k_grads[1][DH:]]).T
        v_grad = jnp.concatenate([v_grads[0][:DH], v_grads[1][DH:]]).T
        put((k_grad * math.log(2.0)).astype(BF), v_grad.astype(BF))

    def put(k_grad, v_grad):
        @pl.when(own)
        def _():
            own_grad_ref[0] = k_grad
            own_grad_ref[1] = v_grad

        @pl.when(jnp.logical_not(own))
        def _():
            got_grad_ref[0] = k_grad
            got_grad_ref[1] = v_grad

    if not causal:
        run([(head, query, False) for head in range(2) for query in range(2)])
    else:
        @pl.when(jnp.logical_not(own) & (core == 0))
        def _():
            put(jnp.zeros((block, 128), BF), jnp.zeros((block, 128), BF))

        @pl.when(jnp.logical_not(own) & (core == 1))
        def _():
            run([(head, query, False) for head in range(2) for query in range(2)])

        for case in range(2):

            @pl.when(step == case)
            def _(case=case):
                run([(head, query, query == case) for head in range(2) for query in range(case, 2)])

    @pl.when(step == 2 * blocks - 1)
    def _():
        q_grad_ref[...] = (jnp.where(left, q_total[0], q_total[1]) * DH**-0.5).astype(BF)


def heads_backward(core, kept, grad, causal, begin=0, width=HALF):
    q, own, got, hot, key_hot, o, log = kept
    n = q.shape[0]
    skip = begin // 128
    block = n // 2
    blocks = 2
    first = lambda b: jnp.minimum(b, blocks - 1)
    second = lambda b: jnp.maximum(b - blocks, 0)
    whole = pl.BlockSpec((n, 128), lambda p, b: (0, skip + p))
    whole_out = pl.BlockSpec((n, 128), lambda p, b: (0, p))
    table = pl.BlockSpec((2 * n, 128), lambda p, b: (0, 0))

    def keys(part, skip):
        return pl.BlockSpec((2, block, 128), lambda p, b: (0, part(b), skip + p))

    return pl.pallas_call(
        partial(backward_kernel, causal=causal),
        grid=(width // 128, 2 * blocks),
        in_specs=[
            pl.BlockSpec(memory_space=pltpu.SMEM),
            whole,
            keys(first, skip),
            keys(second, skip),
            table,
            table,
            whole,
            whole,
            whole,
        ],
        out_specs=[whole_out, keys(first, 0), keys(second, 0)],
        out_shape=[jax.ShapeDtypeStruct(s, BF) for s in ((n, width), (2, n, width), (2, n, width))],
        scratch_shapes=[
            pltpu.VMEM((2, n, 128), BF),
            pltpu.VMEM((2, n, 128), BF),
            pltpu.VMEM((128, n), BF),
            pltpu.VMEM((128, n), BF),
            pltpu.VMEM((2, n, 128), F32),
        ],
        compiler_params=pltpu.CompilerParams(vmem_limit_bytes=VMEM_BYTES),
        cost_estimate=COST,
        name="attention_causal_back" if causal else "attention_back",
    )(core, q, own, got, hot, key_hot, grad, o, log)


def fold_dot(x, w):
    return dot_nn(x[:, :HALF], w[:, :HALF]) + dot_nn(x[:, HALF:], w[:, HALF:])


def fold_dot_t(g, w):
    return jnp.concatenate([dot_nt(g, w[:, :HALF]), dot_nt(g, w[:, HALF:])], axis=1)


def fold_grad(x, g):
    return jnp.concatenate([dot_tn(x[:, :HALF], g), dot_tn(x[:, HALF:], g)], axis=1)


def norm(v, gain, shift):
    centred = v - jnp.mean(v, axis=-1, keepdims=True)
    scale = lax.rsqrt(jnp.mean(centred * centred, axis=-1, keepdims=True) + EPS)
    unit = centred * scale
    return unit * gain + shift, unit, scale


def norm_back(grad, unit, scale, gain):
    inner = grad * gain
    mean_inner = jnp.mean(inner, axis=-1, keepdims=True)
    mean_unit = jnp.mean(inner * unit, axis=-1, keepdims=True)
    return scale * (inner - mean_inner - unit * mean_unit)


def over_rows(v):
    return jnp.sum(v, axis=0, keepdims=True)


GELU_C = math.sqrt(2.0 / math.pi)


def gelu(u):
    return 0.5 * u * (1.0 + jnp.tanh(GELU_C * u * (1.0 + 0.044715 * u * u)))


def gelu_both(u):
    square = u * u
    t = jnp.tanh(GELU_C * u * (1.0 + 0.044715 * square))
    half = 0.5 * (1.0 + t)
    slope = half + 0.5 * u * (1.0 - t * t) * (GELU_C * (1.0 + 3 * 0.044715 * square))
    return u * half, slope


def halt_gate(last, weight):
    logit = jnp.sum(last * weight, axis=-1, keepdims=True)
    return 1.0 / (1.0 + jnp.exp(-logit))


def halt_back(grad, start, last, runs, weight):
    gate = halt_gate(last, weight)
    used = runs * gate
    logit_grad = used * (1.0 - gate) * jnp.sum(grad * (last - start), axis=-1, keepdims=True)
    return grad * (1.0 - used), used * grad + logit_grad * weight, over_rows(logit_grad * last)


def ffn_blocks(own_ref, other_ref, begin):
    for which, ref in ((0, own_ref), (1, other_ref)):
        for j in range(2):
            up = begin + j * D
            down = up + 2 * D
            yield which, ref[up : up + D, :], ref[down : down + D, :], up, down


def ffn(low, own_ref, other_ref, begin):
    total = 0.0
    for _, up, down, _, _ in ffn_blocks(own_ref, other_ref, begin):
        total = total + dot_nn(gelu(dot_nn(low, up)).astype(BF), down)
    return total


def ffn_back(low, out_low, own_ref, other_ref, begin, acc, shift):
    total = 0.0
    for which, up, down, up_at, down_at in ffn_blocks(own_ref, other_ref, begin):
        active, slope = gelu_both(dot_nn(low, up))
        hidden = (dot_nt(out_low, down) * slope).astype(BF)
        up_at, down_at = up_at + shift, down_at + shift
        acc[which, down_at : down_at + D, :] += dot_tn(active.astype(BF), out_low)
        acc[which, up_at : up_at + D, :] += dot_tn(low, hidden)
        total = total + dot_nt(hidden, up)
    return total


def proj_back(o_refs, out_low, projs, acc, begin, o_grad_refs):
    for which in range(2):
        o_grad_refs[which][...] = dot_nt(out_low, projs[which]).astype(BF)
        acc[which, begin : begin + HALF, :] += dot_tn(o_refs[which][...], out_low)


def first_step(*refs):
    @pl.when(pl.program_id(0) == 0)
    def _():
        for ref in refs:
            ref[...] = jnp.zeros_like(ref)


def last_step(core_ref, acc, keep_ref, send_ref, small_acc=None, small_ref=None):
    @pl.when(pl.program_id(0) == pl.num_programs(0) - 1)
    def _():
        rows = acc.shape[1] // 2
        for part, ref in ((core_ref[0], keep_ref), (1 - core_ref[0], send_ref)):
            here = pl.ds(pl.multiple_of(part * rows, 16), rows)
            for which in range(acc.shape[0]):
                ref[which] = acc[which, here, :].astype(BF)
        if small_ref is not None:
            small_ref[...] = small_acc[...]


def join(core_ref, *triples):
    @pl.when(pl.program_id(0) == 0)
    def _():
        for near_ref, far_ref, whole in triples:
            rows = near_ref.shape[0]
            for part, ref in ((core_ref[0], near_ref), (1 - core_ref[0], far_ref)):
                whole[pl.ds(pl.multiple_of(part * rows, 16), rows), :] = ref[...]


def second_part(core_ref, near_ref, far_ref):
    return jnp.where(core_ref[0] == 1, near_ref[...], far_ref[...])


def pre_kernel(
    core_ref, rows_ref, got_ref, place_ref, own_ref, near_ref, far_ref,
    start_ref, q0_ref, q1_ref, kv0_ref, kv1_ref,
    other_ref,
):
    join(core_ref, (near_ref, far_ref, other_ref))
    rows = jnp.where(core_ref[1] == 1, rows_ref[...].astype(F32), got_ref[...].astype(F32))
    start = rows + place_ref[...]
    start_ref[...] = start
    low = start.astype(BF)
    for ref, q_ref, kv_ref in ((own_ref, q0_ref, kv0_ref), (other_ref, q1_ref, kv1_ref)):
        q_ref[...] = (fold_dot(low, ref[0:HALF, :]) * Q_SCALE).astype(BF)
        for kind in range(2):
            w = ref[(kind + 1) * HALF : (kind + 2) * HALF, :]
            kv_ref[kind] = fold_dot(low, w).astype(BF)


def enc_post_kernel(
    core_ref, o0_ref, o1_ref, start_ref, runs_ref, own_ref, near_ref, far_ref, small_ref,
    sum_one_ref, sum_two_ref, states_ref,
    other_ref,
):
    join(core_ref, (near_ref, far_ref, other_ref))
    start = start_ref[...]
    sum_one = start + dot_nn(o0_ref[...], own_ref[:HALF, :]) + dot_nn(o1_ref[...], other_ref[:HALF, :])
    sum_one_ref[...] = sum_one
    middle, _, _ = norm(sum_one, small_ref[0:1, :], small_ref[1:2, :])
    sum_two = middle + ffn(middle.astype(BF), own_ref, other_ref, HALF)
    sum_two_ref[...] = sum_two
    last, _, _ = norm(sum_two, small_ref[2:3, :], small_ref[3:4, :])
    gate = halt_gate(last, small_ref[4:5, :])
    states_ref[...] = (start + runs_ref[:, 0:1] * gate * (last - start)).astype(BF)


def dec_mid_kernel(
    core_ref, o0_ref, o1_ref, start_ref, states_ref, proj_own_ref, proj_near_ref, proj_far_ref,
    own_ref, near_ref, far_ref, small_ref,
    sum_ref, q0_ref, q1_ref, kv0_ref, kv1_ref,
    other_ref,
):
    join(core_ref, (near_ref, far_ref, other_ref))
    total = start_ref[...] + dot_nn(o0_ref[...], proj_own_ref[...])
    total = total + dot_nn(o1_ref[...], second_part(core_ref, proj_near_ref, proj_far_ref))
    sum_ref[...] = total
    middle, _, _ = norm(total, small_ref[0:1, :], small_ref[1:2, :])
    low = middle.astype(BF)
    states = states_ref[...]
    for ref, q_ref, kv_ref in ((own_ref, q0_ref, kv0_ref), (other_ref, q1_ref, kv1_ref)):
        q_ref[...] = (fold_dot(low, ref[0:HALF, :]) * Q_SCALE).astype(BF)
        for kind in range(2):
            w = ref[(kind + 1) * HALF : (kind + 2) * HALF, :]
            kv_ref[kind] = fold_dot(states, w).astype(BF)


def dec_post_kernel(
    core_ref, o0_ref, o1_ref, sum_one_ref, start_ref, runs_ref, cot_ref, own_ref, near_ref, far_ref, small_ref,
    states_ref, start_grad_ref, sum_grad_ref, o0_grad_ref, o1_grad_ref,
    keep_ref, send_ref, small_grad_ref,
    acc, small_acc, other_ref,
):
    join(core_ref, (near_ref, far_ref, other_ref))
    first_step(acc, small_acc)
    start = start_ref[...]
    projs = own_ref[:HALF, :], other_ref[:HALF, :]
    middle, _, _ = norm(sum_one_ref[...], small_ref[0:1, :], small_ref[1:2, :])
    sum_two = middle + dot_nn(o0_ref[...], projs[0]) + dot_nn(o1_ref[...], projs[1])
    gain_two = small_ref[2:3, :]
    mixed, unit_two, scale_two = norm(sum_two, gain_two, small_ref[3:4, :])
    low = mixed.astype(BF)
    sum_three = mixed + ffn(low, own_ref, other_ref, HALF)
    gain_three = small_ref[4:5, :]
    last, unit_three, scale_three = norm(sum_three, gain_three, small_ref[5:6, :])
    weight = small_ref[6:7, :]
    runs = runs_ref[:, 1:2]
    states_ref[...] = (start + runs * halt_gate(last, weight) * (last - start)).astype(BF)
    start_grad, last_grad, weight_grad = halt_back(
        cot_ref[...].astype(F32), start, last, runs, weight
    )
    start_grad_ref[...] = start_grad
    small_acc[4:5, :] += weight_grad
    small_acc[2:3, :] += over_rows(last_grad * unit_three)
    small_acc[3:4, :] += over_rows(last_grad)
    grad = norm_back(last_grad, unit_three, scale_three, gain_three)
    grad = grad + ffn_back(low, grad.astype(BF), own_ref, other_ref, HALF, acc, 0)
    small_acc[0:1, :] += over_rows(grad * unit_two)
    small_acc[1:2, :] += over_rows(grad)
    grad = norm_back(grad, unit_two, scale_two, gain_two)
    sum_grad_ref[...] = grad
    proj_back((o0_ref, o1_ref), grad.astype(BF), projs, acc, 0, (o0_grad_ref, o1_grad_ref))
    last_step(core_ref, acc, keep_ref, send_ref, small_acc, small_grad_ref)


def dec_mid_back_kernel(
    core_ref, q0_grad_ref, q1_grad_ref, sum_grad_ref, sum_one_ref, start_grad_ref, o0_ref, o1_ref,
    cq_own_ref, cq_near_ref, cq_far_ref, proj_own_ref, proj_near_ref, proj_far_ref, small_ref,
    out_ref, o0_grad_ref, o1_grad_ref, keep_ref, send_ref, small_grad_ref,
    acc, small_acc,
):
    cq_other = jnp.where(core_ref[0] == 0, cq_near_ref[:HALF, :], cq_far_ref[:HALF, :])
    first_step(acc, small_acc)
    gain = small_ref[0:1, :]
    middle, unit, scale = norm(sum_one_ref[...], gain, small_ref[1:2, :])
    low = middle.astype(BF)
    grad = sum_grad_ref[...]
    for which, (w, part_ref) in enumerate(((cq_own_ref[...], q0_grad_ref), (cq_other, q1_grad_ref))):
        grad = grad + fold_dot_t(part_ref[...], w)
        acc[which, :HALF, :] += fold_grad(low, part_ref[...])
    small_acc[0:1, :] += over_rows(grad * unit)
    small_acc[1:2, :] += over_rows(grad)
    grad = norm_back(grad, unit, scale, gain)
    out_ref[...] = start_grad_ref[...] + grad
    projs = proj_own_ref[...], second_part(core_ref, proj_near_ref, proj_far_ref)
    proj_back((o0_ref, o1_ref), grad.astype(BF), projs, acc, HALF, (o0_grad_ref, o1_grad_ref))
    last_step(core_ref, acc, keep_ref, send_ref, small_acc, small_grad_ref)


def kv_total(own_ref, got_ref, kind):
    return (own_ref[kind].astype(F32) + got_ref[kind].astype(F32)).astype(BF)


def enc_back_kernel(
    core_ref, kv0_ref, kv1_ref, got0_ref, got1_ref, states_ref, cot_ref, start_ref, sum_one_ref, sum_two_ref,
    o0_ref, o1_ref, runs_ref, cross_own_ref, cross_near_ref, cross_far_ref, own_ref, near_ref, far_ref, small_ref,
    out_ref, o0_grad_ref, o1_grad_ref, keep_ref, send_ref, small_grad_ref,
    acc, small_acc, cross_other_ref, other_ref,
):
    join(core_ref, (near_ref, far_ref, other_ref), (cross_near_ref, cross_far_ref, cross_other_ref))
    first_step(acc, small_acc)
    states = states_ref[...]
    grad = cot_ref[...].astype(F32)
    crosses = (cross_own_ref, kv0_ref, got0_ref), (cross_other_ref, kv1_ref, got1_ref)
    for which, (ref, kv_ref, got_ref) in enumerate(crosses):
        for kind in range(2):
            part = kv_total(kv_ref, got_ref, kind)
            at = kind * HALF
            grad = grad + fold_dot_t(part, ref[at + HALF : at + 2 * HALF, :])
            acc[which, at : at + HALF, :] += fold_grad(states, part)
    gain_one, gain_two, weight = small_ref[0:1, :], small_ref[2:3, :], small_ref[4:5, :]
    last, unit_two, scale_two = norm(sum_two_ref[...], gain_two, small_ref[3:4, :])
    start_grad, last_grad, weight_grad = halt_back(
        grad, start_ref[...], last, runs_ref[:, 0:1], weight
    )
    small_acc[4:5, :] += weight_grad
    small_acc[2:3, :] += over_rows(last_grad * unit_two)
    small_acc[3:4, :] += over_rows(last_grad)
    grad = norm_back(last_grad, unit_two, scale_two, gain_two)
    middle, unit_one, scale_one = norm(sum_one_ref[...], gain_one, small_ref[1:2, :])
    grad = grad + ffn_back(middle.astype(BF), grad.astype(BF), own_ref, other_ref, HALF, acc, 2 * HALF)
    small_acc[0:1, :] += over_rows(grad * unit_one)
    small_acc[1:2, :] += over_rows(grad)
    grad = norm_back(grad, unit_one, scale_one, gain_one)
    out_ref[...] = start_grad + grad
    projs = own_ref[:HALF, :], other_ref[:HALF, :]
    proj_back((o0_ref, o1_ref), grad.astype(BF), projs, acc, 2 * HALF, (o0_grad_ref, o1_grad_ref))
    last_step(core_ref, acc, keep_ref, send_ref, small_acc, small_grad_ref)


def qkv_back(low, parts, w_ref, acc, which):
    grad = 0.0
    for kind, part in enumerate(parts):
        rows = slice(kind * HALF, (kind + 1) * HALF)
        grad = grad + fold_dot_t(part, w_ref[rows, :])
        acc[which, rows, :] += fold_grad(low, part)
    return grad


def qkv_parts(*triples):
    def beside(parts):
        return parts[0] if len(parts) == 1 else jnp.concatenate(parts, axis=1)

    return (
        beside([q_ref[...] for q_ref, _, _ in triples]),
        beside([kv_total(kv_ref, got_ref, 0) for _, kv_ref, got_ref in triples]),
        beside([kv_total(kv_ref, got_ref, 1) for _, kv_ref, got_ref in triples]),
    )


def own_qkv_back_kernel(
    core_ref, qa_ref, kva_ref, gota_ref, qb_ref, kvb_ref, gotb_ref, start_ref, base_ref, w_ref,
    out_ref, keep_ref, send_ref,
    acc,
):
    first_step(acc)
    low = start_ref[...].astype(BF)
    parts = qkv_parts((qa_ref, kva_ref, gota_ref), (qb_ref, kvb_ref, gotb_ref))
    out_ref[...] = base_ref[...] + qkv_back(low, parts, w_ref, acc, 0)
    last_step(core_ref, acc, keep_ref, send_ref)


def other_qkv_back_kernel(
    core_ref, qa_ref, kva_ref, gota_ref, qb_ref, kvb_ref, gotb_ref, start_ref, base_ref, near_ref, far_ref,
    out_ref, keep_ref, send_ref,
    acc, other_ref,
):
    join(core_ref, (near_ref, far_ref, other_ref))
    own_qkv_back_kernel(
        core_ref, qa_ref, kva_ref, gota_ref, qb_ref, kvb_ref, gotb_ref, start_ref, base_ref, other_ref,
        out_ref, keep_ref, send_ref, acc,
    )


def both_qkv_back_kernel(
    core_ref, q0_grad_ref, kv0_ref, got0_ref, q1_grad_ref, kv1_ref, got1_ref, start_ref, base_ref,
    own_ref, near_ref, far_ref, more_keep_ref, more_send_ref,
    out_ref, keep_ref, send_ref,
    acc, other_ref,
):
    first_step(acc)
    join(core_ref, (near_ref, far_ref, other_ref))
    low = start_ref[...].astype(BF)
    grad = base_ref[...] + qkv_back(low, qkv_parts((q0_grad_ref, kv0_ref, got0_ref)), own_ref, acc, 0)
    out_ref[...] = grad + qkv_back(low, qkv_parts((q1_grad_ref, kv1_ref, got1_ref)), other_ref, acc, 1)

    @pl.when(pl.program_id(0) == pl.num_programs(0) - 1)
    def _():
        rows = acc.shape[1] // 2
        ends = (core_ref[0], keep_ref, more_keep_ref), (1 - core_ref[0], send_ref, more_send_ref)
        for part, ref, more_ref in ends:
            here = pl.ds(pl.multiple_of(part * rows, 16), rows)
            for which in range(2):
                ref[which, :rows, :] = acc[which, here, :].astype(BF)
                ref[which, rows:, :] = more_ref[which]


def rows_call(kernel, name, core, by_rows, whole, row_outs, whole_outs=(), scratch=(), block=512):
    n = by_rows[0].shape[-2]

    def row_spec(shape):
        if len(shape) == 3:
            return pl.BlockSpec((shape[0], block, shape[2]), lambda i: (0, i, 0))
        return pl.BlockSpec((block, shape[1]), lambda i: (i, 0))

    def whole_spec(entry):
        if not isinstance(entry, tuple):
            return pl.BlockSpec(entry.shape, lambda i: (0,) * entry.ndim, pipeline_mode=pl.Buffered(1))
        array, rows, index = entry
        return pl.BlockSpec((rows, array.shape[1]), lambda i: (index, 0), pipeline_mode=pl.Buffered(1))

    arrays = [e[0] if isinstance(e, tuple) else e for e in whole]
    return pl.pallas_call(
        kernel,
        grid=(n // block,),
        in_specs=[pl.BlockSpec(memory_space=pltpu.SMEM)]
        + [row_spec(a.shape) for a in by_rows]
        + [whole_spec(e) for e in whole],
        out_specs=[row_spec(s) for s, _ in row_outs]
        + [pl.BlockSpec(s, lambda i, s=s: (0,) * len(s)) for s, _ in whole_outs],
        out_shape=[jax.ShapeDtypeStruct(s, t) for s, t in [*row_outs, *whole_outs]],
        scratch_shapes=[pltpu.VMEM(*s) for s in scratch],
        compiler_params=pltpu.CompilerParams(vmem_limit_bytes=VMEM_BYTES),
        cost_estimate=COST,
        name=name,
    )(core, *by_rows, *arrays)


def put_rows(out_ref, at, values):
    count = values.shape[0]
    if len(out_ref.shape) == 3 or out_ref.shape[1] < D:
        width = out_ref.shape[-1]
        folds = D // width
        depth = out_ref.shape[-2] // folds
        for begin in range(at // depth * depth, at + count, depth):
            low, high = max(begin, at), min(begin + depth, at + count)
            if low < high:
                kind = begin // depth
                ref = out_ref.at[kind] if len(out_ref.shape) == 3 else out_ref
                for fold in range(folds):
                    rows = slice(fold * depth + low - begin, fold * depth + high - begin)
                    ref[rows, :] = values[low - at : high - at, fold * width : (fold + 1) * width]
        return
    depth = out_ref.shape[0]
    for begin in range(0, at + count, depth):
        low, high = max(begin, at), min(begin + depth, at + count)
        if low < high:
            column = begin // depth * D
            out_ref[low - begin : high - begin, column : column + D] = values[low - at : high - at]


def unpack_kernel(order_ref, mine_ref, got_ref, *refs, places):
    outs, rows_in = refs[:-1], refs[-1]
    piece, core = order_ref[0], order_ref[1]
    pieces, rows, _ = mine_ref.shape
    for ref, of in ((mine_ref, core), (got_ref, 1 - core)):
        for k in range(pieces):
            begin = (of * pieces + (piece ^ k)) * rows
            rows_in[pl.ds(pl.multiple_of(begin, 16), rows), :] = ref[k].astype(F32)
    for out, begin, at, count in places:
        put_rows(outs[out], at, rows_in[begin : begin + count, :])


def unpack(order, mine, got, shapes, places):
    pieces, rows, width = mine.shape
    vmem = pl.BlockSpec(memory_space=pltpu.VMEM)
    return pl.pallas_call(
        partial(unpack_kernel, places=places),
        in_specs=[pl.BlockSpec(memory_space=pltpu.SMEM), vmem, vmem],
        out_specs=[vmem] * len(shapes),
        out_shape=[jax.ShapeDtypeStruct(s, F32) for s in shapes],
        scratch_shapes=[pltpu.VMEM((2 * pieces * rows, width), F32)],
        compiler_params=pltpu.CompilerParams(vmem_limit_bytes=VMEM_BYTES),
        cost_estimate=COST,
        name="unpack",
    )(order, mine, got)


class Place:
    def __init__(self, dp_size):
        self.dp_size = dp_size
        dp = lax.axis_index("dp")
        self.c = dp % 2
        self.stays = self.c == lax.axis_index("mp")
        self.masks = [1 << b for b in range(1, dp_size.bit_length() - 1)]
        self.bits = [(dp // mask) % 2 for mask in self.masks]
        self.core = jnp.stack([self.c, self.stays]).astype(jnp.int32)
        piece = jnp.int32(0)
        for bit in self.bits:
            piece = 2 * piece + bit.astype(jnp.int32)
        self.order = jnp.stack([piece, self.c.astype(jnp.int32)])

    def flip(self, values, mask):
        return lax.ppermute(values, "dp", [(d, d ^ mask) for d in range(self.dp_size)])

    def core_swap(self, values):
        return self.flip(values, 1)

    def y_swap(self, values):
        return lax.ppermute(values, "mp", [(0, 1), (1, 0)])

    def cross(self, values):
        perm = []
        for d in range(0, self.dp_size, 2):
            perm += [(2 * d + 1, 2 * d + 2), (2 * d + 2, 2 * d + 1)]
        return lax.ppermute(values, ("dp", "mp"), perm)


class Flow:
    def __init__(self):
        self.fresh = []
        self.chains = []
        self.results = {}

    def add(self, name, chain):
        self.fresh.append((name, chain, next(chain)))

    def go_on(self, name, chain, arrived):
        try:
            self.fresh.append((name, chain, chain.send(arrived)))
        except StopIteration as stop:
            self.results[name] = stop.value

    def step(self, values):
        due = [chain for chain in self.chains if chain[3] == 1]
        self.chains = [(*chain[:3], chain[3] - 1) for chain in self.chains if chain[3] > 1]
        values, arrived = lax.optimization_barrier((values, [chain[2] for chain in due]))
        for (name, chain, _, _), got in zip(due, arrived):
            self.go_on(name, chain, got)
        fresh, self.fresh = self.fresh, []
        values, operands = lax.optimization_barrier((values, [op[1] for _, _, op in fresh]))
        for (name, chain, (send, _, steps)), operand in zip(fresh, operands):
            self.chains.append((name, chain, send(operand), steps))
        return values

    def finish(self):
        while self.chains:
            name, chain, pending, _ = self.chains.pop(0)
            self.go_on(name, chain, pending)
        while self.fresh:
            name, chain, (send, operand, _) = self.fresh.pop(0)
            self.go_on(name, chain, send(operand))


def gathered(at, own, first=1, second=1):
    rows = own.shape[0] // 2
    near = yield at.y_swap, lax.dynamic_slice_in_dim(own, at.c * rows, rows, 0), first
    far = yield at.core_swap, near, second
    return near, far


def moved(at, values, steps):
    return (yield at.cross, values, steps)


def plus(*values):
    return sum(v.astype(F32) for v in values).astype(BF)


def over_chips(at, total, steps, last_steps):
    for mask, bit in zip(at.masks, at.bits):
        rows = total.shape[0] // 2
        half = lax.dynamic_slice_in_dim(total, (1 - bit) * rows, rows, 0)
        got = yield partial(at.flip, mask=mask), half, steps
        total = plus(lax.dynamic_slice_in_dim(total, bit * rows, rows, 0), got)
    total = total[None]
    for mask in at.masks[::-1]:
        got = yield partial(at.flip, mask=mask), total, steps
        total = jnp.concatenate([total, got])
    return total, (yield at.core_swap, total, last_steps)


def summed(at, keep, send, core_steps=1, y_steps=1, steps=1, last_steps=1):
    got = yield at.core_swap, send, core_steps
    near = yield at.y_swap, plus(keep[1], got[1]), y_steps
    return (yield from over_chips(at, plus(keep[0], got[0], near), steps, last_steps))


def summed_other(at, keep, got, y_steps):
    near = yield at.y_swap, plus(keep[0], got[0]), y_steps
    return near


def summed_own(at, keep, send, near):
    got = yield at.core_swap, send, 1
    return (yield from over_chips(at, plus(keep[0], got[0], near), 1, 1))


def summed_small(at, values):
    for mask in [1, *at.masks]:
        values = values + (yield partial(at.flip, mask=mask), values, 1)
    return values + (yield at.y_swap, values, 1)


def rows_of(weight):
    if weight.ndim == 3:
        kinds, depth, width = weight.shape
        folded = jnp.concatenate([weight[:, : depth // 2], weight[:, depth // 2 :]], axis=2)
        return folded.reshape(kinds * depth // 2, 2 * width)
    depth, width = weight.shape
    if width == D:
        return weight
    if width < D:
        return jnp.concatenate([weight[: depth // 2], weight[depth // 2 :]], axis=1)
    return jnp.concatenate([weight[:, :D], weight[:, D:]], axis=0)


Q_SCALE = DH**-0.5 * math.log2(math.e)


def chip_rows(
    source_rows,
    target_rows,
    source_segment,
    target_segment,
    running,
    enc_qkv,
    enc_proj,
    enc_up,
    enc_down,
    enc_gains,
    enc_shifts,
    dec_qkv,
    dec_proj,
    cross_query,
    cross_kv,
    cross_proj,
    dec_up,
    dec_down,
    dec_gains,
    dec_shifts,
    halt_weight,
    enc_cotangent,
    dec_cotangent,
    *,
    dp_size,
):
    at = Place(dp_size)
    flow = Flow()
    n = source_rows.shape[0]
    row = ((n, D), F32)
    row_low = ((n, D), BF)
    half_low = ((n, HALF), BF)
    kv_low = ((2, n, HALF), BF)

    ints = jnp.concatenate([source_segment[0], target_segment[0], running[0, 0], running[1, 0]])
    w_enc_qkv = rows_of(enc_qkv)
    flow.add("source", moved(at, source_rows[:, 0], 1))
    flow.add("w_enc_qkv", gathered(at, w_enc_qkv))
    ints = ints.reshape(6, n)
    flow.add("ints", moved(at, ints, 1))
    (target_rows,) = flow.step((target_rows,))

    w_dec_self = jnp.concatenate([rows_of(dec_qkv), rows_of(dec_proj)])
    w_enc = jnp.concatenate([rows_of(enc_proj), rows_of(enc_up), rows_of(enc_down)])
    w_cross = jnp.concatenate([rows_of(cross_query), rows_of(cross_kv)])
    w_dec = jnp.concatenate([rows_of(cross_proj), rows_of(dec_up), rows_of(dec_down)])
    cots = jnp.concatenate([enc_cotangent[:, 0].astype(BF), dec_cotangent[:, 0].astype(BF)], axis=1)
    pad = jnp.zeros((3, D), F32)
    small_enc = jnp.stack(
        [enc_gains[0], enc_shifts[0], enc_gains[1], enc_shifts[1], halt_weight[0]]
    )
    small_enc = jnp.concatenate([small_enc, pad])
    small_dec = jnp.stack(
        [dec_gains[0], dec_shifts[0], dec_gains[1], dec_shifts[1], dec_gains[2], dec_shifts[2], halt_weight[1]]
    )
    small_dec = jnp.concatenate([small_dec, pad[:1]])
    place = at.core[0] * n + jnp.arange(n, dtype=jnp.int32)
    embedding = signal(place.astype(F32)) + signal(jnp.ones((1,), F32))

    flow.add("target", moved(at, target_rows[:, 0], 2))
    flow.add("w_dec_self", gathered(at, w_dec_self, 2, 1))
    w_enc, w_cross, w_dec, embedding, cots = flow.step((w_enc, w_cross, w_dec, embedding, cots))
    ints = jnp.where(at.stays, ints, flow.results["ints"])
    runs = jnp.transpose(jnp.pad(ints[4:].astype(F32), ((0, 126), (0, 0))))
    lane = jnp.arange(128, dtype=jnp.int32) % DH
    source_hot, target_hot = (ints[:4].reshape(2, 2 * n, 1) == lane).astype(BF)
    source_hot, target_hot = flow.step((source_hot, target_hot))

    def pre(rows, got, own, other):
        return rows_call(
            pre_kernel, "project", at.core, [rows, got, embedding], [own, *other],
            [row, half_low, half_low, kv_low, kv_low], scratch=[(own.shape, BF)],
        )

    def attend(q, kv, got, hot, key_hot, causal=False):
        o, log = heads_forward(at.core, q, kv, got, hot, key_hot, causal)
        return o, (q, kv, got, hot, key_hot, o, log)

    def attend_back(kept, grad):
        return heads_backward(at.core, kept, grad, False)

    def attend_back_pair(kept, grad, pair):
        return heads_backward(at.core, kept, grad, True, 128 * pair, 128)

    w_enc_qkv_got = flow.results["w_enc_qkv"]
    enc_start, q0, q1, kv0, kv1 = pre(source_rows[:, 0], flow.results["source"], w_enc_qkv, w_enc_qkv_got)
    got0, got1 = at.core_swap(kv0), at.core_swap(kv1)
    enc_o0, enc_kept0 = attend(q0, kv0, got0, source_hot, source_hot)
    flow.add("w_enc", gathered(at, w_enc, 2, 1))
    enc_o0, q1, kv1, got1 = flow.step((enc_o0, q1, kv1, got1))
    target = flow.results["target"]
    enc_o1, enc_kept1 = attend(q1, kv1, got1, source_hot, source_hot)
    enc_o1, target = flow.step((enc_o1, target))

    w_dec_self_got = flow.results["w_dec_self"]
    dec_start, q0, q1, kv0, kv1 = pre(target_rows[:, 0], target, w_dec_self, w_dec_self_got)
    got0, got1 = at.core_swap(kv0), at.core_swap(kv1)
    self_o0, self_kept0 = attend(q0, kv0, got0, target_hot, target_hot, True)
    flow.add("w_cross", gathered(at, w_cross))
    self_o0, q1, kv1, got1 = flow.step((self_o0, q1, kv1, got1))
    self_o1, self_kept1 = attend(q1, kv1, got1, target_hot, target_hot, True)
    flow.add("w_dec", gathered(at, w_dec, 3, 1))
    self_o1, enc_o1 = flow.step((self_o1, enc_o1))
    w_enc_got = flow.results["w_enc"]
    enc_sum_one, enc_sum_two, enc_states = rows_call(
        enc_post_kernel, "encoder_feed", at.core, [enc_o0, enc_o1, enc_start, runs],
        [w_enc, *w_enc_got, small_enc], [row, row, row_low], scratch=[(w_enc.shape, BF)],
    )
    flow.add("cots", moved(at, cots, 3))
    (enc_states,) = flow.step((enc_states,))
    w_cross_got = flow.results["w_cross"]
    self_proj = [(w_dec_self, HALF, 3)] + [(w, HALF, 1) for w in w_dec_self_got]
    dec_sum_one, q0, q1, kv0, kv1 = rows_call(
        dec_mid_kernel, "cross_project", at.core, [self_o0, self_o1, dec_start, enc_states],
        [*self_proj, w_cross, *w_cross_got, small_dec],
        [row, half_low, half_low, kv_low, kv_low], scratch=[(w_cross.shape, BF)],
    )
    got0, got1 = at.core_swap(kv0), at.core_swap(kv1)
    q0, q1, kv0, kv1 = flow.step((q0, q1, kv0, kv1))
    cross_o0, cross_kept0 = attend(q0, kv0, got0, target_hot, source_hot)
    cross_o0, q1, kv1, got1 = flow.step((cross_o0, q1, kv1, got1))
    cross_o1, cross_kept1 = attend(q1, kv1, got1, target_hot, source_hot)
    flow.add("enc_states", moved(at, enc_states, 1))
    (cross_o1,) = flow.step((cross_o1,))
    cots = jnp.where(at.stays, cots, flow.results["cots"])
    enc_cot, dec_cot = cots[:, :D], cots[:, D:]

    def grad_outs(rows):
        return [((2, rows // 2, D), BF)] * 2 + [((8, D), F32)]

    def grad_scratch(rows):
        return [((2, rows, D), F32), ((8, D), F32)]

    w_dec_got = flow.results["w_dec"]
    (
        dec_states, start_grad, sum_grad, o0_grad, o1_grad, *dec_parts, small_two,
    ) = rows_call(
        dec_post_kernel, "decoder_feed", at.core,
        [cross_o0, cross_o1, dec_sum_one, dec_start, runs, dec_cot], [w_dec, *w_dec_got, small_dec],
        [row_low, row, row, half_low, half_low], grad_outs(9 * HALF),
        [*grad_scratch(9 * HALF), (w_dec.shape, BF)],
    )
    flow.add("dec", summed(at, *dec_parts))
    flow.add("dec_states", moved(at, dec_states, 1))
    o0_grad, o1_grad = flow.step((o0_grad, o1_grad))

    q0_grad, kv0_grad, kv0_send = attend_back(cross_kept0, o0_grad)
    q0_grad, kv0_grad, kv0_send, o1_grad = flow.step((q0_grad, kv0_grad, kv0_send, o1_grad))
    kv0_got = at.core_swap(kv0_send)
    q1_grad, kv1_grad, kv1_send = attend_back(cross_kept1, o1_grad)
    q1_grad, kv1_grad, kv1_send, kv0_got = flow.step((q1_grad, kv1_grad, kv1_send, kv0_got))
    kv1_got = at.core_swap(kv1_send)

    (
        enc_base, enc_o0_grad, enc_o1_grad, *enc_parts, small_enc_grad,
    ) = rows_call(
        enc_back_kernel, "encoder_feed_back", at.core,
        [kv0_grad, kv1_grad, kv0_got, kv1_got, enc_states, enc_cot, enc_start, enc_sum_one, enc_sum_two,
         enc_o0, enc_o1, runs],
        [w_cross, *w_cross_got, w_enc, *w_enc_got, small_enc],
        [row, half_low, half_low], grad_outs(11 * HALF),
        [*grad_scratch(11 * HALF), (w_cross.shape, BF), (w_enc.shape, BF)],
    )
    flow.add("enc", summed(at, *enc_parts))
    enc_o0_grad, enc_o1_grad, q0_grad = flow.step((enc_o0_grad, enc_o1_grad, q0_grad))
    (
        dec_base, self_o0_grad, self_o1_grad, *mid_parts, small_one,
    ) = rows_call(
        dec_mid_back_kernel, "cross_project_back", at.core,
        [q0_grad, q1_grad, sum_grad, dec_sum_one, start_grad, self_o0, self_o1],
        [(w_cross, HALF, 0), *w_cross_got, *self_proj, small_dec],
        [row, half_low, half_low], grad_outs(2 * HALF), grad_scratch(2 * HALF),
    )
    flow.add("small", summed_small(at, jnp.concatenate([small_enc_grad, small_one, small_two])))
    enc_o1_grad, mid_parts = flow.step((enc_o1_grad, mid_parts))

    q1_grad, kv1_grad, kv1_send = attend_back(enc_kept1, enc_o1_grad)
    kv1_got = at.core_swap(kv1_send)
    q1_grad, kv1_grad, enc_o0_grad = flow.step((q1_grad, kv1_grad, enc_o0_grad))
    q0_grad, kv0_grad, kv0_send = attend_back(enc_kept0, enc_o0_grad)
    kv0_got = at.core_swap(kv0_send)
    q0_grad, kv0_grad, kv1_got, q1_grad = flow.step((q0_grad, kv0_grad, kv1_got, q1_grad))
    source_grad, keep, send = rows_call(
        both_qkv_back_kernel, "project_back", at.core,
        [q0_grad, kv0_grad, kv0_got, q1_grad, kv1_grad, kv1_got, enc_start, enc_base],
        [w_enc_qkv, *w_enc_qkv_got, *mid_parts], [row], [((2, 5 * HALF // 2, D), BF)] * 2,
        [((2, 3 * HALF, D), F32), (w_enc_qkv.shape, BF)],
    )
    source_low = source_grad.astype(BF)
    flow.add("enc_qkv", summed(at, keep, send))
    flow.add("source_grad", moved(at, source_low, 1))
    (self_o1_grad,) = flow.step((self_o1_grad,))

    def heads_back(kept, grad):
        parts = []
        for pair in range(2):
            q_grad, kv_grad, kv_send = attend_back_pair(kept, grad, pair)
            grad, q_grad, kv_grad, kv_send = flow.step((grad, q_grad, kv_grad, kv_send))
            parts += [q_grad, kv_grad, at.core_swap(kv_send)]
        return parts

    parts = heads_back(self_kept1, self_o1_grad)
    part_outs = [((1, 3 * HALF // 2, D), BF)] * 2
    part_scratch = [((1, 3 * HALF, D), F32)]
    target_grad, keep1, send1 = rows_call(
        other_qkv_back_kernel, "project_back", at.core, [*parts, dec_start, dec_base],
        [*w_dec_self_got], [row], part_outs, [*part_scratch, (w_dec_self.shape, BF)],
    )
    flow.add("dec_qkv_other", summed_other(at, keep1, at.core_swap(send1), 1))
    target_grad, self_o0_grad = flow.step((target_grad, self_o0_grad))
    parts = heads_back(self_kept0, self_o0_grad)
    target_grad, keep0, send0 = rows_call(
        own_qkv_back_kernel, "project_back", at.core, [*parts, dec_start, target_grad],
        [(w_dec_self, 3 * HALF, 0)], [row], part_outs, part_scratch,
    )
    target_low = target_grad.astype(BF)
    flow.add("dec_qkv", summed_own(at, keep0, send0, flow.results["dec_qkv_other"]))
    flow.add("target_grad", moved(at, target_low, 2))

    done = flow.results

    def weights(name, *weights):
        places, begin = [], 0
        for i, weight in enumerate(weights):
            places.append((i, begin, 0, weight.size // D))
            begin += weight.size // D
        return unpack(at.order, *done[name], [w.shape for w in weights], places)

    def home(values, name):
        return jnp.where(at.stays, values, done[name].astype(values.dtype))[:, None]

    def mixed_weights(name):
        part, more = 3 * HALF // 2, HALF // 2
        places = []
        for c in range(2):
            begin = c * (part + 2 * more)
            places += [(0, begin, c * part, part), (1 + c, begin + part, 0, 2 * more)]
        shapes = [enc_qkv.shape, cross_query.shape, dec_proj.shape]
        return unpack(at.order, *done[name], shapes, places)

    target_grad, done["dec"] = flow.step((target_grad, done["dec"]))
    dec_grads = weights("dec", cross_proj, dec_up, dec_down)
    dec_grads, done["enc"] = flow.step((dec_grads, done["enc"]))
    enc_grads = weights("enc", cross_kv, enc_proj, enc_up, enc_down)
    enc_grads, source_grad = flow.step((enc_grads, source_grad))
    source_out = home(source_grad, "source_grad")
    source_out, enc_states, dec_states = flow.step((source_out, enc_states, dec_states))
    states_out = home(enc_states, "enc_states"), home(dec_states, "dec_states")
    states_out, done["enc_qkv"] = flow.step((states_out, done["enc_qkv"]))
    mixed_grads = mixed_weights("enc_qkv")
    mixed_grads, target_grad = flow.step((mixed_grads, target_grad))
    target_out = home(target_grad, "target_grad")
    (target_out,) = flow.step((target_out,))
    flow.finish()
    cross_proj_grad, dec_up_grad, dec_down_grad = dec_grads
    cross_kv_grad, enc_proj_grad, enc_up_grad, enc_down_grad = enc_grads
    enc_qkv_grad, cross_query_grad, dec_proj_grad = mixed_grads
    (dec_qkv_grad,) = weights("dec_qkv", dec_qkv)
    small = done["small"]
    enc_small, one, two = small[:8], small[8:16], small[16:]
    return (
        *states_out,
        source_out,
        target_out,
        enc_qkv_grad,
        enc_proj_grad,
        enc_up_grad,
        enc_down_grad,
        enc_small[0:3:2],
        enc_small[1:4:2],
        dec_qkv_grad,
        dec_proj_grad,
        cross_query_grad,
        cross_kv_grad,
        cross_proj_grad,
        dec_up_grad,
        dec_down_grad,
        jnp.concatenate([one[0:1], two[0:3:2]]),
        jnp.concatenate([one[1:2], two[1:4:2]]),
        jnp.stack([enc_small[4], two[4]]),
    )


def solution(mesh):
    dp_size, mp_size = mesh.shape["dp"], mesh.shape["mp"]
    by_chip = mp_size == 2 and dp_size in (4, 8, 16)
    body = partial(chip_rows, dp_size=dp_size) if by_chip else local
    return jax.shard_map(
        body,
        mesh=mesh,
        in_specs=(
            P("mp", "dp", None),
            P("mp", "dp", None),
            P("dp", None),
            P("dp", None),
            P(None, "dp", "mp"),
            P(None, None, "mp"),
            P("mp", None),
            P(None, "mp"),
            P("mp", None),
            P(),
            P(),
            P(None, None, "mp"),
            P("mp", None),
            P(None, "mp"),
            P(None, None, "mp"),
            P("mp", None),
            P(None, "mp"),
            P("mp", None),
            P(),
            P(),
            P(),
            P("mp", "dp", None),
            P("mp", "dp", None),
        ),
        out_specs=(
            P("mp", "dp", None),
            P("mp", "dp", None),
            P("mp", "dp", None),
            P("mp", "dp", None),
            P(None, None, "mp"),
            P("mp", None),
            P(None, "mp"),
            P("mp", None),
            P(),
            P(),
            P(None, None, "mp"),
            P("mp", None),
            P(None, "mp"),
            P(None, None, "mp"),
            P("mp", None),
            P(None, "mp"),
            P("mp", None),
            P(),
            P(),
            P(),
        ),
        check_vma=False,
    )
```

```python
import math
from functools import partial

import jax
import jax.numpy as jnp
from jax import lax
from jax.experimental import pallas as pl
from jax.experimental.layout import Layout, with_layout_constraint
from jax.experimental.pallas import tpu as pltpu
from jax.sharding import PartitionSpec as P

D = 512
DH = 64


EPS = 1e-05
NEGATIVE = -1000000000.0


def signal(position):
    half_width = D // 2
    inverse_rates = jnp.exp(
        jnp.arange(half_width, dtype=jnp.float32) * (-jnp.log(10000.0) / (half_width - 1))
    )
    angles = position[:, None] * inverse_rates[None, :]
    return jnp.concatenate([jnp.sin(angles), jnp.cos(angles)], axis=1)


def normalize(values, norm_gain, norm_shift):
    centred = values - jnp.mean(values, axis=-1, keepdims=True)
    spread = jnp.mean(centred * centred, axis=-1, keepdims=True)
    return centred * lax.rsqrt(spread + EPS) * norm_gain + norm_shift


def halting(running_now, initial, updated, weight):
    halt_prob = jax.nn.sigmoid(jnp.sum(updated * weight, axis=-1, keepdims=True))
    return initial + running_now * halt_prob * (updated - initial)


def dot_last(left, right):
    return lax.dot_general(
        left, right, (((left.ndim - 1,), (1,)), ((), ())), preferred_element_type=jnp.float32
    )


def collect(piece_rows):
    return lax.all_gather(piece_rows, "mp", axis=0, tiled=True)


def collect_grad(piece_rows):
    return lax.all_gather(piece_rows.astype(jnp.bfloat16), "mp", axis=0, tiled=True)


def project_out(hidden, weight, rows):

    def partial_term(begin_row, row_count):
        return jnp.dot(hidden, weight, preferred_element_type=jnp.float32)

    return lax.psum_scatter(
        partial_term(jnp.int32(0), lax.axis_size("mp") * rows).astype(jnp.bfloat16),
        "mp",
        scatter_dimension=0,
        tiled=True,
    ).astype(jnp.float32)


def project_back(gradients, matrices, rows):

    def partial_term(begin_row, row_count):
        summed = jnp.zeros(
            (row_count,) + gradients[0].shape[1:-1] + (matrices[0].shape[0],), jnp.float32
        )
        for gradient, matrix in zip(gradients, matrices):
            summed = summed + dot_last(gradient, matrix)
        return summed

    return lax.psum_scatter(
        partial_term(jnp.int32(0), lax.axis_size("mp") * rows).astype(jnp.bfloat16),
        "mp",
        scatter_dimension=0,
        tiled=True,
    ).astype(jnp.float32)


def to_pairs(values):
    length, row_count, width = values.shape
    return (
        values.reshape(length, row_count, width // DH, DH)
        .transpose(1, 2, 0, 3)
        .reshape(-1, length, DH)
    )


def from_pairs(values, row_count):
    pairs, length, unused = values.shape
    heads_here = pairs // row_count
    return (
        values.reshape(row_count, heads_here, length, DH)
        .transpose(2, 0, 1, 3)
        .reshape(length, row_count, heads_here * DH)
    )


def per_pair(segments, width):
    return jnp.repeat(segments, width // DH, axis=0)


def pair_scores(query_block, key_rows, segment_block, segment_keys, first_row, causal):
    scores = lax.dot_general(
        query_block, key_rows, (((1,), (1,)), ((), ())), preferred_element_type=jnp.float32
    )
    scores = scores * DH ** (-0.5)
    allowed = segment_block[:, None] == segment_keys[None, :]
    if causal:
        query_place = first_row + jnp.arange(query_block.shape[0], dtype=jnp.int32)
        key_place = jnp.arange(key_rows.shape[0], dtype=jnp.int32)
        allowed = allowed & (key_place[None, :] <= query_place[:, None])
    return jnp.where(allowed, scores, NEGATIVE)


def attend_pair(inputs, causal):
    query_rows, key_rows, value_rows, segment_query, segment_keys = inputs
    length = query_rows.shape[0]
    block_rows = min(512, length)
    blocks = length // block_rows
    firsts = jnp.arange(blocks, dtype=jnp.int32) * block_rows

    def one_block(pieces):
        query_block, segment_block, first_row = pieces
        scores = pair_scores(query_block, key_rows, segment_block, segment_keys, first_row, causal)
        highest = jnp.max(scores, axis=1, keepdims=True)
        exponent = jnp.exp(scores - highest)
        totals = jnp.sum(exponent, axis=1, keepdims=True)
        weights = (exponent / totals).astype(jnp.bfloat16)
        mixed = jnp.dot(weights, value_rows, preferred_element_type=jnp.float32)
        return (mixed.astype(jnp.bfloat16), (highest + jnp.log(totals))[:, 0])

    mixed, log_total = lax.map(
        one_block,
        (
            query_rows.reshape(blocks, block_rows, -1),
            segment_query.reshape(blocks, block_rows),
            firsts,
        ),
    )
    return (mixed.reshape(length, -1), log_total.reshape(length))


def attend_pair_back(inputs, causal):
    query_rows, key_rows, value_rows, mixed_grad, log_total, segment_query, segment_keys = inputs
    length = query_rows.shape[0]
    block_rows = min(512, length)
    blocks = length // block_rows
    firsts = jnp.arange(blocks, dtype=jnp.int32) * block_rows

    def one_block(carry, pieces):
        key_total, value_total = carry
        query_block, grad_block, log_block, segment_block, first_row = pieces
        scores = pair_scores(query_block, key_rows, segment_block, segment_keys, first_row, causal)
        probs = jnp.exp(scores - log_block[:, None])
        weights = probs.astype(jnp.bfloat16)
        prob_grad = lax.dot_general(
            grad_block, value_rows, (((1,), (1,)), ((), ())), preferred_element_type=jnp.float32
        )
        inner = jnp.sum(probs * prob_grad, axis=1, keepdims=True)
        score_grad = (probs * (prob_grad - inner)).astype(jnp.bfloat16)
        query_grad = jnp.dot(score_grad, key_rows, preferred_element_type=jnp.float32) * DH ** (
            -0.5
        )
        key_total = key_total + lax.dot_general(
            score_grad, query_block, (((0,), (0,)), ((), ())), preferred_element_type=jnp.float32
        ) * DH ** (-0.5)
        value_total = value_total + lax.dot_general(
            weights, grad_block, (((0,), (0,)), ((), ())), preferred_element_type=jnp.float32
        )
        return ((key_total, value_total), query_grad.astype(jnp.bfloat16))

    zeros_start = jnp.zeros(key_rows.shape, jnp.float32)
    (key_total, value_total), query_grad = lax.scan(
        one_block,
        (zeros_start, zeros_start),
        (
            query_rows.reshape(blocks, block_rows, -1),
            mixed_grad.reshape(blocks, block_rows, -1),
            log_total.reshape(blocks, block_rows),
            segment_query.reshape(blocks, block_rows),
            firsts,
        ),
    )
    return (
        query_grad.reshape(length, -1),
        key_total.astype(jnp.bfloat16),
        value_total.astype(jnp.bfloat16),
    )


def attention_forward(
    query_full,
    key_full,
    weight_query,
    weight_key,
    weight_value,
    weight_out,
    segment_query,
    segment_keys,
    causal,
    rows,
):
    queries = jnp.dot(query_full, weight_query, preferred_element_type=jnp.float32).astype(
        jnp.bfloat16
    )
    keys_low = jnp.dot(key_full, weight_key, preferred_element_type=jnp.float32).astype(
        jnp.bfloat16
    )
    values_low = jnp.dot(key_full, weight_value, preferred_element_type=jnp.float32).astype(
        jnp.bfloat16
    )
    width = queries.shape[2]
    row_count = queries.shape[1]
    mixed, log_total = lax.map(
        partial(attend_pair, causal=causal),
        (
            to_pairs(queries),
            to_pairs(keys_low),
            to_pairs(values_low),
            per_pair(segment_query, width),
            per_pair(segment_keys, width),
        ),
    )
    mixed = from_pairs(mixed, row_count)
    branch = project_out(mixed, weight_out, rows)
    return (branch, (queries, keys_low, values_low, mixed, log_total))


def attention_backward(
    branch_grad, kept, query_full, key_full, weight_out, segment_query, segment_keys, causal
):
    queries, keys_low, values_low, kept_mixed, log_total = kept
    grad_full = collect_grad(branch_grad)
    out_weight_grad = jnp.einsum(
        "lrc,lrd->cd", kept_mixed, grad_full, preferred_element_type=jnp.float32
    )
    mixed_grad = dot_last(grad_full, weight_out).astype(jnp.bfloat16)
    width = queries.shape[2]
    row_count = queries.shape[1]
    query_grad, key_grad, value_grad = lax.map(
        partial(attend_pair_back, causal=causal),
        (
            to_pairs(queries),
            to_pairs(keys_low),
            to_pairs(values_low),
            to_pairs(mixed_grad),
            log_total,
            per_pair(segment_query, width),
            per_pair(segment_keys, width),
        ),
    )
    query_grad = from_pairs(query_grad, row_count)
    key_grad = from_pairs(key_grad, row_count)
    value_grad = from_pairs(value_grad, row_count)
    weight_grads = (
        jnp.einsum("lrd,lrc->dc", query_full, query_grad, preferred_element_type=jnp.float32),
        jnp.einsum("lrd,lrc->dc", key_full, key_grad, preferred_element_type=jnp.float32),
        jnp.einsum("lrd,lrc->dc", key_full, value_grad, preferred_element_type=jnp.float32),
    )
    return (query_grad, key_grad, value_grad, weight_grads, out_weight_grad)


def feed_forward(source_full, weight_up, weight_down, rows):
    hidden = jnp.dot(source_full, weight_up, preferred_element_type=jnp.float32)
    active = jax.nn.gelu(hidden).astype(jnp.bfloat16)
    return (project_out(active, weight_down, rows), hidden)


def feed_backward(branch_grad, source_full, hidden, weight_up, weight_down, rows):
    grad_full = collect_grad(branch_grad)
    active, gelu_back = jax.vjp(jax.nn.gelu, hidden)
    active = active.astype(jnp.bfloat16)
    down_grad = jnp.einsum("lrf,lrd->fd", active, grad_full, preferred_element_type=jnp.float32)
    hidden_grad = gelu_back(dot_last(grad_full, weight_down))[0].astype(jnp.bfloat16)
    up_grad = jnp.einsum(
        "lrd,lrf->df", source_full, hidden_grad, preferred_element_type=jnp.float32
    )
    input_grad = project_back((hidden_grad,), (weight_up,), rows)
    return (input_grad, up_grad, down_grad)


def local(
    source_rows,
    target_rows,
    source_segment,
    target_segment,
    running,
    enc_qkv,
    enc_proj,
    enc_up,
    enc_down,
    enc_gains,
    enc_shifts,
    dec_qkv,
    dec_proj,
    cross_query,
    cross_kv,
    cross_proj,
    dec_up,
    dec_down,
    dec_gains,
    dec_shifts,
    halt_weight,
    enc_cotangent,
    dec_cotangent,
):
    rows = source_rows.shape[0]
    position = (lax.axis_index("mp") * rows + jnp.arange(rows, dtype=jnp.int32)).astype(jnp.float32)
    embedding = (signal(position) + signal(jnp.ones((1,), jnp.float32)))[:, None, :]
    runs_now = jnp.transpose(running, (0, 2, 1)).astype(jnp.float32)[..., None]
    enc_start = source_rows.astype(jnp.float32) + embedding
    enc_start_low = enc_start.astype(jnp.bfloat16)
    enc_start_full = collect(enc_start_low)
    enc_attn, enc_attn_kept = attention_forward(
        enc_start_full,
        enc_start_full,
        enc_qkv[0],
        enc_qkv[1],
        enc_qkv[2],
        enc_proj,
        source_segment,
        source_segment,
        False,
        rows,
    )
    enc_sum_one = enc_start + enc_attn
    enc_middle = normalize(enc_sum_one, enc_gains[0], enc_shifts[0])
    enc_middle_low = enc_middle.astype(jnp.bfloat16)
    enc_middle_full = collect(enc_middle_low)
    enc_ffn, enc_hidden = feed_forward(enc_middle_full, enc_up, enc_down, rows)
    enc_sum_two = enc_middle + enc_ffn
    enc_last = normalize(enc_sum_two, enc_gains[1], enc_shifts[1])
    enc_final = halting(runs_now[0], enc_start, enc_last, halt_weight[0])
    enc_states = enc_final.astype(jnp.bfloat16)
    enc_states_full = collect(enc_states)
    dec_start = target_rows.astype(jnp.float32) + embedding
    dec_start_low = dec_start.astype(jnp.bfloat16)
    dec_start_full = collect(dec_start_low)
    dec_self, dec_self_kept = attention_forward(
        dec_start_full,
        dec_start_full,
        dec_qkv[0],
        dec_qkv[1],
        dec_qkv[2],
        dec_proj,
        target_segment,
        target_segment,
        True,
        rows,
    )
    dec_sum_one = dec_start + dec_self
    dec_middle = normalize(dec_sum_one, dec_gains[0], dec_shifts[0])
    dec_middle_low = dec_middle.astype(jnp.bfloat16)
    dec_middle_full = collect(dec_middle_low)
    dec_cross, dec_cross_kept = attention_forward(
        dec_middle_full,
        enc_states_full,
        cross_query,
        cross_kv[0],
        cross_kv[1],
        cross_proj,
        target_segment,
        source_segment,
        False,
        rows,
    )
    dec_sum_two = dec_middle + dec_cross
    dec_mixed = normalize(dec_sum_two, dec_gains[1], dec_shifts[1])
    dec_mixed_low = dec_mixed.astype(jnp.bfloat16)
    dec_mixed_full = collect(dec_mixed_low)
    dec_ffn, dec_hidden = feed_forward(dec_mixed_full, dec_up, dec_down, rows)
    dec_sum_three = dec_mixed + dec_ffn
    dec_last = normalize(dec_sum_three, dec_gains[2], dec_shifts[2])
    dec_final = halting(runs_now[1], dec_start, dec_last, halt_weight[1])
    dec_states = dec_final.astype(jnp.bfloat16)
    unused, halt_back = jax.vjp(partial(halting, runs_now[1]), dec_start, dec_last, halt_weight[1])
    dec_start_grad, last_grad, dec_halt_grad = halt_back(dec_cotangent)
    unused, norm_back = jax.vjp(normalize, dec_sum_three, dec_gains[2], dec_shifts[2])
    sum_grad, dec_gain_three, dec_shift_three = norm_back(last_grad)
    ffn_input_grad, dec_up_grad, dec_down_grad = feed_backward(
        sum_grad, dec_mixed_full, dec_hidden, dec_up, dec_down, rows
    )
    mixed_grad = sum_grad + ffn_input_grad
    unused, norm_back = jax.vjp(normalize, dec_sum_two, dec_gains[1], dec_shifts[1])
    sum_grad, dec_gain_two, dec_shift_two = norm_back(mixed_grad)
    query_grad, key_grad, value_grad, cross_grads, cross_proj_grad = attention_backward(
        sum_grad,
        dec_cross_kept,
        dec_middle_full,
        enc_states_full,
        cross_proj,
        target_segment,
        source_segment,
        False,
    )
    middle_grad = sum_grad + project_back((query_grad,), (cross_query,), rows)
    enc_extra = project_back((key_grad, value_grad), (cross_kv[0], cross_kv[1]), rows)
    unused, norm_back = jax.vjp(normalize, dec_sum_one, dec_gains[0], dec_shifts[0])
    sum_grad, dec_gain_one, dec_shift_one = norm_back(middle_grad)
    query_grad, key_grad, value_grad, self_grads, dec_proj_grad = attention_backward(
        sum_grad,
        dec_self_kept,
        dec_start_full,
        dec_start_full,
        dec_proj,
        target_segment,
        target_segment,
        True,
    )
    target_grad = (
        sum_grad
        + dec_start_grad
        + project_back(
            (query_grad, key_grad, value_grad), (dec_qkv[0], dec_qkv[1], dec_qkv[2]), rows
        )
    )
    dec_qkv_grad = jnp.stack(self_grads)
    cross_query_grad = cross_grads[0]
    cross_kv_grad = jnp.stack([cross_grads[1], cross_grads[2]])
    enc_final_grad = enc_cotangent + enc_extra
    unused, halt_back = jax.vjp(partial(halting, runs_now[0]), enc_start, enc_last, halt_weight[0])
    enc_start_grad, last_grad, enc_halt_grad = halt_back(enc_final_grad)
    unused, norm_back = jax.vjp(normalize, enc_sum_two, enc_gains[1], enc_shifts[1])
    sum_grad, enc_gain_two, enc_shift_two = norm_back(last_grad)
    ffn_input_grad, enc_up_grad, enc_down_grad = feed_backward(
        sum_grad, enc_middle_full, enc_hidden, enc_up, enc_down, rows
    )
    middle_grad = sum_grad + ffn_input_grad
    unused, norm_back = jax.vjp(normalize, enc_sum_one, enc_gains[0], enc_shifts[0])
    sum_grad, enc_gain_one, enc_shift_one = norm_back(middle_grad)
    query_grad, key_grad, value_grad, self_grads, enc_proj_grad = attention_backward(
        sum_grad,
        enc_attn_kept,
        enc_start_full,
        enc_start_full,
        enc_proj,
        source_segment,
        source_segment,
        False,
    )
    source_grad = (
        sum_grad
        + enc_start_grad
        + project_back(
            (query_grad, key_grad, value_grad), (enc_qkv[0], enc_qkv[1], enc_qkv[2]), rows
        )
    )
    enc_qkv_grad = jnp.stack(self_grads)
    (
        enc_qkv_grad,
        enc_proj_grad,
        enc_up_grad,
        enc_down_grad,
        dec_qkv_grad,
        dec_proj_grad,
        cross_query_grad,
        cross_kv_grad,
        cross_proj_grad,
        dec_up_grad,
        dec_down_grad,
    ) = (
        lax.psum(enc_qkv_grad.astype(jnp.bfloat16), "dp").astype(jnp.float32),
        lax.psum(enc_proj_grad.astype(jnp.bfloat16), "dp").astype(jnp.float32),
        lax.psum(enc_up_grad.astype(jnp.bfloat16), "dp").astype(jnp.float32),
        lax.psum(enc_down_grad.astype(jnp.bfloat16), "dp").astype(jnp.float32),
        lax.psum(dec_qkv_grad.astype(jnp.bfloat16), "dp").astype(jnp.float32),
        lax.psum(dec_proj_grad.astype(jnp.bfloat16), "dp").astype(jnp.float32),
        lax.psum(cross_query_grad.astype(jnp.bfloat16), "dp").astype(jnp.float32),
        lax.psum(cross_kv_grad.astype(jnp.bfloat16), "dp").astype(jnp.float32),
        lax.psum(cross_proj_grad.astype(jnp.bfloat16), "dp").astype(jnp.float32),
        lax.psum(dec_up_grad.astype(jnp.bfloat16), "dp").astype(jnp.float32),
        lax.psum(dec_down_grad.astype(jnp.bfloat16), "dp").astype(jnp.float32),
    )
    enc_gains_grad, enc_shifts_grad, dec_gains_grad, dec_shifts_grad, halt_weight_grad = lax.psum(
        (
            jnp.stack([enc_gain_one, enc_gain_two]),
            jnp.stack([enc_shift_one, enc_shift_two]),
            jnp.stack([dec_gain_one, dec_gain_two, dec_gain_three]),
            jnp.stack([dec_shift_one, dec_shift_two, dec_shift_three]),
            jnp.stack([enc_halt_grad, dec_halt_grad]),
        ),
        ("dp", "mp"),
    )
    return (
        enc_states,
        dec_states,
        source_grad,
        target_grad,
        enc_qkv_grad,
        enc_proj_grad,
        enc_up_grad,
        enc_down_grad,
        enc_gains_grad,
        enc_shifts_grad,
        dec_qkv_grad,
        dec_proj_grad,
        cross_query_grad,
        cross_kv_grad,
        cross_proj_grad,
        dec_up_grad,
        dec_down_grad,
        dec_gains_grad,
        dec_shifts_grad,
        halt_weight_grad,
    )


BIG = -1e30
BF = jnp.bfloat16
F32 = jnp.float32
NN = (((1,), (0,)), ((), ()))
NT = (((1,), (1,)), ((), ()))
TN = (((0,), (0,)), ((), ()))
HALF = D // 2
VMEM_BYTES = 56 * 1024 * 1024
COST = pl.CostEstimate(flops=1, bytes_accessed=1, transcendentals=0)


def dot_nn(a, b):
    return lax.dot_general(a, b, NN, preferred_element_type=F32)


def dot_nt(a, b):
    return lax.dot_general(a, b, NT, preferred_element_type=F32)


def dot_tn(a, b):
    return lax.dot_general(a, b, TN, preferred_element_type=F32)


def lanes():
    lane = lax.broadcasted_iota(jnp.int32, (1, 128), 1)
    return lane < DH, lane % DH


def in_hbm(arrays):
    return [pltpu.with_memory_space_constraint(a, pltpu.HBM) for a in arrays]


def pipelined(tasks, scores_of, after):
    ahead = scores_of(*tasks[0])
    for i, task in enumerate(tasks):
        now = ahead
        if i + 1 < len(tasks):
            ahead = scores_of(*tasks[i + 1])
        after(now, *task)


def forward_kernel(
    core_ref, q_ref, own_ref, got_ref, hot_ref, key_hot_ref, o_ref, log_ref, keys, values, *, causal
):
    n = q_ref.shape[0]
    chunk = n // 2
    core = core_ref[0]
    left, lane = lanes()
    for ref, of in ((own_ref, core), (got_ref, 1 - core)):
        here = pl.ds(pl.multiple_of(of * n, n), n)
        k, hot = ref[0], key_hot_ref[here, :]
        ext = jnp.where((lane >= 8) & (lane < 11), jnp.ones_like(hot), hot)
        keys[0, here, :] = jnp.where(left, k, ext)
        keys[1, here, :] = jnp.where(left, ext, k)
        turned = ref[1].T
        ones = jnp.ones((DH, n), BF)
        values[0, :, here] = jnp.concatenate([turned[:DH], ones])
        values[1, :, here] = jnp.concatenate([ones, turned[DH:]])
    pair = q_ref[...]
    mine = hot_ref[pl.ds(pl.multiple_of(core * n, n), n), :].astype(F32)
    ext = jnp.where(lane < 8, (1.0 - mine) * BIG, 0.0).astype(BF)
    queries = jnp.where(left, pair, ext), jnp.where(left, ext, pair)

    def run(tasks, rows):
        state = {}

        def scores_of(head, query, key, cut):
            q = queries[head][query * rows : (query + 1) * rows]
            scores = dot_nt(keys[head, key * chunk : (key + 1) * chunk, :], q)
            if cut:
                at = lax.broadcasted_iota(jnp.int32, scores.shape, 0)
                to = lax.broadcasted_iota(jnp.int32, scores.shape, 1)
                scores = jnp.where(at <= to, scores, BIG)
            return scores

        def after(scores, head, query, key, cut):
            top = jnp.max(scores, axis=0, keepdims=True)
            total = 0.0
            if (head, query) in state:
                old_top, total = state[head, query]
                top = jnp.maximum(top, old_top)
                total = total * jnp.exp2(old_top - top)
            probs = jnp.exp2(scores - top).astype(BF)
            total = total + dot_nn(values[head, :, key * chunk : (key + 1) * chunk], probs)
            state[head, query] = top, total

        pipelined(tasks, scores_of, after)
        for query in range(n // rows):
            (top0, total0), (top1, total1) = state[0, query], state[1, query]
            out = jnp.concatenate([total0[:DH] / total0[DH:], total1[DH:] / total1[:DH]])
            logs = jnp.concatenate([top1 + jnp.log2(total1[:DH]), top0 + jnp.log2(total0[DH:])])
            here = slice(query * rows, (query + 1) * rows)
            o_ref[here, :] = out.T.astype(BF)
            log_ref[here, :] = logs.T

    if not causal:
        run([(head, 0, key, False) for head in range(2) for key in range(4)], n)
    else:
        for case in range(2):

            @pl.when(core == case)
            def _(case=case):
                run(
                    [
                        (head, query, key, key == 2 * case + query)
                        for head in range(2)
                        for query in range(2)
                        for key in range(2 * case + query + 1)
                    ],
                    chunk,
                )


def heads_forward(core, q, own, got, hot, key_hot, causal):
    n, width = q.shape
    length = 2 * n
    keys = pl.BlockSpec((2, n, 128), lambda p: (0, 0, p))
    queries = pl.BlockSpec((n, 128), lambda p: (0, p))
    table = pl.BlockSpec((length, 128), lambda p: (0, 0))
    return pl.pallas_call(
        partial(forward_kernel, causal=causal),
        grid=(width // 128,),
        in_specs=[
            pl.BlockSpec(memory_space=pltpu.SMEM),
            queries,
            keys,
            keys,
            table,
            table,
        ],
        out_specs=[queries, queries],
        out_shape=[jax.ShapeDtypeStruct((n, width), BF), jax.ShapeDtypeStruct((n, width), F32)],
        scratch_shapes=[pltpu.VMEM((2, length, 128), BF), pltpu.VMEM((2, 128, length), BF)],
        compiler_params=pltpu.CompilerParams(vmem_limit_bytes=VMEM_BYTES),
        cost_estimate=COST,
        name="attention_causal" if causal else "attention",
    )(core, *in_hbm((q, own, got, hot, key_hot)))


def backward_kernel(
    core_ref, q_ref, own_ref, got_ref, hot_ref, key_hot_ref, grad_ref, o_ref, log_ref,
    q_grad_ref, own_grad_ref, got_grad_ref, queries, grads, q_turned, grad_turned, q_total, *, causal,
):
    step = pl.program_id(1)
    n, block = q_ref.shape[0], own_ref.shape[1]
    chunk = n // 2
    blocks = n // block
    core = core_ref[0]
    left, lane = lanes()

    @pl.when(step == 0)
    def _():
        log = log_ref[...]
        high = log.astype(BF).astype(F32)
        middle = (log - high).astype(BF).astype(F32)
        low = log - high - middle
        mine = hot_ref[pl.ds(pl.multiple_of(core * n, n), n), :].astype(F32)
        ext = jnp.where(lane < 8, (1.0 - mine) * BIG, 0.0)
        ext = jnp.where(lane == 10, -low, ext)
        ext = jnp.where(lane == 9, -middle, jnp.where(lane == 8, -high, ext)).astype(BF)
        pair = q_ref[...]
        queries[0] = jnp.where(left, pair, ext)
        queries[1] = jnp.where(left, ext, pair)
        q_turned[...] = pair.T
        pair = grad_ref[...]
        product = pair.astype(F32) * o_ref[...].astype(F32)
        high = product.astype(BF)
        low = (product - high.astype(F32)).astype(BF)
        row = lax.broadcasted_iota(jnp.int32, (128, 128), 0)
        column = lax.broadcasted_iota(jnp.int32, (128, 128), 1)
        across = ((row < DH) != (column < DH)).astype(BF)
        inner = dot_nn(high, across) + dot_nn(low, across)
        high = inner.astype(BF).astype(F32)
        ext = jnp.where(lane == 8, -high, jnp.where(lane == 9, high - inner, 0.0)).astype(BF)
        grads[0] = jnp.where(left, pair, ext)
        grads[1] = jnp.where(left, ext, pair)
        grad_turned[...] = pair.T
        q_total[...] = jnp.zeros_like(q_total)

    own = step < blocks
    k = jnp.where(own, own_ref[0], got_ref[0])
    v = jnp.where(own, own_ref[1], got_ref[1])
    place = jnp.where(own, core * n + step * block, (1 - core) * n + (step - blocks) * block)
    hot = key_hot_ref[pl.ds(pl.multiple_of(place, block), block), :]
    ones = jnp.ones_like(v)
    ext = jnp.where((lane >= 8) & (lane < 11), ones, hot)
    keys = (jnp.where(left, k, ext), jnp.where(left, ext, k))
    values = (jnp.where(left, v, ones), jnp.where(left, ones, v))

    def run(tasks):
        k_grads, v_grads = [0.0, 0.0], [0.0, 0.0]

        def scores_of(head, query, cut):
            here = slice(query * chunk, (query + 1) * chunk)
            scores = dot_nt(queries[head, here, :], keys[head])
            if cut:
                to = lax.broadcasted_iota(jnp.int32, scores.shape, 0)
                at = lax.broadcasted_iota(jnp.int32, scores.shape, 1)
                scores = jnp.where(at <= to, scores, BIG)
            return scores, dot_nt(grads[head, here, :], values[head])

        def after(products, head, query, cut):
            here = slice(query * chunk, (query + 1) * chunk)
            probs = jnp.exp2(products[0])
            score_grad = (probs * products[1]).astype(BF)
            v_grads[head] = v_grads[head] + dot_nn(grad_turned[:, here], probs.astype(BF))
            k_grads[head] = k_grads[head] + dot_nn(q_turned[:, here], score_grad)
            q_total[head, here, :] += dot_nn(score_grad, keys[head])

        pipelined(tasks, scores_of, after)
        k_grad = jnp.concatenate([k_grads[0][:DH], k_grads[1][DH:]]).T
        v_grad = jnp.concatenate([v_grads[0][:DH], v_grads[1][DH:]]).T
        put((k_grad * math.log(2.0)).astype(BF), v_grad.astype(BF))

    def put(k_grad, v_grad):
        @pl.when(own)
        def _():
            own_grad_ref[0] = k_grad
            own_grad_ref[1] = v_grad

        @pl.when(jnp.logical_not(own))
        def _():
            got_grad_ref[0] = k_grad
            got_grad_ref[1] = v_grad

    if not causal:
        run([(head, query, False) for head in range(2) for query in range(2)])
    else:
        @pl.when(jnp.logical_not(own) & (core == 0))
        def _():
            put(jnp.zeros((block, 128), BF), jnp.zeros((block, 128), BF))

        @pl.when(jnp.logical_not(own) & (core == 1))
        def _():
            run([(head, query, False) for head in range(2) for query in range(2)])

        for case in range(2):

            @pl.when(step == case)
            def _(case=case):
                run([(head, query, query == case) for head in range(2) for query in range(case, 2)])

    @pl.when(step == 2 * blocks - 1)
    def _():
        q_grad_ref[...] = (jnp.where(left, q_total[0], q_total[1]) * DH**-0.5).astype(BF)


def heads_backward(core, kept, grad, causal, begin=0, width=HALF):
    q, own, got, hot, key_hot, o, log = kept
    n = q.shape[0]
    skip = begin // 128
    block = n // 2
    blocks = 2
    first = lambda b: jnp.minimum(b, blocks - 1)
    second = lambda b: jnp.maximum(b - blocks, 0)
    whole = pl.BlockSpec((n, 128), lambda p, b: (0, skip + p))
    whole_out = pl.BlockSpec((n, 128), lambda p, b: (0, p))
    table = pl.BlockSpec((2 * n, 128), lambda p, b: (0, 0))

    def keys(part, skip):
        return pl.BlockSpec((2, block, 128), lambda p, b: (0, part(b), skip + p))

    return pl.pallas_call(
        partial(backward_kernel, causal=causal),
        grid=(width // 128, 2 * blocks),
        in_specs=[
            pl.BlockSpec(memory_space=pltpu.SMEM),
            whole,
            keys(first, skip),
            keys(second, skip),
            table,
            table,
            whole,
            whole,
            whole,
        ],
        out_specs=[whole_out, keys(first, 0), keys(second, 0)],
        out_shape=[jax.ShapeDtypeStruct(s, BF) for s in ((n, width), (2, n, width), (2, n, width))],
        scratch_shapes=[
            pltpu.VMEM((2, n, 128), BF),
            pltpu.VMEM((2, n, 128), BF),
            pltpu.VMEM((128, n), BF),
            pltpu.VMEM((128, n), BF),
            pltpu.VMEM((2, n, 128), F32),
        ],
        compiler_params=pltpu.CompilerParams(vmem_limit_bytes=VMEM_BYTES),
        cost_estimate=COST,
        name="attention_causal_back" if causal else "attention_back",
    )(core, *in_hbm((q, own, got, hot, key_hot, grad, o, log)))


def fold_dot(x, w):
    return dot_nn(x[:, :HALF], w[:, :HALF]) + dot_nn(x[:, HALF:], w[:, HALF:])


def fold_dot_t(g, w):
    return jnp.concatenate([dot_nt(g, w[:, :HALF]), dot_nt(g, w[:, HALF:])], axis=1)


def fold_grad(x, g):
    return jnp.concatenate([dot_tn(x[:, :HALF], g), dot_tn(x[:, HALF:], g)], axis=1)


def norm(v, gain, shift):
    centred = v - jnp.mean(v, axis=-1, keepdims=True)
    scale = lax.rsqrt(jnp.mean(centred * centred, axis=-1, keepdims=True) + EPS)
    unit = centred * scale
    return unit * gain + shift, unit, scale


def norm_back(grad, unit, scale, gain):
    inner = grad * gain
    mean_inner = jnp.mean(inner, axis=-1, keepdims=True)
    mean_unit = jnp.mean(inner * unit, axis=-1, keepdims=True)
    return scale * (inner - mean_inner - unit * mean_unit)


def over_rows(v):
    return jnp.sum(v, axis=0, keepdims=True)


GELU_C = math.sqrt(2.0 / math.pi)


def gelu(u):
    return 0.5 * u * (1.0 + jnp.tanh(GELU_C * u * (1.0 + 0.044715 * u * u)))


def gelu_both(u):
    square = u * u
    t = jnp.tanh(GELU_C * u * (1.0 + 0.044715 * square))
    half = 0.5 * (1.0 + t)
    slope = half + 0.5 * u * (1.0 - t * t) * (GELU_C * (1.0 + 3 * 0.044715 * square))
    return u * half, slope


def halt_gate(last, weight):
    logit = jnp.sum(last * weight, axis=-1, keepdims=True)
    return 1.0 / (1.0 + jnp.exp(-logit))


def halt_back(grad, start, last, runs, weight):
    gate = halt_gate(last, weight)
    used = runs * gate
    logit_grad = used * (1.0 - gate) * jnp.sum(grad * (last - start), axis=-1, keepdims=True)
    return grad * (1.0 - used), used * grad + logit_grad * weight, over_rows(logit_grad * last)


def ffn_blocks(own_ref, other_ref, begin):
    for which, ref in ((0, own_ref), (1, other_ref)):
        for j in range(2):
            up = begin + j * D
            down = up + 2 * D
            yield which, ref[up : up + D, :], ref[down : down + D, :], up, down


def ffn(low, own_ref, other_ref, begin, kept=None):
    blocks = list(ffn_blocks(own_ref, other_ref, begin))
    total = []

    def after(hidden, j):
        if kept is None:
            active = gelu(hidden).astype(BF)
        else:
            active, slope = gelu_both(hidden)
            active = active.astype(BF)
            kept[0, :, j * D : (j + 1) * D] = active
            kept[1, :, j * D : (j + 1) * D] = slope.astype(BF)
        total.append(dot_nn(active, blocks[j][2]))

    pipelined([(j,) for j in range(4)], lambda j: dot_nn(low, blocks[j][1]), after)
    return sum(total)


def ffn_back(low, out_low, own_ref, other_ref, begin, acc, shift, kept=None):
    blocks = list(ffn_blocks(own_ref, other_ref, begin))
    total = []

    def products(j):
        _, up, down, _, _ = blocks[j]
        return None if kept is not None else dot_nn(low, up), dot_nt(out_low, down)

    def after(got, j):
        which, up, _, up_at, down_at = blocks[j]
        hidden, active_grad = got
        if kept is None:
            active, slope = gelu_both(hidden)
            active = active.astype(BF)
        else:
            active = kept[0, :, j * D : (j + 1) * D]
            slope = kept[1, :, j * D : (j + 1) * D].astype(F32)
        hidden_grad = (active_grad * slope).astype(BF)
        up_at, down_at = up_at + shift, down_at + shift
        acc[which, down_at : down_at + D, :] += dot_tn(active, out_low)
        acc[which, up_at : up_at + D, :] += dot_tn(low, hidden_grad)
        total.append(dot_nt(hidden_grad, up))

    pipelined([(j,) for j in range(4)], products, after)
    return sum(total)


def proj_back(o_refs, out_low, projs, acc, begin, o_grad_refs):
    for which in range(2):
        o_grad_refs[which][...] = dot_nt(out_low, projs[which]).astype(BF)
        acc[which, begin : begin + HALF, :] += dot_tn(o_refs[which][...], out_low)


def first_step(*refs):
    @pl.when(pl.program_id(0) == 0)
    def _():
        for ref in refs:
            ref[...] = jnp.zeros_like(ref)


def last_step(core_ref, acc, keep_ref, send_ref, small_acc=None, small_ref=None):
    @pl.when(pl.program_id(0) == pl.num_programs(0) - 1)
    def _():
        rows = acc.shape[1] // 2
        for part, ref in ((core_ref[0], keep_ref), (1 - core_ref[0], send_ref)):
            here = pl.ds(pl.multiple_of(part * rows, 16), rows)
            for which in range(acc.shape[0]):
                ref[which] = acc[which, here, :].astype(BF)
        if small_ref is not None:
            small_ref[...] = small_acc[...]


def join(core_ref, *triples):
    @pl.when(pl.program_id(0) == 0)
    def _():
        for near_ref, far_ref, whole in triples:
            rows = near_ref.shape[0]
            for part, ref in ((core_ref[0], near_ref), (1 - core_ref[0], far_ref)):
                whole[pl.ds(pl.multiple_of(part * rows, 16), rows), :] = ref[...]


def second_part(core_ref, near_ref, far_ref):
    return jnp.where(core_ref[0] == 1, near_ref[...], far_ref[...])


def pre_kernel(
    core_ref, rows_ref, got_ref, place_ref, own_ref, near_ref, far_ref,
    start_ref, q0_ref, q1_ref, kv0_ref, kv1_ref,
    other_ref,
):
    join(core_ref, (near_ref, far_ref, other_ref))
    rows = jnp.where(core_ref[1] == 1, rows_ref[...].astype(F32), got_ref[...].astype(F32))
    start = rows + place_ref[...]
    start_ref[...] = start
    low = start.astype(BF)
    for ref, q_ref, kv_ref in ((own_ref, q0_ref, kv0_ref), (other_ref, q1_ref, kv1_ref)):
        q_ref[...] = (fold_dot(low, ref[0:HALF, :]) * Q_SCALE).astype(BF)
        for kind in range(2):
            w = ref[(kind + 1) * HALF : (kind + 2) * HALF, :]
            kv_ref[kind] = fold_dot(low, w).astype(BF)


def enc_post_kernel(
    core_ref, o0_ref, o1_ref, start_ref, runs_ref, own_ref, near_ref, far_ref, small_ref,
    sum_one_ref, sum_two_ref, states_ref,
    other_ref,
):
    join(core_ref, (near_ref, far_ref, other_ref))
    start = start_ref[...]
    sum_one = start + dot_nn(o0_ref[...], own_ref[:HALF, :]) + dot_nn(o1_ref[...], other_ref[:HALF, :])
    sum_one_ref[...] = sum_one
    middle, _, _ = norm(sum_one, small_ref[0:1, :], small_ref[1:2, :])
    sum_two = middle + ffn(middle.astype(BF), own_ref, other_ref, HALF)
    sum_two_ref[...] = sum_two
    last, _, _ = norm(sum_two, small_ref[2:3, :], small_ref[3:4, :])
    gate = halt_gate(last, small_ref[4:5, :])
    states_ref[...] = (start + runs_ref[:, 0:1] * gate * (last - start)).astype(BF)


def dec_mid_kernel(
    core_ref, o0_ref, o1_ref, start_ref, states_ref, proj_own_ref, proj_near_ref, proj_far_ref,
    own_ref, near_ref, far_ref, small_ref,
    sum_ref, q0_ref, q1_ref, kv0_ref, kv1_ref,
    other_ref,
):
    join(core_ref, (near_ref, far_ref, other_ref))
    total = start_ref[...] + dot_nn(o0_ref[...], proj_own_ref[...])
    total = total + dot_nn(o1_ref[...], second_part(core_ref, proj_near_ref, proj_far_ref))
    sum_ref[...] = total
    middle, _, _ = norm(total, small_ref[0:1, :], small_ref[1:2, :])
    low = middle.astype(BF)
    states = states_ref[...]
    for ref, q_ref, kv_ref in ((own_ref, q0_ref, kv0_ref), (other_ref, q1_ref, kv1_ref)):
        q_ref[...] = (fold_dot(low, ref[0:HALF, :]) * Q_SCALE).astype(BF)
        for kind in range(2):
            w = ref[(kind + 1) * HALF : (kind + 2) * HALF, :]
            kv_ref[kind] = fold_dot(states, w).astype(BF)


def dec_post_kernel(
    core_ref, o0_ref, o1_ref, sum_one_ref, start_ref, runs_ref, cot_ref, own_ref, near_ref, far_ref, small_ref,
    states_ref, start_grad_ref, sum_grad_ref, o0_grad_ref, o1_grad_ref,
    keep_ref, send_ref, small_grad_ref,
    acc, small_acc, other_ref, kept,
):
    join(core_ref, (near_ref, far_ref, other_ref))
    first_step(acc, small_acc)
    start = start_ref[...]
    projs = own_ref[:HALF, :], other_ref[:HALF, :]
    middle, _, _ = norm(sum_one_ref[...], small_ref[0:1, :], small_ref[1:2, :])
    sum_two = middle + dot_nn(o0_ref[...], projs[0]) + dot_nn(o1_ref[...], projs[1])
    gain_two = small_ref[2:3, :]
    mixed, unit_two, scale_two = norm(sum_two, gain_two, small_ref[3:4, :])
    low = mixed.astype(BF)
    sum_three = mixed + ffn(low, own_ref, other_ref, HALF, kept)
    gain_three = small_ref[4:5, :]
    last, unit_three, scale_three = norm(sum_three, gain_three, small_ref[5:6, :])
    weight = small_ref[6:7, :]
    runs = runs_ref[:, 1:2]
    states_ref[...] = (start + runs * halt_gate(last, weight) * (last - start)).astype(BF)
    start_grad, last_grad, weight_grad = halt_back(
        cot_ref[...].astype(F32), start, last, runs, weight
    )
    start_grad_ref[...] = start_grad
    small_acc[4:5, :] += weight_grad
    small_acc[2:3, :] += over_rows(last_grad * unit_three)
    small_acc[3:4, :] += over_rows(last_grad)
    grad = norm_back(last_grad, unit_three, scale_three, gain_three)
    grad = grad + ffn_back(low, grad.astype(BF), own_ref, other_ref, HALF, acc, 0, kept)
    small_acc[0:1, :] += over_rows(grad * unit_two)
    small_acc[1:2, :] += over_rows(grad)
    grad = norm_back(grad, unit_two, scale_two, gain_two)
    sum_grad_ref[...] = grad
    proj_back((o0_ref, o1_ref), grad.astype(BF), projs, acc, 0, (o0_grad_ref, o1_grad_ref))
    last_step(core_ref, acc, keep_ref, send_ref, small_acc, small_grad_ref)


def dec_mid_back_kernel(
    core_ref, q0_grad_ref, q1_grad_ref, sum_grad_ref, sum_one_ref, start_grad_ref, o0_ref, o1_ref,
    cq_own_ref, cq_near_ref, cq_far_ref, proj_own_ref, proj_near_ref, proj_far_ref, small_ref,
    out_ref, o0_grad_ref, o1_grad_ref, keep_ref, send_ref, small_grad_ref,
    acc, small_acc,
):
    cq_other = jnp.where(core_ref[0] == 0, cq_near_ref[:HALF, :], cq_far_ref[:HALF, :])
    first_step(acc, small_acc)
    gain = small_ref[0:1, :]
    middle, unit, scale = norm(sum_one_ref[...], gain, small_ref[1:2, :])
    low = middle.astype(BF)
    grad = sum_grad_ref[...]
    for which, (w, part_ref) in enumerate(((cq_own_ref[...], q0_grad_ref), (cq_other, q1_grad_ref))):
        grad = grad + fold_dot_t(part_ref[...], w)
        acc[which, :HALF, :] += fold_grad(low, part_ref[...])
    small_acc[0:1, :] += over_rows(grad * unit)
    small_acc[1:2, :] += over_rows(grad)
    grad = norm_back(grad, unit, scale, gain)
    out_ref[...] = start_grad_ref[...] + grad
    projs = proj_own_ref[...], second_part(core_ref, proj_near_ref, proj_far_ref)
    proj_back((o0_ref, o1_ref), grad.astype(BF), projs, acc, HALF, (o0_grad_ref, o1_grad_ref))
    last_step(core_ref, acc, keep_ref, send_ref, small_acc, small_grad_ref)


def kv_total(own_ref, got_ref, kind):
    return (own_ref[kind].astype(F32) + got_ref[kind].astype(F32)).astype(BF)


def enc_back_kernel(
    core_ref, kv0_ref, kv1_ref, got0_ref, got1_ref, states_ref, cot_ref, start_ref, sum_one_ref, sum_two_ref,
    o0_ref, o1_ref, runs_ref, cross_own_ref, cross_near_ref, cross_far_ref, own_ref, near_ref, far_ref, small_ref,
    out_ref, o0_grad_ref, o1_grad_ref, keep_ref, send_ref, small_grad_ref,
    acc, small_acc, cross_other_ref, other_ref,
):
    join(core_ref, (near_ref, far_ref, other_ref), (cross_near_ref, cross_far_ref, cross_other_ref))
    first_step(acc, small_acc)
    states = states_ref[...]
    grad = cot_ref[...].astype(F32)
    crosses = (cross_own_ref, kv0_ref, got0_ref), (cross_other_ref, kv1_ref, got1_ref)
    for which, (ref, kv_ref, got_ref) in enumerate(crosses):
        for kind in range(2):
            part = kv_total(kv_ref, got_ref, kind)
            at = kind * HALF
            grad = grad + fold_dot_t(part, ref[at + HALF : at + 2 * HALF, :])
            acc[which, at : at + HALF, :] += fold_grad(states, part)
    gain_one, gain_two, weight = small_ref[0:1, :], small_ref[2:3, :], small_ref[4:5, :]
    last, unit_two, scale_two = norm(sum_two_ref[...], gain_two, small_ref[3:4, :])
    start_grad, last_grad, weight_grad = halt_back(
        grad, start_ref[...], last, runs_ref[:, 0:1], weight
    )
    small_acc[4:5, :] += weight_grad
    small_acc[2:3, :] += over_rows(last_grad * unit_two)
    small_acc[3:4, :] += over_rows(last_grad)
    grad = norm_back(last_grad, unit_two, scale_two, gain_two)
    middle, unit_one, scale_one = norm(sum_one_ref[...], gain_one, small_ref[1:2, :])
    grad = grad + ffn_back(middle.astype(BF), grad.astype(BF), own_ref, other_ref, HALF, acc, 2 * HALF)
    small_acc[0:1, :] += over_rows(grad * unit_one)
    small_acc[1:2, :] += over_rows(grad)
    grad = norm_back(grad, unit_one, scale_one, gain_one)
    out_ref[...] = start_grad + grad
    projs = own_ref[:HALF, :], other_ref[:HALF, :]
    proj_back((o0_ref, o1_ref), grad.astype(BF), projs, acc, 2 * HALF, (o0_grad_ref, o1_grad_ref))
    last_step(core_ref, acc, keep_ref, send_ref, small_acc, small_grad_ref)


def qkv_back(low, parts, w_ref, acc, which):
    grad = 0.0
    for kind, part in enumerate(parts):
        rows = slice(kind * HALF, (kind + 1) * HALF)
        grad = grad + fold_dot_t(part, w_ref[rows, :])
        acc[which, rows, :] += fold_grad(low, part)
    return grad


def qkv_parts(*triples):
    def beside(parts):
        return parts[0] if len(parts) == 1 else jnp.concatenate(parts, axis=1)

    return (
        beside([q_ref[...] for q_ref, _, _ in triples]),
        beside([kv_total(kv_ref, got_ref, 0) for _, kv_ref, got_ref in triples]),
        beside([kv_total(kv_ref, got_ref, 1) for _, kv_ref, got_ref in triples]),
    )


def own_qkv_back_kernel(
    core_ref, qa_ref, kva_ref, gota_ref, qb_ref, kvb_ref, gotb_ref, start_ref, base_ref, w_ref,
    out_ref, low_ref, keep_ref, send_ref,
    acc,
):
    first_step(acc)
    low = start_ref[...].astype(BF)
    parts = qkv_parts((qa_ref, kva_ref, gota_ref), (qb_ref, kvb_ref, gotb_ref))
    grad = base_ref[...] + qkv_back(low, parts, w_ref, acc, 0)
    out_ref[...] = grad
    low_ref[...] = grad.astype(BF)
    last_step(core_ref, acc, keep_ref, send_ref)


def other_qkv_back_kernel(
    core_ref, qa_ref, kva_ref, gota_ref, qb_ref, kvb_ref, gotb_ref, start_ref, base_ref, near_ref, far_ref,
    out_ref, low_ref, keep_ref, send_ref,
    acc, other_ref,
):
    join(core_ref, (near_ref, far_ref, other_ref))
    own_qkv_back_kernel(
        core_ref, qa_ref, kva_ref, gota_ref, qb_ref, kvb_ref, gotb_ref, start_ref, base_ref, other_ref,
        out_ref, low_ref, keep_ref, send_ref, acc,
    )


def both_qkv_back_kernel(
    core_ref, q0_grad_ref, kv0_ref, got0_ref, q1_grad_ref, kv1_ref, got1_ref, start_ref, base_ref,
    own_ref, near_ref, far_ref, more_keep_ref, more_send_ref, small_ref,
    out_ref, low_ref, keep_ref, send_ref,
    acc, other_ref,
):
    first_step(acc)
    join(core_ref, (near_ref, far_ref, other_ref))
    low = start_ref[...].astype(BF)
    grad = base_ref[...] + qkv_back(low, qkv_parts((q0_grad_ref, kv0_ref, got0_ref)), own_ref, acc, 0)
    grad = grad + qkv_back(low, qkv_parts((q1_grad_ref, kv1_ref, got1_ref)), other_ref, acc, 1)
    out_ref[...] = grad
    low_ref[...] = grad.astype(BF)

    @pl.when(pl.program_id(0) == pl.num_programs(0) - 1)
    def _():
        rows = acc.shape[1] // 2
        ends = (core_ref[0], keep_ref, more_keep_ref), (1 - core_ref[0], send_ref, more_send_ref)
        for part, ref, more_ref in ends:
            here = pl.ds(pl.multiple_of(part * rows, 16), rows)
            for which in range(2):
                after = rows + more_ref.shape[1]
                ref[which, :rows, :] = acc[which, here, :].astype(BF)
                ref[which, rows:after, :] = more_ref[which]
                ref[which, after : after + 16, :] = small_ref[pl.ds(pl.multiple_of(part * 16, 16), 16), :].astype(BF)
                ref[which, after + 16 :, :] = jnp.zeros((ref.shape[1] - after - 16, D), BF)


def rows_call(kernel, name, core, by_rows, whole, row_outs, whole_outs=(), scratch=(), block=512):
    n = by_rows[0].shape[-2]

    def row_spec(shape):
        if len(shape) == 3:
            return pl.BlockSpec((shape[0], block, shape[2]), lambda i: (0, i, 0))
        return pl.BlockSpec((block, shape[1]), lambda i: (i, 0))

    def whole_spec(entry):
        if not isinstance(entry, tuple):
            return pl.BlockSpec(entry.shape, lambda i: (0,) * entry.ndim, pipeline_mode=pl.Buffered(1))
        array, rows, index = entry
        return pl.BlockSpec((rows, array.shape[1]), lambda i: (index, 0), pipeline_mode=pl.Buffered(1))

    arrays = [e[0] if isinstance(e, tuple) else e for e in whole]
    return pl.pallas_call(
        kernel,
        grid=(n // block,),
        in_specs=[pl.BlockSpec(memory_space=pltpu.SMEM)]
        + [row_spec(a.shape) for a in by_rows]
        + [whole_spec(e) for e in whole],
        out_specs=[row_spec(s) for s, _ in row_outs]
        + [pl.BlockSpec(s, lambda i, s=s: (0,) * len(s)) for s, _ in whole_outs],
        out_shape=[jax.ShapeDtypeStruct(s, t) for s, t in [*row_outs, *whole_outs]],
        scratch_shapes=[pltpu.VMEM(*s) for s in scratch],
        compiler_params=pltpu.CompilerParams(vmem_limit_bytes=VMEM_BYTES),
        cost_estimate=COST,
        name=name,
    )(core, *in_hbm(by_rows), *arrays)


def put_rows(out_ref, at, values):
    count = values.shape[0]
    if len(out_ref.shape) == 3 or out_ref.shape[1] < D:
        width = out_ref.shape[-1]
        folds = D // width
        depth = out_ref.shape[-2] // folds
        for begin in range(at // depth * depth, at + count, depth):
            low, high = max(begin, at), min(begin + depth, at + count)
            if low < high:
                kind = begin // depth
                ref = out_ref.at[kind] if len(out_ref.shape) == 3 else out_ref
                for fold in range(folds):
                    rows = slice(fold * depth + low - begin, fold * depth + high - begin)
                    ref[rows, :] = values[low - at : high - at, fold * width : (fold + 1) * width]
        return
    depth = out_ref.shape[0]
    for begin in range(0, at + count, depth):
        low, high = max(begin, at), min(begin + depth, at + count)
        if low < high:
            column = begin // depth * D
            out_ref[low - begin : high - begin, column : column + D] = values[low - at : high - at]


def unpack_kernel(order_ref, mine_ref, got_ref, *refs, places):
    outs, rows_in = refs[:-1], refs[-1]
    piece, core = order_ref[0], order_ref[1]
    pieces, rows, _ = mine_ref.shape
    for ref, of in ((mine_ref, core), (got_ref, 1 - core)):
        for k in range(pieces):
            begin = (of * pieces + (piece ^ k)) * rows
            rows_in[pl.ds(pl.multiple_of(begin, 16), rows), :] = ref[k].astype(F32)
    for out, begin, at, count in places:
        put_rows(outs[out], at, rows_in[begin : begin + count, :])


def unpack(order, mine, got, shapes, places):
    pieces, rows, width = mine.shape
    vmem = pl.BlockSpec(memory_space=pltpu.VMEM)
    return pl.pallas_call(
        partial(unpack_kernel, places=places),
        in_specs=[pl.BlockSpec(memory_space=pltpu.SMEM), vmem, vmem],
        out_specs=[vmem] * len(shapes),
        out_shape=[jax.ShapeDtypeStruct(s, F32) for s in shapes],
        scratch_shapes=[pltpu.VMEM((2 * pieces * rows, width), F32)],
        compiler_params=pltpu.CompilerParams(vmem_limit_bytes=VMEM_BYTES),
        cost_estimate=COST,
        name="unpack",
    )(order, mine, got)


class Place:
    def __init__(self, dp_size):
        self.dp_size = dp_size
        dp = lax.axis_index("dp")
        self.c = dp % 2
        self.stays = self.c == lax.axis_index("mp")
        self.masks = [1 << b for b in range(1, dp_size.bit_length() - 1)]
        self.bits = [(dp // mask) % 2 for mask in self.masks]
        self.core = jnp.stack([self.c, self.stays]).astype(jnp.int32)
        piece = jnp.int32(0)
        for bit in self.bits:
            piece = 2 * piece + bit.astype(jnp.int32)
        self.order = jnp.stack([piece, self.c.astype(jnp.int32)])

    def flip(self, values, mask):
        return lax.ppermute(values, "dp", [(d, d ^ mask) for d in range(self.dp_size)])

    def core_swap(self, values):
        return self.flip(values, 1)

    def y_swap(self, values):
        return lax.ppermute(values, "mp", [(0, 1), (1, 0)])

    def cross(self, values):
        perm = []
        for d in range(0, self.dp_size, 2):
            perm += [(2 * d + 1, 2 * d + 2), (2 * d + 2, 2 * d + 1)]
        return lax.ppermute(values, ("dp", "mp"), perm)


class Flow:
    def __init__(self):
        self.fresh = []
        self.chains = []
        self.results = {}

    def add(self, name, chain):
        self.fresh.append((name, chain, next(chain)))

    def go_on(self, name, chain, arrived):
        try:
            self.fresh.append((name, chain, chain.send(arrived)))
        except StopIteration as stop:
            self.results[name] = stop.value

    def step(self, values):
        due = [chain for chain in self.chains if chain[3] == 1]
        self.chains = [(*chain[:3], chain[3] - 1) for chain in self.chains if chain[3] > 1]
        values, arrived = lax.optimization_barrier((values, [chain[2] for chain in due]))
        for (name, chain, _, _), got in zip(due, arrived):
            self.go_on(name, chain, got)
        fresh, self.fresh = self.fresh, []
        values, operands = lax.optimization_barrier((values, [op[1] for _, _, op in fresh]))
        for (name, chain, (send, _, steps)), operand in zip(fresh, operands):
            self.chains.append((name, chain, send(operand), steps))
        return values

    def finish(self):
        while self.chains:
            name, chain, pending, _ = self.chains.pop(0)
            self.go_on(name, chain, pending)
        while self.fresh:
            name, chain, (send, operand, _) = self.fresh.pop(0)
            self.go_on(name, chain, send(operand))


def gathered(at, own, first=1, second=1):
    rows = own.shape[0] // 2
    near = yield at.y_swap, lax.dynamic_slice_in_dim(own, at.c * rows, rows, 0), first
    far = yield at.core_swap, near, second
    return near, far


def moved(at, values, steps):
    return (yield at.cross, values, steps)


def plus(*values):
    return sum(v.astype(F32) for v in values).astype(BF)


def over_chips(at, total, last_steps=1, back_steps=(1, 1, 1)):
    for mask, bit in zip(at.masks, at.bits):
        rows = total.shape[0] // 2
        half = lax.dynamic_slice_in_dim(total, (1 - bit) * rows, rows, 0)
        got = yield partial(at.flip, mask=mask), half, 1
        total = plus(lax.dynamic_slice_in_dim(total, bit * rows, rows, 0), got)
    total = total[None]
    for mask, steps in zip(at.masks[::-1], back_steps):
        got = yield partial(at.flip, mask=mask), total, steps
        total = jnp.concatenate([total, got])
    return total, (yield at.core_swap, total, last_steps)


def summed(at, keep, send, back_steps=(1, 1, 1)):
    got = yield at.core_swap, send, 1
    near = yield at.y_swap, plus(keep[1], got[1]), 1
    return (yield from over_chips(at, plus(keep[0], got[0], near), 1, back_steps))


def summed_other(at, keep, got, y_steps):
    near = yield at.y_swap, plus(keep[0], got[0]), y_steps
    return near


def summed_own(at, keep, send, near):
    got = yield at.core_swap, send, 1
    return (yield from over_chips(at, plus(keep[0], got[0], near)))


def rows_of(weight):
    if weight.ndim == 3:
        kinds, depth, width = weight.shape
        folded = jnp.concatenate([weight[:, : depth // 2], weight[:, depth // 2 :]], axis=2)
        return folded.reshape(kinds * depth // 2, 2 * width)
    depth, width = weight.shape
    if width == D:
        return weight
    if width < D:
        return jnp.concatenate([weight[: depth // 2], weight[depth // 2 :]], axis=1)
    return jnp.concatenate([weight[:, :D], weight[:, D:]], axis=0)


Q_SCALE = DH**-0.5 * math.log2(math.e)


def chip_rows(
    source_rows,
    target_rows,
    source_segment,
    target_segment,
    running,
    enc_qkv,
    enc_proj,
    enc_up,
    enc_down,
    enc_gains,
    enc_shifts,
    dec_qkv,
    dec_proj,
    cross_query,
    cross_kv,
    cross_proj,
    dec_up,
    dec_down,
    dec_gains,
    dec_shifts,
    halt_weight,
    enc_cotangent,
    dec_cotangent,
    *,
    dp_size,
):
    at = Place(dp_size)
    flow = Flow()
    n = source_rows.shape[0]
    row = ((n, D), F32)
    row_low = ((n, D), BF)
    half_low = ((n, HALF), BF)
    kv_low = ((2, n, HALF), BF)

    def embedding():
        place = at.core[0] * n + jnp.arange(n, dtype=jnp.int32)
        return signal(place.astype(F32)) + signal(jnp.ones((1,), F32))

    ints = jnp.concatenate([source_segment[0], target_segment[0], running[0, 0], running[1, 0]])
    ints = ints.reshape(6, n)
    flow.add("source", moved(at, source_rows[:, 0], 3))
    flow.add("ints", moved(at, ints, 2))
    (enc_qkv_now,) = flow.step((enc_qkv,))
    w_enc_qkv = rows_of(enc_qkv_now)
    flow.add("w_enc_qkv", gathered(at, w_enc_qkv, 2, 1))
    ints, dec_qkv_now = flow.step((ints, dec_qkv))
    w_dec_self = jnp.concatenate([rows_of(dec_qkv_now), rows_of(dec_proj)])
    ints, w_dec_self, embedding = flow.step((ints, w_dec_self, embedding()))
    ints = jnp.where(at.stays, ints, flow.results["ints"])
    runs = jnp.transpose(jnp.pad(ints[4:].astype(F32), ((0, 126), (0, 0))))
    lane = jnp.arange(128, dtype=jnp.int32) % DH
    source_hot, target_hot = (ints[:4].reshape(2, 2 * n, 1) == lane).astype(BF)

    w_enc = jnp.concatenate([rows_of(enc_proj), rows_of(enc_up), rows_of(enc_down)])
    w_cross = jnp.concatenate([rows_of(cross_query), rows_of(cross_kv)])
    w_dec = jnp.concatenate([rows_of(cross_proj), rows_of(dec_up), rows_of(dec_down)])
    cots = jnp.concatenate([enc_cotangent[:, 0].astype(BF), dec_cotangent[:, 0].astype(BF)], axis=1)
    pad = jnp.zeros((3, D), F32)
    small_enc = jnp.stack(
        [enc_gains[0], enc_shifts[0], enc_gains[1], enc_shifts[1], halt_weight[0]]
    )
    small_enc = jnp.concatenate([small_enc, pad])
    small_dec = jnp.stack(
        [dec_gains[0], dec_shifts[0], dec_gains[1], dec_shifts[1], dec_gains[2], dec_shifts[2], halt_weight[1]]
    )
    small_dec = jnp.concatenate([small_dec, pad[:1]])

    flow.add("target", moved(at, target_rows[:, 0], 2))
    flow.add("w_dec_self", gathered(at, w_dec_self, 2, 1))
    embedding, source_hot, target_hot = flow.step((embedding, source_hot, target_hot))
    (embedding,) = flow.step((embedding,))

    def pre(rows, got, own, other):
        return rows_call(
            pre_kernel, "project", at.core, [rows, got, embedding], [own, *other],
            [row, half_low, half_low, kv_low, kv_low], scratch=[(own.shape, BF)],
        )

    def attend(q, kv, got, hot, key_hot, causal=False):
        o, log = heads_forward(at.core, q, kv, got, hot, key_hot, causal)
        return o, (q, kv, got, hot, key_hot, o, log)

    def attend_back(kept, grad):
        return heads_backward(at.core, kept, grad, False)

    def attend_back_pair(kept, grad, pair):
        return heads_backward(at.core, kept, grad, True, 128 * pair, 128)

    w_enc_qkv_got = flow.results["w_enc_qkv"]
    enc_start, q0, q1, kv0, kv1 = pre(source_rows[:, 0], flow.results["source"], w_enc_qkv, w_enc_qkv_got)
    got0, got1 = at.core_swap(kv0), at.core_swap(kv1)
    enc_o0, enc_kept0 = attend(q0, kv0, got0, source_hot, source_hot)
    flow.add("w_enc", gathered(at, w_enc, 2, 1))
    enc_o0, q1, kv1, got1, w_enc, w_cross = flow.step((enc_o0, q1, kv1, got1, w_enc, w_cross))
    target = flow.results["target"]
    enc_o1, enc_kept1 = attend(q1, kv1, got1, source_hot, source_hot)
    enc_o1, target, w_dec = flow.step((enc_o1, target, w_dec))

    w_dec_self_got = flow.results["w_dec_self"]
    dec_start, q0, q1, kv0, kv1 = pre(target_rows[:, 0], target, w_dec_self, w_dec_self_got)
    got0, got1 = at.core_swap(kv0), at.core_swap(kv1)
    self_o0, self_kept0 = attend(q0, kv0, got0, target_hot, target_hot, True)
    flow.add("w_cross", gathered(at, w_cross))
    self_o0, q1, kv1, got1 = flow.step((self_o0, q1, kv1, got1))
    self_o1, self_kept1 = attend(q1, kv1, got1, target_hot, target_hot, True)
    flow.add("w_dec", gathered(at, w_dec, 3, 1))
    self_o1, enc_o1 = flow.step((self_o1, enc_o1))
    w_enc_got = flow.results["w_enc"]
    enc_sum_one, enc_sum_two, enc_states = rows_call(
        enc_post_kernel, "encoder_feed", at.core, [enc_o0, enc_o1, enc_start, runs],
        [w_enc, *w_enc_got, small_enc], [row, row, row_low], scratch=[(w_enc.shape, BF)],
    )
    flow.add("cots", moved(at, cots, 3))
    (enc_states,) = flow.step((enc_states,))
    w_cross_got = flow.results["w_cross"]
    self_proj = [(w_dec_self, HALF, 3)] + [(w, HALF, 1) for w in w_dec_self_got]
    dec_sum_one, q0, q1, kv0, kv1 = rows_call(
        dec_mid_kernel, "cross_project", at.core, [self_o0, self_o1, dec_start, enc_states],
        [*self_proj, w_cross, *w_cross_got, small_dec],
        [row, half_low, half_low, kv_low, kv_low], scratch=[(w_cross.shape, BF)],
    )
    got0, got1 = at.core_swap(kv0), at.core_swap(kv1)
    q0, q1, kv0, kv1 = flow.step((q0, q1, kv0, kv1))
    cross_o0, cross_kept0 = attend(q0, kv0, got0, target_hot, source_hot)
    cross_o0, q1, kv1, got1 = flow.step((cross_o0, q1, kv1, got1))
    cross_o1, cross_kept1 = attend(q1, kv1, got1, target_hot, source_hot)
    flow.add("enc_states", moved(at, enc_states, 1))
    (cross_o1,) = flow.step((cross_o1,))
    cots = jnp.where(at.stays, cots, flow.results["cots"])
    enc_cot, dec_cot = cots[:, :D], cots[:, D:]

    def grad_outs(rows):
        return [((2, rows // 2, D), BF)] * 2 + [((8, D), F32)]

    def grad_scratch(rows):
        return [((2, rows, D), F32), ((8, D), F32)]

    w_dec_got = flow.results["w_dec"]
    (
        dec_states, start_grad, sum_grad, o0_grad, o1_grad, *dec_parts, small_two,
    ) = rows_call(
        dec_post_kernel, "decoder_feed", at.core,
        [cross_o0, cross_o1, dec_sum_one, dec_start, runs, dec_cot], [w_dec, *w_dec_got, small_dec],
        [row_low, row, row, half_low, half_low], grad_outs(9 * HALF),
        [*grad_scratch(9 * HALF), (w_dec.shape, BF), ((2, 512, 4 * D), BF)],
    )
    flow.add("dec", summed(at, *dec_parts))
    flow.add("dec_states", moved(at, dec_states, 1))
    o0_grad, o1_grad = flow.step((o0_grad, o1_grad))

    q0_grad, kv0_grad, kv0_send = attend_back(cross_kept0, o0_grad)
    q0_grad, kv0_grad, kv0_send, o1_grad = flow.step((q0_grad, kv0_grad, kv0_send, o1_grad))
    kv0_got = at.core_swap(kv0_send)
    q1_grad, kv1_grad, kv1_send = attend_back(cross_kept1, o1_grad)
    q1_grad, kv1_grad, kv1_send, kv0_got = flow.step((q1_grad, kv1_grad, kv1_send, kv0_got))
    kv1_got = at.core_swap(kv1_send)

    (
        enc_base, enc_o0_grad, enc_o1_grad, *enc_parts, small_enc_grad,
    ) = rows_call(
        enc_back_kernel, "encoder_feed_back", at.core,
        [kv0_grad, kv1_grad, kv0_got, kv1_got, enc_states, enc_cot, enc_start, enc_sum_one, enc_sum_two,
         enc_o0, enc_o1, runs],
        [w_cross, *w_cross_got, w_enc, *w_enc_got, small_enc],
        [row, half_low, half_low], grad_outs(11 * HALF),
        [*grad_scratch(11 * HALF), (w_cross.shape, BF), (w_enc.shape, BF)],
    )
    flow.add("enc", summed(at, *enc_parts))
    enc_o0_grad, enc_o1_grad, q0_grad = flow.step((enc_o0_grad, enc_o1_grad, q0_grad))
    (
        dec_base, self_o0_grad, self_o1_grad, *mid_parts, small_one,
    ) = rows_call(
        dec_mid_back_kernel, "cross_project_back", at.core,
        [q0_grad, q1_grad, sum_grad, dec_sum_one, start_grad, self_o0, self_o1],
        [(w_cross, HALF, 0), *w_cross_got, *self_proj, small_dec],
        [row, half_low, half_low], grad_outs(2 * HALF), grad_scratch(2 * HALF),
    )
    smalls = jnp.concatenate([small_enc_grad, small_one, small_two, jnp.zeros((8, D), F32)])
    enc_o1_grad, mid_parts, smalls = flow.step((enc_o1_grad, mid_parts, smalls))

    q1_grad, kv1_grad, kv1_send = attend_back(enc_kept1, enc_o1_grad)
    q1_grad, kv1_grad, kv1_send, enc_o0_grad = flow.step((q1_grad, kv1_grad, kv1_send, enc_o0_grad))
    kv1_got = at.core_swap(kv1_send)
    q0_grad, kv0_grad, kv0_send = attend_back(enc_kept0, enc_o0_grad)
    q0_grad, kv0_grad, kv0_send, kv1_got = flow.step((q0_grad, kv0_grad, kv0_send, kv1_got))
    kv0_got = at.core_swap(kv0_send)
    source_grad, source_low, keep, send = rows_call(
        both_qkv_back_kernel, "project_back", at.core,
        [q0_grad, kv0_grad, kv0_got, q1_grad, kv1_grad, kv1_got, enc_start, enc_base],
        [w_enc_qkv, *w_enc_qkv_got, *mid_parts, smalls], [row, row_low], [((2, 3 * HALF, D), BF)] * 2,
        [((2, 3 * HALF, D), F32), (w_enc_qkv.shape, BF)],
    )
    flow.add("enc_qkv", summed(at, keep, send, (1, 2, 1)))
    flow.add("source_grad", moved(at, source_low, 1))
    self_o1_grad, source_grad = flow.step((self_o1_grad, source_grad))

    def heads_back(kept, grad):
        parts = []
        for pair in range(2):
            q_grad, kv_grad, kv_send = attend_back_pair(kept, grad, pair)
            grad, q_grad, kv_grad, kv_send = flow.step((grad, q_grad, kv_grad, kv_send))
            parts += [q_grad, kv_grad, at.core_swap(kv_send)]
        return parts

    parts = heads_back(self_kept1, self_o1_grad)
    part_outs = [((1, 3 * HALF // 2, D), BF)] * 2
    part_scratch = [((1, 3 * HALF, D), F32)]
    target_grad, _, keep1, send1 = rows_call(
        other_qkv_back_kernel, "project_back", at.core, [*parts, dec_start, dec_base],
        [*w_dec_self_got], [row, row_low], part_outs, [*part_scratch, (w_dec_self.shape, BF)],
    )
    flow.add("dec_qkv_other", summed_other(at, keep1, at.core_swap(send1), 1))
    target_grad, self_o0_grad = flow.step((target_grad, self_o0_grad))
    parts = heads_back(self_kept0, self_o0_grad)
    target_grad, target_low, keep0, send0 = rows_call(
        own_qkv_back_kernel, "project_back", at.core, [*parts, dec_start, target_grad],
        [(w_dec_self, 3 * HALF, 0)], [row, row_low], part_outs, part_scratch,
    )
    flow.add("dec_qkv", summed_own(at, keep0, send0, flow.results["dec_qkv_other"]))
    flow.add("target_grad", moved(at, target_low, 2))

    done = flow.results

    def weights(name, *weights):
        places, begin = [], 0
        for i, weight in enumerate(weights):
            places.append((i, begin, 0, weight.size // D))
            begin += weight.size // D
        return unpack(at.order, *done[name], [w.shape for w in weights], places)

    def home(values, name):
        values = jnp.where(at.stays, values, done[name].astype(values.dtype))[:, None]
        return with_layout_constraint(values, Layout((0, 1, 2))) if values.dtype == F32 else values

    def mixed_weights(name):
        part, more = 3 * HALF // 2, HALF // 2
        places = []
        for c in range(2):
            begin = c * 3 * HALF
            places += [(0, begin, c * part, part), (1 + c, begin + part, 0, 2 * more)]
            places += [(3, begin + part + 2 * more, 16 * c, 16)]
        shapes = [enc_qkv.shape, cross_query.shape, dec_proj.shape, (32, D)]
        return unpack(at.order, *done[name], shapes, places)

    target_grad, done["dec"] = flow.step((target_grad, done["dec"]))
    dec_grads = weights("dec", cross_proj, dec_up, dec_down)
    dec_grads, done["enc"] = flow.step((dec_grads, done["enc"]))
    enc_grads = weights("enc", cross_kv, enc_proj, enc_up, enc_down)
    enc_grads, source_grad = flow.step((enc_grads, source_grad))
    source_out = home(source_grad, "source_grad")
    source_out, enc_states, dec_states = flow.step((source_out, enc_states, dec_states))
    states_out = home(enc_states, "enc_states"), home(dec_states, "dec_states")
    states_out, target_grad = flow.step((states_out, target_grad))
    target_out = home(target_grad, "target_grad")
    target_out, done["enc_qkv"] = flow.step((target_out, done["enc_qkv"]))
    mixed_grads = mixed_weights("enc_qkv")
    (mixed_grads,) = flow.step((mixed_grads,))
    flow.finish()
    cross_proj_grad, dec_up_grad, dec_down_grad = dec_grads
    cross_kv_grad, enc_proj_grad, enc_up_grad, enc_down_grad = enc_grads
    enc_qkv_grad, cross_query_grad, dec_proj_grad, small = mixed_grads
    (dec_qkv_grad,) = weights("dec_qkv", dec_qkv)
    enc_small, one, two = small[:8], small[8:16], small[16:24]
    return (
        *states_out,
        source_out,
        target_out,
        enc_qkv_grad,
        enc_proj_grad,
        enc_up_grad,
        enc_down_grad,
        enc_small[0:3:2],
        enc_small[1:4:2],
        dec_qkv_grad,
        dec_proj_grad,
        cross_query_grad,
        cross_kv_grad,
        cross_proj_grad,
        dec_up_grad,
        dec_down_grad,
        jnp.concatenate([one[0:1], two[0:3:2]]),
        jnp.concatenate([one[1:2], two[1:4:2]]),
        jnp.stack([enc_small[4], two[4]]),
    )


def solution(mesh):
    dp_size, mp_size = mesh.shape["dp"], mesh.shape["mp"]
    by_chip = mp_size == 2 and dp_size in (4, 8, 16)
    body = partial(chip_rows, dp_size=dp_size) if by_chip else local
    return jax.shard_map(
        body,
        mesh=mesh,
        in_specs=(
            P("mp", "dp", None),
            P("mp", "dp", None),
            P("dp", None),
            P("dp", None),
            P(None, "dp", "mp"),
            P(None, None, "mp"),
            P("mp", None),
            P(None, "mp"),
            P("mp", None),
            P(),
            P(),
            P(None, None, "mp"),
            P("mp", None),
            P(None, "mp"),
            P(None, None, "mp"),
            P("mp", None),
            P(None, "mp"),
            P("mp", None),
            P(),
            P(),
            P(),
            P("mp", "dp", None),
            P("mp", "dp", None),
        ),
        out_specs=(
            P("mp", "dp", None),
            P("mp", "dp", None),
            P("mp", "dp", None),
            P("mp", "dp", None),
            P(None, None, "mp"),
            P("mp", None),
            P(None, "mp"),
            P("mp", None),
            P(),
            P(),
            P(None, None, "mp"),
            P("mp", None),
            P(None, "mp"),
            P(None, None, "mp"),
            P("mp", None),
            P(None, "mp"),
            P("mp", None),
            P(),
            P(),
            P(),
        ),
        check_vma=False,
    )
```

```python
import math
from functools import partial

import jax
import jax.numpy as jnp
from jax import lax
from jax.experimental import pallas as pl
from jax.experimental.layout import Layout, with_layout_constraint
from jax.experimental.pallas import tpu as pltpu
from jax.sharding import PartitionSpec as P

D = 512
DH = 64


EPS = 1e-05
NEGATIVE = -1000000000.0


def signal(position):
    half_width = D // 2
    inverse_rates = jnp.exp(
        jnp.arange(half_width, dtype=jnp.float32) * (-jnp.log(10000.0) / (half_width - 1))
    )
    angles = position[:, None] * inverse_rates[None, :]
    return jnp.concatenate([jnp.sin(angles), jnp.cos(angles)], axis=1)


def normalize(values, norm_gain, norm_shift):
    centred = values - jnp.mean(values, axis=-1, keepdims=True)
    spread = jnp.mean(centred * centred, axis=-1, keepdims=True)
    return centred * lax.rsqrt(spread + EPS) * norm_gain + norm_shift


def halting(running_now, initial, updated, weight):
    halt_prob = jax.nn.sigmoid(jnp.sum(updated * weight, axis=-1, keepdims=True))
    return initial + running_now * halt_prob * (updated - initial)


def dot_last(left, right):
    return lax.dot_general(
        left, right, (((left.ndim - 1,), (1,)), ((), ())), preferred_element_type=jnp.float32
    )


def collect(piece_rows):
    return lax.all_gather(piece_rows, "mp", axis=0, tiled=True)


def collect_grad(piece_rows):
    return lax.all_gather(piece_rows.astype(jnp.bfloat16), "mp", axis=0, tiled=True)


def project_out(hidden, weight, rows):

    def partial_term(begin_row, row_count):
        return jnp.dot(hidden, weight, preferred_element_type=jnp.float32)

    return lax.psum_scatter(
        partial_term(jnp.int32(0), lax.axis_size("mp") * rows).astype(jnp.bfloat16),
        "mp",
        scatter_dimension=0,
        tiled=True,
    ).astype(jnp.float32)


def project_back(gradients, matrices, rows):

    def partial_term(begin_row, row_count):
        summed = jnp.zeros(
            (row_count,) + gradients[0].shape[1:-1] + (matrices[0].shape[0],), jnp.float32
        )
        for gradient, matrix in zip(gradients, matrices):
            summed = summed + dot_last(gradient, matrix)
        return summed

    return lax.psum_scatter(
        partial_term(jnp.int32(0), lax.axis_size("mp") * rows).astype(jnp.bfloat16),
        "mp",
        scatter_dimension=0,
        tiled=True,
    ).astype(jnp.float32)


def to_pairs(values):
    length, row_count, width = values.shape
    return (
        values.reshape(length, row_count, width // DH, DH)
        .transpose(1, 2, 0, 3)
        .reshape(-1, length, DH)
    )


def from_pairs(values, row_count):
    pairs, length, unused = values.shape
    heads_here = pairs // row_count
    return (
        values.reshape(row_count, heads_here, length, DH)
        .transpose(2, 0, 1, 3)
        .reshape(length, row_count, heads_here * DH)
    )


def per_pair(segments, width):
    return jnp.repeat(segments, width // DH, axis=0)


def pair_scores(query_block, key_rows, segment_block, segment_keys, first_row, causal):
    scores = lax.dot_general(
        query_block, key_rows, (((1,), (1,)), ((), ())), preferred_element_type=jnp.float32
    )
    scores = scores * DH ** (-0.5)
    allowed = segment_block[:, None] == segment_keys[None, :]
    if causal:
        query_place = first_row + jnp.arange(query_block.shape[0], dtype=jnp.int32)
        key_place = jnp.arange(key_rows.shape[0], dtype=jnp.int32)
        allowed = allowed & (key_place[None, :] <= query_place[:, None])
    return jnp.where(allowed, scores, NEGATIVE)


def attend_pair(inputs, causal):
    query_rows, key_rows, value_rows, segment_query, segment_keys = inputs
    length = query_rows.shape[0]
    block_rows = min(512, length)
    blocks = length // block_rows
    firsts = jnp.arange(blocks, dtype=jnp.int32) * block_rows

    def one_block(pieces):
        query_block, segment_block, first_row = pieces
        scores = pair_scores(query_block, key_rows, segment_block, segment_keys, first_row, causal)
        highest = jnp.max(scores, axis=1, keepdims=True)
        exponent = jnp.exp(scores - highest)
        totals = jnp.sum(exponent, axis=1, keepdims=True)
        weights = (exponent / totals).astype(jnp.bfloat16)
        mixed = jnp.dot(weights, value_rows, preferred_element_type=jnp.float32)
        return (mixed.astype(jnp.bfloat16), (highest + jnp.log(totals))[:, 0])

    mixed, log_total = lax.map(
        one_block,
        (
            query_rows.reshape(blocks, block_rows, -1),
            segment_query.reshape(blocks, block_rows),
            firsts,
        ),
    )
    return (mixed.reshape(length, -1), log_total.reshape(length))


def attend_pair_back(inputs, causal):
    query_rows, key_rows, value_rows, mixed_grad, log_total, segment_query, segment_keys = inputs
    length = query_rows.shape[0]
    block_rows = min(512, length)
    blocks = length // block_rows
    firsts = jnp.arange(blocks, dtype=jnp.int32) * block_rows

    def one_block(carry, pieces):
        key_total, value_total = carry
        query_block, grad_block, log_block, segment_block, first_row = pieces
        scores = pair_scores(query_block, key_rows, segment_block, segment_keys, first_row, causal)
        probs = jnp.exp(scores - log_block[:, None])
        weights = probs.astype(jnp.bfloat16)
        prob_grad = lax.dot_general(
            grad_block, value_rows, (((1,), (1,)), ((), ())), preferred_element_type=jnp.float32
        )
        inner = jnp.sum(probs * prob_grad, axis=1, keepdims=True)
        score_grad = (probs * (prob_grad - inner)).astype(jnp.bfloat16)
        query_grad = jnp.dot(score_grad, key_rows, preferred_element_type=jnp.float32) * DH ** (
            -0.5
        )
        key_total = key_total + lax.dot_general(
            score_grad, query_block, (((0,), (0,)), ((), ())), preferred_element_type=jnp.float32
        ) * DH ** (-0.5)
        value_total = value_total + lax.dot_general(
            weights, grad_block, (((0,), (0,)), ((), ())), preferred_element_type=jnp.float32
        )
        return ((key_total, value_total), query_grad.astype(jnp.bfloat16))

    zeros_start = jnp.zeros(key_rows.shape, jnp.float32)
    (key_total, value_total), query_grad = lax.scan(
        one_block,
        (zeros_start, zeros_start),
        (
            query_rows.reshape(blocks, block_rows, -1),
            mixed_grad.reshape(blocks, block_rows, -1),
            log_total.reshape(blocks, block_rows),
            segment_query.reshape(blocks, block_rows),
            firsts,
        ),
    )
    return (
        query_grad.reshape(length, -1),
        key_total.astype(jnp.bfloat16),
        value_total.astype(jnp.bfloat16),
    )


def attention_forward(
    query_full,
    key_full,
    weight_query,
    weight_key,
    weight_value,
    weight_out,
    segment_query,
    segment_keys,
    causal,
    rows,
):
    queries = jnp.dot(query_full, weight_query, preferred_element_type=jnp.float32).astype(
        jnp.bfloat16
    )
    keys_low = jnp.dot(key_full, weight_key, preferred_element_type=jnp.float32).astype(
        jnp.bfloat16
    )
    values_low = jnp.dot(key_full, weight_value, preferred_element_type=jnp.float32).astype(
        jnp.bfloat16
    )
    width = queries.shape[2]
    row_count = queries.shape[1]
    mixed, log_total = lax.map(
        partial(attend_pair, causal=causal),
        (
            to_pairs(queries),
            to_pairs(keys_low),
            to_pairs(values_low),
            per_pair(segment_query, width),
            per_pair(segment_keys, width),
        ),
    )
    mixed = from_pairs(mixed, row_count)
    branch = project_out(mixed, weight_out, rows)
    return (branch, (queries, keys_low, values_low, mixed, log_total))


def attention_backward(
    branch_grad, kept, query_full, key_full, weight_out, segment_query, segment_keys, causal
):
    queries, keys_low, values_low, kept_mixed, log_total = kept
    grad_full = collect_grad(branch_grad)
    out_weight_grad = jnp.einsum(
        "lrc,lrd->cd", kept_mixed, grad_full, preferred_element_type=jnp.float32
    )
    mixed_grad = dot_last(grad_full, weight_out).astype(jnp.bfloat16)
    width = queries.shape[2]
    row_count = queries.shape[1]
    query_grad, key_grad, value_grad = lax.map(
        partial(attend_pair_back, causal=causal),
        (
            to_pairs(queries),
            to_pairs(keys_low),
            to_pairs(values_low),
            to_pairs(mixed_grad),
            log_total,
            per_pair(segment_query, width),
            per_pair(segment_keys, width),
        ),
    )
    query_grad = from_pairs(query_grad, row_count)
    key_grad = from_pairs(key_grad, row_count)
    value_grad = from_pairs(value_grad, row_count)
    weight_grads = (
        jnp.einsum("lrd,lrc->dc", query_full, query_grad, preferred_element_type=jnp.float32),
        jnp.einsum("lrd,lrc->dc", key_full, key_grad, preferred_element_type=jnp.float32),
        jnp.einsum("lrd,lrc->dc", key_full, value_grad, preferred_element_type=jnp.float32),
    )
    return (query_grad, key_grad, value_grad, weight_grads, out_weight_grad)


def feed_forward(source_full, weight_up, weight_down, rows):
    hidden = jnp.dot(source_full, weight_up, preferred_element_type=jnp.float32)
    active = jax.nn.gelu(hidden).astype(jnp.bfloat16)
    return (project_out(active, weight_down, rows), hidden)


def feed_backward(branch_grad, source_full, hidden, weight_up, weight_down, rows):
    grad_full = collect_grad(branch_grad)
    active, gelu_back = jax.vjp(jax.nn.gelu, hidden)
    active = active.astype(jnp.bfloat16)
    down_grad = jnp.einsum("lrf,lrd->fd", active, grad_full, preferred_element_type=jnp.float32)
    hidden_grad = gelu_back(dot_last(grad_full, weight_down))[0].astype(jnp.bfloat16)
    up_grad = jnp.einsum(
        "lrd,lrf->df", source_full, hidden_grad, preferred_element_type=jnp.float32
    )
    input_grad = project_back((hidden_grad,), (weight_up,), rows)
    return (input_grad, up_grad, down_grad)


def local(
    source_rows,
    target_rows,
    source_segment,
    target_segment,
    running,
    enc_qkv,
    enc_proj,
    enc_up,
    enc_down,
    enc_gains,
    enc_shifts,
    dec_qkv,
    dec_proj,
    cross_query,
    cross_kv,
    cross_proj,
    dec_up,
    dec_down,
    dec_gains,
    dec_shifts,
    halt_weight,
    enc_cotangent,
    dec_cotangent,
):
    rows = source_rows.shape[0]
    position = (lax.axis_index("mp") * rows + jnp.arange(rows, dtype=jnp.int32)).astype(jnp.float32)
    embedding = (signal(position) + signal(jnp.ones((1,), jnp.float32)))[:, None, :]
    runs_now = jnp.transpose(running, (0, 2, 1)).astype(jnp.float32)[..., None]
    enc_start = source_rows.astype(jnp.float32) + embedding
    enc_start_low = enc_start.astype(jnp.bfloat16)
    enc_start_full = collect(enc_start_low)
    enc_attn, enc_attn_kept = attention_forward(
        enc_start_full,
        enc_start_full,
        enc_qkv[0],
        enc_qkv[1],
        enc_qkv[2],
        enc_proj,
        source_segment,
        source_segment,
        False,
        rows,
    )
    enc_sum_one = enc_start + enc_attn
    enc_middle = normalize(enc_sum_one, enc_gains[0], enc_shifts[0])
    enc_middle_low = enc_middle.astype(jnp.bfloat16)
    enc_middle_full = collect(enc_middle_low)
    enc_ffn, enc_hidden = feed_forward(enc_middle_full, enc_up, enc_down, rows)
    enc_sum_two = enc_middle + enc_ffn
    enc_last = normalize(enc_sum_two, enc_gains[1], enc_shifts[1])
    enc_final = halting(runs_now[0], enc_start, enc_last, halt_weight[0])
    enc_states = enc_final.astype(jnp.bfloat16)
    enc_states_full = collect(enc_states)
    dec_start = target_rows.astype(jnp.float32) + embedding
    dec_start_low = dec_start.astype(jnp.bfloat16)
    dec_start_full = collect(dec_start_low)
    dec_self, dec_self_kept = attention_forward(
        dec_start_full,
        dec_start_full,
        dec_qkv[0],
        dec_qkv[1],
        dec_qkv[2],
        dec_proj,
        target_segment,
        target_segment,
        True,
        rows,
    )
    dec_sum_one = dec_start + dec_self
    dec_middle = normalize(dec_sum_one, dec_gains[0], dec_shifts[0])
    dec_middle_low = dec_middle.astype(jnp.bfloat16)
    dec_middle_full = collect(dec_middle_low)
    dec_cross, dec_cross_kept = attention_forward(
        dec_middle_full,
        enc_states_full,
        cross_query,
        cross_kv[0],
        cross_kv[1],
        cross_proj,
        target_segment,
        source_segment,
        False,
        rows,
    )
    dec_sum_two = dec_middle + dec_cross
    dec_mixed = normalize(dec_sum_two, dec_gains[1], dec_shifts[1])
    dec_mixed_low = dec_mixed.astype(jnp.bfloat16)
    dec_mixed_full = collect(dec_mixed_low)
    dec_ffn, dec_hidden = feed_forward(dec_mixed_full, dec_up, dec_down, rows)
    dec_sum_three = dec_mixed + dec_ffn
    dec_last = normalize(dec_sum_three, dec_gains[2], dec_shifts[2])
    dec_final = halting(runs_now[1], dec_start, dec_last, halt_weight[1])
    dec_states = dec_final.astype(jnp.bfloat16)
    unused, halt_back = jax.vjp(partial(halting, runs_now[1]), dec_start, dec_last, halt_weight[1])
    dec_start_grad, last_grad, dec_halt_grad = halt_back(dec_cotangent)
    unused, norm_back = jax.vjp(normalize, dec_sum_three, dec_gains[2], dec_shifts[2])
    sum_grad, dec_gain_three, dec_shift_three = norm_back(last_grad)
    ffn_input_grad, dec_up_grad, dec_down_grad = feed_backward(
        sum_grad, dec_mixed_full, dec_hidden, dec_up, dec_down, rows
    )
    mixed_grad = sum_grad + ffn_input_grad
    unused, norm_back = jax.vjp(normalize, dec_sum_two, dec_gains[1], dec_shifts[1])
    sum_grad, dec_gain_two, dec_shift_two = norm_back(mixed_grad)
    query_grad, key_grad, value_grad, cross_grads, cross_proj_grad = attention_backward(
        sum_grad,
        dec_cross_kept,
        dec_middle_full,
        enc_states_full,
        cross_proj,
        target_segment,
        source_segment,
        False,
    )
    middle_grad = sum_grad + project_back((query_grad,), (cross_query,), rows)
    enc_extra = project_back((key_grad, value_grad), (cross_kv[0], cross_kv[1]), rows)
    unused, norm_back = jax.vjp(normalize, dec_sum_one, dec_gains[0], dec_shifts[0])
    sum_grad, dec_gain_one, dec_shift_one = norm_back(middle_grad)
    query_grad, key_grad, value_grad, self_grads, dec_proj_grad = attention_backward(
        sum_grad,
        dec_self_kept,
        dec_start_full,
        dec_start_full,
        dec_proj,
        target_segment,
        target_segment,
        True,
    )
    target_grad = (
        sum_grad
        + dec_start_grad
        + project_back(
            (query_grad, key_grad, value_grad), (dec_qkv[0], dec_qkv[1], dec_qkv[2]), rows
        )
    )
    dec_qkv_grad = jnp.stack(self_grads)
    cross_query_grad = cross_grads[0]
    cross_kv_grad = jnp.stack([cross_grads[1], cross_grads[2]])
    enc_final_grad = enc_cotangent + enc_extra
    unused, halt_back = jax.vjp(partial(halting, runs_now[0]), enc_start, enc_last, halt_weight[0])
    enc_start_grad, last_grad, enc_halt_grad = halt_back(enc_final_grad)
    unused, norm_back = jax.vjp(normalize, enc_sum_two, enc_gains[1], enc_shifts[1])
    sum_grad, enc_gain_two, enc_shift_two = norm_back(last_grad)
    ffn_input_grad, enc_up_grad, enc_down_grad = feed_backward(
        sum_grad, enc_middle_full, enc_hidden, enc_up, enc_down, rows
    )
    middle_grad = sum_grad + ffn_input_grad
    unused, norm_back = jax.vjp(normalize, enc_sum_one, enc_gains[0], enc_shifts[0])
    sum_grad, enc_gain_one, enc_shift_one = norm_back(middle_grad)
    query_grad, key_grad, value_grad, self_grads, enc_proj_grad = attention_backward(
        sum_grad,
        enc_attn_kept,
        enc_start_full,
        enc_start_full,
        enc_proj,
        source_segment,
        source_segment,
        False,
    )
    source_grad = (
        sum_grad
        + enc_start_grad
        + project_back(
            (query_grad, key_grad, value_grad), (enc_qkv[0], enc_qkv[1], enc_qkv[2]), rows
        )
    )
    enc_qkv_grad = jnp.stack(self_grads)
    (
        enc_qkv_grad,
        enc_proj_grad,
        enc_up_grad,
        enc_down_grad,
        dec_qkv_grad,
        dec_proj_grad,
        cross_query_grad,
        cross_kv_grad,
        cross_proj_grad,
        dec_up_grad,
        dec_down_grad,
    ) = (
        lax.psum(enc_qkv_grad.astype(jnp.bfloat16), "dp").astype(jnp.float32),
        lax.psum(enc_proj_grad.astype(jnp.bfloat16), "dp").astype(jnp.float32),
        lax.psum(enc_up_grad.astype(jnp.bfloat16), "dp").astype(jnp.float32),
        lax.psum(enc_down_grad.astype(jnp.bfloat16), "dp").astype(jnp.float32),
        lax.psum(dec_qkv_grad.astype(jnp.bfloat16), "dp").astype(jnp.float32),
        lax.psum(dec_proj_grad.astype(jnp.bfloat16), "dp").astype(jnp.float32),
        lax.psum(cross_query_grad.astype(jnp.bfloat16), "dp").astype(jnp.float32),
        lax.psum(cross_kv_grad.astype(jnp.bfloat16), "dp").astype(jnp.float32),
        lax.psum(cross_proj_grad.astype(jnp.bfloat16), "dp").astype(jnp.float32),
        lax.psum(dec_up_grad.astype(jnp.bfloat16), "dp").astype(jnp.float32),
        lax.psum(dec_down_grad.astype(jnp.bfloat16), "dp").astype(jnp.float32),
    )
    enc_gains_grad, enc_shifts_grad, dec_gains_grad, dec_shifts_grad, halt_weight_grad = lax.psum(
        (
            jnp.stack([enc_gain_one, enc_gain_two]),
            jnp.stack([enc_shift_one, enc_shift_two]),
            jnp.stack([dec_gain_one, dec_gain_two, dec_gain_three]),
            jnp.stack([dec_shift_one, dec_shift_two, dec_shift_three]),
            jnp.stack([enc_halt_grad, dec_halt_grad]),
        ),
        ("dp", "mp"),
    )
    return (
        enc_states,
        dec_states,
        source_grad,
        target_grad,
        enc_qkv_grad,
        enc_proj_grad,
        enc_up_grad,
        enc_down_grad,
        enc_gains_grad,
        enc_shifts_grad,
        dec_qkv_grad,
        dec_proj_grad,
        cross_query_grad,
        cross_kv_grad,
        cross_proj_grad,
        dec_up_grad,
        dec_down_grad,
        dec_gains_grad,
        dec_shifts_grad,
        halt_weight_grad,
    )


BIG = -1e30
BF = jnp.bfloat16
F32 = jnp.float32
NN = (((1,), (0,)), ((), ()))
NT = (((1,), (1,)), ((), ()))
TN = (((0,), (0,)), ((), ()))
HALF = D // 2
VMEM_BYTES = 56 * 1024 * 1024
COST = pl.CostEstimate(flops=1, bytes_accessed=1, transcendentals=0)


def dot_nn(a, b):
    return lax.dot_general(a, b, NN, preferred_element_type=F32)


def dot_nt(a, b):
    return lax.dot_general(a, b, NT, preferred_element_type=F32)


def dot_tn(a, b):
    return lax.dot_general(a, b, TN, preferred_element_type=F32)


def lanes():
    lane = lax.broadcasted_iota(jnp.int32, (1, 128), 1)
    return lane < DH, lane % DH


def in_hbm(arrays):
    return [pltpu.with_memory_space_constraint(a, pltpu.HBM) for a in arrays]


def pipelined(tasks, scores_of, after):
    ahead = scores_of(*tasks[0])
    for i, task in enumerate(tasks):
        now = ahead
        if i + 1 < len(tasks):
            ahead = scores_of(*tasks[i + 1])
        after(now, *task)


def forward_kernel(
    core_ref, q_ref, own_ref, got_ref, hot_ref, key_hot_ref, o_ref, log_ref, keys, values, *, causal
):
    n = q_ref.shape[0]
    chunk = n // 2
    core = core_ref[0]
    left, lane = lanes()
    for ref, of in ((own_ref, core), (got_ref, 1 - core)):
        here = pl.ds(pl.multiple_of(of * n, n), n)
        k, hot = ref[0], key_hot_ref[here, :]
        ext = jnp.where((lane >= 8) & (lane < 11), jnp.ones_like(hot), hot)
        keys[0, here, :] = jnp.where(left, k, ext)
        keys[1, here, :] = jnp.where(left, ext, k)
        turned = ref[1].T
        ones = jnp.ones((DH, n), BF)
        values[0, :, here] = jnp.concatenate([turned[:DH], ones])
        values[1, :, here] = jnp.concatenate([ones, turned[DH:]])
    pair = q_ref[...]
    mine = hot_ref[pl.ds(pl.multiple_of(core * n, n), n), :].astype(F32)
    ext = jnp.where(lane < 8, (1.0 - mine) * BIG, 0.0).astype(BF)
    queries = jnp.where(left, pair, ext), jnp.where(left, ext, pair)

    def run(tasks, rows):
        state = {}

        def scores_of(head, query, key, cut):
            q = queries[head][query * rows : (query + 1) * rows]
            scores = dot_nt(keys[head, key * chunk : (key + 1) * chunk, :], q)
            if cut:
                at = lax.broadcasted_iota(jnp.int32, scores.shape, 0)
                to = lax.broadcasted_iota(jnp.int32, scores.shape, 1)
                scores = jnp.where(at <= to, scores, BIG)
            return scores

        def after(scores, head, query, key, cut):
            top = jnp.max(scores, axis=0, keepdims=True)
            total = 0.0
            if (head, query) in state:
                old_top, total = state[head, query]
                top = jnp.maximum(top, old_top)
                total = total * jnp.exp2(old_top - top)
            probs = jnp.exp2(scores - top).astype(BF)
            total = total + dot_nn(values[head, :, key * chunk : (key + 1) * chunk], probs)
            state[head, query] = top, total

        pipelined(tasks, scores_of, after)
        for query in range(n // rows):
            (top0, total0), (top1, total1) = state[0, query], state[1, query]
            out = jnp.concatenate([total0[:DH] / total0[DH:], total1[DH:] / total1[:DH]])
            logs = jnp.concatenate([top1 + jnp.log2(total1[:DH]), top0 + jnp.log2(total0[DH:])])
            here = slice(query * rows, (query + 1) * rows)
            o_ref[here, :] = out.T.astype(BF)
            log_ref[here, :] = logs.T

    if not causal:
        run([(head, 0, key, False) for head in range(2) for key in range(4)], n)
    else:
        for case in range(2):

            @pl.when(core == case)
            def _(case=case):
                run(
                    [
                        (head, query, key, key == 2 * case + query)
                        for head in range(2)
                        for query in range(2)
                        for key in range(2 * case + query + 1)
                    ],
                    chunk,
                )


def heads_forward(core, q, own, got, hot, key_hot, causal):
    n, width = q.shape
    length = 2 * n
    keys = pl.BlockSpec((2, n, 128), lambda p: (0, 0, p))
    queries = pl.BlockSpec((n, 128), lambda p: (0, p))
    table = pl.BlockSpec((length, 128), lambda p: (0, 0))
    return pl.pallas_call(
        partial(forward_kernel, causal=causal),
        grid=(width // 128,),
        in_specs=[
            pl.BlockSpec(memory_space=pltpu.SMEM),
            queries,
            keys,
            keys,
            table,
            table,
        ],
        out_specs=[queries, queries],
        out_shape=[jax.ShapeDtypeStruct((n, width), BF), jax.ShapeDtypeStruct((n, width), F32)],
        scratch_shapes=[pltpu.VMEM((2, length, 128), BF), pltpu.VMEM((2, 128, length), BF)],
        compiler_params=pltpu.CompilerParams(vmem_limit_bytes=VMEM_BYTES),
        cost_estimate=COST,
        name="attention_causal" if causal else "attention",
    )(core, *in_hbm((q, own, got, hot, key_hot)))


def backward_kernel(
    core_ref, q_ref, own_ref, got_ref, hot_ref, key_hot_ref, grad_ref, o_ref, log_ref,
    q_grad_ref, own_grad_ref, got_grad_ref, queries, grads, q_turned, grad_turned, q_total, *, causal,
):
    step = pl.program_id(1)
    n, block = q_ref.shape[0], own_ref.shape[1]
    chunk = n // 2
    blocks = n // block
    core = core_ref[0]
    left, lane = lanes()

    @pl.when(step == 0)
    def _():
        log = log_ref[...]
        high = log.astype(BF).astype(F32)
        middle = (log - high).astype(BF).astype(F32)
        low = log - high - middle
        mine = hot_ref[pl.ds(pl.multiple_of(core * n, n), n), :].astype(F32)
        ext = jnp.where(lane < 8, (1.0 - mine) * BIG, 0.0)
        ext = jnp.where(lane == 10, -low, ext)
        ext = jnp.where(lane == 9, -middle, jnp.where(lane == 8, -high, ext)).astype(BF)
        pair = q_ref[...]
        queries[0] = jnp.where(left, pair, ext)
        queries[1] = jnp.where(left, ext, pair)
        q_turned[...] = pair.T
        pair = grad_ref[...]
        product = pair.astype(F32) * o_ref[...].astype(F32)
        high = product.astype(BF)
        low = (product - high.astype(F32)).astype(BF)
        row = lax.broadcasted_iota(jnp.int32, (128, 128), 0)
        column = lax.broadcasted_iota(jnp.int32, (128, 128), 1)
        across = ((row < DH) != (column < DH)).astype(BF)
        inner = dot_nn(high, across) + dot_nn(low, across)
        high = inner.astype(BF).astype(F32)
        ext = jnp.where(lane == 8, -high, jnp.where(lane == 9, high - inner, 0.0)).astype(BF)
        grads[0] = jnp.where(left, pair, ext)
        grads[1] = jnp.where(left, ext, pair)
        grad_turned[...] = pair.T
        q_total[...] = jnp.zeros_like(q_total)

    own = step < blocks
    k = jnp.where(own, own_ref[0], got_ref[0])
    v = jnp.where(own, own_ref[1], got_ref[1])
    place = jnp.where(own, core * n + step * block, (1 - core) * n + (step - blocks) * block)
    hot = key_hot_ref[pl.ds(pl.multiple_of(place, block), block), :]
    ones = jnp.ones_like(v)
    ext = jnp.where((lane >= 8) & (lane < 11), ones, hot)
    keys = (jnp.where(left, k, ext), jnp.where(left, ext, k))
    values = (jnp.where(left, v, ones), jnp.where(left, ones, v))

    def run(tasks):
        k_grads, v_grads = [0.0, 0.0], [0.0, 0.0]

        def scores_of(head, query, cut):
            here = slice(query * chunk, (query + 1) * chunk)
            scores = dot_nt(queries[head, here, :], keys[head])
            if cut:
                to = lax.broadcasted_iota(jnp.int32, scores.shape, 0)
                at = lax.broadcasted_iota(jnp.int32, scores.shape, 1)
                scores = jnp.where(at <= to, scores, BIG)
            return scores, dot_nt(grads[head, here, :], values[head])

        def after(products, head, query, cut):
            here = slice(query * chunk, (query + 1) * chunk)
            probs = jnp.exp2(products[0])
            score_grad = (probs * products[1]).astype(BF)
            v_grads[head] = v_grads[head] + dot_nn(grad_turned[:, here], probs.astype(BF))
            k_grads[head] = k_grads[head] + dot_nn(q_turned[:, here], score_grad)
            q_total[head, here, :] += dot_nn(score_grad, keys[head])

        pipelined(tasks, scores_of, after)
        k_grad = jnp.concatenate([k_grads[0][:DH], k_grads[1][DH:]]).T
        v_grad = jnp.concatenate([v_grads[0][:DH], v_grads[1][DH:]]).T
        put((k_grad * math.log(2.0)).astype(BF), v_grad.astype(BF))

    def put(k_grad, v_grad):
        @pl.when(own)
        def _():
            own_grad_ref[0] = k_grad
            own_grad_ref[1] = v_grad

        @pl.when(jnp.logical_not(own))
        def _():
            got_grad_ref[0] = k_grad
            got_grad_ref[1] = v_grad

    if not causal:
        run([(head, query, False) for head in range(2) for query in range(2)])
    else:
        @pl.when(jnp.logical_not(own) & (core == 0))
        def _():
            put(jnp.zeros((block, 128), BF), jnp.zeros((block, 128), BF))

        @pl.when(jnp.logical_not(own) & (core == 1))
        def _():
            run([(head, query, False) for head in range(2) for query in range(2)])

        for case in range(2):

            @pl.when(step == case)
            def _(case=case):
                run([(head, query, query == case) for head in range(2) for query in range(case, 2)])

    @pl.when(step == 2 * blocks - 1)
    def _():
        q_grad_ref[...] = (jnp.where(left, q_total[0], q_total[1]) * DH**-0.5).astype(BF)


def heads_backward(core, kept, grad, causal, begin=0, width=HALF):
    q, own, got, hot, key_hot, o, log = kept
    n = q.shape[0]
    skip = begin // 128
    block = n // 2
    blocks = 2
    first = lambda b: jnp.minimum(b, blocks - 1)
    second = lambda b: jnp.maximum(b - blocks, 0)
    whole = pl.BlockSpec((n, 128), lambda p, b: (0, skip + p))
    whole_out = pl.BlockSpec((n, 128), lambda p, b: (0, p))
    table = pl.BlockSpec((2 * n, 128), lambda p, b: (0, 0))

    def keys(part, skip):
        return pl.BlockSpec((2, block, 128), lambda p, b: (0, part(b), skip + p))

    return pl.pallas_call(
        partial(backward_kernel, causal=causal),
        grid=(width // 128, 2 * blocks),
        in_specs=[
            pl.BlockSpec(memory_space=pltpu.SMEM),
            whole,
            keys(first, skip),
            keys(second, skip),
            table,
            table,
            whole,
            whole,
            whole,
        ],
        out_specs=[whole_out, keys(first, 0), keys(second, 0)],
        out_shape=[jax.ShapeDtypeStruct(s, BF) for s in ((n, width), (2, n, width), (2, n, width))],
        scratch_shapes=[
            pltpu.VMEM((2, n, 128), BF),
            pltpu.VMEM((2, n, 128), BF),
            pltpu.VMEM((128, n), BF),
            pltpu.VMEM((128, n), BF),
            pltpu.VMEM((2, n, 128), F32),
        ],
        compiler_params=pltpu.CompilerParams(vmem_limit_bytes=VMEM_BYTES),
        cost_estimate=COST,
        name="attention_causal_back" if causal else "attention_back",
    )(core, *in_hbm((q, own, got, hot, key_hot, grad, o, log)))


def fold_dot(x, w):
    return dot_nn(x[:, :HALF], w[:, :HALF]) + dot_nn(x[:, HALF:], w[:, HALF:])


def fold_dot_t(g, w):
    return jnp.concatenate([dot_nt(g, w[:, :HALF]), dot_nt(g, w[:, HALF:])], axis=1)


def fold_grad(x, g):
    return jnp.concatenate([dot_tn(x[:, :HALF], g), dot_tn(x[:, HALF:], g)], axis=1)


def norm(v, gain, shift):
    centred = v - jnp.mean(v, axis=-1, keepdims=True)
    scale = lax.rsqrt(jnp.mean(centred * centred, axis=-1, keepdims=True) + EPS)
    unit = centred * scale
    return unit * gain + shift, unit, scale


def norm_back(grad, unit, scale, gain):
    inner = grad * gain
    mean_inner = jnp.mean(inner, axis=-1, keepdims=True)
    mean_unit = jnp.mean(inner * unit, axis=-1, keepdims=True)
    return scale * (inner - mean_inner - unit * mean_unit)


def over_rows(v):
    return jnp.sum(v, axis=0, keepdims=True)


GELU_C = math.sqrt(2.0 / math.pi)


def gelu(u):
    return 0.5 * u * (1.0 + jnp.tanh(GELU_C * u * (1.0 + 0.044715 * u * u)))


def gelu_both(u):
    square = u * u
    t = jnp.tanh(GELU_C * u * (1.0 + 0.044715 * square))
    half = 0.5 * (1.0 + t)
    slope = half + 0.5 * u * (1.0 - t * t) * (GELU_C * (1.0 + 3 * 0.044715 * square))
    return u * half, slope


def halt_gate(last, weight):
    logit = jnp.sum(last * weight, axis=-1, keepdims=True)
    return 1.0 / (1.0 + jnp.exp(-logit))


def halt_back(grad, start, last, runs, weight):
    gate = halt_gate(last, weight)
    used = runs * gate
    logit_grad = used * (1.0 - gate) * jnp.sum(grad * (last - start), axis=-1, keepdims=True)
    return grad * (1.0 - used), used * grad + logit_grad * weight, over_rows(logit_grad * last)


def ffn_blocks(own_ref, other_ref, begin):
    for which, ref in ((0, own_ref), (1, other_ref)):
        for j in range(2):
            up = begin + j * D
            down = up + 2 * D
            yield which, ref[up : up + D, :], ref[down : down + D, :], up, down


def ffn(low, own_ref, other_ref, begin, kept=None):
    blocks = list(ffn_blocks(own_ref, other_ref, begin))
    total = []

    def after(hidden, j):
        if kept is None:
            active = gelu(hidden).astype(BF)
        else:
            active, slope = gelu_both(hidden)
            active = active.astype(BF)
            kept[0, :, j * D : (j + 1) * D] = active
            kept[1, :, j * D : (j + 1) * D] = slope.astype(BF)
        total.append(dot_nn(active, blocks[j][2]))

    pipelined([(j,) for j in range(4)], lambda j: dot_nn(low, blocks[j][1]), after)
    return sum(total)


def ffn_back(low, out_low, own_ref, other_ref, begin, acc, shift, kept=None):
    blocks = list(ffn_blocks(own_ref, other_ref, begin))
    total = []

    def products(j):
        _, up, down, _, _ = blocks[j]
        return None if kept is not None else dot_nn(low, up), dot_nt(out_low, down)

    def after(got, j):
        which, up, _, up_at, down_at = blocks[j]
        hidden, active_grad = got
        if kept is None:
            active, slope = gelu_both(hidden)
            active = active.astype(BF)
        else:
            active = kept[0, :, j * D : (j + 1) * D]
            slope = kept[1, :, j * D : (j + 1) * D].astype(F32)
        hidden_grad = (active_grad * slope).astype(BF)
        up_at, down_at = up_at + shift, down_at + shift
        acc[which, down_at : down_at + D, :] += dot_tn(active, out_low)
        acc[which, up_at : up_at + D, :] += dot_tn(low, hidden_grad)
        total.append(dot_nt(hidden_grad, up))

    pipelined([(j,) for j in range(4)], products, after)
    return sum(total)


def proj_back(o_refs, out_low, projs, acc, begin, o_grad_refs):
    for which in range(2):
        o_grad_refs[which][...] = dot_nt(out_low, projs[which]).astype(BF)
        acc[which, begin : begin + HALF, :] += dot_tn(o_refs[which][...], out_low)


def first_step(*refs):
    @pl.when(pl.program_id(0) == 0)
    def _():
        for ref in refs:
            ref[...] = jnp.zeros_like(ref)


def last_step(core_ref, acc, keep_ref, send_ref, small_acc=None, small_ref=None):
    @pl.when(pl.program_id(0) == pl.num_programs(0) - 1)
    def _():
        rows = acc.shape[1] // 2
        for part, ref in ((core_ref[0], keep_ref), (1 - core_ref[0], send_ref)):
            here = pl.ds(pl.multiple_of(part * rows, 16), rows)
            for which in range(acc.shape[0]):
                ref[which] = acc[which, here, :].astype(BF)
        if small_ref is not None:
            small_ref[...] = small_acc[...]


def join(core_ref, *triples):
    @pl.when(pl.program_id(0) == 0)
    def _():
        for near_ref, far_ref, whole in triples:
            rows = near_ref.shape[0]
            for part, ref in ((core_ref[0], near_ref), (1 - core_ref[0], far_ref)):
                whole[pl.ds(pl.multiple_of(part * rows, 16), rows), :] = ref[...]


def second_part(core_ref, near_ref, far_ref):
    return jnp.where(core_ref[0] == 1, near_ref[...], far_ref[...])


def pre_kernel(
    core_ref, rows_ref, got_ref, place_ref, own_ref, near_ref, far_ref,
    start_ref, q0_ref, q1_ref, kv0_ref, kv1_ref,
    other_ref,
):
    join(core_ref, (near_ref, far_ref, other_ref))
    rows = jnp.where(core_ref[1] == 1, rows_ref[...].astype(F32), got_ref[...].astype(F32))
    start = rows + place_ref[...]
    start_ref[...] = start
    low = start.astype(BF)
    for ref, q_ref, kv_ref in ((own_ref, q0_ref, kv0_ref), (other_ref, q1_ref, kv1_ref)):
        q_ref[...] = (fold_dot(low, ref[0:HALF, :]) * Q_SCALE).astype(BF)
        for kind in range(2):
            w = ref[(kind + 1) * HALF : (kind + 2) * HALF, :]
            kv_ref[kind] = fold_dot(low, w).astype(BF)


def enc_post_kernel(
    core_ref, o0_ref, o1_ref, start_ref, runs_ref, own_ref, near_ref, far_ref, small_ref,
    sum_one_ref, sum_two_ref, states_ref,
    other_ref,
):
    join(core_ref, (near_ref, far_ref, other_ref))
    start = start_ref[...]
    sum_one = start + dot_nn(o0_ref[...], own_ref[:HALF, :]) + dot_nn(o1_ref[...], other_ref[:HALF, :])
    sum_one_ref[...] = sum_one
    middle, _, _ = norm(sum_one, small_ref[0:1, :], small_ref[1:2, :])
    sum_two = middle + ffn(middle.astype(BF), own_ref, other_ref, HALF)
    sum_two_ref[...] = sum_two
    last, _, _ = norm(sum_two, small_ref[2:3, :], small_ref[3:4, :])
    gate = halt_gate(last, small_ref[4:5, :])
    states_ref[...] = (start + runs_ref[:, 0:1] * gate * (last - start)).astype(BF)


def dec_mid_kernel(
    core_ref, o0_ref, o1_ref, start_ref, states_ref, proj_own_ref, proj_near_ref, proj_far_ref,
    own_ref, near_ref, far_ref, small_ref,
    sum_ref, q0_ref, q1_ref, kv0_ref, kv1_ref,
    other_ref,
):
    join(core_ref, (near_ref, far_ref, other_ref))
    total = start_ref[...] + dot_nn(o0_ref[...], proj_own_ref[...])
    total = total + dot_nn(o1_ref[...], second_part(core_ref, proj_near_ref, proj_far_ref))
    sum_ref[...] = total
    middle, _, _ = norm(total, small_ref[0:1, :], small_ref[1:2, :])
    low = middle.astype(BF)
    states = states_ref[...]
    for ref, q_ref, kv_ref in ((own_ref, q0_ref, kv0_ref), (other_ref, q1_ref, kv1_ref)):
        q_ref[...] = (fold_dot(low, ref[0:HALF, :]) * Q_SCALE).astype(BF)
        for kind in range(2):
            w = ref[(kind + 1) * HALF : (kind + 2) * HALF, :]
            kv_ref[kind] = fold_dot(states, w).astype(BF)


def dec_post_kernel(
    core_ref, o0_ref, o1_ref, sum_one_ref, start_ref, runs_ref, cot_ref, own_ref, near_ref, far_ref, small_ref,
    states_ref, start_grad_ref, sum_grad_ref, o0_grad_ref, o1_grad_ref,
    keep_ref, send_ref, small_grad_ref,
    acc, small_acc, other_ref, kept,
):
    join(core_ref, (near_ref, far_ref, other_ref))
    first_step(acc, small_acc)
    start = start_ref[...]
    projs = own_ref[:HALF, :], other_ref[:HALF, :]
    middle, _, _ = norm(sum_one_ref[...], small_ref[0:1, :], small_ref[1:2, :])
    sum_two = middle + dot_nn(o0_ref[...], projs[0]) + dot_nn(o1_ref[...], projs[1])
    gain_two = small_ref[2:3, :]
    mixed, unit_two, scale_two = norm(sum_two, gain_two, small_ref[3:4, :])
    low = mixed.astype(BF)
    sum_three = mixed + ffn(low, own_ref, other_ref, HALF, kept)
    gain_three = small_ref[4:5, :]
    last, unit_three, scale_three = norm(sum_three, gain_three, small_ref[5:6, :])
    weight = small_ref[6:7, :]
    runs = runs_ref[:, 1:2]
    states_ref[...] = (start + runs * halt_gate(last, weight) * (last - start)).astype(BF)
    start_grad, last_grad, weight_grad = halt_back(
        cot_ref[...].astype(F32), start, last, runs, weight
    )
    start_grad_ref[...] = start_grad
    small_acc[4:5, :] += weight_grad
    small_acc[2:3, :] += over_rows(last_grad * unit_three)
    small_acc[3:4, :] += over_rows(last_grad)
    grad = norm_back(last_grad, unit_three, scale_three, gain_three)
    grad = grad + ffn_back(low, grad.astype(BF), own_ref, other_ref, HALF, acc, 0, kept)
    small_acc[0:1, :] += over_rows(grad * unit_two)
    small_acc[1:2, :] += over_rows(grad)
    grad = norm_back(grad, unit_two, scale_two, gain_two)
    sum_grad_ref[...] = grad
    proj_back((o0_ref, o1_ref), grad.astype(BF), projs, acc, 0, (o0_grad_ref, o1_grad_ref))
    last_step(core_ref, acc, keep_ref, send_ref, small_acc, small_grad_ref)


def dec_mid_back_kernel(
    core_ref, q0_grad_ref, q1_grad_ref, sum_grad_ref, sum_one_ref, start_grad_ref, o0_ref, o1_ref,
    cq_own_ref, cq_near_ref, cq_far_ref, proj_own_ref, proj_near_ref, proj_far_ref, small_ref,
    out_ref, o0_grad_ref, o1_grad_ref, keep_ref, send_ref, small_grad_ref,
    acc, small_acc,
):
    cq_other = jnp.where(core_ref[0] == 0, cq_near_ref[:HALF, :], cq_far_ref[:HALF, :])
    first_step(acc, small_acc)
    gain = small_ref[0:1, :]
    middle, unit, scale = norm(sum_one_ref[...], gain, small_ref[1:2, :])
    low = middle.astype(BF)
    grad = sum_grad_ref[...]
    for which, (w, part_ref) in enumerate(((cq_own_ref[...], q0_grad_ref), (cq_other, q1_grad_ref))):
        grad = grad + fold_dot_t(part_ref[...], w)
        acc[which, :HALF, :] += fold_grad(low, part_ref[...])
    small_acc[0:1, :] += over_rows(grad * unit)
    small_acc[1:2, :] += over_rows(grad)
    grad = norm_back(grad, unit, scale, gain)
    out_ref[...] = start_grad_ref[...] + grad
    projs = proj_own_ref[...], second_part(core_ref, proj_near_ref, proj_far_ref)
    proj_back((o0_ref, o1_ref), grad.astype(BF), projs, acc, HALF, (o0_grad_ref, o1_grad_ref))
    last_step(core_ref, acc, keep_ref, send_ref, small_acc, small_grad_ref)


def kv_total(own_ref, got_ref, kind):
    return (own_ref[kind].astype(F32) + got_ref[kind].astype(F32)).astype(BF)


def enc_back_kernel(
    core_ref, kv0_ref, kv1_ref, got0_ref, got1_ref, states_ref, cot_ref, start_ref, sum_one_ref, sum_two_ref,
    o0_ref, o1_ref, runs_ref, cross_own_ref, cross_near_ref, cross_far_ref, own_ref, near_ref, far_ref, small_ref,
    out_ref, o0_grad_ref, o1_grad_ref, keep_ref, send_ref, small_grad_ref,
    acc, small_acc, cross_other_ref, other_ref,
):
    join(core_ref, (near_ref, far_ref, other_ref), (cross_near_ref, cross_far_ref, cross_other_ref))
    first_step(acc, small_acc)
    states = states_ref[...]
    grad = cot_ref[...].astype(F32)
    crosses = (cross_own_ref, kv0_ref, got0_ref), (cross_other_ref, kv1_ref, got1_ref)
    for which, (ref, kv_ref, got_ref) in enumerate(crosses):
        for kind in range(2):
            part = kv_total(kv_ref, got_ref, kind)
            at = kind * HALF
            grad = grad + fold_dot_t(part, ref[at + HALF : at + 2 * HALF, :])
            acc[which, at : at + HALF, :] += fold_grad(states, part)
    gain_one, gain_two, weight = small_ref[0:1, :], small_ref[2:3, :], small_ref[4:5, :]
    last, unit_two, scale_two = norm(sum_two_ref[...], gain_two, small_ref[3:4, :])
    start_grad, last_grad, weight_grad = halt_back(
        grad, start_ref[...], last, runs_ref[:, 0:1], weight
    )
    small_acc[4:5, :] += weight_grad
    small_acc[2:3, :] += over_rows(last_grad * unit_two)
    small_acc[3:4, :] += over_rows(last_grad)
    grad = norm_back(last_grad, unit_two, scale_two, gain_two)
    middle, unit_one, scale_one = norm(sum_one_ref[...], gain_one, small_ref[1:2, :])
    grad = grad + ffn_back(middle.astype(BF), grad.astype(BF), own_ref, other_ref, HALF, acc, 2 * HALF)
    small_acc[0:1, :] += over_rows(grad * unit_one)
    small_acc[1:2, :] += over_rows(grad)
    grad = norm_back(grad, unit_one, scale_one, gain_one)
    out_ref[...] = start_grad + grad
    projs = own_ref[:HALF, :], other_ref[:HALF, :]
    proj_back((o0_ref, o1_ref), grad.astype(BF), projs, acc, 2 * HALF, (o0_grad_ref, o1_grad_ref))
    last_step(core_ref, acc, keep_ref, send_ref, small_acc, small_grad_ref)


def qkv_back(low, parts, w_ref, acc, which):
    grad = 0.0
    for kind, part in enumerate(parts):
        rows = slice(kind * HALF, (kind + 1) * HALF)
        grad = grad + fold_dot_t(part, w_ref[rows, :])
        acc[which, rows, :] += fold_grad(low, part)
    return grad


def qkv_parts(q_ref, kv_ref, got_ref):
    return q_ref[...], kv_total(kv_ref, got_ref, 0), kv_total(kv_ref, got_ref, 1)


def own_qkv_back_kernel(
    core_ref, q_ref, kv_ref, got_ref, start_ref, base_ref, w_ref,
    out_ref, low_ref, keep_ref, send_ref,
    acc,
):
    first_step(acc)
    low = start_ref[...].astype(BF)
    parts = qkv_parts(q_ref, kv_ref, got_ref)
    grad = base_ref[...] + qkv_back(low, parts, w_ref, acc, 0)
    out_ref[...] = grad
    low_ref[...] = grad.astype(BF)
    last_step(core_ref, acc, keep_ref, send_ref)


def other_qkv_back_kernel(
    core_ref, q_ref, kv_ref, got_ref, start_ref, base_ref, near_ref, far_ref,
    out_ref, low_ref, keep_ref, send_ref,
    acc, other_ref,
):
    join(core_ref, (near_ref, far_ref, other_ref))
    own_qkv_back_kernel(
        core_ref, q_ref, kv_ref, got_ref, start_ref, base_ref, other_ref,
        out_ref, low_ref, keep_ref, send_ref, acc,
    )


def both_qkv_back_kernel(
    core_ref, q0_grad_ref, kv0_ref, got0_ref, q1_grad_ref, kv1_ref, got1_ref, start_ref, base_ref,
    own_ref, near_ref, far_ref, more_keep_ref, more_send_ref, small_ref,
    out_ref, low_ref, keep_ref, send_ref,
    acc, other_ref,
):
    first_step(acc)
    join(core_ref, (near_ref, far_ref, other_ref))
    low = start_ref[...].astype(BF)
    grad = base_ref[...] + qkv_back(low, qkv_parts(q0_grad_ref, kv0_ref, got0_ref), own_ref, acc, 0)
    grad = grad + qkv_back(low, qkv_parts(q1_grad_ref, kv1_ref, got1_ref), other_ref, acc, 1)
    out_ref[...] = grad
    low_ref[...] = grad.astype(BF)

    @pl.when(pl.program_id(0) == pl.num_programs(0) - 1)
    def _():
        rows = acc.shape[1] // 2
        ends = (core_ref[0], keep_ref, more_keep_ref), (1 - core_ref[0], send_ref, more_send_ref)
        for part, ref, more_ref in ends:
            here = pl.ds(pl.multiple_of(part * rows, 16), rows)
            for which in range(2):
                after = rows + more_ref.shape[1]
                ref[which, :rows, :] = acc[which, here, :].astype(BF)
                ref[which, rows:after, :] = more_ref[which]
                ref[which, after : after + 16, :] = small_ref[pl.ds(pl.multiple_of(part * 16, 16), 16), :].astype(BF)
                ref[which, after + 16 :, :] = jnp.zeros((ref.shape[1] - after - 16, D), BF)


def rows_call(kernel, name, core, by_rows, whole, row_outs, whole_outs=(), scratch=(), block=512):
    n = by_rows[0].shape[-2]

    def row_spec(shape):
        if len(shape) == 3:
            return pl.BlockSpec((shape[0], block, shape[2]), lambda i: (0, i, 0))
        return pl.BlockSpec((block, shape[1]), lambda i: (i, 0))

    def whole_spec(entry):
        if not isinstance(entry, tuple):
            return pl.BlockSpec(entry.shape, lambda i: (0,) * entry.ndim, pipeline_mode=pl.Buffered(1))
        array, rows, index = entry
        return pl.BlockSpec((rows, array.shape[1]), lambda i: (index, 0), pipeline_mode=pl.Buffered(1))

    arrays = [e[0] if isinstance(e, tuple) else e for e in whole]
    return pl.pallas_call(
        kernel,
        grid=(n // block,),
        in_specs=[pl.BlockSpec(memory_space=pltpu.SMEM)]
        + [row_spec(a.shape) for a in by_rows]
        + [whole_spec(e) for e in whole],
        out_specs=[row_spec(s) for s, _ in row_outs]
        + [pl.BlockSpec(s, lambda i, s=s: (0,) * len(s)) for s, _ in whole_outs],
        out_shape=[jax.ShapeDtypeStruct(s, t) for s, t in [*row_outs, *whole_outs]],
        scratch_shapes=[pltpu.VMEM(*s) for s in scratch],
        compiler_params=pltpu.CompilerParams(vmem_limit_bytes=VMEM_BYTES),
        cost_estimate=COST,
        name=name,
    )(core, *in_hbm(by_rows), *arrays)


def put_rows(out_ref, at, values):
    count = values.shape[0]
    if len(out_ref.shape) == 3 or out_ref.shape[1] < D:
        width = out_ref.shape[-1]
        folds = D // width
        depth = out_ref.shape[-2] // folds
        for begin in range(at // depth * depth, at + count, depth):
            low, high = max(begin, at), min(begin + depth, at + count)
            if low < high:
                kind = begin // depth
                ref = out_ref.at[kind] if len(out_ref.shape) == 3 else out_ref
                for fold in range(folds):
                    rows = slice(fold * depth + low - begin, fold * depth + high - begin)
                    ref[rows, :] = values[low - at : high - at, fold * width : (fold + 1) * width]
        return
    depth = out_ref.shape[0]
    for begin in range(0, at + count, depth):
        low, high = max(begin, at), min(begin + depth, at + count)
        if low < high:
            column = begin // depth * D
            out_ref[low - begin : high - begin, column : column + D] = values[low - at : high - at]


def unpack_kernel(order_ref, mine_ref, got_ref, *refs, places):
    outs, rows_in = refs[:-1], refs[-1]
    piece, core = order_ref[0], order_ref[1]
    pieces, rows, _ = mine_ref.shape
    for ref, of in ((mine_ref, core), (got_ref, 1 - core)):
        for k in range(pieces):
            begin = (of * pieces + (piece ^ k)) * rows
            rows_in[pl.ds(pl.multiple_of(begin, 16), rows), :] = ref[k].astype(F32)
    for out, begin, at, count in places:
        put_rows(outs[out], at, rows_in[begin : begin + count, :])


def unpack(order, mine, got, shapes, places):
    pieces, rows, width = mine.shape
    vmem = pl.BlockSpec(memory_space=pltpu.VMEM)
    return pl.pallas_call(
        partial(unpack_kernel, places=places),
        in_specs=[pl.BlockSpec(memory_space=pltpu.SMEM), vmem, vmem],
        out_specs=[vmem] * len(shapes),
        out_shape=[jax.ShapeDtypeStruct(s, F32) for s in shapes],
        scratch_shapes=[pltpu.VMEM((2 * pieces * rows, width), F32)],
        compiler_params=pltpu.CompilerParams(vmem_limit_bytes=VMEM_BYTES),
        cost_estimate=COST,
        name="unpack",
    )(order, mine, got)


class Place:
    def __init__(self, dp_size):
        self.dp_size = dp_size
        dp = lax.axis_index("dp")
        self.c = dp % 2
        self.stays = self.c == lax.axis_index("mp")
        self.masks = [1 << b for b in range(1, dp_size.bit_length() - 1)]
        self.bits = [(dp // mask) % 2 for mask in self.masks]
        self.core = jnp.stack([self.c, self.stays]).astype(jnp.int32)
        piece = jnp.int32(0)
        for bit in self.bits:
            piece = 2 * piece + bit.astype(jnp.int32)
        self.order = jnp.stack([piece, self.c.astype(jnp.int32)])

    def flip(self, values, mask):
        return lax.ppermute(values, "dp", [(d, d ^ mask) for d in range(self.dp_size)])

    def core_swap(self, values):
        return self.flip(values, 1)

    def y_swap(self, values):
        return lax.ppermute(values, "mp", [(0, 1), (1, 0)])

    def cross(self, values):
        perm = []
        for d in range(0, self.dp_size, 2):
            perm += [(2 * d + 1, 2 * d + 2), (2 * d + 2, 2 * d + 1)]
        return lax.ppermute(values, ("dp", "mp"), perm)


class Flow:
    def __init__(self):
        self.fresh = []
        self.chains = []
        self.results = {}

    def add(self, name, chain):
        self.fresh.append((name, chain, next(chain)))

    def go_on(self, name, chain, arrived):
        try:
            self.fresh.append((name, chain, chain.send(arrived)))
        except StopIteration as stop:
            self.results[name] = stop.value

    def step(self, values):
        due = [chain for chain in self.chains if chain[3] == 1]
        self.chains = [(*chain[:3], chain[3] - 1) for chain in self.chains if chain[3] > 1]
        values, arrived = lax.optimization_barrier((values, [chain[2] for chain in due]))
        for (name, chain, _, _), got in zip(due, arrived):
            self.go_on(name, chain, got)
        fresh, self.fresh = self.fresh, []
        values, operands = lax.optimization_barrier((values, [op[1] for _, _, op in fresh]))
        for (name, chain, (send, _, steps)), operand in zip(fresh, operands):
            self.chains.append((name, chain, send(operand), steps))
        return values

    def finish(self):
        while self.chains:
            name, chain, pending, _ = self.chains.pop(0)
            self.go_on(name, chain, pending)
        while self.fresh:
            name, chain, (send, operand, _) = self.fresh.pop(0)
            self.go_on(name, chain, send(operand))


def gathered(at, own, first=1, second=1):
    rows = own.shape[0] // 2
    near = yield at.y_swap, lax.dynamic_slice_in_dim(own, at.c * rows, rows, 0), first
    far = yield at.core_swap, near, second
    return near, far


def moved(at, values, steps):
    return (yield at.cross, values, steps)


def plus(*values):
    return sum(v.astype(F32) for v in values).astype(BF)


def over_chips(at, total, last_steps=1, back_steps=(1, 1, 1)):
    for mask, bit in zip(at.masks, at.bits):
        rows = total.shape[0] // 2
        half = lax.dynamic_slice_in_dim(total, (1 - bit) * rows, rows, 0)
        got = yield partial(at.flip, mask=mask), half, 1
        total = plus(lax.dynamic_slice_in_dim(total, bit * rows, rows, 0), got)
    total = total[None]
    for mask, steps in zip(at.masks[::-1], back_steps):
        got = yield partial(at.flip, mask=mask), total, steps
        total = jnp.concatenate([total, got])
    return total, (yield at.core_swap, total, last_steps)


def summed(at, keep, send, back_steps=(1, 1, 1)):
    got = yield at.core_swap, send, 1
    near = yield at.y_swap, plus(keep[1], got[1]), 1
    return (yield from over_chips(at, plus(keep[0], got[0], near), 1, back_steps))


def summed_other(at, keep, got, y_steps):
    near = yield at.y_swap, plus(keep[0], got[0]), y_steps
    return near


def summed_own(at, keep, send, near):
    got = yield at.core_swap, send, 1
    return (yield from over_chips(at, plus(keep[0], got[0], near)))


def rows_of(weight):
    if weight.ndim == 3:
        kinds, depth, width = weight.shape
        folded = jnp.concatenate([weight[:, : depth // 2], weight[:, depth // 2 :]], axis=2)
        return folded.reshape(kinds * depth // 2, 2 * width)
    depth, width = weight.shape
    if width == D:
        return weight
    if width < D:
        return jnp.concatenate([weight[: depth // 2], weight[depth // 2 :]], axis=1)
    return jnp.concatenate([weight[:, :D], weight[:, D:]], axis=0)


Q_SCALE = DH**-0.5 * math.log2(math.e)


def chip_rows(
    source_rows,
    target_rows,
    source_segment,
    target_segment,
    running,
    enc_qkv,
    enc_proj,
    enc_up,
    enc_down,
    enc_gains,
    enc_shifts,
    dec_qkv,
    dec_proj,
    cross_query,
    cross_kv,
    cross_proj,
    dec_up,
    dec_down,
    dec_gains,
    dec_shifts,
    halt_weight,
    enc_cotangent,
    dec_cotangent,
    *,
    dp_size,
):
    at = Place(dp_size)
    flow = Flow()
    n = source_rows.shape[0]
    row = ((n, D), F32)
    row_low = ((n, D), BF)
    half_low = ((n, HALF), BF)
    kv_low = ((2, n, HALF), BF)

    def embedding():
        place = at.core[0] * n + jnp.arange(n, dtype=jnp.int32)
        return signal(place.astype(F32)) + signal(jnp.ones((1,), F32))

    ints = jnp.concatenate([source_segment[0], target_segment[0], running[0, 0], running[1, 0]])
    ints = ints.reshape(6, n)
    flow.add("source", moved(at, source_rows[:, 0], 3))
    flow.add("ints", moved(at, ints, 2))
    (enc_qkv_now,) = flow.step((enc_qkv,))
    w_enc_qkv = rows_of(enc_qkv_now)
    flow.add("w_enc_qkv", gathered(at, w_enc_qkv, 2, 1))
    later = ints, dec_qkv, enc_up, cross_kv, dec_up, enc_cotangent, dec_cotangent, running, enc_gains, dec_gains
    later = flow.step(later)
    ints, dec_qkv_now, enc_up_now, cross_kv_now, dec_up_now, enc_cot, dec_cot, running, enc_gains, dec_gains = later
    w_dec_self = jnp.concatenate([rows_of(dec_qkv_now), rows_of(dec_proj)])
    ints, w_dec_self, embedding = flow.step((ints, w_dec_self, embedding()))
    ints = jnp.where(at.stays, ints, flow.results["ints"])
    runs = jnp.transpose(jnp.pad(ints[4:].astype(F32), ((0, 126), (0, 0))))
    lane = jnp.arange(128, dtype=jnp.int32) % DH
    source_hot, target_hot = (ints[:4].reshape(2, 2 * n, 1) == lane).astype(BF)

    w_enc = jnp.concatenate([rows_of(enc_proj), rows_of(enc_up_now), rows_of(enc_down)])
    w_cross = jnp.concatenate([rows_of(cross_query), rows_of(cross_kv_now)])
    w_dec = jnp.concatenate([rows_of(cross_proj), rows_of(dec_up_now), rows_of(dec_down)])
    cots = jnp.concatenate([enc_cot[:, 0].astype(BF), dec_cot[:, 0].astype(BF)], axis=1)
    pad = jnp.zeros((3, D), F32)
    small_enc = jnp.stack(
        [enc_gains[0], enc_shifts[0], enc_gains[1], enc_shifts[1], halt_weight[0]]
    )
    small_enc = jnp.concatenate([small_enc, pad])
    small_dec = jnp.stack(
        [dec_gains[0], dec_shifts[0], dec_gains[1], dec_shifts[1], dec_gains[2], dec_shifts[2], halt_weight[1]]
    )
    small_dec = jnp.concatenate([small_dec, pad[:1]])

    flow.add("w_dec_self", gathered(at, w_dec_self, 2, 1))
    flow.add("target", moved(at, target_rows[:, 0], 3))
    tables = embedding, source_hot, target_hot, w_enc, cots
    embedding, source_hot, target_hot, w_enc, cots = flow.step(tables)
    (embedding,) = flow.step((embedding,))

    def pre(rows, got, own, other):
        return rows_call(
            pre_kernel, "project", at.core, [rows, got, embedding], [own, *other],
            [row, half_low, half_low, kv_low, kv_low], scratch=[(own.shape, BF)],
        )

    def attend(q, kv, got, hot, key_hot, causal=False):
        o, log = heads_forward(at.core, q, kv, got, hot, key_hot, causal)
        return o, (q, kv, got, hot, key_hot, o, log)

    def attend_back(kept, grad, causal=False):
        return heads_backward(at.core, kept, grad, causal)

    w_enc_qkv_got = flow.results["w_enc_qkv"]
    enc_start, q0, q1, kv0, kv1 = pre(source_rows[:, 0], flow.results["source"], w_enc_qkv, w_enc_qkv_got)
    got0, got1 = at.core_swap(kv0), at.core_swap(kv1)
    enc_o0, enc_kept0 = attend(q0, kv0, got0, source_hot, source_hot)
    flow.add("w_enc", gathered(at, w_enc, 2, 1))
    enc_o0, q1, kv1, got1, w_cross = flow.step((enc_o0, q1, kv1, got1, w_cross))
    enc_o1, enc_kept1 = attend(q1, kv1, got1, source_hot, source_hot)
    (enc_o1,) = flow.step((enc_o1,))

    w_dec_self_got = flow.results["w_dec_self"]
    dec_start, q0, q1, kv0, kv1 = pre(target_rows[:, 0], flow.results["target"], w_dec_self, w_dec_self_got)
    got0, got1 = at.core_swap(kv0), at.core_swap(kv1)
    self_o0, self_kept0 = attend(q0, kv0, got0, target_hot, target_hot, True)
    flow.add("w_cross", gathered(at, w_cross))
    self_o0, q1, kv1, got1 = flow.step((self_o0, q1, kv1, got1))
    self_o1, self_kept1 = attend(q1, kv1, got1, target_hot, target_hot, True)
    flow.add("w_dec", gathered(at, w_dec, 3, 1))
    self_o1, enc_o1 = flow.step((self_o1, enc_o1))
    w_enc_got = flow.results["w_enc"]
    enc_sum_one, enc_sum_two, enc_states = rows_call(
        enc_post_kernel, "encoder_feed", at.core, [enc_o0, enc_o1, enc_start, runs],
        [w_enc, *w_enc_got, small_enc], [row, row, row_low], scratch=[(w_enc.shape, BF)],
    )
    flow.add("cots", moved(at, cots, 3))
    (enc_states,) = flow.step((enc_states,))
    w_cross_got = flow.results["w_cross"]
    self_proj = [(w_dec_self, HALF, 3)] + [(w, HALF, 1) for w in w_dec_self_got]
    dec_sum_one, q0, q1, kv0, kv1 = rows_call(
        dec_mid_kernel, "cross_project", at.core, [self_o0, self_o1, dec_start, enc_states],
        [*self_proj, w_cross, *w_cross_got, small_dec],
        [row, half_low, half_low, kv_low, kv_low], scratch=[(w_cross.shape, BF)],
    )
    got0, got1 = at.core_swap(kv0), at.core_swap(kv1)
    q0, q1, kv0, kv1 = flow.step((q0, q1, kv0, kv1))
    cross_o0, cross_kept0 = attend(q0, kv0, got0, target_hot, source_hot)
    cross_o0, q1, kv1, got1 = flow.step((cross_o0, q1, kv1, got1))
    cross_o1, cross_kept1 = attend(q1, kv1, got1, target_hot, source_hot)
    flow.add("enc_states", moved(at, enc_states, 1))
    (cross_o1,) = flow.step((cross_o1,))
    cots = jnp.where(at.stays, cots, flow.results["cots"])
    enc_cot, dec_cot = cots[:, :D], cots[:, D:]

    def grad_outs(rows):
        return [((2, rows // 2, D), BF)] * 2 + [((8, D), F32)]

    def grad_scratch(rows):
        return [((2, rows, D), F32), ((8, D), F32)]

    w_dec_got = flow.results["w_dec"]
    (
        dec_states, start_grad, sum_grad, o0_grad, o1_grad, *dec_parts, small_two,
    ) = rows_call(
        dec_post_kernel, "decoder_feed", at.core,
        [cross_o0, cross_o1, dec_sum_one, dec_start, runs, dec_cot], [w_dec, *w_dec_got, small_dec],
        [row_low, row, row, half_low, half_low], grad_outs(9 * HALF),
        [*grad_scratch(9 * HALF), (w_dec.shape, BF), ((2, 512, 4 * D), BF)],
    )
    flow.add("dec", summed(at, *dec_parts))
    flow.add("dec_states", moved(at, dec_states, 1))
    o0_grad, o1_grad = flow.step((o0_grad, o1_grad))

    q0_grad, kv0_grad, kv0_send = attend_back(cross_kept0, o0_grad)
    q0_grad, kv0_grad, kv0_send, o1_grad = flow.step((q0_grad, kv0_grad, kv0_send, o1_grad))
    kv0_got = at.core_swap(kv0_send)
    q1_grad, kv1_grad, kv1_send = attend_back(cross_kept1, o1_grad)
    q1_grad, kv1_grad, kv1_send, kv0_got = flow.step((q1_grad, kv1_grad, kv1_send, kv0_got))
    kv1_got = at.core_swap(kv1_send)

    (
        enc_base, enc_o0_grad, enc_o1_grad, *enc_parts, small_enc_grad,
    ) = rows_call(
        enc_back_kernel, "encoder_feed_back", at.core,
        [kv0_grad, kv1_grad, kv0_got, kv1_got, enc_states, enc_cot, enc_start, enc_sum_one, enc_sum_two,
         enc_o0, enc_o1, runs],
        [w_cross, *w_cross_got, w_enc, *w_enc_got, small_enc],
        [row, half_low, half_low], grad_outs(11 * HALF),
        [*grad_scratch(11 * HALF), (w_cross.shape, BF), (w_enc.shape, BF)],
    )
    flow.add("enc", summed(at, *enc_parts, (1, 1, 2)))
    enc_o0_grad, enc_o1_grad, q0_grad = flow.step((enc_o0_grad, enc_o1_grad, q0_grad))
    (
        dec_base, self_o0_grad, self_o1_grad, *mid_parts, small_one,
    ) = rows_call(
        dec_mid_back_kernel, "cross_project_back", at.core,
        [q0_grad, q1_grad, sum_grad, dec_sum_one, start_grad, self_o0, self_o1],
        [(w_cross, HALF, 0), *w_cross_got, *self_proj, small_dec],
        [row, half_low, half_low], grad_outs(2 * HALF), grad_scratch(2 * HALF),
    )
    smalls = jnp.concatenate([small_enc_grad, small_one, small_two, jnp.zeros((8, D), F32)])
    enc_o1_grad, mid_parts, smalls = flow.step((enc_o1_grad, mid_parts, smalls))

    q1_grad, kv1_grad, kv1_send = attend_back(enc_kept1, enc_o1_grad)
    q1_grad, kv1_grad, kv1_send, enc_o0_grad = flow.step((q1_grad, kv1_grad, kv1_send, enc_o0_grad))
    kv1_got = at.core_swap(kv1_send)
    q0_grad, kv0_grad, kv0_send = attend_back(enc_kept0, enc_o0_grad)
    q0_grad, kv0_grad, kv0_send, kv1_got = flow.step((q0_grad, kv0_grad, kv0_send, kv1_got))
    kv0_got = at.core_swap(kv0_send)
    source_grad, source_low, keep, send = rows_call(
        both_qkv_back_kernel, "project_back", at.core,
        [q0_grad, kv0_grad, kv0_got, q1_grad, kv1_grad, kv1_got, enc_start, enc_base],
        [w_enc_qkv, *w_enc_qkv_got, *mid_parts, smalls], [row, row_low], [((2, 3 * HALF, D), BF)] * 2,
        [((2, 3 * HALF, D), F32), (w_enc_qkv.shape, BF)],
    )
    flow.add("enc_qkv", summed(at, keep, send))
    flow.add("source_grad", moved(at, source_low, 1))
    self_o1_grad, source_grad = flow.step((self_o1_grad, source_grad))

    def heads_back(kept, grad):
        q_grad, kv_grad, kv_send = attend_back(kept, grad, True)
        q_grad, kv_grad, kv_send = flow.step((q_grad, kv_grad, kv_send))
        return q_grad, kv_grad, at.core_swap(kv_send)

    parts = heads_back(self_kept1, self_o1_grad)
    part_outs = [((1, 3 * HALF // 2, D), BF)] * 2
    part_scratch = [((1, 3 * HALF, D), F32)]
    target_grad, _, keep1, send1 = rows_call(
        other_qkv_back_kernel, "project_back", at.core, [*parts, dec_start, dec_base],
        [*w_dec_self_got], [row, row_low], part_outs, [*part_scratch, (w_dec_self.shape, BF)],
    )
    flow.add("dec_qkv_other", summed_other(at, keep1, at.core_swap(send1), 1))
    target_grad, self_o0_grad = flow.step((target_grad, self_o0_grad))
    parts = heads_back(self_kept0, self_o0_grad)
    target_grad, target_low, keep0, send0 = rows_call(
        own_qkv_back_kernel, "project_back", at.core, [*parts, dec_start, target_grad],
        [(w_dec_self, 3 * HALF, 0)], [row, row_low], part_outs, part_scratch,
    )
    flow.add("dec_qkv", summed_own(at, keep0, send0, flow.results["dec_qkv_other"]))
    flow.add("target_grad", moved(at, target_low, 2))

    done = flow.results

    def weights(name, *weights):
        places, begin = [], 0
        for i, weight in enumerate(weights):
            places.append((i, begin, 0, weight.size // D))
            begin += weight.size // D
        return unpack(at.order, *done[name], [w.shape for w in weights], places)

    def home(values, name):
        values = jnp.where(at.stays, values, done[name].astype(values.dtype))[:, None]
        return with_layout_constraint(values, Layout((0, 1, 2))) if values.dtype == F32 else values

    def mixed_weights(name):
        part, more = 3 * HALF // 2, HALF // 2
        places = []
        for c in range(2):
            begin = c * 3 * HALF
            places += [(0, begin, c * part, part), (1 + c, begin + part, 0, 2 * more)]
        after = part + 2 * more
        one, two = after + 8, 3 * HALF + after
        for out, rows in (
            (3, (after, after + 2)),
            (4, (after + 1, after + 3)),
            (5, (one, two, two + 2)),
            (6, (one + 1, two + 1, two + 3)),
            (7, (after + 4, two + 4)),
        ):
            places += [(out, row, at_row, 1) for at_row, row in enumerate(rows)]
        shapes = [enc_qkv.shape, cross_query.shape, dec_proj.shape, (2, D), (2, D), (3, D), (3, D), (2, D)]
        return unpack(at.order, *done[name], shapes, places)

    target_grad, done["dec"] = flow.step((target_grad, done["dec"]))
    dec_grads = weights("dec", cross_proj, dec_up, dec_down)
    dec_grads, source_grad = flow.step((dec_grads, source_grad))
    source_out = home(source_grad, "source_grad")
    (source_out,) = flow.step((source_out,))
    enc_grads = weights("enc", cross_kv, enc_proj, enc_up, enc_down)
    enc_grads, enc_states, dec_states = flow.step((enc_grads, enc_states, dec_states))
    states_out = home(enc_states, "enc_states"), home(dec_states, "dec_states")
    states_out, target_grad = flow.step((states_out, target_grad))
    target_out = home(target_grad, "target_grad")
    (target_out,) = flow.step((target_out,))
    (target_out,) = flow.step((target_out,))
    mixed_grads = mixed_weights("enc_qkv")
    (mixed_grads,) = flow.step((mixed_grads,))
    flow.finish()
    cross_proj_grad, dec_up_grad, dec_down_grad = dec_grads
    cross_kv_grad, enc_proj_grad, enc_up_grad, enc_down_grad = enc_grads
    enc_qkv_grad, cross_query_grad, dec_proj_grad, *small_grads = mixed_grads
    (dec_qkv_grad,) = weights("dec_qkv", dec_qkv)
    enc_gains_grad, enc_shifts_grad, dec_gains_grad, dec_shifts_grad, halt_grad = small_grads
    return (
        *states_out,
        source_out,
        target_out,
        enc_qkv_grad,
        enc_proj_grad,
        enc_up_grad,
        enc_down_grad,
        enc_gains_grad,
        enc_shifts_grad,
        dec_qkv_grad,
        dec_proj_grad,
        cross_query_grad,
        cross_kv_grad,
        cross_proj_grad,
        dec_up_grad,
        dec_down_grad,
        dec_gains_grad,
        dec_shifts_grad,
        halt_grad,
    )


def solution(mesh):
    dp_size, mp_size = mesh.shape["dp"], mesh.shape["mp"]
    by_chip = mp_size == 2 and dp_size in (4, 8, 16)
    body = partial(chip_rows, dp_size=dp_size) if by_chip else local
    return jax.shard_map(
        body,
        mesh=mesh,
        in_specs=(
            P("mp", "dp", None),
            P("mp", "dp", None),
            P("dp", None),
            P("dp", None),
            P(None, "dp", "mp"),
            P(None, None, "mp"),
            P("mp", None),
            P(None, "mp"),
            P("mp", None),
            P(),
            P(),
            P(None, None, "mp"),
            P("mp", None),
            P(None, "mp"),
            P(None, None, "mp"),
            P("mp", None),
            P(None, "mp"),
            P("mp", None),
            P(),
            P(),
            P(),
            P("mp", "dp", None),
            P("mp", "dp", None),
        ),
        out_specs=(
            P("mp", "dp", None),
            P("mp", "dp", None),
            P("mp", "dp", None),
            P("mp", "dp", None),
            P(None, None, "mp"),
            P("mp", None),
            P(None, "mp"),
            P("mp", None),
            P(),
            P(),
            P(None, None, "mp"),
            P("mp", None),
            P(None, "mp"),
            P(None, None, "mp"),
            P("mp", None),
            P(None, "mp"),
            P("mp", None),
            P(),
            P(),
            P(),
        ),
        check_vma=False,
    )
```

```python
import math
from functools import partial

import jax
import jax.numpy as jnp
from jax import lax
from jax.experimental import pallas as pl
from jax.experimental.layout import Layout, with_layout_constraint
from jax.experimental.pallas import tpu as pltpu
from jax.sharding import PartitionSpec as P

D = 512
DH = 64


EPS = 1e-05
NEGATIVE = -1000000000.0


def signal(position):
    half_width = D // 2
    inverse_rates = jnp.exp(
        jnp.arange(half_width, dtype=jnp.float32) * (-jnp.log(10000.0) / (half_width - 1))
    )
    angles = position[:, None] * inverse_rates[None, :]
    return jnp.concatenate([jnp.sin(angles), jnp.cos(angles)], axis=1)


def normalize(values, norm_gain, norm_shift):
    centred = values - jnp.mean(values, axis=-1, keepdims=True)
    spread = jnp.mean(centred * centred, axis=-1, keepdims=True)
    return centred * lax.rsqrt(spread + EPS) * norm_gain + norm_shift


def halting(running_now, initial, updated, weight):
    halt_prob = jax.nn.sigmoid(jnp.sum(updated * weight, axis=-1, keepdims=True))
    return initial + running_now * halt_prob * (updated - initial)


def dot_last(left, right):
    return lax.dot_general(
        left, right, (((left.ndim - 1,), (1,)), ((), ())), preferred_element_type=jnp.float32
    )


def collect(piece_rows):
    return lax.all_gather(piece_rows, "mp", axis=0, tiled=True)


def collect_grad(piece_rows):
    return lax.all_gather(piece_rows.astype(jnp.bfloat16), "mp", axis=0, tiled=True)


def project_out(hidden, weight, rows):

    def partial_term(begin_row, row_count):
        return jnp.dot(hidden, weight, preferred_element_type=jnp.float32)

    return lax.psum_scatter(
        partial_term(jnp.int32(0), lax.axis_size("mp") * rows).astype(jnp.bfloat16),
        "mp",
        scatter_dimension=0,
        tiled=True,
    ).astype(jnp.float32)


def project_back(gradients, matrices, rows):

    def partial_term(begin_row, row_count):
        summed = jnp.zeros(
            (row_count,) + gradients[0].shape[1:-1] + (matrices[0].shape[0],), jnp.float32
        )
        for gradient, matrix in zip(gradients, matrices):
            summed = summed + dot_last(gradient, matrix)
        return summed

    return lax.psum_scatter(
        partial_term(jnp.int32(0), lax.axis_size("mp") * rows).astype(jnp.bfloat16),
        "mp",
        scatter_dimension=0,
        tiled=True,
    ).astype(jnp.float32)


def to_pairs(values):
    length, row_count, width = values.shape
    return (
        values.reshape(length, row_count, width // DH, DH)
        .transpose(1, 2, 0, 3)
        .reshape(-1, length, DH)
    )


def from_pairs(values, row_count):
    pairs, length, unused = values.shape
    heads_here = pairs // row_count
    return (
        values.reshape(row_count, heads_here, length, DH)
        .transpose(2, 0, 1, 3)
        .reshape(length, row_count, heads_here * DH)
    )


def per_pair(segments, width):
    return jnp.repeat(segments, width // DH, axis=0)


def pair_scores(query_block, key_rows, segment_block, segment_keys, first_row, causal):
    scores = lax.dot_general(
        query_block, key_rows, (((1,), (1,)), ((), ())), preferred_element_type=jnp.float32
    )
    scores = scores * DH ** (-0.5)
    allowed = segment_block[:, None] == segment_keys[None, :]
    if causal:
        query_place = first_row + jnp.arange(query_block.shape[0], dtype=jnp.int32)
        key_place = jnp.arange(key_rows.shape[0], dtype=jnp.int32)
        allowed = allowed & (key_place[None, :] <= query_place[:, None])
    return jnp.where(allowed, scores, NEGATIVE)


def attend_pair(inputs, causal):
    query_rows, key_rows, value_rows, segment_query, segment_keys = inputs
    length = query_rows.shape[0]
    block_rows = min(512, length)
    blocks = length // block_rows
    firsts = jnp.arange(blocks, dtype=jnp.int32) * block_rows

    def one_block(pieces):
        query_block, segment_block, first_row = pieces
        scores = pair_scores(query_block, key_rows, segment_block, segment_keys, first_row, causal)
        highest = jnp.max(scores, axis=1, keepdims=True)
        exponent = jnp.exp(scores - highest)
        totals = jnp.sum(exponent, axis=1, keepdims=True)
        weights = (exponent / totals).astype(jnp.bfloat16)
        mixed = jnp.dot(weights, value_rows, preferred_element_type=jnp.float32)
        return (mixed.astype(jnp.bfloat16), (highest + jnp.log(totals))[:, 0])

    mixed, log_total = lax.map(
        one_block,
        (
            query_rows.reshape(blocks, block_rows, -1),
            segment_query.reshape(blocks, block_rows),
            firsts,
        ),
    )
    return (mixed.reshape(length, -1), log_total.reshape(length))


def attend_pair_back(inputs, causal):
    query_rows, key_rows, value_rows, mixed_grad, log_total, segment_query, segment_keys = inputs
    length = query_rows.shape[0]
    block_rows = min(512, length)
    blocks = length // block_rows
    firsts = jnp.arange(blocks, dtype=jnp.int32) * block_rows

    def one_block(carry, pieces):
        key_total, value_total = carry
        query_block, grad_block, log_block, segment_block, first_row = pieces
        scores = pair_scores(query_block, key_rows, segment_block, segment_keys, first_row, causal)
        probs = jnp.exp(scores - log_block[:, None])
        weights = probs.astype(jnp.bfloat16)
        prob_grad = lax.dot_general(
            grad_block, value_rows, (((1,), (1,)), ((), ())), preferred_element_type=jnp.float32
        )
        inner = jnp.sum(probs * prob_grad, axis=1, keepdims=True)
        score_grad = (probs * (prob_grad - inner)).astype(jnp.bfloat16)
        query_grad = jnp.dot(score_grad, key_rows, preferred_element_type=jnp.float32) * DH ** (
            -0.5
        )
        key_total = key_total + lax.dot_general(
            score_grad, query_block, (((0,), (0,)), ((), ())), preferred_element_type=jnp.float32
        ) * DH ** (-0.5)
        value_total = value_total + lax.dot_general(
            weights, grad_block, (((0,), (0,)), ((), ())), preferred_element_type=jnp.float32
        )
        return ((key_total, value_total), query_grad.astype(jnp.bfloat16))

    zeros_start = jnp.zeros(key_rows.shape, jnp.float32)
    (key_total, value_total), query_grad = lax.scan(
        one_block,
        (zeros_start, zeros_start),
        (
            query_rows.reshape(blocks, block_rows, -1),
            mixed_grad.reshape(blocks, block_rows, -1),
            log_total.reshape(blocks, block_rows),
            segment_query.reshape(blocks, block_rows),
            firsts,
        ),
    )
    return (
        query_grad.reshape(length, -1),
        key_total.astype(jnp.bfloat16),
        value_total.astype(jnp.bfloat16),
    )


def attention_forward(
    query_full,
    key_full,
    weight_query,
    weight_key,
    weight_value,
    weight_out,
    segment_query,
    segment_keys,
    causal,
    rows,
):
    queries = jnp.dot(query_full, weight_query, preferred_element_type=jnp.float32).astype(
        jnp.bfloat16
    )
    keys_low = jnp.dot(key_full, weight_key, preferred_element_type=jnp.float32).astype(
        jnp.bfloat16
    )
    values_low = jnp.dot(key_full, weight_value, preferred_element_type=jnp.float32).astype(
        jnp.bfloat16
    )
    width = queries.shape[2]
    row_count = queries.shape[1]
    mixed, log_total = lax.map(
        partial(attend_pair, causal=causal),
        (
            to_pairs(queries),
            to_pairs(keys_low),
            to_pairs(values_low),
            per_pair(segment_query, width),
            per_pair(segment_keys, width),
        ),
    )
    mixed = from_pairs(mixed, row_count)
    branch = project_out(mixed, weight_out, rows)
    return (branch, (queries, keys_low, values_low, mixed, log_total))


def attention_backward(
    branch_grad, kept, query_full, key_full, weight_out, segment_query, segment_keys, causal
):
    queries, keys_low, values_low, kept_mixed, log_total = kept
    grad_full = collect_grad(branch_grad)
    out_weight_grad = jnp.einsum(
        "lrc,lrd->cd", kept_mixed, grad_full, preferred_element_type=jnp.float32
    )
    mixed_grad = dot_last(grad_full, weight_out).astype(jnp.bfloat16)
    width = queries.shape[2]
    row_count = queries.shape[1]
    query_grad, key_grad, value_grad = lax.map(
        partial(attend_pair_back, causal=causal),
        (
            to_pairs(queries),
            to_pairs(keys_low),
            to_pairs(values_low),
            to_pairs(mixed_grad),
            log_total,
            per_pair(segment_query, width),
            per_pair(segment_keys, width),
        ),
    )
    query_grad = from_pairs(query_grad, row_count)
    key_grad = from_pairs(key_grad, row_count)
    value_grad = from_pairs(value_grad, row_count)
    weight_grads = (
        jnp.einsum("lrd,lrc->dc", query_full, query_grad, preferred_element_type=jnp.float32),
        jnp.einsum("lrd,lrc->dc", key_full, key_grad, preferred_element_type=jnp.float32),
        jnp.einsum("lrd,lrc->dc", key_full, value_grad, preferred_element_type=jnp.float32),
    )
    return (query_grad, key_grad, value_grad, weight_grads, out_weight_grad)


def feed_forward(source_full, weight_up, weight_down, rows):
    hidden = jnp.dot(source_full, weight_up, preferred_element_type=jnp.float32)
    active = jax.nn.gelu(hidden).astype(jnp.bfloat16)
    return (project_out(active, weight_down, rows), hidden)


def feed_backward(branch_grad, source_full, hidden, weight_up, weight_down, rows):
    grad_full = collect_grad(branch_grad)
    active, gelu_back = jax.vjp(jax.nn.gelu, hidden)
    active = active.astype(jnp.bfloat16)
    down_grad = jnp.einsum("lrf,lrd->fd", active, grad_full, preferred_element_type=jnp.float32)
    hidden_grad = gelu_back(dot_last(grad_full, weight_down))[0].astype(jnp.bfloat16)
    up_grad = jnp.einsum(
        "lrd,lrf->df", source_full, hidden_grad, preferred_element_type=jnp.float32
    )
    input_grad = project_back((hidden_grad,), (weight_up,), rows)
    return (input_grad, up_grad, down_grad)


def local(
    source_rows,
    target_rows,
    source_segment,
    target_segment,
    running,
    enc_qkv,
    enc_proj,
    enc_up,
    enc_down,
    enc_gains,
    enc_shifts,
    dec_qkv,
    dec_proj,
    cross_query,
    cross_kv,
    cross_proj,
    dec_up,
    dec_down,
    dec_gains,
    dec_shifts,
    halt_weight,
    enc_cotangent,
    dec_cotangent,
):
    rows = source_rows.shape[0]
    position = (lax.axis_index("mp") * rows + jnp.arange(rows, dtype=jnp.int32)).astype(jnp.float32)
    embedding = (signal(position) + signal(jnp.ones((1,), jnp.float32)))[:, None, :]
    runs_now = jnp.transpose(running, (0, 2, 1)).astype(jnp.float32)[..., None]
    enc_start = source_rows.astype(jnp.float32) + embedding
    enc_start_low = enc_start.astype(jnp.bfloat16)
    enc_start_full = collect(enc_start_low)
    enc_attn, enc_attn_kept = attention_forward(
        enc_start_full,
        enc_start_full,
        enc_qkv[0],
        enc_qkv[1],
        enc_qkv[2],
        enc_proj,
        source_segment,
        source_segment,
        False,
        rows,
    )
    enc_sum_one = enc_start + enc_attn
    enc_middle = normalize(enc_sum_one, enc_gains[0], enc_shifts[0])
    enc_middle_low = enc_middle.astype(jnp.bfloat16)
    enc_middle_full = collect(enc_middle_low)
    enc_ffn, enc_hidden = feed_forward(enc_middle_full, enc_up, enc_down, rows)
    enc_sum_two = enc_middle + enc_ffn
    enc_last = normalize(enc_sum_two, enc_gains[1], enc_shifts[1])
    enc_final = halting(runs_now[0], enc_start, enc_last, halt_weight[0])
    enc_states = enc_final.astype(jnp.bfloat16)
    enc_states_full = collect(enc_states)
    dec_start = target_rows.astype(jnp.float32) + embedding
    dec_start_low = dec_start.astype(jnp.bfloat16)
    dec_start_full = collect(dec_start_low)
    dec_self, dec_self_kept = attention_forward(
        dec_start_full,
        dec_start_full,
        dec_qkv[0],
        dec_qkv[1],
        dec_qkv[2],
        dec_proj,
        target_segment,
        target_segment,
        True,
        rows,
    )
    dec_sum_one = dec_start + dec_self
    dec_middle = normalize(dec_sum_one, dec_gains[0], dec_shifts[0])
    dec_middle_low = dec_middle.astype(jnp.bfloat16)
    dec_middle_full = collect(dec_middle_low)
    dec_cross, dec_cross_kept = attention_forward(
        dec_middle_full,
        enc_states_full,
        cross_query,
        cross_kv[0],
        cross_kv[1],
        cross_proj,
        target_segment,
        source_segment,
        False,
        rows,
    )
    dec_sum_two = dec_middle + dec_cross
    dec_mixed = normalize(dec_sum_two, dec_gains[1], dec_shifts[1])
    dec_mixed_low = dec_mixed.astype(jnp.bfloat16)
    dec_mixed_full = collect(dec_mixed_low)
    dec_ffn, dec_hidden = feed_forward(dec_mixed_full, dec_up, dec_down, rows)
    dec_sum_three = dec_mixed + dec_ffn
    dec_last = normalize(dec_sum_three, dec_gains[2], dec_shifts[2])
    dec_final = halting(runs_now[1], dec_start, dec_last, halt_weight[1])
    dec_states = dec_final.astype(jnp.bfloat16)
    unused, halt_back = jax.vjp(partial(halting, runs_now[1]), dec_start, dec_last, halt_weight[1])
    dec_start_grad, last_grad, dec_halt_grad = halt_back(dec_cotangent)
    unused, norm_back = jax.vjp(normalize, dec_sum_three, dec_gains[2], dec_shifts[2])
    sum_grad, dec_gain_three, dec_shift_three = norm_back(last_grad)
    ffn_input_grad, dec_up_grad, dec_down_grad = feed_backward(
        sum_grad, dec_mixed_full, dec_hidden, dec_up, dec_down, rows
    )
    mixed_grad = sum_grad + ffn_input_grad
    unused, norm_back = jax.vjp(normalize, dec_sum_two, dec_gains[1], dec_shifts[1])
    sum_grad, dec_gain_two, dec_shift_two = norm_back(mixed_grad)
    query_grad, key_grad, value_grad, cross_grads, cross_proj_grad = attention_backward(
        sum_grad,
        dec_cross_kept,
        dec_middle_full,
        enc_states_full,
        cross_proj,
        target_segment,
        source_segment,
        False,
    )
    middle_grad = sum_grad + project_back((query_grad,), (cross_query,), rows)
    enc_extra = project_back((key_grad, value_grad), (cross_kv[0], cross_kv[1]), rows)
    unused, norm_back = jax.vjp(normalize, dec_sum_one, dec_gains[0], dec_shifts[0])
    sum_grad, dec_gain_one, dec_shift_one = norm_back(middle_grad)
    query_grad, key_grad, value_grad, self_grads, dec_proj_grad = attention_backward(
        sum_grad,
        dec_self_kept,
        dec_start_full,
        dec_start_full,
        dec_proj,
        target_segment,
        target_segment,
        True,
    )
    target_grad = (
        sum_grad
        + dec_start_grad
        + project_back(
            (query_grad, key_grad, value_grad), (dec_qkv[0], dec_qkv[1], dec_qkv[2]), rows
        )
    )
    dec_qkv_grad = jnp.stack(self_grads)
    cross_query_grad = cross_grads[0]
    cross_kv_grad = jnp.stack([cross_grads[1], cross_grads[2]])
    enc_final_grad = enc_cotangent + enc_extra
    unused, halt_back = jax.vjp(partial(halting, runs_now[0]), enc_start, enc_last, halt_weight[0])
    enc_start_grad, last_grad, enc_halt_grad = halt_back(enc_final_grad)
    unused, norm_back = jax.vjp(normalize, enc_sum_two, enc_gains[1], enc_shifts[1])
    sum_grad, enc_gain_two, enc_shift_two = norm_back(last_grad)
    ffn_input_grad, enc_up_grad, enc_down_grad = feed_backward(
        sum_grad, enc_middle_full, enc_hidden, enc_up, enc_down, rows
    )
    middle_grad = sum_grad + ffn_input_grad
    unused, norm_back = jax.vjp(normalize, enc_sum_one, enc_gains[0], enc_shifts[0])
    sum_grad, enc_gain_one, enc_shift_one = norm_back(middle_grad)
    query_grad, key_grad, value_grad, self_grads, enc_proj_grad = attention_backward(
        sum_grad,
        enc_attn_kept,
        enc_start_full,
        enc_start_full,
        enc_proj,
        source_segment,
        source_segment,
        False,
    )
    source_grad = (
        sum_grad
        + enc_start_grad
        + project_back(
            (query_grad, key_grad, value_grad), (enc_qkv[0], enc_qkv[1], enc_qkv[2]), rows
        )
    )
    enc_qkv_grad = jnp.stack(self_grads)
    (
        enc_qkv_grad,
        enc_proj_grad,
        enc_up_grad,
        enc_down_grad,
        dec_qkv_grad,
        dec_proj_grad,
        cross_query_grad,
        cross_kv_grad,
        cross_proj_grad,
        dec_up_grad,
        dec_down_grad,
    ) = (
        lax.psum(enc_qkv_grad.astype(jnp.bfloat16), "dp").astype(jnp.float32),
        lax.psum(enc_proj_grad.astype(jnp.bfloat16), "dp").astype(jnp.float32),
        lax.psum(enc_up_grad.astype(jnp.bfloat16), "dp").astype(jnp.float32),
        lax.psum(enc_down_grad.astype(jnp.bfloat16), "dp").astype(jnp.float32),
        lax.psum(dec_qkv_grad.astype(jnp.bfloat16), "dp").astype(jnp.float32),
        lax.psum(dec_proj_grad.astype(jnp.bfloat16), "dp").astype(jnp.float32),
        lax.psum(cross_query_grad.astype(jnp.bfloat16), "dp").astype(jnp.float32),
        lax.psum(cross_kv_grad.astype(jnp.bfloat16), "dp").astype(jnp.float32),
        lax.psum(cross_proj_grad.astype(jnp.bfloat16), "dp").astype(jnp.float32),
        lax.psum(dec_up_grad.astype(jnp.bfloat16), "dp").astype(jnp.float32),
        lax.psum(dec_down_grad.astype(jnp.bfloat16), "dp").astype(jnp.float32),
    )
    enc_gains_grad, enc_shifts_grad, dec_gains_grad, dec_shifts_grad, halt_weight_grad = lax.psum(
        (
            jnp.stack([enc_gain_one, enc_gain_two]),
            jnp.stack([enc_shift_one, enc_shift_two]),
            jnp.stack([dec_gain_one, dec_gain_two, dec_gain_three]),
            jnp.stack([dec_shift_one, dec_shift_two, dec_shift_three]),
            jnp.stack([enc_halt_grad, dec_halt_grad]),
        ),
        ("dp", "mp"),
    )
    return (
        enc_states,
        dec_states,
        source_grad,
        target_grad,
        enc_qkv_grad,
        enc_proj_grad,
        enc_up_grad,
        enc_down_grad,
        enc_gains_grad,
        enc_shifts_grad,
        dec_qkv_grad,
        dec_proj_grad,
        cross_query_grad,
        cross_kv_grad,
        cross_proj_grad,
        dec_up_grad,
        dec_down_grad,
        dec_gains_grad,
        dec_shifts_grad,
        halt_weight_grad,
    )


BIG = -1e30
BF = jnp.bfloat16
F32 = jnp.float32
NN = (((1,), (0,)), ((), ()))
NT = (((1,), (1,)), ((), ()))
TN = (((0,), (0,)), ((), ()))
HALF = D // 2
VMEM_BYTES = 56 * 1024 * 1024
COST = pl.CostEstimate(flops=1, bytes_accessed=1, transcendentals=0)


def dot_nn(a, b):
    return lax.dot_general(a, b, NN, preferred_element_type=F32)


def dot_nt(a, b):
    return lax.dot_general(a, b, NT, preferred_element_type=F32)


def dot_tn(a, b):
    return lax.dot_general(a, b, TN, preferred_element_type=F32)


def lanes():
    lane = lax.broadcasted_iota(jnp.int32, (1, 128), 1)
    return lane < DH, lane % DH


def in_hbm(arrays):
    return [pltpu.with_memory_space_constraint(a, pltpu.HBM) for a in arrays]


def pipelined(tasks, scores_of, after):
    ahead = scores_of(*tasks[0])
    for i, task in enumerate(tasks):
        now = ahead
        if i + 1 < len(tasks):
            ahead = scores_of(*tasks[i + 1])
        after(now, *task)


def forward_kernel(
    core_ref, q_ref, own_ref, got_ref, hot_ref, key_hot_ref, o_ref, log_ref, keys, values, *, causal
):
    n = q_ref.shape[0]
    chunk = n // 2
    core = core_ref[0]
    left, lane = lanes()
    for ref, of in ((own_ref, core), (got_ref, 1 - core)):
        here = pl.ds(pl.multiple_of(of * n, n), n)
        k, hot = ref[0], key_hot_ref[here, :]
        ext = jnp.where((lane >= 8) & (lane < 11), jnp.ones_like(hot), hot)
        keys[0, here, :] = jnp.where(left, k, ext)
        keys[1, here, :] = jnp.where(left, ext, k)
        turned = ref[1].T
        ones = jnp.ones((DH, n), BF)
        values[0, :, here] = jnp.concatenate([turned[:DH], ones])
        values[1, :, here] = jnp.concatenate([ones, turned[DH:]])
    pair = q_ref[...]
    mine = hot_ref[pl.ds(pl.multiple_of(core * n, n), n), :].astype(F32)
    ext = jnp.where(lane < 8, (1.0 - mine) * BIG, 0.0).astype(BF)
    queries = jnp.where(left, pair, ext), jnp.where(left, ext, pair)

    def run(tasks, rows):
        state = {}

        def scores_of(head, query, key, cut):
            q = queries[head][query * rows : (query + 1) * rows]
            scores = dot_nt(keys[head, key * chunk : (key + 1) * chunk, :], q)
            if cut:
                at = lax.broadcasted_iota(jnp.int32, scores.shape, 0)
                to = lax.broadcasted_iota(jnp.int32, scores.shape, 1)
                scores = jnp.where(at <= to, scores, BIG)
            return scores

        def after(scores, head, query, key, cut):
            top = jnp.max(scores, axis=0, keepdims=True)
            total = 0.0
            if (head, query) in state:
                old_top, total = state[head, query]
                top = jnp.maximum(top, old_top)
                total = total * jnp.exp2(old_top - top)
            probs = jnp.exp2(scores - top).astype(BF)
            total = total + dot_nn(values[head, :, key * chunk : (key + 1) * chunk], probs)
            state[head, query] = top, total

        pipelined(tasks, scores_of, after)
        for query in range(n // rows):
            (top0, total0), (top1, total1) = state[0, query], state[1, query]
            out = jnp.concatenate([total0[:DH] / total0[DH:], total1[DH:] / total1[:DH]])
            logs = jnp.concatenate([top1 + jnp.log2(total1[:DH]), top0 + jnp.log2(total0[DH:])])
            here = slice(query * rows, (query + 1) * rows)
            o_ref[here, :] = out.T.astype(BF)
            log_ref[here, :] = logs.T

    if not causal:
        run([(head, 0, key, False) for head in range(2) for key in range(4)], n)
    else:
        for case in range(2):

            @pl.when(core == case)
            def _(case=case):
                run(
                    [
                        (head, query, key, key == 2 * case + query)
                        for head in range(2)
                        for query in range(2)
                        for key in range(2 * case + query + 1)
                    ],
                    chunk,
                )


def heads_forward(core, q, own, got, hot, key_hot, causal):
    n, width = q.shape
    length = 2 * n
    keys = pl.BlockSpec((2, n, 128), lambda p: (0, 0, p))
    queries = pl.BlockSpec((n, 128), lambda p: (0, p))
    table = pl.BlockSpec((length, 128), lambda p: (0, 0))
    return pl.pallas_call(
        partial(forward_kernel, causal=causal),
        grid=(width // 128,),
        in_specs=[
            pl.BlockSpec(memory_space=pltpu.SMEM),
            queries,
            keys,
            keys,
            table,
            table,
        ],
        out_specs=[queries, queries],
        out_shape=[jax.ShapeDtypeStruct((n, width), BF), jax.ShapeDtypeStruct((n, width), F32)],
        scratch_shapes=[pltpu.VMEM((2, length, 128), BF), pltpu.VMEM((2, 128, length), BF)],
        compiler_params=pltpu.CompilerParams(vmem_limit_bytes=VMEM_BYTES),
        cost_estimate=COST,
        name="attention_causal" if causal else "attention",
    )(core, *in_hbm((q, own, got, hot, key_hot)))


def backward_kernel(
    core_ref, q_ref, own_ref, got_ref, hot_ref, key_hot_ref, grad_ref, o_ref, log_ref,
    q_grad_ref, own_grad_ref, got_grad_ref, queries, grads, q_turned, grad_turned, q_total, *, causal,
):
    step = pl.program_id(1)
    n, block = q_ref.shape[0], own_ref.shape[1]
    chunk = n // 2
    blocks = n // block
    core = core_ref[0]
    left, lane = lanes()

    @pl.when(step == 0)
    def _():
        log = log_ref[...]
        high = log.astype(BF).astype(F32)
        middle = (log - high).astype(BF).astype(F32)
        low = log - high - middle
        mine = hot_ref[pl.ds(pl.multiple_of(core * n, n), n), :].astype(F32)
        ext = jnp.where(lane < 8, (1.0 - mine) * BIG, 0.0)
        ext = jnp.where(lane == 10, -low, ext)
        ext = jnp.where(lane == 9, -middle, jnp.where(lane == 8, -high, ext)).astype(BF)
        pair = q_ref[...]
        queries[0] = jnp.where(left, pair, ext)
        queries[1] = jnp.where(left, ext, pair)
        q_turned[...] = pair.T
        pair = grad_ref[...]
        product = pair.astype(F32) * o_ref[...].astype(F32)
        high = product.astype(BF)
        low = (product - high.astype(F32)).astype(BF)
        row = lax.broadcasted_iota(jnp.int32, (128, 128), 0)
        column = lax.broadcasted_iota(jnp.int32, (128, 128), 1)
        across = ((row < DH) != (column < DH)).astype(BF)
        inner = dot_nn(high, across) + dot_nn(low, across)
        high = inner.astype(BF).astype(F32)
        ext = jnp.where(lane == 8, -high, jnp.where(lane == 9, high - inner, 0.0)).astype(BF)
        grads[0] = jnp.where(left, pair, ext)
        grads[1] = jnp.where(left, ext, pair)
        grad_turned[...] = pair.T
        q_total[...] = jnp.zeros_like(q_total)

    own = step < blocks
    k = jnp.where(own, own_ref[0], got_ref[0])
    v = jnp.where(own, own_ref[1], got_ref[1])
    place = jnp.where(own, core * n + step * block, (1 - core) * n + (step - blocks) * block)
    hot = key_hot_ref[pl.ds(pl.multiple_of(place, block), block), :]
    ones = jnp.ones_like(v)
    ext = jnp.where((lane >= 8) & (lane < 11), ones, hot)
    keys = (jnp.where(left, k, ext), jnp.where(left, ext, k))
    values = (jnp.where(left, v, ones), jnp.where(left, ones, v))

    def run(tasks):
        k_grads, v_grads = [0.0, 0.0], [0.0, 0.0]

        def scores_of(head, query, cut):
            here = slice(query * chunk, (query + 1) * chunk)
            scores = dot_nt(queries[head, here, :], keys[head])
            if cut:
                to = lax.broadcasted_iota(jnp.int32, scores.shape, 0)
                at = lax.broadcasted_iota(jnp.int32, scores.shape, 1)
                scores = jnp.where(at <= to, scores, BIG)
            return scores, dot_nt(grads[head, here, :], values[head])

        def after(products, head, query, cut):
            here = slice(query * chunk, (query + 1) * chunk)
            probs = jnp.exp2(products[0])
            score_grad = (probs * products[1]).astype(BF)
            v_grads[head] = v_grads[head] + dot_nn(grad_turned[:, here], probs.astype(BF))
            k_grads[head] = k_grads[head] + dot_nn(q_turned[:, here], score_grad)
            q_total[head, here, :] += dot_nn(score_grad, keys[head])

        pipelined(tasks, scores_of, after)
        k_grad = jnp.concatenate([k_grads[0][:DH], k_grads[1][DH:]]).T
        v_grad = jnp.concatenate([v_grads[0][:DH], v_grads[1][DH:]]).T
        put((k_grad * math.log(2.0)).astype(BF), v_grad.astype(BF))

    def put(k_grad, v_grad):
        @pl.when(own)
        def _():
            own_grad_ref[0] = k_grad
            own_grad_ref[1] = v_grad

        @pl.when(jnp.logical_not(own))
        def _():
            got_grad_ref[0] = k_grad
            got_grad_ref[1] = v_grad

    if not causal:
        run([(head, query, False) for head in range(2) for query in range(2)])
    else:
        @pl.when(jnp.logical_not(own) & (core == 0))
        def _():
            put(jnp.zeros((block, 128), BF), jnp.zeros((block, 128), BF))

        @pl.when(jnp.logical_not(own) & (core == 1))
        def _():
            run([(head, query, False) for head in range(2) for query in range(2)])

        for case in range(2):

            @pl.when(step == case)
            def _(case=case):
                run([(head, query, query == case) for head in range(2) for query in range(case, 2)])

    @pl.when(step == 2 * blocks - 1)
    def _():
        q_grad_ref[...] = (jnp.where(left, q_total[0], q_total[1]) * DH**-0.5).astype(BF)


def heads_backward(core, kept, grad, causal, begin=0, width=HALF):
    q, own, got, hot, key_hot, o, log = kept
    n = q.shape[0]
    skip = begin // 128
    block = n // 2
    blocks = 2
    first = lambda b: jnp.minimum(b, blocks - 1)
    second = lambda b: jnp.maximum(b - blocks, 0)
    whole = pl.BlockSpec((n, 128), lambda p, b: (0, skip + p))
    whole_out = pl.BlockSpec((n, 128), lambda p, b: (0, p))
    table = pl.BlockSpec((2 * n, 128), lambda p, b: (0, 0))

    def keys(part, skip):
        return pl.BlockSpec((2, block, 128), lambda p, b: (0, part(b), skip + p))

    return pl.pallas_call(
        partial(backward_kernel, causal=causal),
        grid=(width // 128, 2 * blocks),
        in_specs=[
            pl.BlockSpec(memory_space=pltpu.SMEM),
            whole,
            keys(first, skip),
            keys(second, skip),
            table,
            table,
            whole,
            whole,
            whole,
        ],
        out_specs=[whole_out, keys(first, 0), keys(second, 0)],
        out_shape=[jax.ShapeDtypeStruct(s, BF) for s in ((n, width), (2, n, width), (2, n, width))],
        scratch_shapes=[
            pltpu.VMEM((2, n, 128), BF),
            pltpu.VMEM((2, n, 128), BF),
            pltpu.VMEM((128, n), BF),
            pltpu.VMEM((128, n), BF),
            pltpu.VMEM((2, n, 128), F32),
        ],
        compiler_params=pltpu.CompilerParams(vmem_limit_bytes=VMEM_BYTES),
        cost_estimate=COST,
        name="attention_causal_back" if causal else "attention_back",
    )(core, *in_hbm((q, own, got, hot, key_hot, grad, o, log)))


def fold_dot(x, w):
    return dot_nn(x[:, :HALF], w[:, :HALF]) + dot_nn(x[:, HALF:], w[:, HALF:])


def fold_dot_t(g, w):
    return jnp.concatenate([dot_nt(g, w[:, :HALF]), dot_nt(g, w[:, HALF:])], axis=1)


def fold_grad(x, g):
    return jnp.concatenate([dot_tn(x[:, :HALF], g), dot_tn(x[:, HALF:], g)], axis=1)


def norm(v, gain, shift):
    centred = v - jnp.mean(v, axis=-1, keepdims=True)
    scale = lax.rsqrt(jnp.mean(centred * centred, axis=-1, keepdims=True) + EPS)
    unit = centred * scale
    return unit * gain + shift, unit, scale


def norm_back(grad, unit, scale, gain):
    inner = grad * gain
    mean_inner = jnp.mean(inner, axis=-1, keepdims=True)
    mean_unit = jnp.mean(inner * unit, axis=-1, keepdims=True)
    return scale * (inner - mean_inner - unit * mean_unit)


def over_rows(v):
    return jnp.sum(v, axis=0, keepdims=True)


GELU_C = math.sqrt(2.0 / math.pi)


def gelu(u):
    return 0.5 * u * (1.0 + jnp.tanh(GELU_C * u * (1.0 + 0.044715 * u * u)))


def gelu_both(u):
    square = u * u
    t = jnp.tanh(GELU_C * u * (1.0 + 0.044715 * square))
    half = 0.5 * (1.0 + t)
    slope = half + 0.5 * u * (1.0 - t * t) * (GELU_C * (1.0 + 3 * 0.044715 * square))
    return u * half, slope


def halt_gate(last, weight):
    logit = jnp.sum(last * weight, axis=-1, keepdims=True)
    return 1.0 / (1.0 + jnp.exp(-logit))


def halt_back(grad, start, last, runs, weight):
    gate = halt_gate(last, weight)
    used = runs * gate
    logit_grad = used * (1.0 - gate) * jnp.sum(grad * (last - start), axis=-1, keepdims=True)
    return grad * (1.0 - used), used * grad + logit_grad * weight, over_rows(logit_grad * last)


def ffn_blocks(own_ref, other_ref, begin):
    for which, ref in ((0, own_ref), (1, other_ref)):
        for j in range(2):
            up = begin + j * D
            down = up + 2 * D
            yield which, ref[up : up + D, :], ref[down : down + D, :], up, down


def ffn(low, own_ref, other_ref, begin, kept=None):
    blocks = list(ffn_blocks(own_ref, other_ref, begin))
    total = []

    def after(hidden, j):
        if kept is None:
            active = gelu(hidden).astype(BF)
        else:
            active, slope = gelu_both(hidden)
            active = active.astype(BF)
            kept[0, :, j * D : (j + 1) * D] = active
            kept[1, :, j * D : (j + 1) * D] = slope.astype(BF)
        total.append(dot_nn(active, blocks[j][2]))

    pipelined([(j,) for j in range(4)], lambda j: dot_nn(low, blocks[j][1]), after)
    return sum(total)


def ffn_back(low, out_low, own_ref, other_ref, begin, acc, shift, kept=None):
    blocks = list(ffn_blocks(own_ref, other_ref, begin))
    total = []

    def products(j):
        _, up, down, _, _ = blocks[j]
        return None if kept is not None else dot_nn(low, up), dot_nt(out_low, down)

    def after(got, j):
        which, up, _, up_at, down_at = blocks[j]
        hidden, active_grad = got
        if kept is None:
            active, slope = gelu_both(hidden)
            active = active.astype(BF)
        else:
            active = kept[0, :, j * D : (j + 1) * D]
            slope = kept[1, :, j * D : (j + 1) * D].astype(F32)
        hidden_grad = (active_grad * slope).astype(BF)
        up_at, down_at = up_at + shift, down_at + shift
        acc[which, down_at : down_at + D, :] += dot_tn(active, out_low)
        acc[which, up_at : up_at + D, :] += dot_tn(low, hidden_grad)
        total.append(dot_nt(hidden_grad, up))

    pipelined([(j,) for j in range(4)], products, after)
    return sum(total)


def proj_back(o_refs, out_low, projs, acc, begin, o_grad_refs):
    for which in range(2):
        o_grad_refs[which][...] = dot_nt(out_low, projs[which]).astype(BF)
        acc[which, begin : begin + HALF, :] += dot_tn(o_refs[which][...], out_low)


def first_step(*refs):
    @pl.when(pl.program_id(0) == 0)
    def _():
        for ref in refs:
            ref[...] = jnp.zeros_like(ref)


def last_step(core_ref, acc, keep_ref, send_ref, small_acc=None, small_ref=None):
    @pl.when(pl.program_id(0) == pl.num_programs(0) - 1)
    def _():
        rows = acc.shape[1] // 2
        for part, ref in ((core_ref[0], keep_ref), (1 - core_ref[0], send_ref)):
            here = pl.ds(pl.multiple_of(part * rows, 16), rows)
            for which in range(acc.shape[0]):
                ref[which] = acc[which, here, :].astype(BF)
        if small_ref is not None:
            small_ref[...] = small_acc[...]


def join(core_ref, *triples):
    @pl.when(pl.program_id(0) == 0)
    def _():
        for near_ref, far_ref, whole in triples:
            rows = near_ref.shape[0]
            for part, ref in ((core_ref[0], near_ref), (1 - core_ref[0], far_ref)):
                whole[pl.ds(pl.multiple_of(part * rows, 16), rows), :] = ref[...]


def second_part(core_ref, near_ref, far_ref):
    return jnp.where(core_ref[0] == 1, near_ref[...], far_ref[...])


def pre_kernel(
    core_ref, rows_ref, got_ref, place_ref, own_ref, near_ref, far_ref,
    start_ref, q0_ref, q1_ref, kv0_ref, kv1_ref,
    other_ref,
):
    join(core_ref, (near_ref, far_ref, other_ref))
    rows = jnp.where(core_ref[1] == 1, rows_ref[...].astype(F32), got_ref[...].astype(F32))
    start = rows + place_ref[...]
    start_ref[...] = start
    low = start.astype(BF)
    for ref, q_ref, kv_ref in ((own_ref, q0_ref, kv0_ref), (other_ref, q1_ref, kv1_ref)):
        q_ref[...] = (fold_dot(low, ref[0:HALF, :]) * Q_SCALE).astype(BF)
        for kind in range(2):
            w = ref[(kind + 1) * HALF : (kind + 2) * HALF, :]
            kv_ref[kind] = fold_dot(low, w).astype(BF)


def enc_post_kernel(
    core_ref, o0_ref, o1_ref, start_ref, runs_ref, own_ref, near_ref, far_ref, small_ref,
    sum_one_ref, sum_two_ref, states_ref,
    other_ref,
):
    join(core_ref, (near_ref, far_ref, other_ref))
    start = start_ref[...]
    sum_one = start + dot_nn(o0_ref[...], own_ref[:HALF, :]) + dot_nn(o1_ref[...], other_ref[:HALF, :])
    sum_one_ref[...] = sum_one
    middle, _, _ = norm(sum_one, small_ref[0:1, :], small_ref[1:2, :])
    sum_two = middle + ffn(middle.astype(BF), own_ref, other_ref, HALF)
    sum_two_ref[...] = sum_two
    last, _, _ = norm(sum_two, small_ref[2:3, :], small_ref[3:4, :])
    gate = halt_gate(last, small_ref[4:5, :])
    states_ref[...] = (start + runs_ref[:, 0:1] * gate * (last - start)).astype(BF)


def dec_mid_kernel(
    core_ref, o0_ref, o1_ref, start_ref, states_ref, proj_own_ref, proj_near_ref, proj_far_ref,
    own_ref, near_ref, far_ref, small_ref,
    sum_ref, q0_ref, q1_ref, kv0_ref, kv1_ref,
    other_ref,
):
    join(core_ref, (near_ref, far_ref, other_ref))
    total = start_ref[...] + dot_nn(o0_ref[...], proj_own_ref[...])
    total = total + dot_nn(o1_ref[...], second_part(core_ref, proj_near_ref, proj_far_ref))
    sum_ref[...] = total
    middle, _, _ = norm(total, small_ref[0:1, :], small_ref[1:2, :])
    low = middle.astype(BF)
    states = states_ref[...]
    for ref, q_ref, kv_ref in ((own_ref, q0_ref, kv0_ref), (other_ref, q1_ref, kv1_ref)):
        q_ref[...] = (fold_dot(low, ref[0:HALF, :]) * Q_SCALE).astype(BF)
        for kind in range(2):
            w = ref[(kind + 1) * HALF : (kind + 2) * HALF, :]
            kv_ref[kind] = fold_dot(states, w).astype(BF)


def dec_post_kernel(
    core_ref, o0_ref, o1_ref, sum_one_ref, start_ref, runs_ref, cot_ref, own_ref, near_ref, far_ref, small_ref,
    states_ref, start_grad_ref, sum_grad_ref, o0_grad_ref, o1_grad_ref,
    keep_ref, send_ref, small_grad_ref,
    acc, small_acc, other_ref, kept,
):
    join(core_ref, (near_ref, far_ref, other_ref))
    first_step(acc, small_acc)
    start = start_ref[...]
    projs = own_ref[:HALF, :], other_ref[:HALF, :]
    middle, _, _ = norm(sum_one_ref[...], small_ref[0:1, :], small_ref[1:2, :])
    sum_two = middle + dot_nn(o0_ref[...], projs[0]) + dot_nn(o1_ref[...], projs[1])
    gain_two = small_ref[2:3, :]
    mixed, unit_two, scale_two = norm(sum_two, gain_two, small_ref[3:4, :])
    low = mixed.astype(BF)
    sum_three = mixed + ffn(low, own_ref, other_ref, HALF, kept)
    gain_three = small_ref[4:5, :]
    last, unit_three, scale_three = norm(sum_three, gain_three, small_ref[5:6, :])
    weight = small_ref[6:7, :]
    runs = runs_ref[:, 1:2]
    states_ref[...] = (start + runs * halt_gate(last, weight) * (last - start)).astype(BF)
    start_grad, last_grad, weight_grad = halt_back(
        cot_ref[...].astype(F32), start, last, runs, weight
    )
    start_grad_ref[...] = start_grad
    small_acc[4:5, :] += weight_grad
    small_acc[2:3, :] += over_rows(last_grad * unit_three)
    small_acc[3:4, :] += over_rows(last_grad)
    grad = norm_back(last_grad, unit_three, scale_three, gain_three)
    grad = grad + ffn_back(low, grad.astype(BF), own_ref, other_ref, HALF, acc, 0, kept)
    small_acc[0:1, :] += over_rows(grad * unit_two)
    small_acc[1:2, :] += over_rows(grad)
    grad = norm_back(grad, unit_two, scale_two, gain_two)
    sum_grad_ref[...] = grad
    proj_back((o0_ref, o1_ref), grad.astype(BF), projs, acc, 0, (o0_grad_ref, o1_grad_ref))
    last_step(core_ref, acc, keep_ref, send_ref, small_acc, small_grad_ref)


def dec_mid_back_kernel(
    core_ref, q0_grad_ref, q1_grad_ref, sum_grad_ref, sum_one_ref, start_grad_ref, o0_ref, o1_ref,
    cq_own_ref, cq_near_ref, cq_far_ref, proj_own_ref, proj_near_ref, proj_far_ref, small_ref,
    out_ref, o0_grad_ref, o1_grad_ref, keep_ref, send_ref, small_grad_ref,
    acc, small_acc,
):
    cq_other = jnp.where(core_ref[0] == 0, cq_near_ref[:HALF, :], cq_far_ref[:HALF, :])
    first_step(acc, small_acc)
    gain = small_ref[0:1, :]
    middle, unit, scale = norm(sum_one_ref[...], gain, small_ref[1:2, :])
    low = middle.astype(BF)
    grad = sum_grad_ref[...]
    for which, (w, part_ref) in enumerate(((cq_own_ref[...], q0_grad_ref), (cq_other, q1_grad_ref))):
        grad = grad + fold_dot_t(part_ref[...], w)
        acc[which, :HALF, :] += fold_grad(low, part_ref[...])
    small_acc[0:1, :] += over_rows(grad * unit)
    small_acc[1:2, :] += over_rows(grad)
    grad = norm_back(grad, unit, scale, gain)
    out_ref[...] = start_grad_ref[...] + grad
    projs = proj_own_ref[...], second_part(core_ref, proj_near_ref, proj_far_ref)
    proj_back((o0_ref, o1_ref), grad.astype(BF), projs, acc, HALF, (o0_grad_ref, o1_grad_ref))
    last_step(core_ref, acc, keep_ref, send_ref, small_acc, small_grad_ref)


def kv_total(own_ref, got_ref, kind):
    return (own_ref[kind].astype(F32) + got_ref[kind].astype(F32)).astype(BF)


def enc_back_kernel(
    core_ref, kv0_ref, kv1_ref, got0_ref, got1_ref, states_ref, cot_ref, start_ref, sum_one_ref, sum_two_ref,
    o0_ref, o1_ref, runs_ref, cross_own_ref, cross_near_ref, cross_far_ref, own_ref, near_ref, far_ref, small_ref,
    out_ref, o0_grad_ref, o1_grad_ref, keep_ref, send_ref, small_grad_ref,
    acc, small_acc, cross_other_ref, other_ref,
):
    join(core_ref, (near_ref, far_ref, other_ref), (cross_near_ref, cross_far_ref, cross_other_ref))
    first_step(acc, small_acc)
    states = states_ref[...]
    grad = cot_ref[...].astype(F32)
    crosses = (cross_own_ref, kv0_ref, got0_ref), (cross_other_ref, kv1_ref, got1_ref)
    for which, (ref, kv_ref, got_ref) in enumerate(crosses):
        for kind in range(2):
            part = kv_total(kv_ref, got_ref, kind)
            at = kind * HALF
            grad = grad + fold_dot_t(part, ref[at + HALF : at + 2 * HALF, :])
            acc[which, at : at + HALF, :] += fold_grad(states, part)
    gain_one, gain_two, weight = small_ref[0:1, :], small_ref[2:3, :], small_ref[4:5, :]
    last, unit_two, scale_two = norm(sum_two_ref[...], gain_two, small_ref[3:4, :])
    start_grad, last_grad, weight_grad = halt_back(
        grad, start_ref[...], last, runs_ref[:, 0:1], weight
    )
    small_acc[4:5, :] += weight_grad
    small_acc[2:3, :] += over_rows(last_grad * unit_two)
    small_acc[3:4, :] += over_rows(last_grad)
    grad = norm_back(last_grad, unit_two, scale_two, gain_two)
    middle, unit_one, scale_one = norm(sum_one_ref[...], gain_one, small_ref[1:2, :])
    grad = grad + ffn_back(middle.astype(BF), grad.astype(BF), own_ref, other_ref, HALF, acc, 2 * HALF)
    small_acc[0:1, :] += over_rows(grad * unit_one)
    small_acc[1:2, :] += over_rows(grad)
    grad = norm_back(grad, unit_one, scale_one, gain_one)
    out_ref[...] = start_grad + grad
    projs = own_ref[:HALF, :], other_ref[:HALF, :]
    proj_back((o0_ref, o1_ref), grad.astype(BF), projs, acc, 2 * HALF, (o0_grad_ref, o1_grad_ref))
    last_step(core_ref, acc, keep_ref, send_ref, small_acc, small_grad_ref)


def qkv_back(low, parts, w_ref, acc, which):
    grad = 0.0
    for kind, part in enumerate(parts):
        rows = slice(kind * HALF, (kind + 1) * HALF)
        grad = grad + fold_dot_t(part, w_ref[rows, :])
        acc[which, rows, :] += fold_grad(low, part)
    return grad


def qkv_parts(q_ref, kv_ref, got_ref):
    return q_ref[...], kv_total(kv_ref, got_ref, 0), kv_total(kv_ref, got_ref, 1)


def own_qkv_back_kernel(
    core_ref, q_ref, kv_ref, got_ref, start_ref, base_ref, w_ref,
    out_ref, low_ref, keep_ref, send_ref,
    acc,
):
    first_step(acc)
    low = start_ref[...].astype(BF)
    parts = qkv_parts(q_ref, kv_ref, got_ref)
    grad = base_ref[...] + qkv_back(low, parts, w_ref, acc, 0)
    out_ref[...] = grad
    low_ref[...] = grad.astype(BF)
    last_step(core_ref, acc, keep_ref, send_ref)


def other_qkv_back_kernel(
    core_ref, q_ref, kv_ref, got_ref, start_ref, base_ref, near_ref, far_ref,
    out_ref, low_ref, keep_ref, send_ref,
    acc, other_ref,
):
    join(core_ref, (near_ref, far_ref, other_ref))
    own_qkv_back_kernel(
        core_ref, q_ref, kv_ref, got_ref, start_ref, base_ref, other_ref,
        out_ref, low_ref, keep_ref, send_ref, acc,
    )


def both_qkv_back_kernel(
    core_ref, q0_grad_ref, kv0_ref, got0_ref, q1_grad_ref, kv1_ref, got1_ref, start_ref, base_ref,
    own_ref, near_ref, far_ref, more_keep_ref, more_send_ref, small_ref,
    out_ref, low_ref, keep_ref, send_ref,
    acc, other_ref,
):
    first_step(acc)
    join(core_ref, (near_ref, far_ref, other_ref))
    low = start_ref[...].astype(BF)
    grad = base_ref[...] + qkv_back(low, qkv_parts(q0_grad_ref, kv0_ref, got0_ref), own_ref, acc, 0)
    grad = grad + qkv_back(low, qkv_parts(q1_grad_ref, kv1_ref, got1_ref), other_ref, acc, 1)
    out_ref[...] = grad
    low_ref[...] = grad.astype(BF)

    @pl.when(pl.program_id(0) == pl.num_programs(0) - 1)
    def _():
        rows = acc.shape[1] // 2
        ends = (core_ref[0], keep_ref, more_keep_ref), (1 - core_ref[0], send_ref, more_send_ref)
        for part, ref, more_ref in ends:
            here = pl.ds(pl.multiple_of(part * rows, 16), rows)
            for which in range(2):
                after = rows + more_ref.shape[1]
                ref[which, :rows, :] = acc[which, here, :].astype(BF)
                ref[which, rows:after, :] = more_ref[which]
                ref[which, after : after + 16, :] = small_ref[pl.ds(pl.multiple_of(part * 16, 16), 16), :].astype(BF)
                ref[which, after + 16 :, :] = jnp.zeros((ref.shape[1] - after - 16, D), BF)


def rows_call(kernel, name, core, by_rows, whole, row_outs, whole_outs=(), scratch=(), block=512):
    n = by_rows[0].shape[-2]

    def row_spec(shape):
        if len(shape) == 3:
            return pl.BlockSpec((shape[0], block, shape[2]), lambda i: (0, i, 0))
        return pl.BlockSpec((block, shape[1]), lambda i: (i, 0))

    def whole_spec(entry):
        if not isinstance(entry, tuple):
            return pl.BlockSpec(entry.shape, lambda i: (0,) * entry.ndim, pipeline_mode=pl.Buffered(1))
        array, rows, index = entry
        return pl.BlockSpec((rows, array.shape[1]), lambda i: (index, 0), pipeline_mode=pl.Buffered(1))

    arrays = [e[0] if isinstance(e, tuple) else e for e in whole]
    return pl.pallas_call(
        kernel,
        grid=(n // block,),
        in_specs=[pl.BlockSpec(memory_space=pltpu.SMEM)]
        + [row_spec(a.shape) for a in by_rows]
        + [whole_spec(e) for e in whole],
        out_specs=[row_spec(s) for s, _ in row_outs]
        + [pl.BlockSpec(s, lambda i, s=s: (0,) * len(s)) for s, _ in whole_outs],
        out_shape=[jax.ShapeDtypeStruct(s, t) for s, t in [*row_outs, *whole_outs]],
        scratch_shapes=[pltpu.VMEM(*s) for s in scratch],
        compiler_params=pltpu.CompilerParams(vmem_limit_bytes=VMEM_BYTES),
        cost_estimate=COST,
        name=name,
    )(core, *in_hbm(by_rows), *arrays)


def put_rows(out_ref, at, values):
    count = values.shape[0]
    if len(out_ref.shape) == 3 or out_ref.shape[1] < D:
        width = out_ref.shape[-1]
        folds = D // width
        depth = out_ref.shape[-2] // folds
        for begin in range(at // depth * depth, at + count, depth):
            low, high = max(begin, at), min(begin + depth, at + count)
            if low < high:
                kind = begin // depth
                ref = out_ref.at[kind] if len(out_ref.shape) == 3 else out_ref
                for fold in range(folds):
                    rows = slice(fold * depth + low - begin, fold * depth + high - begin)
                    ref[rows, :] = values[low - at : high - at, fold * width : (fold + 1) * width]
        return
    depth = out_ref.shape[0]
    for begin in range(0, at + count, depth):
        low, high = max(begin, at), min(begin + depth, at + count)
        if low < high:
            column = begin // depth * D
            out_ref[low - begin : high - begin, column : column + D] = values[low - at : high - at]


def unpack_kernel(order_ref, mine_ref, got_ref, *refs, places):
    outs, rows_in = refs[:-1], refs[-1]
    piece, core = order_ref[0], order_ref[1]
    pieces, rows, _ = mine_ref.shape
    for ref, of in ((mine_ref, core), (got_ref, 1 - core)):
        for k in range(pieces):
            begin = (of * pieces + (piece ^ k)) * rows
            rows_in[pl.ds(pl.multiple_of(begin, 16), rows), :] = ref[k].astype(F32)
    for out, begin, at, count in places:
        put_rows(outs[out], at, rows_in[begin : begin + count, :])


def unpack(order, mine, got, shapes, places):
    pieces, rows, width = mine.shape
    vmem = pl.BlockSpec(memory_space=pltpu.VMEM)
    return pl.pallas_call(
        partial(unpack_kernel, places=places),
        in_specs=[pl.BlockSpec(memory_space=pltpu.SMEM), vmem, vmem],
        out_specs=[vmem] * len(shapes),
        out_shape=[jax.ShapeDtypeStruct(s, F32) for s in shapes],
        scratch_shapes=[pltpu.VMEM((2 * pieces * rows, width), F32)],
        compiler_params=pltpu.CompilerParams(vmem_limit_bytes=VMEM_BYTES),
        cost_estimate=COST,
        name="unpack",
    )(order, mine, got)


class Place:
    def __init__(self, dp_size):
        self.dp_size = dp_size
        dp = lax.axis_index("dp")
        self.c = dp % 2
        self.stays = self.c == lax.axis_index("mp")
        self.masks = [1 << b for b in range(1, dp_size.bit_length() - 1)]
        self.bits = [(dp // mask) % 2 for mask in self.masks]
        self.core = jnp.stack([self.c, self.stays]).astype(jnp.int32)
        piece = jnp.int32(0)
        for bit in self.bits:
            piece = 2 * piece + bit.astype(jnp.int32)
        self.order = jnp.stack([piece, self.c.astype(jnp.int32)])

    def flip(self, values, mask):
        return lax.ppermute(values, "dp", [(d, d ^ mask) for d in range(self.dp_size)])

    def core_swap(self, values):
        return self.flip(values, 1)

    def y_swap(self, values):
        return lax.ppermute(values, "mp", [(0, 1), (1, 0)])

    def cross(self, values):
        perm = []
        for d in range(0, self.dp_size, 2):
            perm += [(2 * d + 1, 2 * d + 2), (2 * d + 2, 2 * d + 1)]
        return lax.ppermute(values, ("dp", "mp"), perm)


class Flow:
    def __init__(self):
        self.fresh = []
        self.chains = []
        self.results = {}

    def add(self, name, chain):
        self.fresh.append((name, chain, next(chain)))

    def go_on(self, name, chain, arrived):
        try:
            self.fresh.append((name, chain, chain.send(arrived)))
        except StopIteration as stop:
            self.results[name] = stop.value

    def step(self, values):
        due = [chain for chain in self.chains if chain[3] == 1]
        self.chains = [(*chain[:3], chain[3] - 1) for chain in self.chains if chain[3] > 1]
        values, arrived = lax.optimization_barrier((values, [chain[2] for chain in due]))
        for (name, chain, _, _), got in zip(due, arrived):
            self.go_on(name, chain, got)
        fresh, self.fresh = self.fresh, []
        values, operands = lax.optimization_barrier((values, [op[1] for _, _, op in fresh]))
        for (name, chain, (send, _, steps)), operand in zip(fresh, operands):
            self.chains.append((name, chain, send(operand), steps))
        return values

    def finish(self):
        while self.chains:
            name, chain, pending, _ = self.chains.pop(0)
            self.go_on(name, chain, pending)
        while self.fresh:
            name, chain, (send, operand, _) = self.fresh.pop(0)
            self.go_on(name, chain, send(operand))


def gathered(at, own, first=1, second=1):
    rows = own.shape[0] // 2
    near = yield at.y_swap, lax.dynamic_slice_in_dim(own, at.c * rows, rows, 0), first
    far = yield at.core_swap, near, second
    return near, far


def moved(at, values, steps):
    return (yield at.cross, values, steps)


def plus(*values):
    return sum(v.astype(F32) for v in values).astype(BF)


def over_chips(at, total, last_steps=1, back_steps=(1, 1, 1)):
    for mask, bit in zip(at.masks, at.bits):
        rows = total.shape[0] // 2
        half = lax.dynamic_slice_in_dim(total, (1 - bit) * rows, rows, 0)
        got = yield partial(at.flip, mask=mask), half, 1
        total = plus(lax.dynamic_slice_in_dim(total, bit * rows, rows, 0), got)
    total = total[None]
    for mask, steps in zip(at.masks[::-1], back_steps):
        got = yield partial(at.flip, mask=mask), total, steps
        total = jnp.concatenate([total, got])
    return total, (yield at.core_swap, total, last_steps)


def summed(at, keep, send, back_steps=(1, 1, 1)):
    got = yield at.core_swap, send, 1
    near = yield at.y_swap, plus(keep[1], got[1]), 1
    return (yield from over_chips(at, plus(keep[0], got[0], near), 1, back_steps))


def summed_other(at, keep, got, y_steps):
    near = yield at.y_swap, plus(keep[0], got[0]), y_steps
    return near


def summed_own(at, keep, send, near):
    got = yield at.core_swap, send, 1
    return (yield from over_chips(at, plus(keep[0], got[0], near)))


def rows_of(weight):
    if weight.ndim == 3:
        kinds, depth, width = weight.shape
        folded = jnp.concatenate([weight[:, : depth // 2], weight[:, depth // 2 :]], axis=2)
        return folded.reshape(kinds * depth // 2, 2 * width)
    depth, width = weight.shape
    if width == D:
        return weight
    if width < D:
        return jnp.concatenate([weight[: depth // 2], weight[depth // 2 :]], axis=1)
    return jnp.concatenate([weight[:, :D], weight[:, D:]], axis=0)


Q_SCALE = DH**-0.5 * math.log2(math.e)


def chip_rows(
    source_rows,
    target_rows,
    source_segment,
    target_segment,
    running,
    enc_qkv,
    enc_proj,
    enc_up,
    enc_down,
    enc_gains,
    enc_shifts,
    dec_qkv,
    dec_proj,
    cross_query,
    cross_kv,
    cross_proj,
    dec_up,
    dec_down,
    dec_gains,
    dec_shifts,
    halt_weight,
    enc_cotangent,
    dec_cotangent,
    *,
    dp_size,
):
    at = Place(dp_size)
    flow = Flow()
    n = source_rows.shape[0]
    row = ((n, D), F32)
    row_low = ((n, D), BF)
    half_low = ((n, HALF), BF)
    kv_low = ((2, n, HALF), BF)

    def embedding():
        place = at.core[0] * n + jnp.arange(n, dtype=jnp.int32)
        return signal(place.astype(F32)) + signal(jnp.ones((1,), F32))

    ints = jnp.concatenate([source_segment[0], target_segment[0], running[0, 0], running[1, 0]])
    ints = ints.reshape(6, n)
    flow.add("source", moved(at, source_rows[:, 0], 3))
    flow.add("ints", moved(at, ints, 2))
    (enc_qkv_now,) = flow.step((enc_qkv,))
    w_enc_qkv = rows_of(enc_qkv_now)
    flow.add("w_enc_qkv", gathered(at, w_enc_qkv, 2, 1))
    later = ints, dec_qkv, enc_up, cross_kv, dec_up, enc_cotangent, dec_cotangent, running, enc_gains, dec_gains
    later = flow.step(later)
    ints, dec_qkv_now, enc_up_now, cross_kv_now, dec_up_now, enc_cot, dec_cot, running, enc_gains, dec_gains = later
    w_dec_self = jnp.concatenate([rows_of(dec_qkv_now), rows_of(dec_proj)])
    ints, w_dec_self, embedding = flow.step((ints, w_dec_self, embedding()))
    ints = jnp.where(at.stays, ints, flow.results["ints"])
    runs = jnp.transpose(jnp.pad(ints[4:].astype(F32), ((0, 126), (0, 0))))
    lane = jnp.arange(128, dtype=jnp.int32) % DH
    source_hot, target_hot = (ints[:4].reshape(2, 2 * n, 1) == lane).astype(BF)

    w_enc = jnp.concatenate([rows_of(enc_proj), rows_of(enc_up_now), rows_of(enc_down)])
    w_cross = jnp.concatenate([rows_of(cross_query), rows_of(cross_kv_now)])
    w_dec = jnp.concatenate([rows_of(cross_proj), rows_of(dec_up_now), rows_of(dec_down)])
    cots = jnp.concatenate([enc_cot[:, 0].astype(BF), dec_cot[:, 0].astype(BF)], axis=1)
    pad = jnp.zeros((3, D), F32)
    small_enc = jnp.stack(
        [enc_gains[0], enc_shifts[0], enc_gains[1], enc_shifts[1], halt_weight[0]]
    )
    small_enc = jnp.concatenate([small_enc, pad])
    small_dec = jnp.stack(
        [dec_gains[0], dec_shifts[0], dec_gains[1], dec_shifts[1], dec_gains[2], dec_shifts[2], halt_weight[1]]
    )
    small_dec = jnp.concatenate([small_dec, pad[:1]])

    flow.add("w_dec_self", gathered(at, w_dec_self, 2, 1))
    flow.add("target", moved(at, target_rows[:, 0], 3))
    tables = embedding, source_hot, target_hot, w_enc, cots
    embedding, source_hot, target_hot, w_enc, cots = flow.step(tables)
    (embedding,) = flow.step((embedding,))

    def pre(rows, got, own, other):
        return rows_call(
            pre_kernel, "project", at.core, [rows, got, embedding], [own, *other],
            [row, half_low, half_low, kv_low, kv_low], scratch=[(own.shape, BF)],
        )

    def attend(q, kv, got, hot, key_hot, causal=False):
        o, log = heads_forward(at.core, q, kv, got, hot, key_hot, causal)
        return o, (q, kv, got, hot, key_hot, o, log)

    def attend_back(kept, grad, causal=False):
        return heads_backward(at.core, kept, grad, causal)

    w_enc_qkv_got = flow.results["w_enc_qkv"]
    enc_start, q0, q1, kv0, kv1 = pre(source_rows[:, 0], flow.results["source"], w_enc_qkv, w_enc_qkv_got)
    got0, got1 = at.core_swap(kv0), at.core_swap(kv1)
    enc_o0, enc_kept0 = attend(q0, kv0, got0, source_hot, source_hot)
    flow.add("w_enc", gathered(at, w_enc, 2, 1))
    enc_o0, q1, kv1, got1, w_cross = flow.step((enc_o0, q1, kv1, got1, w_cross))
    enc_o1, enc_kept1 = attend(q1, kv1, got1, source_hot, source_hot)
    (enc_o1,) = flow.step((enc_o1,))

    w_dec_self_got = flow.results["w_dec_self"]
    dec_start, q0, q1, kv0, kv1 = pre(target_rows[:, 0], flow.results["target"], w_dec_self, w_dec_self_got)
    got0, got1 = at.core_swap(kv0), at.core_swap(kv1)
    self_o0, self_kept0 = attend(q0, kv0, got0, target_hot, target_hot, True)
    flow.add("w_cross", gathered(at, w_cross))
    self_o0, q1, kv1, got1 = flow.step((self_o0, q1, kv1, got1))
    self_o1, self_kept1 = attend(q1, kv1, got1, target_hot, target_hot, True)
    flow.add("w_dec", gathered(at, w_dec, 3, 1))
    self_o1, enc_o1 = flow.step((self_o1, enc_o1))
    w_enc_got = flow.results["w_enc"]
    enc_sum_one, enc_sum_two, enc_states = rows_call(
        enc_post_kernel, "encoder_feed", at.core, [enc_o0, enc_o1, enc_start, runs],
        [w_enc, *w_enc_got, small_enc], [row, row, row_low], scratch=[(w_enc.shape, BF)],
    )
    flow.add("cots", moved(at, cots, 3))
    (enc_states,) = flow.step((enc_states,))
    w_cross_got = flow.results["w_cross"]
    self_proj = [(w_dec_self, HALF, 3)] + [(w, HALF, 1) for w in w_dec_self_got]
    dec_sum_one, q0, q1, kv0, kv1 = rows_call(
        dec_mid_kernel, "cross_project", at.core, [self_o0, self_o1, dec_start, enc_states],
        [*self_proj, w_cross, *w_cross_got, small_dec],
        [row, half_low, half_low, kv_low, kv_low], scratch=[(w_cross.shape, BF)],
    )
    got0, got1 = at.core_swap(kv0), at.core_swap(kv1)
    q0, q1, kv0, kv1 = flow.step((q0, q1, kv0, kv1))
    cross_o0, cross_kept0 = attend(q0, kv0, got0, target_hot, source_hot)
    cross_o0, q1, kv1, got1 = flow.step((cross_o0, q1, kv1, got1))
    cross_o1, cross_kept1 = attend(q1, kv1, got1, target_hot, source_hot)
    flow.add("enc_states", moved(at, enc_states, 1))
    (cross_o1,) = flow.step((cross_o1,))
    cots = jnp.where(at.stays, cots, flow.results["cots"])
    enc_cot, dec_cot = cots[:, :D], cots[:, D:]

    def grad_outs(rows):
        return [((2, rows // 2, D), BF)] * 2 + [((8, D), F32)]

    def grad_scratch(rows):
        return [((2, rows, D), F32), ((8, D), F32)]

    w_dec_got = flow.results["w_dec"]
    (
        dec_states, start_grad, sum_grad, o0_grad, o1_grad, *dec_parts, small_two,
    ) = rows_call(
        dec_post_kernel, "decoder_feed", at.core,
        [cross_o0, cross_o1, dec_sum_one, dec_start, runs, dec_cot], [w_dec, *w_dec_got, small_dec],
        [row_low, row, row, half_low, half_low], grad_outs(9 * HALF),
        [*grad_scratch(9 * HALF), (w_dec.shape, BF), ((2, 512, 4 * D), BF)],
    )
    flow.add("dec", summed(at, *dec_parts))
    flow.add("dec_states", moved(at, dec_states, 1))
    o0_grad, o1_grad = flow.step((o0_grad, o1_grad))

    q0_grad, kv0_grad, kv0_send = attend_back(cross_kept0, o0_grad)
    q0_grad, kv0_grad, kv0_send, o1_grad = flow.step((q0_grad, kv0_grad, kv0_send, o1_grad))
    kv0_got = at.core_swap(kv0_send)
    q1_grad, kv1_grad, kv1_send = attend_back(cross_kept1, o1_grad)
    q1_grad, kv1_grad, kv1_send, kv0_got = flow.step((q1_grad, kv1_grad, kv1_send, kv0_got))
    kv1_got = at.core_swap(kv1_send)

    (
        enc_base, enc_o0_grad, enc_o1_grad, *enc_parts, small_enc_grad,
    ) = rows_call(
        enc_back_kernel, "encoder_feed_back", at.core,
        [kv0_grad, kv1_grad, kv0_got, kv1_got, enc_states, enc_cot, enc_start, enc_sum_one, enc_sum_two,
         enc_o0, enc_o1, runs],
        [w_cross, *w_cross_got, w_enc, *w_enc_got, small_enc],
        [row, half_low, half_low], grad_outs(11 * HALF),
        [*grad_scratch(11 * HALF), (w_cross.shape, BF), (w_enc.shape, BF)],
    )
    flow.add("enc", summed(at, *enc_parts, (1, 1, 2)))
    enc_o0_grad, enc_o1_grad, q0_grad = flow.step((enc_o0_grad, enc_o1_grad, q0_grad))
    (
        dec_base, self_o0_grad, self_o1_grad, *mid_parts, small_one,
    ) = rows_call(
        dec_mid_back_kernel, "cross_project_back", at.core,
        [q0_grad, q1_grad, sum_grad, dec_sum_one, start_grad, self_o0, self_o1],
        [(w_cross, HALF, 0), *w_cross_got, *self_proj, small_dec],
        [row, half_low, half_low], grad_outs(2 * HALF), grad_scratch(2 * HALF),
    )
    smalls = jnp.concatenate([small_enc_grad, small_one, small_two, jnp.zeros((8, D), F32)])
    enc_o1_grad, mid_parts, smalls = flow.step((enc_o1_grad, mid_parts, smalls))

    q1_grad, kv1_grad, kv1_send = attend_back(enc_kept1, enc_o1_grad)
    q1_grad, kv1_grad, kv1_send, enc_o0_grad = flow.step((q1_grad, kv1_grad, kv1_send, enc_o0_grad))
    kv1_got = at.core_swap(kv1_send)
    q0_grad, kv0_grad, kv0_send = attend_back(enc_kept0, enc_o0_grad)
    q0_grad, kv0_grad, kv0_send, kv1_got = flow.step((q0_grad, kv0_grad, kv0_send, kv1_got))
    kv0_got = at.core_swap(kv0_send)
    source_grad, source_low, keep, send = rows_call(
        both_qkv_back_kernel, "project_back", at.core,
        [q0_grad, kv0_grad, kv0_got, q1_grad, kv1_grad, kv1_got, enc_start, enc_base],
        [w_enc_qkv, *w_enc_qkv_got, *mid_parts, smalls], [row, row_low], [((2, 3 * HALF, D), BF)] * 2,
        [((2, 3 * HALF, D), F32), (w_enc_qkv.shape, BF)],
    )
    flow.add("enc_qkv", summed(at, keep, send))
    flow.add("source_grad", moved(at, source_low, 1))
    self_o1_grad, source_grad = flow.step((self_o1_grad, source_grad))

    def heads_back(kept, grad):
        q_grad, kv_grad, kv_send = attend_back(kept, grad, True)
        q_grad, kv_grad, kv_send = flow.step((q_grad, kv_grad, kv_send))
        return q_grad, kv_grad, at.core_swap(kv_send)

    parts = heads_back(self_kept1, self_o1_grad)
    part_outs = [((1, 3 * HALF // 2, D), BF)] * 2
    part_scratch = [((1, 3 * HALF, D), F32)]
    target_grad, _, keep1, send1 = rows_call(
        other_qkv_back_kernel, "project_back", at.core, [*parts, dec_start, dec_base],
        [*w_dec_self_got], [row, row_low], part_outs, [*part_scratch, (w_dec_self.shape, BF)],
    )
    flow.add("dec_qkv_other", summed_other(at, keep1, at.core_swap(send1), 1))
    target_grad, self_o0_grad = flow.step((target_grad, self_o0_grad))
    parts = heads_back(self_kept0, self_o0_grad)
    target_grad, target_low, keep0, send0 = rows_call(
        own_qkv_back_kernel, "project_back", at.core, [*parts, dec_start, target_grad],
        [(w_dec_self, 3 * HALF, 0)], [row, row_low], part_outs, part_scratch,
    )
    flow.add("dec_qkv", summed_own(at, keep0, send0, flow.results["dec_qkv_other"]))
    flow.add("target_grad", moved(at, target_low, 4))

    done = flow.results

    def weights(name, *weights):
        places, begin = [], 0
        for i, weight in enumerate(weights):
            places.append((i, begin, 0, weight.size // D))
            begin += weight.size // D
        return unpack(at.order, *done[name], [w.shape for w in weights], places)

    def home(values, name):
        values = jnp.where(at.stays, values, done[name].astype(values.dtype))[:, None]
        return with_layout_constraint(values, Layout((0, 1, 2))) if values.dtype == F32 else values

    def mixed_weights(name):
        part, more = 3 * HALF // 2, HALF // 2
        places = []
        for c in range(2):
            begin = c * 3 * HALF
            places += [(0, begin, c * part, part), (1 + c, begin + part, 0, 2 * more)]
        after = part + 2 * more
        one, two = after + 8, 3 * HALF + after
        for out, rows in (
            (3, (after, after + 2)),
            (4, (after + 1, after + 3)),
            (5, (one, two, two + 2)),
            (6, (one + 1, two + 1, two + 3)),
            (7, (after + 4, two + 4)),
        ):
            places += [(out, row, at_row, 1) for at_row, row in enumerate(rows)]
        shapes = [enc_qkv.shape, cross_query.shape, dec_proj.shape, (2, D), (2, D), (3, D), (3, D), (2, D)]
        return unpack(at.order, *done[name], shapes, places)

    target_grad, done["dec"] = flow.step((target_grad, done["dec"]))
    dec_grads = weights("dec", cross_proj, dec_up, dec_down)
    dec_grads, source_grad = flow.step((dec_grads, source_grad))
    source_out = home(source_grad, "source_grad")
    (source_out,) = flow.step((source_out,))
    enc_grads = weights("enc", cross_kv, enc_proj, enc_up, enc_down)
    enc_grads, enc_states, dec_states = flow.step((enc_grads, enc_states, dec_states))
    states_out = home(enc_states, "enc_states"), home(dec_states, "dec_states")
    states_out, target_grad = flow.step((states_out, target_grad))
    target_out = home(target_grad, "target_grad")
    (target_out,) = flow.step((target_out,))
    (target_out,) = flow.step((target_out,))
    mixed_grads = mixed_weights("enc_qkv")
    (mixed_grads,) = flow.step((mixed_grads,))
    flow.finish()
    cross_proj_grad, dec_up_grad, dec_down_grad = dec_grads
    cross_kv_grad, enc_proj_grad, enc_up_grad, enc_down_grad = enc_grads
    enc_qkv_grad, cross_query_grad, dec_proj_grad, *small_grads = mixed_grads
    (dec_qkv_grad,) = weights("dec_qkv", dec_qkv)
    enc_gains_grad, enc_shifts_grad, dec_gains_grad, dec_shifts_grad, halt_grad = small_grads
    return (
        *states_out,
        source_out,
        target_out,
        enc_qkv_grad,
        enc_proj_grad,
        enc_up_grad,
        enc_down_grad,
        enc_gains_grad,
        enc_shifts_grad,
        dec_qkv_grad,
        dec_proj_grad,
        cross_query_grad,
        cross_kv_grad,
        cross_proj_grad,
        dec_up_grad,
        dec_down_grad,
        dec_gains_grad,
        dec_shifts_grad,
        halt_grad,
    )


def solution(mesh):
    dp_size, mp_size = mesh.shape["dp"], mesh.shape["mp"]
    by_chip = mp_size == 2 and dp_size in (4, 8, 16)
    body = partial(chip_rows, dp_size=dp_size) if by_chip else local
    return jax.shard_map(
        body,
        mesh=mesh,
        in_specs=(
            P("mp", "dp", None),
            P("mp", "dp", None),
            P("dp", None),
            P("dp", None),
            P(None, "dp", "mp"),
            P(None, None, "mp"),
            P("mp", None),
            P(None, "mp"),
            P("mp", None),
            P(),
            P(),
            P(None, None, "mp"),
            P("mp", None),
            P(None, "mp"),
            P(None, None, "mp"),
            P("mp", None),
            P(None, "mp"),
            P("mp", None),
            P(),
            P(),
            P(),
            P("mp", "dp", None),
            P("mp", "dp", None),
        ),
        out_specs=(
            P("mp", "dp", None),
            P("mp", "dp", None),
            P("mp", "dp", None),
            P("mp", "dp", None),
            P(None, None, "mp"),
            P("mp", None),
            P(None, "mp"),
            P("mp", None),
            P(),
            P(),
            P(None, None, "mp"),
            P("mp", None),
            P(None, "mp"),
            P(None, None, "mp"),
            P("mp", None),
            P(None, "mp"),
            P("mp", None),
            P(),
            P(),
            P(),
        ),
        check_vma=False,
    )
```
